32 devices in a mesh: dp: 4 (over z), seq: 8 (over y, x, core).
Axes of the slice: x: 2, y: 2, z: 4, core: 2. Of those that a mesh axis runs over, the one named last changes fastest.
Arguments:
- inputs: bfloat16 [12, 1152, 1024], P('dp', 'seq'), may hold values from -6 to 6
- doc_lengths: int32 [12, 4], P('dp'), may hold values from 1 to 1080, 1152 in all within a row
- gain_attn: float32 [1024], replicated, may hold values from 0.25 to 1.75
- w_query: bfloat16 [1024, 256], replicated, may hold values from -0.1875 to 0.1875
- w_key: bfloat16 [1024, 256], replicated, may hold values from -0.1875 to 0.1875
- w_value: bfloat16 [1024, 1024], replicated, may hold values from -0.1875 to 0.1875
- w_out: bfloat16 [1024, 1024], replicated, may hold values from -1 to 1
- gain_ffn: float32 [1024], replicated, may hold values from 0.25 to 1.75
- w_gate: bfloat16 [1024, 2752], replicated, may hold values from -0.1875 to 0.1875
- w_up: bfloat16 [1024, 2752], replicated, may hold values from -0.1875 to 0.1875
- w_down: bfloat16 [2752, 1024], replicated, may hold values from -0.109375 to 0.109375
- cotangent: bfloat16 [12, 1152, 1024], P('dp', 'seq'), may hold values from -6 to 6
Outputs:
- output: bfloat16 [12, 1152, 1024], P('dp', 'seq')
- input_grad: bfloat16 [12, 1152, 1024], P('dp', 'seq')
- gain_attn_grad: float32 [1024], P(('dp', 'seq'))
- query_grad: float32 [1024, 256], P(('dp', 'seq'))
- key_grad: float32 [1024, 256], P(('dp', 'seq'))
- value_grad: float32 [1024, 1024], P(('dp', 'seq'))
- out_grad: float32 [1024, 1024], P(('dp', 'seq'))
- gain_ffn_grad: float32 [1024], P(('dp', 'seq'))
- gate_grad: float32 [1024, 2752], P(('dp', 'seq'))
- up_grad: float32 [1024, 2752], P(('dp', 'seq'))
- down_grad: float32 [2752, 1024], P(None, ('dp', 'seq'))
The draws below stay inside these ranges and needn't reach their ends.
Inputs may be any that keep to these rules, and one draw needn't show every extreme that they name: `doc_lengths`: each row's 4 document lengths sum to 1152.
All inputs are finite; a program needn't handle non-finite values.
Results may differ from the reference program's by a relative error of at most 0.01.
Values may be sent and summed in bfloat16 or wider, within the bound.
A program may use at most 256 MiB of HBM per device.

```python
import math
import jax
import jax.numpy as jnp
import numpy as np
from jax import lax

D = 1024
H = 16
F = 16
HV = 64
FF = 2752
SHARD_LEN = 144
DOCS = 4
BLOCK = 576
ROW_LEN = 1152
BATCH = 12


def spiked(result, key, source, target, parts, factor):
    owner, partner = [(jnp.arange(result.shape[position]) // (result.shape[position] // parts)).reshape([-1 if axis == position else 1 for axis in range(result.ndim)]) for position in (source, target)]
    chosen = jax.random.permutation(key, parts)[partner]
    strong = (owner == chosen) | (owner == (partner + parts // 2) % parts)
    return jnp.where(strong, factor * result, result)


def block_scale(rng, dims, cuts, least, high):
    loudness = 1.0
    for position, shards_of in cuts:
        heights = jax.random.uniform(jax.random.fold_in(jax.random.fold_in(rng, 6), position), (shards_of,), jnp.float32, least / len(cuts), high / len(cuts))
        loudness = loudness * jnp.repeat(jnp.exp(heights), dims[position] // shards_of).reshape((-1,) + (1,) * (len(dims) - 1 - position))
    return loudness


def profile(amount, total, bound, skew):
    weights = [(1 << 20) // math.isqrt(rank ** skew) + 1 for rank in range(2, amount + 1)]
    surplus, given = total - bound - (amount - 1), [1] * (amount - 1)
    while surplus > 0:
        candidates = [i for i in range(amount - 1) if given[i] < bound]
        whole, left = sum([weights[i] for i in candidates]), surplus
        for i in candidates:
            extra = min(bound - given[i], max(1, left * weights[i] // whole), surplus)
            given[i] = given[i] + extra
            surplus = surplus - extra
    return np.array([bound] + given)


def uneven_parts(rng, count, total, bound, slope):
    if count == 2:
        one = jax.random.randint(rng, (), max(1, total - bound), min(bound, total - 1) + 1)
        return jnp.stack([one, total - one])
    lengths = jnp.asarray(profile(count, total, bound, slope), jnp.int32)
    twos = (count - 1) // 2
    source_of, receiver = lengths[1:1 + 2 * twos:2], lengths[2:2 + 2 * twos:2]
    room = jnp.minimum(source_of - 1, bound - receiver)
    moved = jax.random.randint(jax.random.fold_in(rng, 1), (twos,), 0, 1 << 20) % (room + 1)
    lengths = lengths.at[1:1 + 2 * twos:2].set(source_of - moved).at[2:2 + 2 * twos:2].set(receiver + moved)
    return lengths[jax.random.permutation(jax.random.fold_in(rng, 2), count)]


def normal_values(rng, dims, scale, reach, shards=(), held_as=jnp.bfloat16):
    values = jax.random.normal(rng, dims, jnp.float32) * scale
    if len(shards) > 0:
        values = block_scale(rng, dims, shards, -0.22, 0.18) * values
    return jnp.clip(values, min=-reach, max=reach).astype(held_as)


def bell_draw_with(key, extent, spread, limit, cuts, heavy, kind=jnp.bfloat16):
    array = spread * jax.random.normal(key, extent, jnp.float32)
    if cuts:
        array = array * block_scale(key, extent, cuts, -0.22, 0.18)
    return jnp.clip(spiked(array, jax.random.fold_in(key, 3), *heavy), -limit, limit).astype(kind)


def setup_inputs(seed: int = 0) -> dict:
    key_of = jax.random.split(jax.random.key(seed), 13)
    return {
        "inputs": normal_values(key_of[0], (BATCH, ROW_LEN, D), 1.0, 6.0, ((0, 4), (1, 8))),
        "doc_lengths": jax.vmap(lambda own: uneven_parts(own, DOCS, ROW_LEN, ROW_LEN - SHARD_LEN // 2, 2))(jax.random.split(key_of[1], BATCH)).reshape((BATCH, DOCS)).astype(jnp.int32),
        "gain_attn": jnp.clip(1.0 + 0.15 * jax.random.normal(key_of[2], (D,), jnp.float32), 0.25, 1.75),
        "w_query": normal_values(key_of[3], (D, H * F), D ** -0.5, 0.1875),
        "w_key": normal_values(key_of[4], (D, H * F), D ** -0.5, 0.1875),
        "w_value": normal_values(key_of[5], (D, D), D ** -0.5, 0.1875),
        "w_out": normal_values(key_of[6], (D, D), (D // 32) ** -0.5, 1.0),
        "gain_ffn": jnp.clip(1.0 + 0.15 * jax.random.normal(key_of[7], (D,), jnp.float32), 0.25, 1.75),
        "w_gate": normal_values(key_of[8], (D, FF), D ** -0.5, 0.1875),
        "w_up": normal_values(key_of[9], (D, FF), D ** -0.5, 0.1875),
        "w_down": normal_values(key_of[10], (FF, D), FF ** -0.5, 0.109375),
        "cotangent": bell_draw_with(key_of[11], (BATCH, ROW_LEN, D), 1.0, 6.0, ((0, 4), (1, 8)), (1, 2, 8, 2.0)),
    }


@jax.custom_vjp
def low(v):
    return lax.optimization_barrier(v.astype(jnp.bfloat16)).astype(jnp.float32)

@jax.custom_vjp
def low_back(v):
    return v

def low_keep(v):
    return (low(v), None)

def low_pass(kept, grad):
    return (grad,)

def back_keep(v):
    return (v, None)

def back_low(kept, grad):
    return (low(grad),)
low.defvjp(low_keep, low_pass)
low_back.defvjp(back_keep, back_low)
eps_norm = 1e-05

def rms_scale(stream, gain_vec):
    return stream * lax.rsqrt(lax.optimization_barrier(jnp.mean(stream * stream, axis=-1, keepdims=True)) + eps_norm) * gain_vec

def taylor_features(vectors):
    feat_width = vectors.shape[-1]
    outer_prod = (vectors[..., :, None] * vectors[..., None, :]).reshape(vectors.shape[:-1] + (feat_width * feat_width,))
    ones_part = jnp.ones(vectors.shape[:-1] + (1,), jnp.float32)
    return jnp.concatenate([ones_part, vectors * feat_width ** (-0.25), outer_prod * (0.5 / feat_width) ** 0.5], axis=-1)

def document_ids(doc_lens, seq_length):
    doc_ends = jnp.cumsum(doc_lens, dtype=jnp.int32)
    positions = jnp.arange(seq_length, dtype=jnp.int32)
    return lax.optimization_barrier(jnp.sum((positions[:, None] >= doc_ends[None, :]).astype(jnp.int32), axis=1, dtype=jnp.int32))

def attend_row(queries, key_proj, value_proj, doc_row, block_rows):
    seq_length, head_count, feat_width = queries.shape
    value_width = value_proj.shape[-1]
    feat_count = 1 + feat_width + feat_width * feat_width
    block_count = seq_length // block_rows
    highest = lax.Precision.HIGHEST
    query_blocks = queries.reshape(block_count, block_rows, head_count, feat_width)
    key_blocks = key_proj.reshape(block_count, block_rows, head_count, feat_width)
    value_blocks = value_proj.reshape(block_count, block_rows, head_count, value_width)
    doc_blocks = doc_row.reshape(block_count, block_rows)
    previous = jnp.concatenate([jnp.full((1,), -1, jnp.int32), doc_blocks[:-1, -1]])
    positions = jnp.arange(block_rows, dtype=jnp.int32)
    causal = positions[:, None] >= positions[None, :]

    def block_step(carried, pieces):
        state_sum, norm_sum = carried
        query_block, key_block, value_block, doc_block, prior_doc = pieces
        scores = jnp.einsum('thf,shf->hts', query_block, key_block, precision=highest) * feat_width ** (-0.5)
        weights = 1.0 + scores + 0.5 * scores * scores
        same_doc = causal & (doc_block[:, None] == doc_block[None, :])
        weights = jnp.where(same_doc[None, :, :], weights, 0.0)
        numerator = jnp.einsum('hts,shv->thv', weights, value_block, precision=highest)
        denominator = jnp.transpose(lax.optimization_barrier(jnp.sum(weights, axis=2)))
        use_state = (doc_block == prior_doc).astype(jnp.float32)[:, None]
        query_feats = taylor_features(query_block)
        numerator = numerator + use_state[:, :, None] * jnp.einsum('thp,hpv->thv', query_feats, state_sum, precision=highest)
        denominator = denominator + use_state * jnp.einsum('thp,hp->th', query_feats, norm_sum, precision=highest)
        last_doc = doc_block[-1]
        keep_state = (last_doc == prior_doc).astype(jnp.float32)
        key_feats = taylor_features(key_block) * (doc_block == last_doc).astype(jnp.float32)[:, None, None]
        state_sum = keep_state * state_sum + jnp.einsum('shp,shv->hpv', key_feats, value_block, precision=highest)
        norm_sum = keep_state * norm_sum + lax.optimization_barrier(jnp.sum(key_feats, axis=0))
        return ((state_sum, norm_sum), numerator / denominator[:, :, None])
    initial = (jnp.zeros((head_count, feat_count, value_width), jnp.float32), jnp.zeros((head_count, feat_count), jnp.float32))
    _, results = lax.scan(jax.checkpoint(block_step), initial, (query_blocks, key_blocks, value_blocks, doc_blocks, previous))
    return results.reshape(seq_length, head_count, value_width)

def layer_row(stream, doc_lens, gain_attn, w_query, w_key, w_value, w_out, gain_ffn, w_gate, w_up, w_down):
    highest = lax.Precision.HIGHEST
    seq_length = stream.shape[0]
    normed = low(rms_scale(stream, gain_attn))
    queries = low(low_back(jnp.dot(normed, w_query, precision=highest)))
    key_proj = low(low_back(jnp.dot(normed, w_key, precision=highest)))
    value_proj = low(low_back(jnp.dot(normed, w_value, precision=highest)))
    doc_row = document_ids(doc_lens, seq_length)
    mixed_out = attend_row(queries.reshape(seq_length, H, F), key_proj.reshape(seq_length, H, F), value_proj.reshape(seq_length, H, HV), doc_row, BLOCK)
    mixed_out = low(low_back(mixed_out.reshape(seq_length, D)))
    branch = low_back(jnp.dot(mixed_out, w_out, precision=highest))
    residual = stream + branch
    normed_ffn = low(rms_scale(residual, gain_ffn))
    gate_proj = low_back(jnp.dot(normed_ffn, w_gate, precision=highest))
    up_proj = low_back(jnp.dot(normed_ffn, w_up, precision=highest))
    hidden = low(jax.nn.silu(gate_proj) * up_proj)
    return residual + jnp.dot(hidden, w_down, precision=highest)

def reference(inputs, doc_lengths, gain_attn, w_query, w_key, w_value, w_out, gain_ffn, w_gate, w_up, w_down, cotangent):
    params = tuple((param.astype(jnp.float32) for param in (gain_attn, w_query, w_key, w_value, w_out, gain_ffn, w_gate, w_up, w_down)))

    def forward(stream, *weights):

        def one_row(pieces):
            return layer_row(pieces[0], pieces[1], *weights)
        return lax.map(jax.checkpoint(one_row), (stream, doc_lengths))
    output, pull_back = jax.vjp(forward, inputs.astype(jnp.float32), *params)
    grads = pull_back(cotangent.astype(jnp.float32))
    return (output.astype(jnp.bfloat16), grads[0].astype(jnp.bfloat16), grads[1], grads[2], grads[3], grads[4], grads[5], grads[6], grads[7], grads[8], grads[9])
```

```python
import functools

import jax
import jax.numpy as jnp
from jax import lax
from jax.experimental import pallas as pl
from jax.experimental.pallas import tpu as pltpu
from jax.sharding import PartitionSpec as P

D = 1024
H = 16
F = 16
HV = 64
BLOCK = 576


eps_norm = 1e-05


def rms_scale(stream, gain_vec):
    return (
        stream * lax.rsqrt(jnp.mean(stream * stream, axis=-1, keepdims=True) + eps_norm) * gain_vec
    )


def taylor_features(vectors):
    feat_width = vectors.shape[-1]
    outer_prod = (vectors[..., :, None] * vectors[..., None, :]).reshape(
        vectors.shape[:-1] + (feat_width * feat_width,)
    )
    ones_part = jnp.ones(vectors.shape[:-1] + (1,), jnp.float32)
    return jnp.concatenate(
        [ones_part, vectors * feat_width ** (-0.25), outer_prod * (0.5 / feat_width) ** 0.5],
        axis=-1,
    )


def document_ids(doc_lens, seq_length):
    doc_ends = jnp.cumsum(doc_lens, dtype=jnp.int32)
    positions = jnp.arange(seq_length, dtype=jnp.int32)
    return jnp.sum(
        (positions[:, None] >= doc_ends[None, :]).astype(jnp.int32), axis=1, dtype=jnp.int32
    )


def attend_row(queries, key_proj, value_proj, doc_row, block_rows):
    seq_length, head_count, feat_width = queries.shape
    value_width = value_proj.shape[-1]
    feat_count = 1 + feat_width + feat_width * feat_width
    block_count = seq_length // block_rows
    highest = lax.Precision.HIGHEST
    query_blocks = queries.reshape(block_count, block_rows, head_count, feat_width)
    key_blocks = key_proj.reshape(block_count, block_rows, head_count, feat_width)
    value_blocks = value_proj.reshape(block_count, block_rows, head_count, value_width)
    doc_blocks = doc_row.reshape(block_count, block_rows)
    previous = jnp.concatenate([jnp.full((1,), -1, jnp.int32), doc_blocks[:-1, -1]])
    positions = jnp.arange(block_rows, dtype=jnp.int32)
    causal = positions[:, None] >= positions[None, :]

    def block_step(carried, pieces):
        state_sum, norm_sum = carried
        query_block, key_block, value_block, doc_block, prior_doc = pieces
        scores = jnp.einsum(
            "thf,shf->hts", query_block, key_block, precision=highest
        ) * feat_width ** (-0.5)
        weights = 1.0 + scores + 0.5 * scores * scores
        same_doc = causal & (doc_block[:, None] == doc_block[None, :])
        weights = jnp.where(same_doc[None, :, :], weights, 0.0)
        numerator = jnp.einsum("hts,shv->thv", weights, value_block, precision=highest)
        denominator = jnp.transpose(jnp.sum(weights, axis=2))
        use_state = (doc_block == prior_doc).astype(jnp.float32)[:, None]
        query_feats = taylor_features(query_block)
        numerator = numerator + use_state[:, :, None] * jnp.einsum(
            "thp,hpv->thv", query_feats, state_sum, precision=highest
        )
        denominator = denominator + use_state * jnp.einsum(
            "thp,hp->th", query_feats, norm_sum, precision=highest
        )
        last_doc = doc_block[-1]
        keep_state = (last_doc == prior_doc).astype(jnp.float32)
        key_feats = (
            taylor_features(key_block) * (doc_block == last_doc).astype(jnp.float32)[:, None, None]
        )
        state_sum = keep_state * state_sum + jnp.einsum(
            "shp,shv->hpv", key_feats, value_block, precision=highest
        )
        norm_sum = keep_state * norm_sum + jnp.sum(key_feats, axis=0)
        return ((state_sum, norm_sum), numerator / denominator[:, :, None])

    initial = (
        jnp.zeros((head_count, feat_count, value_width), jnp.float32),
        jnp.zeros((head_count, feat_count), jnp.float32),
    )
    _, results = lax.scan(
        jax.checkpoint(block_step),
        initial,
        (query_blocks, key_blocks, value_blocks, doc_blocks, previous),
    )
    return results.reshape(seq_length, head_count, value_width)


def project(left, right):
    return jnp.dot(left, right, preferred_element_type=jnp.float32)


def back_project(left, right):
    return lax.dot_general(
        left, right, (((1,), (1,)), ((), ())), preferred_element_type=jnp.float32
    )


def weight_grad(left, right):
    return lax.dot_general(
        left, right, (((0,), (0,)), ((), ())), preferred_element_type=jnp.float32
    )


def swiglu(gate_proj, up_proj):
    return jax.nn.silu(gate_proj) * up_proj


def general_body(
    inputs,
    doc_lengths,
    gain_attn,
    w_query,
    w_key,
    w_value,
    w_out,
    gain_ffn,
    w_gate,
    w_up,
    w_down,
    cotangent,
):
    row_count, shard_len, _ = inputs.shape
    token_count = row_count * shard_len
    stream = inputs.reshape(token_count, D).astype(jnp.float32)
    normed, attn_norm_back = jax.vjp(rms_scale, stream, gain_attn)
    normed_low = normed.astype(jnp.bfloat16)
    query_proj = project(normed_low, w_query).astype(jnp.bfloat16)
    key_proj = project(normed_low, w_key).astype(jnp.bfloat16)
    value_proj = project(normed_low, w_value).astype(jnp.bfloat16)
    query_heads, key_heads, value_heads = (
        lax.all_to_all(
            query_proj.reshape(row_count, shard_len, H, F),
            "seq",
            split_axis=2,
            concat_axis=1,
            tiled=True,
        ),
        lax.all_to_all(
            key_proj.reshape(row_count, shard_len, H, F),
            "seq",
            split_axis=2,
            concat_axis=1,
            tiled=True,
        ),
        lax.all_to_all(
            value_proj.reshape(row_count, shard_len, H, HV),
            "seq",
            split_axis=2,
            concat_axis=1,
            tiled=True,
        ),
    )
    seq_length = query_heads.shape[1]
    doc_rows = jax.vmap(lambda doc_lens: document_ids(doc_lens, seq_length))(doc_lengths)

    def attend_all(queries, keys_in, values_in):
        return jax.vmap(attend_row, in_axes=(0, 0, 0, 0, None))(
            queries, keys_in, values_in, doc_rows, BLOCK
        )

    mixed_heads, attend_back = jax.vjp(
        attend_all,
        query_heads.astype(jnp.float32),
        key_heads.astype(jnp.float32),
        value_heads.astype(jnp.float32),
    )
    mixed_rows = lax.all_to_all(
        mixed_heads.astype(jnp.bfloat16), "seq", split_axis=1, concat_axis=2, tiled=True
    )
    mixed_flat = mixed_rows.reshape(token_count, D)
    residual = stream + project(mixed_flat, w_out)
    normed_ffn, ffn_norm_back = jax.vjp(rms_scale, residual, gain_ffn)
    ffn_low = normed_ffn.astype(jnp.bfloat16)
    gate_proj = project(ffn_low, w_gate)
    up_proj = project(ffn_low, w_up)
    hidden, act_back = jax.vjp(swiglu, gate_proj, up_proj)
    hidden_low = hidden.astype(jnp.bfloat16)
    output = residual + project(hidden_low, w_down)
    grad_out = cotangent.reshape(token_count, D)
    grad_gate, grad_up = act_back(back_project(grad_out, w_down))
    grad_gate_low = grad_gate.astype(jnp.bfloat16)
    grad_up_low = grad_up.astype(jnp.bfloat16)
    down_grad_t = weight_grad(grad_out, hidden_low)
    gate_grad = weight_grad(ffn_low, grad_gate_low)
    up_grad = weight_grad(ffn_low, grad_up_low)
    grad_normed_ffn = back_project(grad_gate_low, w_gate) + back_project(grad_up_low, w_up)
    grad_residual, gain_ffn_grad = ffn_norm_back(grad_normed_ffn)
    grad_residual = grad_residual + grad_out.astype(jnp.float32)
    grad_branch = grad_residual.astype(jnp.bfloat16)
    out_grad = weight_grad(mixed_flat, grad_branch)
    grad_mixed = (
        back_project(grad_branch, w_out).astype(jnp.bfloat16).reshape(row_count, shard_len, H, HV)
    )
    grad_heads = lax.all_to_all(grad_mixed, "seq", split_axis=2, concat_axis=1, tiled=True)
    grad_query, grad_key, grad_value = attend_back(grad_heads.astype(jnp.float32))
    back_query, back_key, back_value = (
        lax.all_to_all(
            grad_query.astype(jnp.bfloat16), "seq", split_axis=1, concat_axis=2, tiled=True
        ),
        lax.all_to_all(
            grad_key.astype(jnp.bfloat16), "seq", split_axis=1, concat_axis=2, tiled=True
        ),
        lax.all_to_all(
            grad_value.astype(jnp.bfloat16), "seq", split_axis=1, concat_axis=2, tiled=True
        ),
    )
    back_query = back_query.reshape(token_count, H * F)
    back_key = back_key.reshape(token_count, H * F)
    back_value = back_value.reshape(token_count, D)
    query_grad = weight_grad(normed_low, back_query)
    key_grad = weight_grad(normed_low, back_key)
    value_grad = weight_grad(normed_low, back_value)
    grad_normed = (
        back_project(back_query, w_query)
        + back_project(back_key, w_key)
        + back_project(back_value, w_value)
    )
    grad_stream, gain_attn_grad = attn_norm_back(grad_normed)
    input_grad = grad_residual + grad_stream
    (
        gain_attn_part,
        query_part,
        key_part,
        value_part,
        out_part,
        gain_ffn_part,
        gate_part,
        up_part,
        down_part,
    ) = (
        lax.psum_scatter(gain_attn_grad, ("dp", "seq"), scatter_dimension=0, tiled=True),
        lax.psum_scatter(query_grad, ("dp", "seq"), scatter_dimension=0, tiled=True),
        lax.psum_scatter(key_grad, ("dp", "seq"), scatter_dimension=0, tiled=True),
        lax.psum_scatter(value_grad, ("dp", "seq"), scatter_dimension=0, tiled=True),
        lax.psum_scatter(out_grad, ("dp", "seq"), scatter_dimension=0, tiled=True),
        lax.psum_scatter(gain_ffn_grad, ("dp", "seq"), scatter_dimension=0, tiled=True),
        lax.psum_scatter(gate_grad, ("dp", "seq"), scatter_dimension=0, tiled=True),
        lax.psum_scatter(up_grad, ("dp", "seq"), scatter_dimension=0, tiled=True),
        lax.psum_scatter(down_grad_t, ("dp", "seq"), scatter_dimension=0, tiled=True),
    )
    return (
        output.reshape(row_count, shard_len, D).astype(jnp.bfloat16),
        input_grad.reshape(row_count, shard_len, D).astype(jnp.bfloat16),
        gain_attn_part,
        query_part,
        key_part,
        value_part,
        out_part,
        gain_ffn_part,
        gate_part,
        up_part,
        jnp.transpose(down_part),
    )


F32 = jnp.float32
BF16 = jnp.bfloat16
MESH = pl.DeviceIdType.MESH
TILE = 384
PAIR = 2 * HV


def nt(left, right):
    return lax.dot_general(left, right, (((1,), (1,)), ((), ())), preferred_element_type=F32)


def nn(left, right):
    return jnp.dot(left, right, preferred_element_type=F32)


def lanes_of(shape):
    return lax.broadcasted_iota(jnp.int32, shape, len(shape) - 1)


def first_visible(ends, positions):
    start = jnp.zeros_like(positions)
    for end in ends:
        start = jnp.where(positions >= end, end, start)
    return start


def row_ends(doc_ref, row):
    ends, total = [], 0
    for j in range(doc_ref.shape[1] - 1):
        total = total + doc_ref[row, j]
        ends.append(total)
    return ends


def spread_matrix():
    half = H * F
    shape = (2 * half, (H // 2) * 128)
    source = lax.broadcasted_iota(jnp.int32, shape, 0)
    column = lax.broadcasted_iota(jnp.int32, shape, 1)
    pair, lane = column // 128, column % 64
    wanted = pair * 32 + lane + jnp.where(lane < 32, 0, half - 32)
    return jnp.where(source == wanted, 1.0, 0.0).astype(BF16)


def gather_matrix():
    half = H * F
    shape = (2 * half, 2 * half)
    source = lax.broadcasted_iota(jnp.int32, shape, 0)
    column = lax.broadcasted_iota(jnp.int32, shape, 1)
    pair, lane = source // 64, source % 64
    wanted = pair * 32 + lane + jnp.where(lane < 32, 0, half - 32)
    return jnp.where(column == wanted, 1.0, 0.0).astype(BF16)


def packed_rows(length):
    return (length // 2 + 15) // 16 * 16


def prepare_row(got_ref, row, qa_ref, ka_ref, ve_ref, seq_devices, length):
    low = packed_rows(length)

    def part(peer, carry):
        values = got_ref[row, peer, :length, :].astype(F32)
        packed = got_ref[row, peer, length : length + low, :].astype(F32)
        turned = pltpu.roll(packed, 64, 1)
        both = jnp.concatenate([packed, turned[2 * low - length :]], axis=0)
        lane = lanes_of((length, 128))
        keys = pltpu.roll(both, 96, 1)
        at = pl.ds(pl.multiple_of(peer * length, 16), length)
        one = jnp.where(lane == 32, 1.0, 0.0)
        qa_ref[at, :] = jnp.where(lane < 32, both * 0.25, one).astype(BF16)
        ka_ref[0, at, :] = jnp.where(lane < 16, keys, one).astype(BF16)
        ka_ref[1, at, :] = jnp.where((lane >= 16) & (lane < 32), keys, one).astype(BF16)
        ve_ref[0, at, :] = jnp.where(lane < 64, values, 1.0).astype(BF16)
        ve_ref[1, at, :] = jnp.where(lane >= 64, values, 1.0).astype(BF16)
        return carry

    lax.fori_loop(0, seq_devices, part, 0)


def attend_forward(ends, qa_ref, ka_ref, ve_ref, mixed_ref, inverse_ref):
    length = qa_ref.shape[0]
    for block in range(length // TILE):
        reach = (block + 1) * TILE
        at = pl.ds(block * TILE, TILE)
        queries = qa_ref[at, :]
        t = lax.broadcasted_iota(jnp.int32, (TILE, 1), 0) + block * TILE
        start = first_visible(ends, t)
        s = lax.broadcasted_iota(jnp.int32, (TILE, reach), 1)
        visible = (s >= start) & (s <= t)
        sums = []
        for head in range(2):
            base = nt(queries, ka_ref[head, :reach, :])
            weights = jnp.where(visible, base * base + 1.0, 0.0).astype(BF16)
            sums.append(nn(weights, ve_ref[head, :reach, :]))
        lower = lanes_of((TILE, 128)) < 64
        numerator = jnp.where(lower, sums[0], sums[1])
        inverse = 1.0 / pltpu.roll(jnp.where(lower, sums[1], sums[0]), 64, 1)
        mixed_ref[at, :] = (numerator * inverse).astype(BF16)
        inverse_ref[at, :] = inverse


def attend_backward(
    ends, grad_ref, qa_ref, ka_ref, ve_ref, mixed_ref, inverse_ref, dn_ref, qs_ref, kt_ref, dqt_ref, gqk_ref, gv_ref
):
    length = qa_ref.shape[0]
    lane = lanes_of((length, 128))
    lower = lane < 64
    scaled = grad_ref[...].astype(F32) * inverse_ref[...]
    away = pltpu.roll(-scaled * mixed_ref[...].astype(F32), 64, 1)
    dn_ref[0] = jnp.where(lower, scaled, away).astype(BF16)
    dn_ref[1] = jnp.where(lower, away, scaled).astype(BF16)
    shifted = pltpu.roll(qa_ref[...].astype(F32), 32, 1)
    qs_ref[...] = jnp.where((lane >= 32) & (lane < 64), shifted * 2.0, 0.0).astype(BF16)
    for head in range(2):
        kt_ref[head] = ka_ref[head].astype(F32).T[:32].astype(BF16)
    dqt_ref[...] = jnp.zeros_like(dqt_ref)
    for block in range(length // TILE):
        first = block * TILE
        at = pl.ds(first, TILE)
        rest = pl.ds(first, length - first)
        shape = (TILE, length - first)
        t = lax.broadcasted_iota(jnp.int32, (1, shape[1]), 1) + first
        s = lax.broadcasted_iota(jnp.int32, shape, 0) + first
        visible = (s >= first_visible(ends, t)) & (s <= t)
        value_sums, key_sums = [], []
        for head in range(2):
            base = nt(ka_ref[head, at, :], qa_ref[rest, :])
            grad_weights = nt(ve_ref[head, at, :], dn_ref[head, rest, :])
            weights = jnp.where(visible, base * base + 1.0, 0.0).astype(BF16)
            grad_base = jnp.where(visible, grad_weights * base, 0.0).astype(BF16)
            value_sums.append(nn(weights, dn_ref[head, rest, :]))
            key_sums.append(nn(grad_base, qs_ref[rest, :]))
            dqt_ref[:, rest] += nn(kt_ref[head, :, at], grad_base)
        lane = lanes_of((TILE, 128))
        gv_ref[at, :] = jnp.where(lane < 64, value_sums[0], value_sums[1]).astype(BF16)
        gqk_ref[at, :] = jnp.where(
            (lane >= 32) & (lane < 48), key_sums[0], jnp.where((lane >= 48) & (lane < 64), key_sums[1], 0.0)
        )
    queries = jnp.concatenate([dqt_ref[...] * 0.5, jnp.zeros((96, length), F32)], axis=0)
    gqk_ref[...] += queries.T


def greet(seq_devices):
    row_group, me = lax.axis_index("dp"), lax.axis_index("seq")
    barrier = pltpu.get_barrier_semaphore()
    for step in range(1, seq_devices):
        peer = lax.rem(me + step, seq_devices)
        pl.semaphore_signal(barrier, inc=1, device_id=(row_group, peer), device_id_type=MESH)
    pl.semaphore_wait(barrier, seq_devices - 1)
    return row_group, me


def sending(source, target, send_sem, recv_sem, row_group, peer):
    return pltpu.make_async_remote_copy(
        src_ref=source,
        dst_ref=target,
        send_sem=send_sem,
        recv_sem=recv_sem,
        device_id=(row_group, peer),
        device_id_type=MESH,
    )


def forward_kernel(
    seq_devices, rows, length,
    x_ref, doc_ref, gain_ref, wq_ref, wk_ref, wv_ref,
    branch_ref, got_out, head_out, inverse_ref,
    out_buf, got, heads, back, spread, qa, ka, ve, send_a, recv_a, send_b, recv_b,
):
    row_group, me = greet(seq_devices)
    low = packed_rows(length)
    lower = lanes_of((low, 128)) < 64
    spread[...] = spread_matrix()

    def outgoing(row, step):
        peer = lax.rem(me + step, seq_devices)
        return sending(
            out_buf.at[row, peer], got.at[row, me], send_a.at[row, step], recv_a.at[row, step], row_group, peer
        )

    def returning(row, step):
        peer = lax.rem(me + step, seq_devices)
        there = pl.ds(pl.multiple_of(peer * length, 16), length)
        mine = pl.ds(pl.multiple_of(me * PAIR, 128), PAIR)
        return sending(
            heads.at[row, there, :], back.at[row, :, mine], send_b.at[row, step], recv_b.at[row, step], row_group, peer
        )

    def project_row(row, carry):
        stream = x_ref[row].astype(F32)
        normed = rms_scale(stream, gain_ref[...]).astype(BF16)
        both = jnp.concatenate([nn(normed, wq_ref[...]), nn(normed, wk_ref[...])], axis=1).astype(BF16)
        tiles = nn(both, spread[...])
        values = nn(normed, wv_ref[...]).astype(BF16)
        for pair in range(seq_devices):
            tile = tiles[:, pair * 128 : (pair + 1) * 128]
            out_buf[row, pair, :length, :] = values[:, pair * PAIR : (pair + 1) * PAIR]
            out_buf[row, pair, length:, :] = jnp.where(lower, tile[:low], tile[length - low :]).astype(BF16)
        for step in range(1, seq_devices):
            outgoing(row, step).start()
        got[row, me] = out_buf[row, me]
        return carry

    lax.fori_loop(0, rows, project_row, 0)

    def attend(row, carry):
        for step in range(1, seq_devices):
            outgoing(row, step).wait_recv()
        prepare_row(got, row, qa, ka, ve, seq_devices, length)
        attend_forward(row_ends(doc_ref, row), qa, ka, ve, heads.at[row], inverse_ref.at[row])
        for step in range(1, seq_devices):
            returning(row, step).start()
        here = pl.ds(pl.multiple_of(me * length, 16), length)
        back[row, :, pl.ds(pl.multiple_of(me * PAIR, 128), PAIR)] = heads[row, here, :]
        return carry

    lax.fori_loop(0, rows, attend, 0)
    got_out[...] = got[...]
    head_out[...] = heads[...]

    def finish(row, carry):
        for step in range(1, seq_devices):
            outgoing(row, step).wait_send()
            returning(row, step).wait()
        branch_ref[row] = back[row]
        return carry

    lax.fori_loop(0, rows, finish, 0)


def backward_kernel(
    seq_devices, rows, length,
    grad_ref, doc_ref, got, heads, inverse_ref,
    gqk_out, gv_out,
    arrived, out_buf, back, gather, qa, ka, ve, dn, qs, kt, dqt, gqk, gv, send_a, recv_a, send_b, recv_b,
):
    row_group, me = greet(seq_devices)
    low = packed_rows(length)
    lower = lanes_of((low, 128)) < 64
    here = pl.ds(pl.multiple_of(me * length, 16), length)

    def outgoing(row, step):
        peer = lax.rem(me + step, seq_devices)
        theirs = pl.ds(pl.multiple_of(peer * PAIR, 128), PAIR)
        return sending(
            grad_ref.at[row, :, theirs], arrived.at[row, here, :], send_a.at[row, step], recv_a.at[row, step],
            row_group, peer,
        )

    def returning(row, step):
        peer = lax.rem(me + step, seq_devices)
        return sending(
            out_buf.at[row, peer], back.at[row, me], send_b.at[row, step], recv_b.at[row, step], row_group, peer
        )

    def send_row(row, carry):
        for step in range(1, seq_devices):
            outgoing(row, step).start()
        arrived[row, here, :] = grad_ref[row, :, pl.ds(pl.multiple_of(me * PAIR, 128), PAIR)]
        return carry

    lax.fori_loop(0, rows, send_row, 0)
    gather[...] = gather_matrix()

    def attend(row, carry):
        prepare_row(got, row, qa, ka, ve, seq_devices, length)
        for step in range(1, seq_devices):
            outgoing(row, step).wait_recv()
        attend_backward(
            row_ends(doc_ref, row), arrived.at[row], qa, ka, ve, heads.at[row], inverse_ref.at[row],
            dn, qs, kt, dqt, gqk, gv,
        )

        def pack(peer, inner):
            at = pl.multiple_of(peer * length, 16)
            out_buf[row, peer, :length, :] = gv[pl.ds(at, length), :]
            first = gqk[pl.ds(at, low), :]
            second = pltpu.roll(gqk[pl.ds(at + length - low, low), :], 64, 1)
            out_buf[row, peer, length:, :] = jnp.where(lower, first, second).astype(BF16)
            return inner

        lax.fori_loop(0, seq_devices, pack, 0)
        for step in range(1, seq_devices):
            returning(row, step).start()
        back[row, me] = out_buf[row, me]
        return carry

    lax.fori_loop(0, rows, attend, 0)

    def finish(row, carry):
        for step in range(1, seq_devices):
            outgoing(row, step).wait_send()
            returning(row, step).wait()
        tiles = []
        for pair in range(0, seq_devices, 2):
            halves = []
            for one in (pair, pair + 1):
                packed = back[row, one, length:, :].astype(F32)
                turned = pltpu.roll(packed, 64, 1)
                if one == pair:
                    halves.append(jnp.concatenate([packed, turned[2 * low - length :]], axis=0))
                else:
                    halves.append(jnp.concatenate([turned, packed[2 * low - length :]], axis=0))
            tiles.append(jnp.where(lanes_of((length, 128)) < 64, halves[0], halves[1]).astype(BF16))
        gqk_out[row] = nn(jnp.concatenate(tiles, axis=1), gather[...]).astype(BF16)
        for pair in range(seq_devices):
            gv_out[row, :, pair * PAIR : (pair + 1) * PAIR] = back[row, pair, :length, :]
        return carry

    lax.fori_loop(0, rows, finish, 0)


VMEM_SPEC = pl.BlockSpec(memory_space=pltpu.VMEM)
SMEM_SPEC = pl.BlockSpec(memory_space=pltpu.SMEM)


def attention_forward(seq_devices, x, doc_lengths, gain, w_query, w_key, w_value):
    rows, length, _ = x.shape
    total = seq_devices * length
    message = (rows, seq_devices, length + packed_rows(length), 128)
    sems = pltpu.SemaphoreType.DMA((rows, seq_devices))
    return pl.pallas_call(
        functools.partial(forward_kernel, seq_devices, rows, length),
        name="attention_forward",
        out_shape=[
            jax.ShapeDtypeStruct((rows, length, D), BF16),
            jax.ShapeDtypeStruct(message, BF16),
            jax.ShapeDtypeStruct((rows, total, 128), BF16),
            jax.ShapeDtypeStruct((rows, total, 128), F32),
        ],
        in_specs=[VMEM_SPEC, SMEM_SPEC, VMEM_SPEC, VMEM_SPEC, VMEM_SPEC, VMEM_SPEC],
        out_specs=[VMEM_SPEC] * 4,
        scratch_shapes=[
            pltpu.VMEM(message, BF16),
            pltpu.VMEM(message, BF16),
            pltpu.VMEM((rows, total, 128), BF16),
            pltpu.VMEM((rows, length, D), BF16),
            pltpu.VMEM((2 * H * F, D), BF16),
            pltpu.VMEM((total, 128), BF16),
            pltpu.VMEM((2, total, 128), BF16),
            pltpu.VMEM((2, total, 128), BF16),
            sems, sems, sems, sems,
        ],
        compiler_params=pltpu.CompilerParams(collective_id=0, has_side_effects=True, vmem_limit_bytes=56 << 20),
    )(x, doc_lengths, gain.reshape(1, D), w_query, w_key, w_value)


def attention_backward(seq_devices, grad, doc_lengths, got, heads, inverse):
    rows, length, _ = grad.shape
    total = seq_devices * length
    message = (rows, seq_devices, length + packed_rows(length), 128)
    sems = pltpu.SemaphoreType.DMA((rows, seq_devices))
    return pl.pallas_call(
        functools.partial(backward_kernel, seq_devices, rows, length),
        name="attention_backward",
        out_shape=[
            jax.ShapeDtypeStruct((rows, length, 2 * H * F), BF16),
            jax.ShapeDtypeStruct((rows, length, D), BF16),
        ],
        in_specs=[VMEM_SPEC, SMEM_SPEC, VMEM_SPEC, VMEM_SPEC, VMEM_SPEC],
        out_specs=[VMEM_SPEC] * 2,
        scratch_shapes=[
            pltpu.VMEM((rows, total, 128), BF16),
            pltpu.VMEM(message, BF16),
            pltpu.VMEM(message, BF16),
            pltpu.VMEM((2 * H * F, 2 * H * F), BF16),
            pltpu.VMEM((total, 128), BF16),
            pltpu.VMEM((2, total, 128), BF16),
            pltpu.VMEM((2, total, 128), BF16),
            pltpu.VMEM((2, total, 128), BF16),
            pltpu.VMEM((total, 128), BF16),
            pltpu.VMEM((2, 32, total), BF16),
            pltpu.VMEM((32, total), F32),
            pltpu.VMEM((total, 128), F32),
            pltpu.VMEM((total, 128), BF16),
            sems, sems, sems, sems,
        ],
        compiler_params=pltpu.CompilerParams(collective_id=1, has_side_effects=True, vmem_limit_bytes=56 << 20),
    )(grad, doc_lengths, got, heads, inverse)


def body(
    seq_devices,
    inputs,
    doc_lengths,
    gain_attn,
    w_query,
    w_key,
    w_value,
    w_out,
    gain_ffn,
    w_gate,
    w_up,
    w_down,
    cotangent,
):
    row_count, shard_len, _ = inputs.shape
    token_count = row_count * shard_len
    stream = inputs.reshape(token_count, D).astype(jnp.float32)
    normed, attn_norm_back = jax.vjp(rms_scale, stream, gain_attn)
    normed_low = normed.astype(jnp.bfloat16)
    branch, got, heads, inverse = attention_forward(
        seq_devices, inputs, doc_lengths, gain_attn, w_query, w_key, w_value
    )
    mixed_flat = branch.reshape(token_count, D)
    residual = stream + project(mixed_flat, w_out)
    normed_ffn, ffn_norm_back = jax.vjp(rms_scale, residual, gain_ffn)
    ffn_low = normed_ffn.astype(jnp.bfloat16)
    gate_proj = project(ffn_low, w_gate)
    up_proj = project(ffn_low, w_up)
    hidden, act_back = jax.vjp(swiglu, gate_proj, up_proj)
    hidden_low = hidden.astype(jnp.bfloat16)
    output = residual + project(hidden_low, w_down)
    grad_out = cotangent.reshape(token_count, D)
    grad_gate, grad_up = act_back(back_project(grad_out, w_down))
    grad_gate_low = grad_gate.astype(jnp.bfloat16)
    grad_up_low = grad_up.astype(jnp.bfloat16)
    down_grad_t = weight_grad(grad_out, hidden_low)
    gate_grad = weight_grad(ffn_low, grad_gate_low)
    up_grad = weight_grad(ffn_low, grad_up_low)
    grad_normed_ffn = back_project(grad_gate_low, w_gate) + back_project(grad_up_low, w_up)
    grad_residual, gain_ffn_grad = ffn_norm_back(grad_normed_ffn)
    grad_residual = grad_residual + grad_out.astype(jnp.float32)
    grad_branch = grad_residual.astype(jnp.bfloat16)
    out_grad = weight_grad(mixed_flat, grad_branch)
    grad_mixed = back_project(grad_branch, w_out).astype(jnp.bfloat16)
    back_both, back_value = attention_backward(
        seq_devices, grad_mixed.reshape(row_count, shard_len, D), doc_lengths, got, heads, inverse
    )
    back_query = back_both.reshape(token_count, 2 * H * F)[:, : H * F]
    back_key = back_both.reshape(token_count, 2 * H * F)[:, H * F :]
    back_value = back_value.reshape(token_count, D)
    query_grad = weight_grad(normed_low, back_query)
    key_grad = weight_grad(normed_low, back_key)
    value_grad = weight_grad(normed_low, back_value)
    grad_normed = (
        back_project(back_query, w_query)
        + back_project(back_key, w_key)
        + back_project(back_value, w_value)
    )
    grad_stream, gain_attn_grad = attn_norm_back(grad_normed)
    input_grad = grad_residual + grad_stream
    (
        gain_attn_part,
        query_part,
        key_part,
        value_part,
        out_part,
        gain_ffn_part,
        gate_part,
        up_part,
        down_part,
    ) = (
        lax.psum_scatter(gain_attn_grad, ("dp", "seq"), scatter_dimension=0, tiled=True),
        lax.psum_scatter(query_grad, ("dp", "seq"), scatter_dimension=0, tiled=True),
        lax.psum_scatter(key_grad, ("dp", "seq"), scatter_dimension=0, tiled=True),
        lax.psum_scatter(value_grad, ("dp", "seq"), scatter_dimension=0, tiled=True),
        lax.psum_scatter(out_grad, ("dp", "seq"), scatter_dimension=0, tiled=True),
        lax.psum_scatter(gain_ffn_grad, ("dp", "seq"), scatter_dimension=0, tiled=True),
        lax.psum_scatter(gate_grad, ("dp", "seq"), scatter_dimension=0, tiled=True),
        lax.psum_scatter(up_grad, ("dp", "seq"), scatter_dimension=0, tiled=True),
        lax.psum_scatter(down_grad_t, ("dp", "seq"), scatter_dimension=0, tiled=True),
    )
    return (
        output.reshape(row_count, shard_len, D).astype(jnp.bfloat16),
        input_grad.reshape(row_count, shard_len, D).astype(jnp.bfloat16),
        gain_attn_part,
        query_part,
        key_part,
        value_part,
        out_part,
        gain_ffn_part,
        gate_part,
        up_part,
        jnp.transpose(down_part),
    )


def solution(mesh):
    in_specs = (
        P("dp", "seq", None),
        P("dp", None),
        P(),
        P(),
        P(),
        P(),
        P(),
        P(),
        P(),
        P(),
        P(),
        P("dp", "seq", None),
    )
    out_specs = (
        P("dp", "seq", None),
        P("dp", "seq", None),
        P(("dp", "seq")),
        P(("dp", "seq"), None),
        P(("dp", "seq"), None),
        P(("dp", "seq"), None),
        P(("dp", "seq"), None),
        P(("dp", "seq")),
        P(("dp", "seq"), None),
        P(("dp", "seq"), None),
        P(None, ("dp", "seq")),
    )
    seq_devices = mesh.shape["seq"]
    step = functools.partial(body, seq_devices) if seq_devices * 2 == H else general_body
    return jax.shard_map(step, mesh=mesh, in_specs=in_specs, out_specs=out_specs, check_vma=False)
```

```python
import functools

import jax
import jax.numpy as jnp
from jax import lax
from jax.experimental import pallas as pl
from jax.experimental.pallas import tpu as pltpu
from jax.sharding import PartitionSpec as P

D = 1024
H = 16
F = 16
HV = 64
BLOCK = 576


eps_norm = 1e-05


def rms_scale(stream, gain_vec):
    return (
        stream * lax.rsqrt(jnp.mean(stream * stream, axis=-1, keepdims=True) + eps_norm) * gain_vec
    )


def taylor_features(vectors):
    feat_width = vectors.shape[-1]
    outer_prod = (vectors[..., :, None] * vectors[..., None, :]).reshape(
        vectors.shape[:-1] + (feat_width * feat_width,)
    )
    ones_part = jnp.ones(vectors.shape[:-1] + (1,), jnp.float32)
    return jnp.concatenate(
        [ones_part, vectors * feat_width ** (-0.25), outer_prod * (0.5 / feat_width) ** 0.5],
        axis=-1,
    )


def document_ids(doc_lens, seq_length):
    doc_ends = jnp.cumsum(doc_lens, dtype=jnp.int32)
    positions = jnp.arange(seq_length, dtype=jnp.int32)
    return jnp.sum(
        (positions[:, None] >= doc_ends[None, :]).astype(jnp.int32), axis=1, dtype=jnp.int32
    )


def attend_row(queries, key_proj, value_proj, doc_row, block_rows):
    seq_length, head_count, feat_width = queries.shape
    value_width = value_proj.shape[-1]
    feat_count = 1 + feat_width + feat_width * feat_width
    block_count = seq_length // block_rows
    highest = lax.Precision.HIGHEST
    query_blocks = queries.reshape(block_count, block_rows, head_count, feat_width)
    key_blocks = key_proj.reshape(block_count, block_rows, head_count, feat_width)
    value_blocks = value_proj.reshape(block_count, block_rows, head_count, value_width)
    doc_blocks = doc_row.reshape(block_count, block_rows)
    previous = jnp.concatenate([jnp.full((1,), -1, jnp.int32), doc_blocks[:-1, -1]])
    positions = jnp.arange(block_rows, dtype=jnp.int32)
    causal = positions[:, None] >= positions[None, :]

    def block_step(carried, pieces):
        state_sum, norm_sum = carried
        query_block, key_block, value_block, doc_block, prior_doc = pieces
        scores = jnp.einsum(
            "thf,shf->hts", query_block, key_block, precision=highest
        ) * feat_width ** (-0.5)
        weights = 1.0 + scores + 0.5 * scores * scores
        same_doc = causal & (doc_block[:, None] == doc_block[None, :])
        weights = jnp.where(same_doc[None, :, :], weights, 0.0)
        numerator = jnp.einsum("hts,shv->thv", weights, value_block, precision=highest)
        denominator = jnp.transpose(jnp.sum(weights, axis=2))
        use_state = (doc_block == prior_doc).astype(jnp.float32)[:, None]
        query_feats = taylor_features(query_block)
        numerator = numerator + use_state[:, :, None] * jnp.einsum(
            "thp,hpv->thv", query_feats, state_sum, precision=highest
        )
        denominator = denominator + use_state * jnp.einsum(
            "thp,hp->th", query_feats, norm_sum, precision=highest
        )
        last_doc = doc_block[-1]
        keep_state = (last_doc == prior_doc).astype(jnp.float32)
        key_feats = (
            taylor_features(key_block) * (doc_block == last_doc).astype(jnp.float32)[:, None, None]
        )
        state_sum = keep_state * state_sum + jnp.einsum(
            "shp,shv->hpv", key_feats, value_block, precision=highest
        )
        norm_sum = keep_state * norm_sum + jnp.sum(key_feats, axis=0)
        return ((state_sum, norm_sum), numerator / denominator[:, :, None])

    initial = (
        jnp.zeros((head_count, feat_count, value_width), jnp.float32),
        jnp.zeros((head_count, feat_count), jnp.float32),
    )
    _, results = lax.scan(
        jax.checkpoint(block_step),
        initial,
        (query_blocks, key_blocks, value_blocks, doc_blocks, previous),
    )
    return results.reshape(seq_length, head_count, value_width)


def project(left, right):
    return jnp.dot(left, right, preferred_element_type=jnp.float32)


def back_project(left, right):
    return lax.dot_general(
        left, right, (((1,), (1,)), ((), ())), preferred_element_type=jnp.float32
    )


def weight_grad(left, right):
    return lax.dot_general(
        left, right, (((0,), (0,)), ((), ())), preferred_element_type=jnp.float32
    )


def swiglu(gate_proj, up_proj):
    return jax.nn.silu(gate_proj) * up_proj


def general_body(
    inputs,
    doc_lengths,
    gain_attn,
    w_query,
    w_key,
    w_value,
    w_out,
    gain_ffn,
    w_gate,
    w_up,
    w_down,
    cotangent,
):
    row_count, shard_len, _ = inputs.shape
    token_count = row_count * shard_len
    stream = inputs.reshape(token_count, D).astype(jnp.float32)
    normed, attn_norm_back = jax.vjp(rms_scale, stream, gain_attn)
    normed_low = normed.astype(jnp.bfloat16)
    query_proj = project(normed_low, w_query).astype(jnp.bfloat16)
    key_proj = project(normed_low, w_key).astype(jnp.bfloat16)
    value_proj = project(normed_low, w_value).astype(jnp.bfloat16)
    query_heads, key_heads, value_heads = (
        lax.all_to_all(
            query_proj.reshape(row_count, shard_len, H, F),
            "seq",
            split_axis=2,
            concat_axis=1,
            tiled=True,
        ),
        lax.all_to_all(
            key_proj.reshape(row_count, shard_len, H, F),
            "seq",
            split_axis=2,
            concat_axis=1,
            tiled=True,
        ),
        lax.all_to_all(
            value_proj.reshape(row_count, shard_len, H, HV),
            "seq",
            split_axis=2,
            concat_axis=1,
            tiled=True,
        ),
    )
    seq_length = query_heads.shape[1]
    doc_rows = jax.vmap(lambda doc_lens: document_ids(doc_lens, seq_length))(doc_lengths)

    def attend_all(queries, keys_in, values_in):
        return jax.vmap(attend_row, in_axes=(0, 0, 0, 0, None))(
            queries, keys_in, values_in, doc_rows, BLOCK
        )

    mixed_heads, attend_back = jax.vjp(
        attend_all,
        query_heads.astype(jnp.float32),
        key_heads.astype(jnp.float32),
        value_heads.astype(jnp.float32),
    )
    mixed_rows = lax.all_to_all(
        mixed_heads.astype(jnp.bfloat16), "seq", split_axis=1, concat_axis=2, tiled=True
    )
    mixed_flat = mixed_rows.reshape(token_count, D)
    residual = stream + project(mixed_flat, w_out)
    normed_ffn, ffn_norm_back = jax.vjp(rms_scale, residual, gain_ffn)
    ffn_low = normed_ffn.astype(jnp.bfloat16)
    gate_proj = project(ffn_low, w_gate)
    up_proj = project(ffn_low, w_up)
    hidden, act_back = jax.vjp(swiglu, gate_proj, up_proj)
    hidden_low = hidden.astype(jnp.bfloat16)
    output = residual + project(hidden_low, w_down)
    grad_out = cotangent.reshape(token_count, D)
    grad_gate, grad_up = act_back(back_project(grad_out, w_down))
    grad_gate_low = grad_gate.astype(jnp.bfloat16)
    grad_up_low = grad_up.astype(jnp.bfloat16)
    down_grad_t = weight_grad(grad_out, hidden_low)
    gate_grad = weight_grad(ffn_low, grad_gate_low)
    up_grad = weight_grad(ffn_low, grad_up_low)
    grad_normed_ffn = back_project(grad_gate_low, w_gate) + back_project(grad_up_low, w_up)
    grad_residual, gain_ffn_grad = ffn_norm_back(grad_normed_ffn)
    grad_residual = grad_residual + grad_out.astype(jnp.float32)
    grad_branch = grad_residual.astype(jnp.bfloat16)
    out_grad = weight_grad(mixed_flat, grad_branch)
    grad_mixed = (
        back_project(grad_branch, w_out).astype(jnp.bfloat16).reshape(row_count, shard_len, H, HV)
    )
    grad_heads = lax.all_to_all(grad_mixed, "seq", split_axis=2, concat_axis=1, tiled=True)
    grad_query, grad_key, grad_value = attend_back(grad_heads.astype(jnp.float32))
    back_query, back_key, back_value = (
        lax.all_to_all(
            grad_query.astype(jnp.bfloat16), "seq", split_axis=1, concat_axis=2, tiled=True
        ),
        lax.all_to_all(
            grad_key.astype(jnp.bfloat16), "seq", split_axis=1, concat_axis=2, tiled=True
        ),
        lax.all_to_all(
            grad_value.astype(jnp.bfloat16), "seq", split_axis=1, concat_axis=2, tiled=True
        ),
    )
    back_query = back_query.reshape(token_count, H * F)
    back_key = back_key.reshape(token_count, H * F)
    back_value = back_value.reshape(token_count, D)
    query_grad = weight_grad(normed_low, back_query)
    key_grad = weight_grad(normed_low, back_key)
    value_grad = weight_grad(normed_low, back_value)
    grad_normed = (
        back_project(back_query, w_query)
        + back_project(back_key, w_key)
        + back_project(back_value, w_value)
    )
    grad_stream, gain_attn_grad = attn_norm_back(grad_normed)
    input_grad = grad_residual + grad_stream
    (
        gain_attn_part,
        query_part,
        key_part,
        value_part,
        out_part,
        gain_ffn_part,
        gate_part,
        up_part,
        down_part,
    ) = (
        lax.psum_scatter(gain_attn_grad, ("dp", "seq"), scatter_dimension=0, tiled=True),
        lax.psum_scatter(query_grad, ("dp", "seq"), scatter_dimension=0, tiled=True),
        lax.psum_scatter(key_grad, ("dp", "seq"), scatter_dimension=0, tiled=True),
        lax.psum_scatter(value_grad, ("dp", "seq"), scatter_dimension=0, tiled=True),
        lax.psum_scatter(out_grad, ("dp", "seq"), scatter_dimension=0, tiled=True),
        lax.psum_scatter(gain_ffn_grad, ("dp", "seq"), scatter_dimension=0, tiled=True),
        lax.psum_scatter(gate_grad, ("dp", "seq"), scatter_dimension=0, tiled=True),
        lax.psum_scatter(up_grad, ("dp", "seq"), scatter_dimension=0, tiled=True),
        lax.psum_scatter(down_grad_t, ("dp", "seq"), scatter_dimension=0, tiled=True),
    )
    return (
        output.reshape(row_count, shard_len, D).astype(jnp.bfloat16),
        input_grad.reshape(row_count, shard_len, D).astype(jnp.bfloat16),
        gain_attn_part,
        query_part,
        key_part,
        value_part,
        out_part,
        gain_ffn_part,
        gate_part,
        up_part,
        jnp.transpose(down_part),
    )


F32 = jnp.float32
BF16 = jnp.bfloat16
MESH = pl.DeviceIdType.MESH
TILE = 384
PAIR = 2 * HV


def nt(left, right):
    return lax.dot_general(left, right, (((1,), (1,)), ((), ())), preferred_element_type=F32)


def nn(left, right):
    return jnp.dot(left, right, preferred_element_type=F32)


def lanes_of(shape):
    return lax.broadcasted_iota(jnp.int32, shape, len(shape) - 1)


def first_visible(ends, positions):
    start = jnp.zeros_like(positions)
    for end in ends:
        start = jnp.where(positions >= end, end, start)
    return start


def row_ends(doc_ref, row):
    ends, total = [], 0
    for j in range(doc_ref.shape[1] - 1):
        total = total + doc_ref[row, j]
        ends.append(total)
    return ends


def spread_matrix():
    half = H * F
    shape = (2 * half, (H // 2) * 128)
    source = lax.broadcasted_iota(jnp.int32, shape, 0)
    column = lax.broadcasted_iota(jnp.int32, shape, 1)
    pair, lane = column // 128, column % 64
    wanted = pair * 32 + lane + jnp.where(lane < 32, 0, half - 32)
    return jnp.where(source == wanted, 1.0, 0.0).astype(BF16)


def gather_matrix():
    half = H * F
    shape = (2 * half, 2 * half)
    source = lax.broadcasted_iota(jnp.int32, shape, 0)
    column = lax.broadcasted_iota(jnp.int32, shape, 1)
    pair, lane = source // 64, source % 64
    wanted = pair * 32 + lane + jnp.where(lane < 32, 0, half - 32)
    return jnp.where(column == wanted, 1.0, 0.0).astype(BF16)


def packed_rows(length):
    return (length // 2 + 15) // 16 * 16


def prepare_row(got_ref, row, qa_ref, ka_ref, ve_ref, seq_devices, length):
    low = packed_rows(length)

    def part(peer, carry):
        values = got_ref[row, peer, :length, :].astype(F32)
        packed = got_ref[row, peer, length : length + low, :].astype(F32)
        turned = pltpu.roll(packed, 64, 1)
        both = jnp.concatenate([packed, turned[2 * low - length :]], axis=0)
        lane = lanes_of((length, 128))
        keys = pltpu.roll(both, 96, 1)
        at = pl.ds(pl.multiple_of(peer * length, 16), length)
        one = jnp.where(lane == 32, 1.0, 0.0)
        qa_ref[at, :] = jnp.where(lane < 32, both * 0.25, one).astype(BF16)
        ka_ref[0, at, :] = jnp.where(lane < 16, keys, one).astype(BF16)
        ka_ref[1, at, :] = jnp.where((lane >= 16) & (lane < 32), keys, one).astype(BF16)
        ve_ref[0, at, :] = jnp.where(lane < 64, values, 1.0).astype(BF16)
        ve_ref[1, at, :] = jnp.where(lane >= 64, values, 1.0).astype(BF16)
        return carry

    lax.fori_loop(0, seq_devices, part, 0)


def attend_forward(ends, qa_ref, ka_ref, ve_ref, mixed_ref, inverse_ref):
    length = qa_ref.shape[0]
    for block in range(length // TILE):
        reach = (block + 1) * TILE
        at = pl.ds(block * TILE, TILE)
        queries = qa_ref[at, :]
        t = lax.broadcasted_iota(jnp.int32, (TILE, 1), 0) + block * TILE
        start = first_visible(ends, t)
        s = lax.broadcasted_iota(jnp.int32, (TILE, reach), 1)
        visible = (s >= start) & (s <= t)
        sums = []
        for head in range(2):
            base = nt(queries, ka_ref[head, :reach, :])
            weights = jnp.where(visible, base * base + 1.0, 0.0).astype(BF16)
            sums.append(nn(weights, ve_ref[head, :reach, :]))
        lower = lanes_of((TILE, 128)) < 64
        numerator = jnp.where(lower, sums[0], sums[1])
        inverse = 1.0 / pltpu.roll(jnp.where(lower, sums[1], sums[0]), 64, 1)
        mixed_ref[at, :] = (numerator * inverse).astype(BF16)
        inverse_ref[at, :] = inverse


def attend_backward(
    ends, grad_ref, qa_ref, ka_ref, ve_ref, mixed_ref, inverse_ref, dn_ref, qs_ref, kt_ref, dqt_ref, gqk_ref, gv_ref
):
    length = qa_ref.shape[0]
    lane = lanes_of((length, 128))
    lower = lane < 64
    scaled = grad_ref[...].astype(F32) * inverse_ref[...]
    away = pltpu.roll(-scaled * mixed_ref[...].astype(F32), 64, 1)
    dn_ref[0] = jnp.where(lower, scaled, away).astype(BF16)
    dn_ref[1] = jnp.where(lower, away, scaled).astype(BF16)
    shifted = pltpu.roll(qa_ref[...].astype(F32), 32, 1)
    qs_ref[...] = jnp.where((lane >= 32) & (lane < 64), shifted * 2.0, 0.0).astype(BF16)
    for head in range(2):
        kt_ref[head] = ka_ref[head].astype(F32).T[:32].astype(BF16)
    dqt_ref[...] = jnp.zeros_like(dqt_ref)
    for block in range(length // TILE):
        first = block * TILE
        at = pl.ds(first, TILE)
        rest = pl.ds(first, length - first)
        shape = (TILE, length - first)
        t = lax.broadcasted_iota(jnp.int32, (1, shape[1]), 1) + first
        s = lax.broadcasted_iota(jnp.int32, shape, 0) + first
        visible = (s >= first_visible(ends, t)) & (s <= t)
        value_sums, key_sums = [], []
        for head in range(2):
            base = nt(ka_ref[head, at, :], qa_ref[rest, :])
            grad_weights = nt(ve_ref[head, at, :], dn_ref[head, rest, :])
            weights = jnp.where(visible, base * base + 1.0, 0.0).astype(BF16)
            grad_base = jnp.where(visible, grad_weights * base, 0.0).astype(BF16)
            value_sums.append(nn(weights, dn_ref[head, rest, :]))
            key_sums.append(nn(grad_base, qs_ref[rest, :]))
            dqt_ref[:, rest] += nn(kt_ref[head, :, at], grad_base)
        lane = lanes_of((TILE, 128))
        gv_ref[at, :] = jnp.where(lane < 64, value_sums[0], value_sums[1]).astype(BF16)
        gqk_ref[at, :] = jnp.where(
            (lane >= 32) & (lane < 48), key_sums[0], jnp.where((lane >= 48) & (lane < 64), key_sums[1], 0.0)
        )
    queries = jnp.concatenate([dqt_ref[...] * 0.5, jnp.zeros((96, length), F32)], axis=0)
    gqk_ref[...] += queries.T


def greet(seq_devices):
    row_group, me = lax.axis_index("dp"), lax.axis_index("seq")
    barrier = pltpu.get_barrier_semaphore()
    for step in range(1, seq_devices):
        peer = lax.rem(me + step, seq_devices)
        pl.semaphore_signal(barrier, inc=1, device_id=(row_group, peer), device_id_type=MESH)
    pl.semaphore_wait(barrier, seq_devices - 1)
    return row_group, me


def sending(source, target, send_sem, recv_sem, row_group, peer):
    return pltpu.make_async_remote_copy(
        src_ref=source,
        dst_ref=target,
        send_sem=send_sem,
        recv_sem=recv_sem,
        device_id=(row_group, peer),
        device_id_type=MESH,
    )


def forward_kernel(
    seq_devices, rows, length,
    x_ref, doc_ref, gain_ref, wq_ref, wk_ref, wv_ref,
    branch_ref, got_out, head_out, inverse_ref,
    out_buf, got, heads, back, spread, qa, ka, ve, send_a, recv_a, send_b, recv_b,
):
    row_group, me = greet(seq_devices)
    low = packed_rows(length)
    lower = lanes_of((low, 128)) < 64
    spread[...] = spread_matrix()

    def outgoing(row, step):
        peer = lax.rem(me + step, seq_devices)
        return sending(
            out_buf.at[row, peer], got.at[row, me], send_a.at[row, step], recv_a.at[row, step], row_group, peer
        )

    def returning(row, step):
        peer = lax.rem(me + step, seq_devices)
        there = pl.ds(pl.multiple_of(peer * length, 16), length)
        mine = pl.ds(pl.multiple_of(me * PAIR, 128), PAIR)
        return sending(
            heads.at[row, there, :], back.at[row, :, mine], send_b.at[row, step], recv_b.at[row, step], row_group, peer
        )

    def project_row(row, carry):
        stream = x_ref[row].astype(F32)
        normed = rms_scale(stream, gain_ref[...]).astype(BF16)
        both = jnp.concatenate([nn(normed, wq_ref[...]), nn(normed, wk_ref[...])], axis=1).astype(BF16)
        tiles = nn(both, spread[...])
        values = nn(normed, wv_ref[...]).astype(BF16)
        for pair in range(seq_devices):
            tile = tiles[:, pair * 128 : (pair + 1) * 128]
            out_buf[row, pair, :length, :] = values[:, pair * PAIR : (pair + 1) * PAIR]
            out_buf[row, pair, length:, :] = jnp.where(lower, tile[:low], tile[length - low :]).astype(BF16)
        for step in range(1, seq_devices):
            outgoing(row, step).start()
        got[row, me] = out_buf[row, me]
        return carry

    lax.fori_loop(0, rows, project_row, 0)

    def attend(row, carry):
        for step in range(1, seq_devices):
            outgoing(row, step).wait_recv()
        prepare_row(got, row, qa, ka, ve, seq_devices, length)
        attend_forward(row_ends(doc_ref, row), qa, ka, ve, heads.at[row], inverse_ref.at[row])
        for step in range(1, seq_devices):
            returning(row, step).start()
        here = pl.ds(pl.multiple_of(me * length, 16), length)
        back[row, :, pl.ds(pl.multiple_of(me * PAIR, 128), PAIR)] = heads[row, here, :]
        return carry

    lax.fori_loop(0, rows, attend, 0)
    got_out[...] = got[...]
    head_out[...] = heads[...]

    def finish(row, carry):
        for step in range(1, seq_devices):
            outgoing(row, step).wait_send()
            returning(row, step).wait()
        branch_ref[row] = back[row]
        return carry

    lax.fori_loop(0, rows, finish, 0)


VMEM_SPEC = pl.BlockSpec(memory_space=pltpu.VMEM)
SMEM_SPEC = pl.BlockSpec(memory_space=pltpu.SMEM)


def attention_forward(seq_devices, x, doc_lengths, gain, w_query, w_key, w_value):
    rows, length, _ = x.shape
    total = seq_devices * length
    message = (rows, seq_devices, length + packed_rows(length), 128)
    sems = pltpu.SemaphoreType.DMA((rows, seq_devices))
    return pl.pallas_call(
        functools.partial(forward_kernel, seq_devices, rows, length),
        name="attention_forward",
        out_shape=[
            jax.ShapeDtypeStruct((rows, length, D), BF16),
            jax.ShapeDtypeStruct(message, BF16),
            jax.ShapeDtypeStruct((rows, total, 128), BF16),
            jax.ShapeDtypeStruct((rows, total, 128), F32),
        ],
        in_specs=[VMEM_SPEC, SMEM_SPEC, VMEM_SPEC, VMEM_SPEC, VMEM_SPEC, VMEM_SPEC],
        out_specs=[VMEM_SPEC] * 4,
        scratch_shapes=[
            pltpu.VMEM(message, BF16),
            pltpu.VMEM(message, BF16),
            pltpu.VMEM((rows, total, 128), BF16),
            pltpu.VMEM((rows, length, D), BF16),
            pltpu.VMEM((2 * H * F, D), BF16),
            pltpu.VMEM((total, 128), BF16),
            pltpu.VMEM((2, total, 128), BF16),
            pltpu.VMEM((2, total, 128), BF16),
            sems, sems, sems, sems,
        ],
        compiler_params=pltpu.CompilerParams(collective_id=0, has_side_effects=True, vmem_limit_bytes=56 << 20),
    )(x, doc_lengths, gain.reshape(1, D), w_query, w_key, w_value)


CHUNK = 256
STEP_ROWS = 48
EARLY = 4


def place(me):
    core = lax.rem(me, 2)
    return core, 2 + 2 * core, 4 - 2 * core


def blocks_of(core, groups):
    first, second = 2 + 2 * core, 4 - 2 * core
    return [
        pl.multiple_of(32 * (8 * group + first * i + second * j + core), 32)
        for i in range(2)
        for j in range(2)
        for group in range(groups)
    ]


class Reduction:
    def __init__(self, groups, source, got_a, got_b, got_z, a_sems, b_sems, z_send, z_recv):
        self.groups, self.source = groups, source
        self.got_a, self.got_b, self.got_z = got_a, got_b, got_z
        self.a_sems, self.b_sems, self.z_send, self.z_recv = a_sems, b_sems, z_send, z_recv
        self.group, self.me = lax.axis_index("dp"), lax.axis_index("seq")
        core, first, second = place(self.me)
        self.bit_a, self.bit_b = lax.rem(self.me // first, 2), lax.rem(self.me // second, 2)
        self.peer_a = self.me + first * (1 - 2 * self.bit_a)
        self.peer_b = self.me + second * (1 - 2 * self.bit_b)

    def a_copy(self, unit):
        return sending(
            self.source.at[unit, 1 - self.bit_a], self.got_a.at[unit], self.a_sems.at[0, unit],
            self.a_sems.at[1, unit], self.group, self.peer_a,
        )

    def b_copy(self, unit):
        return sending(
            self.got_a.at[unit, 1 - self.bit_b], self.got_b.at[unit], self.b_sems.at[0, unit],
            self.b_sems.at[1, unit], self.group, self.peer_b,
        )

    def z_copy(self, unit, step):
        other = lax.rem(self.group + step, self.groups)
        block = pl.ds(pl.multiple_of(other * 32, 32), 32)
        return sending(
            self.got_b.at[unit, block, :], self.got_z.at[unit, step - 1], self.z_send.at[unit, step - 1],
            self.z_recv.at[unit, step - 1], other, self.me,
        )

    def a_step(self, unit):
        self.a_copy(unit).wait_recv()
        self.got_a[unit] = (self.source[unit, self.bit_a].astype(F32) + self.got_a[unit].astype(F32)).astype(BF16)
        self.b_copy(unit).start()

    def b_step(self, unit):
        self.b_copy(unit).wait_recv()
        self.got_b[unit] = (self.got_a[unit, self.bit_b].astype(F32) + self.got_b[unit].astype(F32)).astype(BF16)
        for step in range(1, self.groups):
            self.z_copy(unit, step).start()

    def z_step(self, unit):
        total = self.got_b[unit, pl.ds(pl.multiple_of(self.group * 32, 32), 32), :].astype(F32)
        for step in range(1, self.groups):
            self.z_copy(unit, step).wait_recv()
            total += self.got_z[unit, step - 1].astype(F32)
        return total

    def wait_sent(self, unit):
        self.a_copy(unit).wait_send()
        self.b_copy(unit).wait_send()
        for step in range(1, self.groups):
            self.z_copy(unit, step).wait_send()


def reduction_scratch(groups, units, cols, source=True):
    rows = 32 * groups
    dma = pltpu.SemaphoreType.DMA
    buffers = [pltpu.VMEM((units, 2, 2, rows, cols), BF16)] if source else []
    return buffers + [
        pltpu.VMEM((units, 2, rows, cols), BF16),
        pltpu.VMEM((units, rows, cols), BF16),
        pltpu.VMEM((units, groups - 1, 32, cols), BF16),
        dma((2, units)),
        dma((2, units)),
        dma((units, groups - 1)),
        dma((units, groups - 1)),
    ]


def store_blocks(target, unit, col, values, groups):
    rows = 32 * groups
    for i in range(2):
        for j in range(2):
            at = (2 * i + j) * rows
            target[unit, i, j, :, col : col + values.shape[1]] = values[at : at + rows].astype(BF16)


def turn(source, tokens, padded, turned):
    turned[...] = jnp.concatenate([source, jnp.zeros((padded - tokens, D), BF16)], axis=0).T


def split_rows(turned, mine_ref, theirs_ref, core, groups):
    padded = turned.shape[1]
    for i, (mine, theirs) in enumerate(zip(blocks_of(core, groups), blocks_of(1 - core, groups))):
        mine_ref[i * 32 : (i + 1) * 32, :padded] = turned[pl.ds(mine, 32), :]
        theirs_ref[i * 32 : (i + 1) * 32, :] = turned[pl.ds(theirs, 32), :]


def write_unit(total, at, w, gate_out, up_out, down_out):
    down_out[:, pl.ds(at, w)] = total[:, :w]
    gate_out[:, pl.ds(at, w)] = total[:, CHUNK : CHUNK + w]
    up_out[:, pl.ds(at, w)] = total[:, 2 * CHUNK : 2 * CHUNK + w]


def ffn_kernel(
    groups, tokens, width,
    branch_ref, x_ref, cot_ref, gain_ref, wo_ref, wg_hbm, wu_hbm, wd_hbm,
    output_ref, gres_ref, gmixed_ref, gate_out, up_out, down_out, rest, parts_o, gain_out,
    residual, normed, out_acc, gnf, w_buf, turned, lhs, lhs_send, right, right_out, parts,
    got_a, got_b, got_z, a_sems, b_sems, z_send, z_recv, w_sem, lhs_sems, pair_sems,
):
    row_group, me = lax.axis_index("dp"), lax.axis_index("seq")
    core, _, _ = place(me)
    partner = me + 1 - 2 * core
    reduction = Reduction(groups, parts, got_a, got_b, got_z, a_sems, b_sems, z_send, z_recv)
    full = width // CHUNK
    tail = width - full * CHUNK
    padded = turned.shape[1]

    barrier = pltpu.get_barrier_semaphore()
    for peer in (partner, reduction.peer_a, reduction.peer_b):
        pl.semaphore_signal(barrier, inc=1, device_id=(row_group, peer), device_id_type=MESH)
    for step in range(1, groups):
        other = lax.rem(row_group + step, groups)
        pl.semaphore_signal(barrier, inc=1, device_id=(other, me), device_id_type=MESH)

    def loads(chunk, slot, w):
        at = pl.ds(pl.multiple_of(chunk * CHUNK, CHUNK), w)
        return [
            pltpu.make_async_copy(hbm.at[at, :], w_buf.at[slot, which, pl.ds(0, w), :], w_sem.at[slot, which])
            for which, hbm in enumerate((wg_hbm, wu_hbm, wd_hbm))
        ]

    for copy in loads(0, 0, CHUNK):
        copy.start()

    def norm_forward(step, carry):
        at = pl.ds(pl.multiple_of(step * STEP_ROWS, 16), STEP_ROWS)
        value = x_ref[at, :].astype(F32) + residual[at, :]
        residual[at, :] = value
        out_acc[at, :] = value
        normed[at, :] = rms_scale(value, gain_ref[...]).astype(BF16)
        return carry

    residual[...] = nn(branch_ref[...], wo_ref[...])
    lax.fori_loop(0, tokens // STEP_ROWS, norm_forward, 0)
    gnf[...] = jnp.zeros_like(gnf)

    pl.semaphore_wait(barrier, 2 + groups)

    def lhs_copy(which):
        return sending(
            lhs_send.at[which], lhs.at[which, :, pl.ds(padded, padded)],
            lhs_sems.at[0, which], lhs_sems.at[1, which], row_group, partner,
        )

    for which, source in enumerate((cot_ref, normed, branch_ref)):
        turn(source[...], tokens, padded, turned)
        split_rows(turned, lhs.at[which], lhs_send.at[which], core, groups)
        lhs_copy(which).start()
    slots = right.shape[0]
    gap = padded - tokens
    for base in (tokens, padded + tokens):
        right[:, base : base + gap, :] = jnp.zeros((slots, gap, 3 * CHUNK), BF16)
        right_out[base : base + gap, :] = jnp.zeros((gap, D), BF16)

    def pair_copy(chunk):
        slot = lax.rem(chunk, slots)
        return sending(
            right.at[slot, pl.ds(0, tokens), :], right.at[slot, pl.ds(padded, tokens), :],
            pair_sems.at[0, chunk], pair_sems.at[1, chunk], row_group, partner,
        )

    def forward_part(chunk, wg, wu, wd, w):
        slot = lax.rem(chunk, slots)
        gate = nt(normed[...], wg)
        up = nt(normed[...], wu)
        sigmoid = 1.0 / (1.0 + jnp.exp(-gate))
        silu = gate * sigmoid
        hidden = (silu * up).astype(BF16)
        grad_hidden = nt(cot_ref[...], wd)
        grad_gate = (grad_hidden * up * (sigmoid * (1.0 + gate * (1.0 - sigmoid)))).astype(BF16)
        grad_up = (grad_hidden * silu).astype(BF16)
        for part, values in enumerate((hidden, grad_gate, grad_up)):
            right[slot, :tokens, part * CHUNK : part * CHUNK + w] = values
            if w < CHUNK:
                right[slot, :tokens, part * CHUNK + w : (part + 1) * CHUNK] = jnp.zeros((tokens, CHUNK - w), BF16)
        pair_copy(chunk).start()
        out_acc[...] += nn(hidden, wd)
        gnf[...] += nn(grad_gate, wg) + nn(grad_up, wu)

    def grad_part(chunk, early):
        pair_copy(chunk).wait()
        slot = lax.rem(chunk, slots)
        down = nn(lhs[0], right[slot, :, 0:CHUNK])
        both = nn(lhs[1], right[slot, :, CHUNK:])
        target, unit = (parts, chunk) if early else (rest, chunk - EARLY)
        store_blocks(target, unit, 0, down, groups)
        store_blocks(target, unit, CHUNK, both, groups)
        if early:
            reduction.a_copy(chunk).start()

    for which in range(3):
        lhs_copy(which).wait()

    def forward_step(chunk):
        slot = lax.rem(chunk, 2)
        for copy in loads(chunk, slot, CHUNK):
            copy.wait()
        forward_part(chunk, w_buf[slot, 0], w_buf[slot, 1], w_buf[slot, 2], CHUNK)

    def main(early, chunk, carry):
        for copy in loads(chunk + 1, lax.rem(chunk + 1, 2), CHUNK):
            copy.start()
        forward_step(chunk)
        grad_part(chunk - 1, early)

        @pl.when((chunk >= 4) & (chunk < 4 + EARLY))
        def _():
            reduction.a_step(chunk - 4)

        @pl.when((chunk >= 6) & (chunk < 6 + EARLY))
        def _():
            reduction.b_step(chunk - 6)

        return carry

    for copy in loads(1, 1, CHUNK):
        copy.start()
    forward_step(0)
    lax.fori_loop(1, EARLY + 1, functools.partial(main, True), 0)
    lax.fori_loop(EARLY + 1, full - 1, functools.partial(main, False), 0)
    for copy in loads(full, full % 2, tail):
        copy.start()
    forward_step(full - 1)
    grad_part(full - 2, False)
    for unit in range(max(0, full - 5), EARLY):
        reduction.a_step(unit)
    for unit in range(max(0, full - 7), EARLY):
        reduction.b_step(unit)
    for copy in loads(full, full % 2, tail):
        copy.wait()
    slot = full % 2
    forward_part(full, w_buf[slot, 0, :tail], w_buf[slot, 1, :tail], w_buf[slot, 2, :tail], tail)
    grad_part(full - 1, False)

    gain_out[...] = jnp.zeros_like(gain_out)

    def norm_backward(step, carry):
        at = pl.ds(pl.multiple_of(step * STEP_ROWS, 16), STEP_ROWS)
        value, grad = residual[at, :], gnf[at, :]
        scale = lax.rsqrt(jnp.mean(value * value, axis=-1, keepdims=True) + eps_norm)
        gain_out[0:1, :] += jnp.sum(grad * value * scale, axis=0, keepdims=True)
        weighted = grad * gain_ref[...]
        mean = jnp.mean(weighted * value, axis=-1, keepdims=True)
        total = cot_ref[at, :].astype(F32) + scale * weighted - value * (scale * scale * scale * mean)
        gres_ref[at, :] = total
        right_out[at, :] = total.astype(BF16)
        output_ref[at, :] = out_acc[at, :].astype(BF16)
        return carry

    lax.fori_loop(0, tokens // STEP_ROWS, norm_backward, 0)
    out_pair = sending(
        right_out.at[pl.ds(0, tokens), :], right_out.at[pl.ds(padded, tokens), :],
        pair_sems.at[0, full + 1], pair_sems.at[1, full + 1], row_group, partner,
    )
    out_pair.start()
    grad_part(full, False)
    gmixed_ref[...] = nt(right_out[:tokens, :], wo_ref[...]).astype(BF16)
    out_pair.wait()
    for col in range(0, D, CHUNK):
        store_blocks(parts_o, 0, col, nn(lhs[2], right_out[:, col : col + CHUNK]), groups)

    def finish(unit, carry):
        write_unit(reduction.z_step(unit), pl.multiple_of(unit * CHUNK, CHUNK), CHUNK, gate_out, up_out, down_out)
        return carry

    lax.fori_loop(0, EARLY, finish, 0)

    def sent(unit, carry):
        reduction.wait_sent(unit)
        return carry

    lax.fori_loop(0, EARLY, sent, 0)


ANY_SPEC = pl.BlockSpec(memory_space=pl.ANY)


def feed_forward(groups, branch, x, cotangent, gain, w_out, w_gate_t, w_up_t, w_down):
    tokens = branch.shape[0]
    width = w_down.shape[0]
    full = width // CHUNK
    padded = (tokens + 127) // 128 * 128
    cols = 3 * CHUNK
    rows = 32 * groups
    dma = pltpu.SemaphoreType.DMA
    return pl.pallas_call(
        functools.partial(ffn_kernel, groups, tokens, width),
        name="feed_forward",
        out_shape=[
            jax.ShapeDtypeStruct((tokens, D), BF16),
            jax.ShapeDtypeStruct((tokens, D), F32),
            jax.ShapeDtypeStruct((tokens, D), BF16),
            jax.ShapeDtypeStruct((32, EARLY * CHUNK), F32),
            jax.ShapeDtypeStruct((32, EARLY * CHUNK), F32),
            jax.ShapeDtypeStruct((32, EARLY * CHUNK), F32),
            jax.ShapeDtypeStruct((full + 1 - EARLY, 2, 2, rows, cols), BF16),
            jax.ShapeDtypeStruct((1, 2, 2, rows, D), BF16),
            jax.ShapeDtypeStruct((8, D), F32),
        ],
        in_specs=[VMEM_SPEC] * 5 + [ANY_SPEC] * 3,
        out_specs=[VMEM_SPEC] * 9,
        scratch_shapes=[
            pltpu.VMEM((tokens, D), F32),
            pltpu.VMEM((tokens, D), BF16),
            pltpu.VMEM((tokens, D), F32),
            pltpu.VMEM((tokens, D), F32),
            pltpu.VMEM((2, 3, CHUNK, D), BF16),
            pltpu.VMEM((D, padded), BF16),
            pltpu.VMEM((3, D // 2, 2 * padded), BF16),
            pltpu.VMEM((3, D // 2, padded), BF16),
            pltpu.VMEM((4, 2 * padded, cols), BF16),
            pltpu.VMEM((2 * padded, D), BF16),
        ]
        + reduction_scratch(groups, EARLY, cols)
        + [dma((2, 3)), dma((2, 3)), dma((2, full + 2))],
        compiler_params=pltpu.CompilerParams(collective_id=2, has_side_effects=True, vmem_limit_bytes=60 << 20),
    )(branch, x, cotangent, gain.reshape(1, D), w_out, w_gate_t, w_up_t, w_down)


def last_kernel(
    groups, seq_devices, rows, length, width,
    grad_ref, doc_ref, got, heads, inverse_ref, x_ref, gres_ref, gain_ref, wq_ref, wk_ref, wv_ref,
    rest, parts_o, gate_early, up_early, down_early, gain_rows,
    input_out, gate_out, up_out, down_out, wout_out, query_out, key_out, value_out, gains_out,
    arrived, out_buf, back, gather, qa, ka, ve, dn, qs, kt, dqt, gqk, gv, turned, lhs, lhs_send, right, gnorm,
    gains, gains_got,
    send_a, recv_a, send_b, recv_b, lhs_sems, pair_sems, gain_send, gain_recv,
    f_a, f_b, f_z, fa_sems, fb_sems, fz_send, fz_recv,
    o_a, o_b, o_z, oa_sems, ob_sems, oz_send, oz_recv,
    q_source, q_a, q_b, q_z, qa_sems, qb_sems, qz_send, qz_recv,
):
    row_group, me = lax.axis_index("dp"), lax.axis_index("seq")
    core, _, _ = place(me)
    partner = me + 1 - 2 * core
    tokens = rows * length
    padded = turned.shape[1]
    low = packed_rows(length)
    lower = lanes_of((low, 128)) < 64
    here = pl.ds(pl.multiple_of(me * length, 16), length)
    f_units = rest.shape[0]
    feed = Reduction(groups, rest, f_a, f_b, f_z, fa_sems, fb_sems, fz_send, fz_recv)
    outer = Reduction(groups, parts_o, o_a, o_b, o_z, oa_sems, ob_sems, oz_send, oz_recv)
    qkv = Reduction(groups, q_source, q_a, q_b, q_z, qa_sems, qb_sems, qz_send, qz_recv)

    barrier = pltpu.get_barrier_semaphore()
    for step in range(1, seq_devices):
        peer = lax.rem(me + step, seq_devices)
        pl.semaphore_signal(barrier, inc=1, device_id=(row_group, peer), device_id_type=MESH)
    for step in range(1, groups):
        other = lax.rem(row_group + step, groups)
        pl.semaphore_signal(barrier, inc=1, device_id=(other, me), device_id_type=MESH)
    pl.semaphore_wait(barrier, seq_devices + groups - 2)

    def outgoing(row, step):
        peer = lax.rem(me + step, seq_devices)
        theirs = pl.ds(pl.multiple_of(peer * PAIR, 128), PAIR)
        return sending(
            grad_ref.at[row, :, theirs], arrived.at[row, here, :], send_a.at[row, step], recv_a.at[row, step],
            row_group, peer,
        )

    def returning(row, step):
        peer = lax.rem(me + step, seq_devices)
        return sending(
            out_buf.at[row, peer], back.at[row, me], send_b.at[row, step], recv_b.at[row, step], row_group, peer
        )

    def send_row(row, carry):
        for step in range(1, seq_devices):
            outgoing(row, step).start()
        arrived[row, here, :] = grad_ref[row, :, pl.ds(pl.multiple_of(me * PAIR, 128), PAIR)]
        return carry

    lax.fori_loop(0, rows, send_row, 0)

    def norm_forward(row, carry):
        at = pl.ds(pl.multiple_of(row * length, 16), length)
        right[at, :D] = rms_scale(x_ref[at, :].astype(F32), gain_ref[...]).astype(BF16)
        return carry

    lax.fori_loop(0, rows, norm_forward, 0)
    turn(right[:tokens, :D], tokens, padded, turned)
    split_rows(turned, lhs, lhs_send, core, groups)
    lhs_copy = sending(
        lhs_send, lhs.at[:, pl.ds(padded, padded)], lhs_sems.at[0], lhs_sems.at[1], row_group, partner
    )
    lhs_copy.start()
    gap = padded - tokens
    for base in (tokens, padded + tokens):
        right[base : base + gap, :] = jnp.zeros((gap, right.shape[1]), BF16)
    gather[...] = gather_matrix()

    def attend(row, carry):
        prepare_row(got, row, qa, ka, ve, seq_devices, length)
        for step in range(1, seq_devices):
            outgoing(row, step).wait_recv()
        attend_backward(
            row_ends(doc_ref, row), arrived.at[row], qa, ka, ve, heads.at[row], inverse_ref.at[row],
            dn, qs, kt, dqt, gqk, gv,
        )

        def pack(peer, inner):
            at = pl.multiple_of(peer * length, 16)
            out_buf[row, peer, :length, :] = gv[pl.ds(at, length), :]
            first = gqk[pl.ds(at, low), :]
            second = pltpu.roll(gqk[pl.ds(at + length - low, low), :], 64, 1)
            out_buf[row, peer, length:, :] = jnp.where(lower, first, second).astype(BF16)
            return inner

        lax.fori_loop(0, seq_devices, pack, 0)
        for step in range(1, seq_devices):
            returning(row, step).start()
        back[row, me] = out_buf[row, me]
        feed.a_copy(row).start()
        return carry

    lax.fori_loop(0, rows, attend, 0)
    for unit in range(rows, f_units):
        feed.a_copy(unit).start()
    outer.a_copy(0).start()
    feed.a_step(0)
    feed.a_step(1)
    feed.a_step(2)

    def unpack(row, carry):
        for step in range(1, seq_devices):
            outgoing(row, step).wait_send()
            returning(row, step).wait()
        tiles = []
        for pair in range(0, seq_devices, 2):
            halves = []
            for one in (pair, pair + 1):
                packed = back[row, one, length:, :].astype(F32)
                turned_over = pltpu.roll(packed, 64, 1)
                straight, other = (packed, turned_over) if one == pair else (turned_over, packed)
                halves.append(jnp.concatenate([straight, other[2 * low - length :]], axis=0))
            tiles.append(jnp.where(lanes_of((length, 128)) < 64, halves[0], halves[1]).astype(BF16))
        at = pl.ds(pl.multiple_of(row * length, 16), length)
        right[at, : 2 * H * F] = nn(jnp.concatenate(tiles, axis=1), gather[...]).astype(BF16)
        for pair in range(seq_devices):
            col = 2 * H * F + pair * PAIR
            right[at, col : col + PAIR] = back[row, pair, :length, :]
        return carry

    lax.fori_loop(0, rows, unpack, 0)
    pair = sending(
        right.at[pl.ds(0, tokens), :], right.at[pl.ds(padded, tokens), :], pair_sems.at[0], pair_sems.at[1],
        row_group, partner,
    )
    pair.start()
    half = H * F
    gnorm[...] = (
        nt(right[:tokens, :half], wq_ref[...])
        + nt(right[:tokens, half : 2 * half], wk_ref[...])
        + nt(right[:tokens, 2 * half :], wv_ref[...])
    )
    lhs_copy.wait()
    pair.wait()
    for col in range(0, right.shape[1], CHUNK):
        store_blocks(q_source, 0, col, nn(lhs[...], right[:, col : col + CHUNK]), groups)
    qkv.a_copy(0).start()

    gains[...] = gain_rows[...]

    def norm_backward(step, carry):
        at = pl.ds(pl.multiple_of(step * STEP_ROWS, 16), STEP_ROWS)
        value, grad = x_ref[at, :].astype(F32), gnorm[at, :]
        scale = lax.rsqrt(jnp.mean(value * value, axis=-1, keepdims=True) + eps_norm)
        gains[1:2, :] += jnp.sum(grad * value * scale, axis=0, keepdims=True)
        weighted = grad * gain_ref[...]
        mean = jnp.mean(weighted * value, axis=-1, keepdims=True)
        total = gres_ref[at, :] + scale * weighted - value * (scale * scale * scale * mean)
        input_out[at, :] = total.astype(BF16)
        return carry

    lax.fori_loop(0, tokens // STEP_ROWS, norm_backward, 0)

    def gain_copy(step, target_group, target):
        return sending(
            gains, gains_got.at[step], gain_send.at[step], gain_recv.at[step], target_group, target
        )

    gain_copies = [
        gain_copy(0, row_group, partner),
        gain_copy(1, row_group, feed.peer_a),
        gain_copy(2, row_group, feed.peer_b),
    ] + [gain_copy(2 + step, lax.rem(row_group + step, groups), me) for step in range(1, groups)]
    gain_copies[0].start()
    early = gate_early.shape[1]
    gate_out[:, :early] = gate_early[...]
    up_out[:, :early] = up_early[...]
    down_out[:, :early] = down_early[...]
    gain_copies[0].wait()
    gains[...] += gains_got[0]
    gain_copies[1].start()
    for unit in range(3, f_units):
        feed.a_step(unit)
        feed.b_step(unit - 3)
    gain_copies[1].wait()
    gains[...] += gains_got[1]
    gain_copies[2].start()
    outer.a_step(0)
    feed.b_step(f_units - 3)
    qkv.a_step(0)
    feed.b_step(f_units - 2)
    feed.b_step(f_units - 1)
    gain_copies[2].wait()
    gains[...] += gains_got[2]
    for copy in gain_copies[3:]:
        copy.start()

    def write_feed(unit, w):
        at = early + unit * CHUNK
        at = at if isinstance(at, int) else pl.multiple_of(at, CHUNK)
        write_unit(feed.z_step(unit), at, w, gate_out, up_out, down_out)

    def finish(unit, carry):
        write_feed(unit, CHUNK)
        return carry

    lax.fori_loop(0, f_units - 3, finish, 0)
    outer.b_step(0)
    lax.fori_loop(f_units - 3, f_units - 1, finish, 0)
    write_feed(f_units - 1, width - early - (f_units - 1) * CHUNK)
    for copy in gain_copies[3:]:
        copy.wait()
    for step in range(1, groups):
        gains[...] += gains_got[2 + step]
    picked = lax.broadcasted_iota(jnp.int32, (D, 128), 0) == 32 * (seq_devices * row_group + me) + lanes_of((D, 128))
    gains_out[...] = jnp.dot(
        gains[...], jnp.where(picked, 1.0, 0.0), precision=lax.Precision.HIGHEST, preferred_element_type=F32
    )
    qkv.b_step(0)
    wout_out[...] = outer.z_step(0)
    total = qkv.z_step(0)
    query_out[...] = total[:, :half]
    key_out[...] = total[:, half : 2 * half]
    value_out[...] = total[:, 2 * half :]

    def sent(unit, carry):
        feed.wait_sent(unit)
        return carry

    lax.fori_loop(0, f_units, sent, 0)
    outer.wait_sent(0)
    qkv.wait_sent(0)


def last_part(
    groups, seq_devices, grad, doc_lengths, got, heads, inverse, x, gres, gain, w_query, w_key, w_value,
    rest, parts_o, gate_early, up_early, down_early, gain_rows, width,
):
    rows, length, _ = grad.shape
    tokens = rows * length
    total = seq_devices * length
    padded = (tokens + 127) // 128 * 128
    message = (rows, seq_devices, length + packed_rows(length), 128)
    dma = pltpu.SemaphoreType.DMA
    sems = dma((rows, seq_devices))
    cols = 2 * H * F + D
    return pl.pallas_call(
        functools.partial(last_kernel, groups, seq_devices, rows, length, width),
        name="attention_backward",
        out_shape=[
            jax.ShapeDtypeStruct((tokens, D), BF16),
            jax.ShapeDtypeStruct((32, width), F32),
            jax.ShapeDtypeStruct((32, width), F32),
            jax.ShapeDtypeStruct((32, width), F32),
            jax.ShapeDtypeStruct((32, D), F32),
            jax.ShapeDtypeStruct((32, H * F), F32),
            jax.ShapeDtypeStruct((32, H * F), F32),
            jax.ShapeDtypeStruct((32, D), F32),
            jax.ShapeDtypeStruct((8, 128), F32),
        ],
        in_specs=[VMEM_SPEC, SMEM_SPEC] + [VMEM_SPEC] * 15,
        out_specs=[VMEM_SPEC] * 9,
        scratch_shapes=[
            pltpu.VMEM((rows, total, 128), BF16),
            pltpu.VMEM(message, BF16),
            pltpu.VMEM(message, BF16),
            pltpu.VMEM((2 * H * F, 2 * H * F), BF16),
            pltpu.VMEM((total, 128), BF16),
            pltpu.VMEM((2, total, 128), BF16),
            pltpu.VMEM((2, total, 128), BF16),
            pltpu.VMEM((2, total, 128), BF16),
            pltpu.VMEM((total, 128), BF16),
            pltpu.VMEM((2, 32, total), BF16),
            pltpu.VMEM((32, total), F32),
            pltpu.VMEM((total, 128), F32),
            pltpu.VMEM((total, 128), BF16),
            pltpu.VMEM((D, padded), BF16),
            pltpu.VMEM((D // 2, 2 * padded), BF16),
            pltpu.VMEM((D // 2, padded), BF16),
            pltpu.VMEM((2 * padded, cols), BF16),
            pltpu.VMEM((tokens, D), F32),
            pltpu.VMEM((8, D), F32),
            pltpu.VMEM((2 + groups, 8, D), F32),
            sems, sems, sems, sems,
            dma((2,)), dma((2,)), dma((2 + groups,)), dma((2 + groups,)),
        ]
        + reduction_scratch(groups, rest.shape[0], 3 * CHUNK, source=False)
        + reduction_scratch(groups, 1, D, source=False)
        + reduction_scratch(groups, 1, cols),
        compiler_params=pltpu.CompilerParams(collective_id=1, has_side_effects=True, vmem_limit_bytes=60 << 20),
    )(
        grad, doc_lengths, got, heads, inverse, x, gres, gain.reshape(1, D), w_query, w_key, w_value,
        rest, parts_o, gate_early, up_early, down_early, gain_rows,
    )


def tuned_body(
    seq_devices, groups, inputs, doc_lengths, gain_attn, w_query, w_key, w_value, w_out, gain_ffn, w_gate, w_up,
    w_down, cotangent,
):
    row_count, shard_len, _ = inputs.shape
    token_count = row_count * shard_len
    stream = inputs.reshape(token_count, D)
    branch, got, heads, inverse = attention_forward(
        seq_devices, inputs, doc_lengths, gain_attn, w_query, w_key, w_value
    )
    output, gres, gmixed, gate_early, up_early, down_early, rest, parts_o, gain_rows = feed_forward(
        groups, branch.reshape(token_count, D), stream, cotangent.reshape(token_count, D), gain_ffn, w_out,
        w_gate.T, w_up.T, w_down,
    )
    input_grad, gate, up, down, out, query, key, value, gains = last_part(
        groups, seq_devices, gmixed.reshape(row_count, shard_len, D), doc_lengths, got, heads, inverse, stream, gres,
        gain_attn, w_query, w_key, w_value, rest, parts_o, gate_early, up_early, down_early, gain_rows,
        w_down.shape[0],
    )
    return (
        output.reshape(row_count, shard_len, D),
        input_grad.reshape(row_count, shard_len, D),
        gains[1, :32],
        query,
        key,
        value,
        out,
        gains[0, :32],
        gate,
        up,
        down.T,
    )


def solution(mesh):
    in_specs = (
        P("dp", "seq", None),
        P("dp", None),
        P(),
        P(),
        P(),
        P(),
        P(),
        P(),
        P(),
        P(),
        P(),
        P("dp", "seq", None),
    )
    out_specs = (
        P("dp", "seq", None),
        P("dp", "seq", None),
        P(("dp", "seq")),
        P(("dp", "seq"), None),
        P(("dp", "seq"), None),
        P(("dp", "seq"), None),
        P(("dp", "seq"), None),
        P(("dp", "seq")),
        P(("dp", "seq"), None),
        P(("dp", "seq"), None),
        P(None, ("dp", "seq")),
    )
    seq_devices, groups = mesh.shape["seq"], mesh.shape["dp"]
    tuned = seq_devices == 8 and seq_devices * groups * 32 == D
    step = functools.partial(tuned_body, seq_devices, groups) if tuned else general_body
    return jax.shard_map(step, mesh=mesh, in_specs=in_specs, out_specs=out_specs, check_vma=False)
```

```python
import functools

import jax
import jax.numpy as jnp
from jax import lax
from jax.experimental import pallas as pl
from jax.experimental.pallas import tpu as pltpu
from jax.sharding import PartitionSpec as P

D = 1024
H = 16
F = 16
HV = 64
BLOCK = 576


eps_norm = 1e-05


def rms_scale(stream, gain_vec):
    return (
        stream * lax.rsqrt(jnp.mean(stream * stream, axis=-1, keepdims=True) + eps_norm) * gain_vec
    )


def taylor_features(vectors):
    feat_width = vectors.shape[-1]
    outer_prod = (vectors[..., :, None] * vectors[..., None, :]).reshape(
        vectors.shape[:-1] + (feat_width * feat_width,)
    )
    ones_part = jnp.ones(vectors.shape[:-1] + (1,), jnp.float32)
    return jnp.concatenate(
        [ones_part, vectors * feat_width ** (-0.25), outer_prod * (0.5 / feat_width) ** 0.5],
        axis=-1,
    )


def document_ids(doc_lens, seq_length):
    doc_ends = jnp.cumsum(doc_lens, dtype=jnp.int32)
    positions = jnp.arange(seq_length, dtype=jnp.int32)
    return jnp.sum(
        (positions[:, None] >= doc_ends[None, :]).astype(jnp.int32), axis=1, dtype=jnp.int32
    )


def attend_row(queries, key_proj, value_proj, doc_row, block_rows):
    seq_length, head_count, feat_width = queries.shape
    value_width = value_proj.shape[-1]
    feat_count = 1 + feat_width + feat_width * feat_width
    block_count = seq_length // block_rows
    highest = lax.Precision.HIGHEST
    query_blocks = queries.reshape(block_count, block_rows, head_count, feat_width)
    key_blocks = key_proj.reshape(block_count, block_rows, head_count, feat_width)
    value_blocks = value_proj.reshape(block_count, block_rows, head_count, value_width)
    doc_blocks = doc_row.reshape(block_count, block_rows)
    previous = jnp.concatenate([jnp.full((1,), -1, jnp.int32), doc_blocks[:-1, -1]])
    positions = jnp.arange(block_rows, dtype=jnp.int32)
    causal = positions[:, None] >= positions[None, :]

    def block_step(carried, pieces):
        state_sum, norm_sum = carried
        query_block, key_block, value_block, doc_block, prior_doc = pieces
        scores = jnp.einsum(
            "thf,shf->hts", query_block, key_block, precision=highest
        ) * feat_width ** (-0.5)
        weights = 1.0 + scores + 0.5 * scores * scores
        same_doc = causal & (doc_block[:, None] == doc_block[None, :])
        weights = jnp.where(same_doc[None, :, :], weights, 0.0)
        numerator = jnp.einsum("hts,shv->thv", weights, value_block, precision=highest)
        denominator = jnp.transpose(jnp.sum(weights, axis=2))
        use_state = (doc_block == prior_doc).astype(jnp.float32)[:, None]
        query_feats = taylor_features(query_block)
        numerator = numerator + use_state[:, :, None] * jnp.einsum(
            "thp,hpv->thv", query_feats, state_sum, precision=highest
        )
        denominator = denominator + use_state * jnp.einsum(
            "thp,hp->th", query_feats, norm_sum, precision=highest
        )
        last_doc = doc_block[-1]
        keep_state = (last_doc == prior_doc).astype(jnp.float32)
        key_feats = (
            taylor_features(key_block) * (doc_block == last_doc).astype(jnp.float32)[:, None, None]
        )
        state_sum = keep_state * state_sum + jnp.einsum(
            "shp,shv->hpv", key_feats, value_block, precision=highest
        )
        norm_sum = keep_state * norm_sum + jnp.sum(key_feats, axis=0)
        return ((state_sum, norm_sum), numerator / denominator[:, :, None])

    initial = (
        jnp.zeros((head_count, feat_count, value_width), jnp.float32),
        jnp.zeros((head_count, feat_count), jnp.float32),
    )
    _, results = lax.scan(
        jax.checkpoint(block_step),
        initial,
        (query_blocks, key_blocks, value_blocks, doc_blocks, previous),
    )
    return results.reshape(seq_length, head_count, value_width)


def project(left, right):
    return jnp.dot(left, right, preferred_element_type=jnp.float32)


def back_project(left, right):
    return lax.dot_general(
        left, right, (((1,), (1,)), ((), ())), preferred_element_type=jnp.float32
    )


def weight_grad(left, right):
    return lax.dot_general(
        left, right, (((0,), (0,)), ((), ())), preferred_element_type=jnp.float32
    )


def swiglu(gate_proj, up_proj):
    return jax.nn.silu(gate_proj) * up_proj


def general_body(
    inputs,
    doc_lengths,
    gain_attn,
    w_query,
    w_key,
    w_value,
    w_out,
    gain_ffn,
    w_gate,
    w_up,
    w_down,
    cotangent,
):
    row_count, shard_len, _ = inputs.shape
    token_count = row_count * shard_len
    stream = inputs.reshape(token_count, D).astype(jnp.float32)
    normed, attn_norm_back = jax.vjp(rms_scale, stream, gain_attn)
    normed_low = normed.astype(jnp.bfloat16)
    query_proj = project(normed_low, w_query).astype(jnp.bfloat16)
    key_proj = project(normed_low, w_key).astype(jnp.bfloat16)
    value_proj = project(normed_low, w_value).astype(jnp.bfloat16)
    query_heads, key_heads, value_heads = (
        lax.all_to_all(
            query_proj.reshape(row_count, shard_len, H, F),
            "seq",
            split_axis=2,
            concat_axis=1,
            tiled=True,
        ),
        lax.all_to_all(
            key_proj.reshape(row_count, shard_len, H, F),
            "seq",
            split_axis=2,
            concat_axis=1,
            tiled=True,
        ),
        lax.all_to_all(
            value_proj.reshape(row_count, shard_len, H, HV),
            "seq",
            split_axis=2,
            concat_axis=1,
            tiled=True,
        ),
    )
    seq_length = query_heads.shape[1]
    doc_rows = jax.vmap(lambda doc_lens: document_ids(doc_lens, seq_length))(doc_lengths)

    def attend_all(queries, keys_in, values_in):
        return jax.vmap(attend_row, in_axes=(0, 0, 0, 0, None))(
            queries, keys_in, values_in, doc_rows, BLOCK
        )

    mixed_heads, attend_back = jax.vjp(
        attend_all,
        query_heads.astype(jnp.float32),
        key_heads.astype(jnp.float32),
        value_heads.astype(jnp.float32),
    )
    mixed_rows = lax.all_to_all(
        mixed_heads.astype(jnp.bfloat16), "seq", split_axis=1, concat_axis=2, tiled=True
    )
    mixed_flat = mixed_rows.reshape(token_count, D)
    residual = stream + project(mixed_flat, w_out)
    normed_ffn, ffn_norm_back = jax.vjp(rms_scale, residual, gain_ffn)
    ffn_low = normed_ffn.astype(jnp.bfloat16)
    gate_proj = project(ffn_low, w_gate)
    up_proj = project(ffn_low, w_up)
    hidden, act_back = jax.vjp(swiglu, gate_proj, up_proj)
    hidden_low = hidden.astype(jnp.bfloat16)
    output = residual + project(hidden_low, w_down)
    grad_out = cotangent.reshape(token_count, D)
    grad_gate, grad_up = act_back(back_project(grad_out, w_down))
    grad_gate_low = grad_gate.astype(jnp.bfloat16)
    grad_up_low = grad_up.astype(jnp.bfloat16)
    down_grad_t = weight_grad(grad_out, hidden_low)
    gate_grad = weight_grad(ffn_low, grad_gate_low)
    up_grad = weight_grad(ffn_low, grad_up_low)
    grad_normed_ffn = back_project(grad_gate_low, w_gate) + back_project(grad_up_low, w_up)
    grad_residual, gain_ffn_grad = ffn_norm_back(grad_normed_ffn)
    grad_residual = grad_residual + grad_out.astype(jnp.float32)
    grad_branch = grad_residual.astype(jnp.bfloat16)
    out_grad = weight_grad(mixed_flat, grad_branch)
    grad_mixed = (
        back_project(grad_branch, w_out).astype(jnp.bfloat16).reshape(row_count, shard_len, H, HV)
    )
    grad_heads = lax.all_to_all(grad_mixed, "seq", split_axis=2, concat_axis=1, tiled=True)
    grad_query, grad_key, grad_value = attend_back(grad_heads.astype(jnp.float32))
    back_query, back_key, back_value = (
        lax.all_to_all(
            grad_query.astype(jnp.bfloat16), "seq", split_axis=1, concat_axis=2, tiled=True
        ),
        lax.all_to_all(
            grad_key.astype(jnp.bfloat16), "seq", split_axis=1, concat_axis=2, tiled=True
        ),
        lax.all_to_all(
            grad_value.astype(jnp.bfloat16), "seq", split_axis=1, concat_axis=2, tiled=True
        ),
    )
    back_query = back_query.reshape(token_count, H * F)
    back_key = back_key.reshape(token_count, H * F)
    back_value = back_value.reshape(token_count, D)
    query_grad = weight_grad(normed_low, back_query)
    key_grad = weight_grad(normed_low, back_key)
    value_grad = weight_grad(normed_low, back_value)
    grad_normed = (
        back_project(back_query, w_query)
        + back_project(back_key, w_key)
        + back_project(back_value, w_value)
    )
    grad_stream, gain_attn_grad = attn_norm_back(grad_normed)
    input_grad = grad_residual + grad_stream
    (
        gain_attn_part,
        query_part,
        key_part,
        value_part,
        out_part,
        gain_ffn_part,
        gate_part,
        up_part,
        down_part,
    ) = (
        lax.psum_scatter(gain_attn_grad, ("dp", "seq"), scatter_dimension=0, tiled=True),
        lax.psum_scatter(query_grad, ("dp", "seq"), scatter_dimension=0, tiled=True),
        lax.psum_scatter(key_grad, ("dp", "seq"), scatter_dimension=0, tiled=True),
        lax.psum_scatter(value_grad, ("dp", "seq"), scatter_dimension=0, tiled=True),
        lax.psum_scatter(out_grad, ("dp", "seq"), scatter_dimension=0, tiled=True),
        lax.psum_scatter(gain_ffn_grad, ("dp", "seq"), scatter_dimension=0, tiled=True),
        lax.psum_scatter(gate_grad, ("dp", "seq"), scatter_dimension=0, tiled=True),
        lax.psum_scatter(up_grad, ("dp", "seq"), scatter_dimension=0, tiled=True),
        lax.psum_scatter(down_grad_t, ("dp", "seq"), scatter_dimension=0, tiled=True),
    )
    return (
        output.reshape(row_count, shard_len, D).astype(jnp.bfloat16),
        input_grad.reshape(row_count, shard_len, D).astype(jnp.bfloat16),
        gain_attn_part,
        query_part,
        key_part,
        value_part,
        out_part,
        gain_ffn_part,
        gate_part,
        up_part,
        jnp.transpose(down_part),
    )


F32 = jnp.float32
BF16 = jnp.bfloat16
MESH = pl.DeviceIdType.MESH
TILE = 384
PAIR = 2 * HV


def nt(left, right):
    return lax.dot_general(left, right, (((1,), (1,)), ((), ())), preferred_element_type=F32)


def nn(left, right):
    return jnp.dot(left, right, preferred_element_type=F32)


def lanes_of(shape):
    return lax.broadcasted_iota(jnp.int32, shape, len(shape) - 1)


def first_visible(ends, positions):
    start = jnp.zeros_like(positions)
    for end in ends:
        start = jnp.where(positions >= end, end, start)
    return start


def row_ends(doc_ref, row):
    ends, total = [], 0
    for j in range(doc_ref.shape[1] - 1):
        total = total + doc_ref[row, j]
        ends.append(total)
    return ends


def spread_matrix():
    half = H * F
    shape = (2 * half, (H // 2) * 128)
    source = lax.broadcasted_iota(jnp.int32, shape, 0)
    column = lax.broadcasted_iota(jnp.int32, shape, 1)
    pair, lane = column // 128, column % 64
    wanted = pair * 32 + lane + jnp.where(lane < 32, 0, half - 32)
    return jnp.where(source == wanted, 1.0, 0.0).astype(BF16)


def gather_matrix():
    half = H * F
    shape = (2 * half, 2 * half)
    source = lax.broadcasted_iota(jnp.int32, shape, 0)
    column = lax.broadcasted_iota(jnp.int32, shape, 1)
    pair, lane = source // 64, source % 64
    wanted = pair * 32 + lane + jnp.where(lane < 32, 0, half - 32)
    return jnp.where(column == wanted, 1.0, 0.0).astype(BF16)


def packed_rows(length):
    return (length // 2 + 15) // 16 * 16


def prepare_row(got_ref, row, qa_ref, ka_ref, ve_ref, seq_devices, length):
    low = packed_rows(length)

    def part(peer, carry):
        values = got_ref[row, peer, :length, :].astype(F32)
        packed = got_ref[row, peer, length : length + low, :].astype(F32)
        turned = pltpu.roll(packed, 64, 1)
        both = jnp.concatenate([packed, turned[2 * low - length :]], axis=0)
        lane = lanes_of((length, 128))
        keys = pltpu.roll(both, 96, 1)
        at = pl.ds(pl.multiple_of(peer * length, 16), length)
        one = jnp.where(lane == 32, 1.0, 0.0)
        qa_ref[at, :] = jnp.where(lane < 32, both * 0.25, one).astype(BF16)
        ka_ref[0, at, :] = jnp.where(lane < 16, keys, one).astype(BF16)
        ka_ref[1, at, :] = jnp.where((lane >= 16) & (lane < 32), keys, one).astype(BF16)
        ve_ref[0, at, :] = jnp.where(lane < 64, values, 1.0).astype(BF16)
        ve_ref[1, at, :] = jnp.where(lane >= 64, values, 1.0).astype(BF16)
        return carry

    lax.fori_loop(0, seq_devices, part, 0)


def attend_forward(ends, qa_ref, ka_ref, ve_ref, mixed_ref, inverse_ref):
    length = qa_ref.shape[0]
    for block in range(length // TILE):
        reach = (block + 1) * TILE
        at = pl.ds(block * TILE, TILE)
        queries = qa_ref[at, :]
        t = lax.broadcasted_iota(jnp.int32, (TILE, 1), 0) + block * TILE
        start = first_visible(ends, t)
        s = lax.broadcasted_iota(jnp.int32, (TILE, reach), 1)
        visible = (s >= start) & (s <= t)
        sums = []
        for head in range(2):
            base = nt(queries, ka_ref[head, :reach, :])
            weights = jnp.where(visible, base * base + 1.0, 0.0).astype(BF16)
            sums.append(nn(weights, ve_ref[head, :reach, :]))
        lower = lanes_of((TILE, 128)) < 64
        numerator = jnp.where(lower, sums[0], sums[1])
        inverse = 1.0 / pltpu.roll(jnp.where(lower, sums[1], sums[0]), 64, 1)
        mixed_ref[at, :] = (numerator * inverse).astype(BF16)
        inverse_ref[at, :] = inverse


def attend_backward(
    ends, grad_ref, qa_ref, ka_ref, ve_ref, mixed_ref, inverse_ref, dn_ref, qs_ref, kt_ref, dqt_ref, gqk_ref, gv_ref
):
    length = qa_ref.shape[0]
    lane = lanes_of((length, 128))
    lower = lane < 64
    scaled = grad_ref[...].astype(F32) * inverse_ref[...]
    away = pltpu.roll(-scaled * mixed_ref[...].astype(F32), 64, 1)
    dn_ref[0] = jnp.where(lower, scaled, away).astype(BF16)
    dn_ref[1] = jnp.where(lower, away, scaled).astype(BF16)
    shifted = pltpu.roll(qa_ref[...].astype(F32), 32, 1)
    qs_ref[...] = jnp.where((lane >= 32) & (lane < 64), shifted * 2.0, 0.0).astype(BF16)
    for head in range(2):
        kt_ref[head] = ka_ref[head].astype(F32).T[:32].astype(BF16)
    dqt_ref[...] = jnp.zeros_like(dqt_ref)
    for block in range(length // TILE):
        first = block * TILE
        at = pl.ds(first, TILE)
        rest = pl.ds(first, length - first)
        shape = (TILE, length - first)
        t = lax.broadcasted_iota(jnp.int32, (1, shape[1]), 1) + first
        s = lax.broadcasted_iota(jnp.int32, shape, 0) + first
        visible = (s >= first_visible(ends, t)) & (s <= t)
        value_sums, key_sums = [], []
        for head in range(2):
            base = nt(ka_ref[head, at, :], qa_ref[rest, :])
            grad_weights = nt(ve_ref[head, at, :], dn_ref[head, rest, :])
            weights = jnp.where(visible, base * base + 1.0, 0.0).astype(BF16)
            grad_base = jnp.where(visible, grad_weights * base, 0.0).astype(BF16)
            value_sums.append(nn(weights, dn_ref[head, rest, :]))
            key_sums.append(nn(grad_base, qs_ref[rest, :]))
            dqt_ref[:, rest] += nn(kt_ref[head, :, at], grad_base)
        lane = lanes_of((TILE, 128))
        gv_ref[at, :] = jnp.where(lane < 64, value_sums[0], value_sums[1]).astype(BF16)
        gqk_ref[at, :] = jnp.where(
            (lane >= 32) & (lane < 48), key_sums[0], jnp.where((lane >= 48) & (lane < 64), key_sums[1], 0.0)
        )
    queries = jnp.concatenate([dqt_ref[...] * 0.5, jnp.zeros((96, length), F32)], axis=0)
    gqk_ref[...] += queries.T


def greet(seq_devices):
    row_group, me = lax.axis_index("dp"), lax.axis_index("seq")
    barrier = pltpu.get_barrier_semaphore()
    for step in range(1, seq_devices):
        peer = lax.rem(me + step, seq_devices)
        pl.semaphore_signal(barrier, inc=1, device_id=(row_group, peer), device_id_type=MESH)
    pl.semaphore_wait(barrier, seq_devices - 1)
    return row_group, me


def sending(source, target, send_sem, recv_sem, row_group, peer):
    return pltpu.make_async_remote_copy(
        src_ref=source,
        dst_ref=target,
        send_sem=send_sem,
        recv_sem=recv_sem,
        device_id=(row_group, peer),
        device_id_type=MESH,
    )


def forward_kernel(
    seq_devices, rows, length,
    x_ref, doc_ref, gain_ref, wq_ref, wk_ref, wv_ref,
    branch_ref, got_out, head_out, inverse_ref,
    out_buf, got, heads, back, spread, qa, ka, ve, send_a, recv_a, send_b, recv_b,
):
    row_group, me = greet(seq_devices)
    low = packed_rows(length)
    lower = lanes_of((low, 128)) < 64
    spread[...] = spread_matrix()

    def outgoing(row, step):
        peer = lax.rem(me + step, seq_devices)
        return sending(
            out_buf.at[row, peer], got.at[row, me], send_a.at[row, step], recv_a.at[row, step], row_group, peer
        )

    def returning(row, step):
        peer = lax.rem(me + step, seq_devices)
        there = pl.ds(pl.multiple_of(peer * length, 16), length)
        mine = pl.ds(pl.multiple_of(me * PAIR, 128), PAIR)
        return sending(
            heads.at[row, there, :], back.at[row, :, mine], send_b.at[row, step], recv_b.at[row, step], row_group, peer
        )

    def project_row(row, carry):
        stream = x_ref[row].astype(F32)
        normed = rms_scale(stream, gain_ref[...]).astype(BF16)
        both = jnp.concatenate([nn(normed, wq_ref[...]), nn(normed, wk_ref[...])], axis=1).astype(BF16)
        tiles = nn(both, spread[...])
        values = nn(normed, wv_ref[...]).astype(BF16)
        for pair in range(seq_devices):
            tile = tiles[:, pair * 128 : (pair + 1) * 128]
            out_buf[row, pair, :length, :] = values[:, pair * PAIR : (pair + 1) * PAIR]
            out_buf[row, pair, length:, :] = jnp.where(lower, tile[:low], tile[length - low :]).astype(BF16)
        for step in range(1, seq_devices):
            outgoing(row, step).start()
        got[row, me] = out_buf[row, me]
        return carry

    lax.fori_loop(0, rows, project_row, 0)

    def attend(row, carry):
        for step in range(1, seq_devices):
            outgoing(row, step).wait_recv()
        prepare_row(got, row, qa, ka, ve, seq_devices, length)
        attend_forward(row_ends(doc_ref, row), qa, ka, ve, heads.at[row], inverse_ref.at[row])
        for step in range(1, seq_devices):
            returning(row, step).start()
        here = pl.ds(pl.multiple_of(me * length, 16), length)
        back[row, :, pl.ds(pl.multiple_of(me * PAIR, 128), PAIR)] = heads[row, here, :]
        return carry

    lax.fori_loop(0, rows, attend, 0)
    got_out[...] = got[...]
    head_out[...] = heads[...]

    def finish(row, carry):
        for step in range(1, seq_devices):
            outgoing(row, step).wait_send()
            returning(row, step).wait()
        branch_ref[row] = back[row]
        return carry

    lax.fori_loop(0, rows, finish, 0)


VMEM_SPEC = pl.BlockSpec(memory_space=pltpu.VMEM)
SMEM_SPEC = pl.BlockSpec(memory_space=pltpu.SMEM)


def attention_forward(seq_devices, x, doc_lengths, gain, w_query, w_key, w_value):
    rows, length, _ = x.shape
    total = seq_devices * length
    message = (rows, seq_devices, length + packed_rows(length), 128)
    sems = pltpu.SemaphoreType.DMA((rows, seq_devices))
    return pl.pallas_call(
        functools.partial(forward_kernel, seq_devices, rows, length),
        name="attention_forward",
        out_shape=[
            jax.ShapeDtypeStruct((rows, length, D), BF16),
            jax.ShapeDtypeStruct(message, BF16),
            jax.ShapeDtypeStruct((rows, total, 128), BF16),
            jax.ShapeDtypeStruct((rows, total, 128), F32),
        ],
        in_specs=[VMEM_SPEC, SMEM_SPEC, VMEM_SPEC, VMEM_SPEC, VMEM_SPEC, VMEM_SPEC],
        out_specs=[VMEM_SPEC] * 4,
        scratch_shapes=[
            pltpu.VMEM(message, BF16),
            pltpu.VMEM(message, BF16),
            pltpu.VMEM((rows, total, 128), BF16),
            pltpu.VMEM((rows, length, D), BF16),
            pltpu.VMEM((2 * H * F, D), BF16),
            pltpu.VMEM((total, 128), BF16),
            pltpu.VMEM((2, total, 128), BF16),
            pltpu.VMEM((2, total, 128), BF16),
            sems, sems, sems, sems,
        ],
        compiler_params=pltpu.CompilerParams(collective_id=0, has_side_effects=True, vmem_limit_bytes=56 << 20),
    )(x, doc_lengths, gain.reshape(1, D), w_query, w_key, w_value)


CHUNK = 256
STEP_ROWS = 48
XY_EARLY = 6
SLOTS = 7
VMEM_BYTES = 63 << 20


def place(me):
    core = lax.rem(me, 2)
    return core, 2 + 2 * core, 4 - 2 * core


def blocks_of(core, groups):
    first, second = 2 + 2 * core, 4 - 2 * core
    return [
        pl.multiple_of(32 * (8 * group + first * i + second * j + core), 32)
        for i in range(2)
        for j in range(2)
        for group in range(groups)
    ]


class Reduction:
    def __init__(self, groups, source, buffers, slot_of=None, place_of=None):
        self.groups, self.source = groups, source
        self.got_a, self.got_b, self.got_z, self.a_sems, self.b_sems, self.z_send, self.z_recv = buffers
        self.slot_of = slot_of or (lambda unit: unit)
        self.place_of = place_of or (lambda unit: unit)
        self.group, self.me = lax.axis_index("dp"), lax.axis_index("seq")
        core, first, second = place(self.me)
        self.bit_a, self.bit_b = lax.rem(self.me // first, 2), lax.rem(self.me // second, 2)
        self.peer_a = self.me + first * (1 - 2 * self.bit_a)
        self.peer_b = self.me + second * (1 - 2 * self.bit_b)

    def block(self, group):
        return pl.ds(pl.multiple_of(group * 32, 32), 32)

    def other(self, step):
        return lax.rem(self.group + step, self.groups)

    def a_copy(self, unit):
        at = self.place_of(unit)
        return sending(
            self.source.at[self.slot_of(unit), 1 - self.bit_a], self.got_a.at[at], self.a_sems.at[0, at],
            self.a_sems.at[1, at], self.group, self.peer_a,
        )

    def b_copy(self, unit):
        at = self.place_of(unit)
        return sending(
            self.got_a.at[at, 1 - self.bit_b], self.got_b.at[at], self.b_sems.at[0, at], self.b_sems.at[1, at],
            self.group, self.peer_b,
        )

    def z_copy(self, unit, step):
        at = self.place_of(unit)
        return sending(
            self.got_b.at[at, self.block(self.other(step)), :], self.got_z.at[at, step - 1],
            self.z_send.at[at, step - 1], self.z_recv.at[at, step - 1], self.other(step), self.me,
        )

    def a_step(self, unit):
        at = self.place_of(unit)
        self.a_copy(unit).wait_recv()
        mine = self.source[self.slot_of(unit), self.bit_a].astype(F32)
        self.got_a[at] = (mine + self.got_a[at].astype(F32)).astype(BF16)
        self.b_copy(unit).start()

    def b_step(self, unit):
        at = self.place_of(unit)
        self.b_copy(unit).wait_recv()
        self.got_b[at] = (self.got_a[at, self.bit_b].astype(F32) + self.got_b[at].astype(F32)).astype(BF16)
        for step in range(1, self.groups):
            self.z_copy(unit, step).start()

    def z_step(self, unit):
        at = self.place_of(unit)
        total = self.got_b[at, self.block(self.group), :].astype(F32)
        for step in range(1, self.groups):
            self.z_copy(unit, step).wait_recv()
            total += self.got_z[at, step - 1].astype(F32)
        return total

    def wait_sent(self, unit):
        self.b_copy(unit).wait_send()
        for step in range(1, self.groups):
            self.z_copy(unit, step).wait_send()


class GroupsFirst(Reduction):
    def z_copy(self, unit, step):
        at = self.place_of(unit)
        return sending(
            self.source.at[self.slot_of(unit), :, :, self.block(self.other(step)), :], self.got_z.at[at, step - 1],
            self.z_send.at[at, step - 1], self.z_recv.at[at, step - 1], self.other(step), self.me,
        )

    def a_copy(self, unit):
        at = self.place_of(unit)
        return sending(
            self.got_z.at[at, 0, 1 - self.bit_a], self.got_a.at[at], self.a_sems.at[0, at], self.a_sems.at[1, at],
            self.group, self.peer_a,
        )

    def start(self, unit):
        for step in range(1, self.groups):
            self.z_copy(unit, step).start()

    def z_step(self, unit):
        at = self.place_of(unit)
        total = self.source[self.slot_of(unit), :, :, self.block(self.group), :].astype(F32)
        for step in range(1, self.groups):
            self.z_copy(unit, step).wait_recv()
            total += self.got_z[at, step - 1].astype(F32)
        self.got_z[at, 0] = total.astype(BF16)
        self.a_copy(unit).start()

    def a_step(self, unit):
        at = self.place_of(unit)
        self.a_copy(unit).wait_recv()
        self.got_a[at] = (self.got_z[at, 0, self.bit_a].astype(F32) + self.got_a[at].astype(F32)).astype(BF16)
        self.b_copy(unit).start()

    def b_step(self, unit):
        at = self.place_of(unit)
        self.b_copy(unit).wait_recv()
        return self.got_a[at, self.bit_b].astype(F32) + self.got_b[at].astype(F32)

    def wait_sent(self, unit):
        self.a_copy(unit).wait_send()
        self.b_copy(unit).wait_send()
        for step in range(1, self.groups):
            self.z_copy(unit, step).wait_send()


def reduction_buffers(groups, units, cols):
    rows = 32 * groups
    dma = pltpu.SemaphoreType.DMA
    return [
        pltpu.VMEM((units, 2, rows, cols), BF16),
        pltpu.VMEM((units, rows, cols), BF16),
        pltpu.VMEM((units, groups - 1, 32, cols), BF16),
        dma((2, units)),
        dma((2, units)),
        dma((units, groups - 1)),
        dma((units, groups - 1)),
    ]


def groups_first_buffers(groups, units, cols):
    dma = pltpu.SemaphoreType.DMA
    return [
        pltpu.VMEM((units, 2, 32, cols), BF16),
        pltpu.VMEM((units, 32, cols), BF16),
        pltpu.VMEM((units, groups - 1, 2, 2, 32, cols), BF16),
        dma((2, units)),
        dma((2, units)),
        dma((units, groups - 1)),
        dma((units, groups - 1)),
    ]


def store_blocks(target, unit, col, values, groups):
    rows = 32 * groups
    for i in range(2):
        for j in range(2):
            at = (2 * i + j) * rows
            target[unit, i, j, :, col : col + values.shape[1]] = values[at : at + rows].astype(BF16)


def turn(source, tokens, padded, turned):
    turned[...] = jnp.concatenate([source, jnp.zeros((padded - tokens, D), BF16)], axis=0).T


def split_rows(turned, mine_ref, theirs_ref, core, groups):
    for i, (mine, theirs) in enumerate(zip(blocks_of(core, groups), blocks_of(1 - core, groups))):
        a, b, group = i // (2 * groups), i // groups % 2, i % groups
        mine_ref[a, b, group * 32 : (group + 1) * 32, :] = turned[pl.ds(mine, 32), :]
        theirs_ref[a, b, group * 32 : (group + 1) * 32, :] = turned[pl.ds(theirs, 32), :]


def write_unit(total, at, w, gate_out, up_out, down_out):
    down_out[:, pl.ds(at, w)] = total[:, :w]
    gate_out[:, pl.ds(at, w)] = total[:, CHUNK : CHUNK + w]
    up_out[:, pl.ds(at, w)] = total[:, 2 * CHUNK : 2 * CHUNK + w]


def backward_kernel(
    groups, seq_devices, rows, length, width,
    branch_ref, x_ref, cot_ref, gain_ref, wo_ref, wg_hbm, wu_hbm, wd_hbm,
    doc_ref, got_hbm, heads_hbm, inverse_hbm, gain_attn_ref, wq_ref, wk_ref, wv_hbm,
    output_ref, input_out, gate_out, up_out, down_out, wout_out, query_out, key_out, value_out, gains_out,
    residual, normed, out_acc, gnf, w_buf, lhs, right, parts, parts_o, q_source,
    got, heads, inverse, arrived, back, qa, ka, ve, dn, qs, kt, dqt, gqk, gv, gains, gains_got,
    w_sem, wv_sems, in_sems, lhs_sems, pair_sems, send_a, recv_a, send_b, recv_b, gain_send, gain_recv,
    *buffers,
):
    row_group, me = lax.axis_index("dp"), lax.axis_index("seq")
    core, _, _ = place(me)
    partner = me + 1 - 2 * core
    tokens = rows * length
    padded = right.shape[1] // 2
    full = width // CHUNK
    tail = width - full * CHUNK
    low = packed_rows(length)
    lower = lanes_of((low, 128)) < 64
    here = pl.ds(pl.multiple_of(me * length, 16), length)
    half = H * F

    def slot_of(unit):
        return lax.rem(unit, SLOTS)

    z_units = full - 1 - XY_EARLY

    def place_of(unit):
        return unit if isinstance(unit, int) and unit < XY_EARLY else jnp.where(unit < XY_EARLY, unit, unit - z_units)

    feed = Reduction(groups, parts, buffers[:7], slot_of, place_of)
    outer = Reduction(groups, parts_o, buffers[7:14])
    qkv = Reduction(groups, q_source, buffers[14:21])
    first = GroupsFirst(groups, parts, buffers[21:28], slot_of, lambda unit: unit - XY_EARLY)

    barrier = pltpu.get_barrier_semaphore()
    for step in range(1, seq_devices):
        peer = lax.rem(me + step, seq_devices)
        pl.semaphore_signal(barrier, inc=1, device_id=(row_group, peer), device_id_type=MESH)
    for step in range(1, groups):
        other = lax.rem(row_group + step, groups)
        pl.semaphore_signal(barrier, inc=1, device_id=(other, me), device_id_type=MESH)

    def loads(chunk, slot, w):
        at = pl.ds(pl.multiple_of(chunk * CHUNK, CHUNK), w)
        return [
            pltpu.make_async_copy(hbm.at[at, :], w_buf.at[slot, which, pl.ds(0, w), :], w_sem.at[slot, which])
            for which, hbm in enumerate((wg_hbm, wu_hbm, wd_hbm))
        ]

    def value_load(part):
        return pltpu.make_async_copy(
            wv_hbm.at[pl.ds(part * CHUNK, CHUNK), :], w_buf.at[part // 3, part % 3], wv_sems.at[part]
        )

    for chunk in range(2):
        for copy in loads(chunk, chunk, CHUNK):
            copy.start()
    saved = [
        pltpu.make_async_copy(source, target, in_sems.at[i])
        for i, (source, target) in enumerate(((got_hbm, got), (heads_hbm, heads), (inverse_hbm, inverse)))
    ]
    for copy in saved:
        copy.start()

    def norm_forward(step, carry):
        at = pl.ds(pl.multiple_of(step * STEP_ROWS, 16), STEP_ROWS)
        value = x_ref[at, :].astype(F32) + residual[at, :]
        residual[at, :] = value
        out_acc[at, :] = value
        normed[at, :] = rms_scale(value, gain_ref[...]).astype(BF16)
        return carry

    residual[...] = nn(branch_ref[...], wo_ref[...])
    lax.fori_loop(0, tokens // STEP_ROWS, norm_forward, 0)
    gnf[...] = jnp.zeros_like(gnf)

    pl.semaphore_wait(barrier, seq_devices + groups - 2)

    def lhs_copy(which):
        return sending(
            q_source.at[0, :, :, :, pl.ds(which % 3 * padded, padded)],
            lhs.at[which % 3, :, :, :, pl.ds(padded, padded)],
            lhs_sems.at[0, which], lhs_sems.at[1, which], row_group, partner,
        )

    def prepare_lhs(which, source):
        turned = right.at[3 if which < 3 else 1, :, pl.ds(0, padded)]
        turn(source, tokens, padded, turned)
        at = which % 3 * padded
        split_rows(
            turned, lhs.at[which % 3, :, :, :, pl.ds(0, padded)], q_source.at[0, :, :, :, pl.ds(at, padded)], core, groups
        )

    def left(which):
        return lhs[which].reshape(D // 2, 2 * padded)

    for which, source in enumerate((cot_ref, normed, branch_ref)):
        prepare_lhs(which, source[...])
        lhs_copy(which).start()
    gap = padded - tokens

    def clear(slot, count):
        for base in (tokens, padded + tokens):
            right[slot : slot + count, base : base + gap, :] = jnp.zeros((count, gap, 3 * CHUNK), BF16)

    clear(0, 4)

    def right_copy(slot, cols, sem):
        return sending(
            right.at[slot, pl.ds(0, tokens), pl.ds(0, cols)], right.at[slot, pl.ds(padded, tokens), pl.ds(0, cols)],
            pair_sems.at[0, sem], pair_sems.at[1, sem], row_group, partner,
        )

    def pair_copy(chunk):
        return right_copy(lax.rem(chunk, 4), 3 * CHUNK, chunk)

    def forward_part(chunk, wg, wu, wd, w):
        slot = lax.rem(chunk, 4)
        gate = nt(normed[...], wg)
        up = nt(normed[...], wu)
        sigmoid = 1.0 / (1.0 + jnp.exp(-gate))
        silu = gate * sigmoid
        hidden = (silu * up).astype(BF16)
        grad_hidden = nt(cot_ref[...], wd)
        grad_gate = (grad_hidden * up * (sigmoid * (1.0 + gate * (1.0 - sigmoid)))).astype(BF16)
        grad_up = (grad_hidden * silu).astype(BF16)
        for part, values in enumerate((hidden, grad_gate, grad_up)):
            right[slot, :tokens, part * CHUNK : part * CHUNK + w] = values
            if w < CHUNK:
                right[slot, :tokens, part * CHUNK + w : (part + 1) * CHUNK] = jnp.zeros((tokens, CHUNK - w), BF16)
        pair_copy(chunk).start()
        out_acc[...] += nn(hidden, wd)
        gnf[...] += nn(grad_gate, wg) + nn(grad_up, wu)

    def grad_part(chunk):
        pair_copy(chunk).wait()
        slot = lax.rem(chunk, 4)
        store_blocks(parts, slot_of(chunk), 0, nn(left(0), right[slot, :, 0:CHUNK]), groups)
        store_blocks(parts, slot_of(chunk), CHUNK, nn(left(1), right[slot, :, CHUNK:]), groups)

    def forward_step(chunk):
        slot = lax.rem(chunk, 2)
        for copy in loads(chunk, slot, CHUNK):
            copy.wait()
        forward_part(chunk, w_buf[slot, 0], w_buf[slot, 1], w_buf[slot, 2], CHUNK)

    def ticks(chunk):
        @pl.when((chunk >= 4) & (lax.rem(chunk, 2) == 0))
        def _():
            feed.a_step((chunk - 4) // 2)

        @pl.when((chunk >= 7) & (lax.rem(chunk, 2) == 1))
        def _():
            feed.b_step((chunk - 7) // 2)

    def xy_main(chunk, carry):
        for copy in loads(chunk + 1, lax.rem(chunk + 1, 2), CHUNK):
            copy.start()
        forward_step(chunk)
        grad_part(chunk - 1)
        feed.a_copy(chunk - 1).start()
        ticks(chunk)
        return carry

    def z_main(chunk, carry):
        @pl.when(chunk < full - 1)
        def _():
            for copy in loads(chunk + 1, lax.rem(chunk + 1, 2), CHUNK):
                copy.start()

        @pl.when(chunk == full - 1)
        def _():
            for copy in loads(full, full % 2, tail):
                copy.start()

        forward_step(chunk)

        @pl.when(chunk - 1 >= SLOTS)
        def _():
            feed.a_copy(chunk - 1 - SLOTS).wait_send()

        grad_part(chunk - 1)
        first.start(chunk - 1)
        ticks(chunk)
        return carry

    forward_step(0)
    for which in range(3):
        lhs_copy(which).wait()
    lax.fori_loop(1, XY_EARLY + 1, xy_main, 0)
    lax.fori_loop(XY_EARLY + 1, full, z_main, 0)
    slot = full % 2
    for copy in loads(full, slot, tail):
        copy.wait()
    forward_part(full, w_buf[slot, 0, :tail], w_buf[slot, 1, :tail], w_buf[slot, 2, :tail], tail)
    for part in range(D // CHUNK):
        value_load(part).start()
    feed.a_copy(full - 1 - SLOTS).wait_send()
    grad_part(full - 1)

    gains[...] = jnp.zeros_like(gains)

    def norm_backward_ffn(step, carry):
        at = pl.ds(pl.multiple_of(step * STEP_ROWS, 16), STEP_ROWS)
        value, grad = residual[at, :], gnf[at, :]
        scale = lax.rsqrt(jnp.mean(value * value, axis=-1, keepdims=True) + eps_norm)
        gains[0:1, :] += jnp.sum(grad * value * scale, axis=0, keepdims=True)
        weighted = grad * gain_ref[...]
        mean = jnp.mean(weighted * value, axis=-1, keepdims=True)
        total = cot_ref[at, :].astype(F32) + scale * weighted - value * (scale * scale * scale * mean)
        gnf[at, :] = total
        right[3, at, :] = total[:, : 3 * CHUNK].astype(BF16)
        right[0, at, :CHUNK] = total[:, 3 * CHUNK :].astype(BF16)
        output_ref[at, :] = out_acc[at, :].astype(BF16)
        return carry

    lax.fori_loop(0, tokens // STEP_ROWS, norm_backward_ffn, 0)
    normed[...] = (
        nt(right[3, :tokens, :], wo_ref[:, : 3 * CHUNK]) + nt(right[0, :tokens, :CHUNK], wo_ref[:, 3 * CHUNK :])
    ).astype(BF16)

    def outgoing(row, step):
        peer = lax.rem(me + step, seq_devices)
        theirs = pl.ds(pl.multiple_of(peer * PAIR, 128), PAIR)
        at = pl.ds(pl.multiple_of(row * length, 16), length)
        return sending(
            normed.at[at, theirs], arrived.at[row, here, :], send_a.at[row, step], recv_a.at[row, step],
            row_group, peer,
        )

    def returning(row, step):
        peer = lax.rem(me + step, seq_devices)
        return sending(
            got.at[row, peer], back.at[row, me], send_b.at[row, step], recv_b.at[row, step], row_group, peer
        )

    def send_row(row, carry):
        for step in range(1, seq_devices):
            outgoing(row, step).start()
        at = pl.ds(pl.multiple_of(row * length, 16), length)
        arrived[row, here, :] = normed[at, pl.ds(pl.multiple_of(me * PAIR, 128), PAIR)]
        return carry

    lax.fori_loop(0, rows, send_row, 0)
    feed.a_step(3)
    feed.a_copy(full - SLOTS).wait_send()
    grad_part(full)
    out_pairs = [right_copy(3, 3 * CHUNK, full + 1), right_copy(0, CHUNK, full + 2)]
    for copy in out_pairs:
        copy.start()
    feed.a_copy(full - 1).start()
    feed.a_copy(full).start()
    prepare_lhs(3, rms_scale(x_ref[...].astype(F32), gain_attn_ref[...]).astype(BF16))
    clear(1, 1)
    for copy in out_pairs:
        copy.wait()
    lhs_copy(3).start()
    for col in range(0, D, CHUNK):
        columns = right[3, :, col : col + CHUNK] if col < 3 * CHUNK else right[0, :, :CHUNK]
        store_blocks(parts_o, 0, col, nn(left(2), columns), groups)
    gather = right.at[3, pl.ds(0, 2 * half), pl.ds(0, 2 * half)]
    gather[...] = gather_matrix()
    for copy in saved:
        copy.wait()

    def attend(row, carry):
        prepare_row(got, row, qa, ka, ve, seq_devices, length)
        for step in range(1, seq_devices):
            outgoing(row, step).wait_recv()
        attend_backward(
            row_ends(doc_ref, row), arrived.at[row], qa, ka, ve, heads.at[row], inverse.at[row],
            dn, qs, kt, dqt, gqk, gv,
        )

        def pack(peer, inner):
            at = pl.multiple_of(peer * length, 16)
            got[row, peer, :length, :] = gv[pl.ds(at, length), :]
            front = gqk[pl.ds(at, low), :]
            rear = pltpu.roll(gqk[pl.ds(at + length - low, low), :], 64, 1)
            got[row, peer, length:, :] = jnp.where(lower, front, rear).astype(BF16)
            return inner

        lax.fori_loop(0, seq_devices, pack, 0)
        for step in range(1, seq_devices):
            returning(row, step).start()
        back[row, me] = got[row, me]

        @pl.when(row < 2)
        def _():
            feed.a_step(4 + row)

        feed.b_step(2 + row)
        return carry

    lax.fori_loop(0, rows, attend, 0)
    outer.a_copy(0).start()
    feed.b_step(2 + rows)
    feed.a_step(full - 1)
    first.z_step(XY_EARLY)
    feed.a_step(full)

    def unpack(row, carry):
        for step in range(1, seq_devices):
            outgoing(row, step).wait_send()
            returning(row, step).wait()
        tiles = []
        for pair in range(0, seq_devices, 2):
            halves = []
            for one in (pair, pair + 1):
                packed = back[row, one, length:, :].astype(F32)
                turned_over = pltpu.roll(packed, 64, 1)
                straight, other = (packed, turned_over) if one == pair else (turned_over, packed)
                halves.append(jnp.concatenate([straight, other[2 * low - length :]], axis=0))
            tiles.append(jnp.where(lanes_of((length, 128)) < 64, halves[0], halves[1]).astype(BF16))
        at = pl.ds(pl.multiple_of(row * length, 16), length)
        right[1, at, : 2 * half] = nn(jnp.concatenate(tiles, axis=1), gather[...]).astype(BF16)
        for pair in range(seq_devices):
            slot, col = divmod(2 * half + pair * PAIR, 3 * CHUNK)
            right[1 + slot, at, col : col + PAIR] = back[row, pair, :length, :]
        return carry

    lax.fori_loop(0, rows, unpack, 0)
    q_pairs = [right_copy(1, 3 * CHUNK, full + 3), right_copy(2, 3 * CHUNK, full + 4)]
    for copy in q_pairs:
        copy.start()
    for part in range(D // CHUNK):
        value_load(part).wait()
    q_and_k = nt(right[1, :tokens, :half], wq_ref[...]) + nt(right[1, :tokens, half : 2 * half], wk_ref[...])
    for part in range(D // CHUNK):
        at = slice(part * CHUNK, (part + 1) * CHUNK)
        block = w_buf[part // 3, part % 3]
        out_acc[:, at] = (
            q_and_k[:, at]
            + nt(right[1, :tokens, 2 * half :], block[:, : 3 * CHUNK - 2 * half])
            + nt(right[2, :tokens, :], block[:, 3 * CHUNK - 2 * half :])
        )
    lhs_copy(3).wait()
    for copy in q_pairs:
        copy.wait()
    for slot in range(2):
        for col in range(0, 3 * CHUNK, CHUNK):
            grads = nn(left(0), right[1 + slot, :, col : col + CHUNK])
            store_blocks(q_source, 0, slot * 3 * CHUNK + col, grads, groups)
    qkv.a_copy(0).start()

    def norm_backward(step, carry):
        at = pl.ds(pl.multiple_of(step * STEP_ROWS, 16), STEP_ROWS)
        value, grad = x_ref[at, :].astype(F32), out_acc[at, :]
        scale = lax.rsqrt(jnp.mean(value * value, axis=-1, keepdims=True) + eps_norm)
        gains[1:2, :] += jnp.sum(grad * value * scale, axis=0, keepdims=True)
        weighted = grad * gain_attn_ref[...]
        mean = jnp.mean(weighted * value, axis=-1, keepdims=True)
        total = gnf[at, :] + scale * weighted - value * (scale * scale * scale * mean)
        input_out[at, :] = total.astype(BF16)
        return carry

    lax.fori_loop(0, tokens // STEP_ROWS, norm_backward, 0)

    def gain_copy(step, target_group, target):
        return sending(
            gains, gains_got.at[step], gain_send.at[step], gain_recv.at[step], target_group, target
        )

    gain_copies = [
        gain_copy(0, row_group, partner),
        gain_copy(1, row_group, feed.peer_a),
        gain_copy(2, row_group, feed.peer_b),
    ] + [gain_copy(2 + step, lax.rem(row_group + step, groups), me) for step in range(1, groups)]

    def write_feed(unit, total, w):
        at = unit * CHUNK if isinstance(unit, int) else pl.multiple_of(unit * CHUNK, CHUNK)
        write_unit(total, at, w, gate_out, up_out, down_out)

    def finish(unit, carry):
        write_feed(unit, feed.z_step(unit), CHUNK)
        return carry

    gain_copies[0].start()
    first.z_step(XY_EARLY + 1)
    outer.a_step(0)
    gain_copies[0].wait()
    gains[...] += gains_got[0]
    gain_copies[1].start()
    feed.b_step(full - 1)
    first.a_step(XY_EARLY)
    first.z_step(XY_EARLY + 2)
    feed.b_step(full)
    gain_copies[1].wait()
    gains[...] += gains_got[1]
    gain_copies[2].start()
    qkv.a_step(0)
    outer.b_step(0)
    first.a_step(XY_EARLY + 1)
    gain_copies[2].wait()
    gains[...] += gains_got[2]
    for copy in gain_copies[3:]:
        copy.start()
    first.a_step(XY_EARLY + 2)
    lax.fori_loop(0, XY_EARLY, finish, 0)
    qkv.b_step(0)
    lax.fori_loop(full - 1, full, finish, 0)
    write_feed(full, feed.z_step(full), tail)
    for unit in range(XY_EARLY, full - 1):
        write_feed(unit, first.b_step(unit), CHUNK)
    for copy in gain_copies[3:]:
        copy.wait()
    for step in range(1, groups):
        gains[...] += gains_got[2 + step]
    picked = lax.broadcasted_iota(jnp.int32, (D, 128), 0) == 32 * (seq_devices * row_group + me) + lanes_of((D, 128))
    gains_out[...] = jnp.dot(
        gains[...], jnp.where(picked, 1.0, 0.0), precision=lax.Precision.HIGHEST, preferred_element_type=F32
    )
    wout_out[...] = outer.z_step(0)
    total = qkv.z_step(0)
    query_out[...] = total[:, :half]
    key_out[...] = total[:, half : 2 * half]
    value_out[...] = total[:, 2 * half :]

    for unit in range(XY_EARLY, full - 1):
        first.wait_sent(unit)
    for unit in range(full + 1):
        if unit < XY_EARLY or unit >= full - 1:
            feed.wait_sent(unit)
            if unit > full - SLOTS:
                feed.a_copy(unit).wait_send()
    for one in (outer, qkv):
        one.wait_sent(0)
        one.a_copy(0).wait_send()


ANY_SPEC = pl.BlockSpec(memory_space=pl.ANY)


def backward_part(
    groups, seq_devices, branch, x, cotangent, gain_ffn, w_out, w_gate_t, w_up_t, w_down,
    doc_lengths, got, heads, inverse, gain_attn, w_query, w_key, w_value,
):
    tokens = branch.shape[0]
    rows = doc_lengths.shape[0]
    length = tokens // rows
    total = seq_devices * length
    width = w_down.shape[0]
    full = width // CHUNK
    padded = (tokens + 127) // 128 * 128
    unit_rows = 32 * groups
    dma = pltpu.SemaphoreType.DMA
    sems = dma((rows, seq_devices))
    z_units = full - 1 - XY_EARLY
    return pl.pallas_call(
        functools.partial(backward_kernel, groups, seq_devices, rows, length, width),
        name="backward",
        out_shape=[
            jax.ShapeDtypeStruct((tokens, D), BF16),
            jax.ShapeDtypeStruct((tokens, D), BF16),
            jax.ShapeDtypeStruct((32, width), F32),
            jax.ShapeDtypeStruct((32, width), F32),
            jax.ShapeDtypeStruct((32, width), F32),
            jax.ShapeDtypeStruct((32, D), F32),
            jax.ShapeDtypeStruct((32, H * F), F32),
            jax.ShapeDtypeStruct((32, H * F), F32),
            jax.ShapeDtypeStruct((32, D), F32),
            jax.ShapeDtypeStruct((8, 128), F32),
        ],
        in_specs=[VMEM_SPEC] * 5 + [ANY_SPEC] * 3 + [SMEM_SPEC] + [ANY_SPEC] * 3 + [VMEM_SPEC] * 3 + [ANY_SPEC],
        out_specs=[VMEM_SPEC] * 10,
        scratch_shapes=[
            pltpu.VMEM((tokens, D), F32),
            pltpu.VMEM((tokens, D), BF16),
            pltpu.VMEM((tokens, D), F32),
            pltpu.VMEM((tokens, D), F32),
            pltpu.VMEM((2, 3, CHUNK, D), BF16),
            pltpu.VMEM((3, 2, 2, unit_rows, 2 * padded), BF16),
            pltpu.VMEM((4, 2 * padded, 3 * CHUNK), BF16),
            pltpu.VMEM((SLOTS, 2, 2, unit_rows, 3 * CHUNK), BF16),
            pltpu.VMEM((1, 2, 2, unit_rows, D), BF16),
            pltpu.VMEM((1, 2, 2, unit_rows, 6 * CHUNK), BF16),
            pltpu.VMEM(got.shape, BF16),
            pltpu.VMEM(heads.shape, BF16),
            pltpu.VMEM(inverse.shape, F32),
            pltpu.VMEM((rows, total, 128), BF16),
            pltpu.VMEM(got.shape, BF16),
            pltpu.VMEM((total, 128), BF16),
            pltpu.VMEM((2, total, 128), BF16),
            pltpu.VMEM((2, total, 128), BF16),
            pltpu.VMEM((2, total, 128), BF16),
            pltpu.VMEM((total, 128), BF16),
            pltpu.VMEM((2, 32, total), BF16),
            pltpu.VMEM((32, total), F32),
            pltpu.VMEM((total, 128), F32),
            pltpu.VMEM((total, 128), BF16),
            pltpu.VMEM((8, D), F32),
            pltpu.VMEM((2 + groups, 8, D), F32),
            dma((2, 3)), dma((D // CHUNK,)), dma((3,)), dma((2, 4)), dma((2, full + 5)),
            sems, sems, sems, sems, dma((2 + groups,)), dma((2 + groups,)),
        ]
        + reduction_buffers(groups, full + 1 - z_units, 3 * CHUNK)
        + reduction_buffers(groups, 1, D)
        + reduction_buffers(groups, 1, 6 * CHUNK)
        + groups_first_buffers(groups, z_units, 3 * CHUNK),
        compiler_params=pltpu.CompilerParams(collective_id=1, has_side_effects=True, vmem_limit_bytes=VMEM_BYTES),
    )(
        branch, x, cotangent, gain_ffn.reshape(1, D), w_out, w_gate_t, w_up_t, w_down,
        doc_lengths, got, heads, inverse, gain_attn.reshape(1, D), w_query, w_key, w_value,
    )


def tuned_body(
    seq_devices, groups, inputs, doc_lengths, gain_attn, w_query, w_key, w_value, w_out, gain_ffn, w_gate, w_up,
    w_down, cotangent,
):
    row_count, shard_len, _ = inputs.shape
    token_count = row_count * shard_len
    branch, got, heads, inverse = attention_forward(
        seq_devices, inputs, doc_lengths, gain_attn, w_query, w_key, w_value
    )
    output, input_grad, gate, up, down, out, query, key, value, gains = backward_part(
        groups, seq_devices, branch.reshape(token_count, D), inputs.reshape(token_count, D),
        cotangent.reshape(token_count, D), gain_ffn, w_out, w_gate.T, w_up.T, w_down,
        doc_lengths, got, heads, inverse, gain_attn, w_query, w_key, w_value,
    )
    return (
        output.reshape(row_count, shard_len, D),
        input_grad.reshape(row_count, shard_len, D),
        gains[1, :32],
        query,
        key,
        value,
        out,
        gains[0, :32],
        gate,
        up,
        down.T,
    )


def solution(mesh):
    in_specs = (
        P("dp", "seq", None),
        P("dp", None),
        P(),
        P(),
        P(),
        P(),
        P(),
        P(),
        P(),
        P(),
        P(),
        P("dp", "seq", None),
    )
    out_specs = (
        P("dp", "seq", None),
        P("dp", "seq", None),
        P(("dp", "seq")),
        P(("dp", "seq"), None),
        P(("dp", "seq"), None),
        P(("dp", "seq"), None),
        P(("dp", "seq"), None),
        P(("dp", "seq")),
        P(("dp", "seq"), None),
        P(("dp", "seq"), None),
        P(None, ("dp", "seq")),
    )
    seq_devices, groups = mesh.shape["seq"], mesh.shape["dp"]
    tuned = seq_devices == 8 and seq_devices * groups * 32 == D
    step = functools.partial(tuned_body, seq_devices, groups) if tuned else general_body
    return jax.shard_map(step, mesh=mesh, in_specs=in_specs, out_specs=out_specs, check_vma=False)
```

```python
import functools

import jax
import jax.numpy as jnp
from jax import lax
from jax.experimental import pallas as pl
from jax.experimental.pallas import tpu as pltpu
from jax.sharding import PartitionSpec as P

D = 1024
H = 16
F = 16
HV = 64
BLOCK = 576


eps_norm = 1e-05


def rms_scale(stream, gain_vec):
    return (
        stream * lax.rsqrt(jnp.mean(stream * stream, axis=-1, keepdims=True) + eps_norm) * gain_vec
    )


def taylor_features(vectors):
    feat_width = vectors.shape[-1]
    outer_prod = (vectors[..., :, None] * vectors[..., None, :]).reshape(
        vectors.shape[:-1] + (feat_width * feat_width,)
    )
    ones_part = jnp.ones(vectors.shape[:-1] + (1,), jnp.float32)
    return jnp.concatenate(
        [ones_part, vectors * feat_width ** (-0.25), outer_prod * (0.5 / feat_width) ** 0.5],
        axis=-1,
    )


def document_ids(doc_lens, seq_length):
    doc_ends = jnp.cumsum(doc_lens, dtype=jnp.int32)
    positions = jnp.arange(seq_length, dtype=jnp.int32)
    return jnp.sum(
        (positions[:, None] >= doc_ends[None, :]).astype(jnp.int32), axis=1, dtype=jnp.int32
    )


def attend_row(queries, key_proj, value_proj, doc_row, block_rows):
    seq_length, head_count, feat_width = queries.shape
    value_width = value_proj.shape[-1]
    feat_count = 1 + feat_width + feat_width * feat_width
    block_count = seq_length // block_rows
    highest = lax.Precision.HIGHEST
    query_blocks = queries.reshape(block_count, block_rows, head_count, feat_width)
    key_blocks = key_proj.reshape(block_count, block_rows, head_count, feat_width)
    value_blocks = value_proj.reshape(block_count, block_rows, head_count, value_width)
    doc_blocks = doc_row.reshape(block_count, block_rows)
    previous = jnp.concatenate([jnp.full((1,), -1, jnp.int32), doc_blocks[:-1, -1]])
    positions = jnp.arange(block_rows, dtype=jnp.int32)
    causal = positions[:, None] >= positions[None, :]

    def block_step(carried, pieces):
        state_sum, norm_sum = carried
        query_block, key_block, value_block, doc_block, prior_doc = pieces
        scores = jnp.einsum(
            "thf,shf->hts", query_block, key_block, precision=highest
        ) * feat_width ** (-0.5)
        weights = 1.0 + scores + 0.5 * scores * scores
        same_doc = causal & (doc_block[:, None] == doc_block[None, :])
        weights = jnp.where(same_doc[None, :, :], weights, 0.0)
        numerator = jnp.einsum("hts,shv->thv", weights, value_block, precision=highest)
        denominator = jnp.transpose(jnp.sum(weights, axis=2))
        use_state = (doc_block == prior_doc).astype(jnp.float32)[:, None]
        query_feats = taylor_features(query_block)
        numerator = numerator + use_state[:, :, None] * jnp.einsum(
            "thp,hpv->thv", query_feats, state_sum, precision=highest
        )
        denominator = denominator + use_state * jnp.einsum(
            "thp,hp->th", query_feats, norm_sum, precision=highest
        )
        last_doc = doc_block[-1]
        keep_state = (last_doc == prior_doc).astype(jnp.float32)
        key_feats = (
            taylor_features(key_block) * (doc_block == last_doc).astype(jnp.float32)[:, None, None]
        )
        state_sum = keep_state * state_sum + jnp.einsum(
            "shp,shv->hpv", key_feats, value_block, precision=highest
        )
        norm_sum = keep_state * norm_sum + jnp.sum(key_feats, axis=0)
        return ((state_sum, norm_sum), numerator / denominator[:, :, None])

    initial = (
        jnp.zeros((head_count, feat_count, value_width), jnp.float32),
        jnp.zeros((head_count, feat_count), jnp.float32),
    )
    _, results = lax.scan(
        jax.checkpoint(block_step),
        initial,
        (query_blocks, key_blocks, value_blocks, doc_blocks, previous),
    )
    return results.reshape(seq_length, head_count, value_width)


def project(left, right):
    return jnp.dot(left, right, preferred_element_type=jnp.float32)


def back_project(left, right):
    return lax.dot_general(
        left, right, (((1,), (1,)), ((), ())), preferred_element_type=jnp.float32
    )


def weight_grad(left, right):
    return lax.dot_general(
        left, right, (((0,), (0,)), ((), ())), preferred_element_type=jnp.float32
    )


def swiglu(gate_proj, up_proj):
    return jax.nn.silu(gate_proj) * up_proj


def general_body(
    inputs,
    doc_lengths,
    gain_attn,
    w_query,
    w_key,
    w_value,
    w_out,
    gain_ffn,
    w_gate,
    w_up,
    w_down,
    cotangent,
):
    row_count, shard_len, _ = inputs.shape
    token_count = row_count * shard_len
    stream = inputs.reshape(token_count, D).astype(jnp.float32)
    normed, attn_norm_back = jax.vjp(rms_scale, stream, gain_attn)
    normed_low = normed.astype(jnp.bfloat16)
    query_proj = project(normed_low, w_query).astype(jnp.bfloat16)
    key_proj = project(normed_low, w_key).astype(jnp.bfloat16)
    value_proj = project(normed_low, w_value).astype(jnp.bfloat16)
    query_heads, key_heads, value_heads = (
        lax.all_to_all(
            query_proj.reshape(row_count, shard_len, H, F),
            "seq",
            split_axis=2,
            concat_axis=1,
            tiled=True,
        ),
        lax.all_to_all(
            key_proj.reshape(row_count, shard_len, H, F),
            "seq",
            split_axis=2,
            concat_axis=1,
            tiled=True,
        ),
        lax.all_to_all(
            value_proj.reshape(row_count, shard_len, H, HV),
            "seq",
            split_axis=2,
            concat_axis=1,
            tiled=True,
        ),
    )
    seq_length = query_heads.shape[1]
    doc_rows = jax.vmap(lambda doc_lens: document_ids(doc_lens, seq_length))(doc_lengths)

    def attend_all(queries, keys_in, values_in):
        return jax.vmap(attend_row, in_axes=(0, 0, 0, 0, None))(
            queries, keys_in, values_in, doc_rows, BLOCK
        )

    mixed_heads, attend_back = jax.vjp(
        attend_all,
        query_heads.astype(jnp.float32),
        key_heads.astype(jnp.float32),
        value_heads.astype(jnp.float32),
    )
    mixed_rows = lax.all_to_all(
        mixed_heads.astype(jnp.bfloat16), "seq", split_axis=1, concat_axis=2, tiled=True
    )
    mixed_flat = mixed_rows.reshape(token_count, D)
    residual = stream + project(mixed_flat, w_out)
    normed_ffn, ffn_norm_back = jax.vjp(rms_scale, residual, gain_ffn)
    ffn_low = normed_ffn.astype(jnp.bfloat16)
    gate_proj = project(ffn_low, w_gate)
    up_proj = project(ffn_low, w_up)
    hidden, act_back = jax.vjp(swiglu, gate_proj, up_proj)
    hidden_low = hidden.astype(jnp.bfloat16)
    output = residual + project(hidden_low, w_down)
    grad_out = cotangent.reshape(token_count, D)
    grad_gate, grad_up = act_back(back_project(grad_out, w_down))
    grad_gate_low = grad_gate.astype(jnp.bfloat16)
    grad_up_low = grad_up.astype(jnp.bfloat16)
    down_grad_t = weight_grad(grad_out, hidden_low)
    gate_grad = weight_grad(ffn_low, grad_gate_low)
    up_grad = weight_grad(ffn_low, grad_up_low)
    grad_normed_ffn = back_project(grad_gate_low, w_gate) + back_project(grad_up_low, w_up)
    grad_residual, gain_ffn_grad = ffn_norm_back(grad_normed_ffn)
    grad_residual = grad_residual + grad_out.astype(jnp.float32)
    grad_branch = grad_residual.astype(jnp.bfloat16)
    out_grad = weight_grad(mixed_flat, grad_branch)
    grad_mixed = (
        back_project(grad_branch, w_out).astype(jnp.bfloat16).reshape(row_count, shard_len, H, HV)
    )
    grad_heads = lax.all_to_all(grad_mixed, "seq", split_axis=2, concat_axis=1, tiled=True)
    grad_query, grad_key, grad_value = attend_back(grad_heads.astype(jnp.float32))
    back_query, back_key, back_value = (
        lax.all_to_all(
            grad_query.astype(jnp.bfloat16), "seq", split_axis=1, concat_axis=2, tiled=True
        ),
        lax.all_to_all(
            grad_key.astype(jnp.bfloat16), "seq", split_axis=1, concat_axis=2, tiled=True
        ),
        lax.all_to_all(
            grad_value.astype(jnp.bfloat16), "seq", split_axis=1, concat_axis=2, tiled=True
        ),
    )
    back_query = back_query.reshape(token_count, H * F)
    back_key = back_key.reshape(token_count, H * F)
    back_value = back_value.reshape(token_count, D)
    query_grad = weight_grad(normed_low, back_query)
    key_grad = weight_grad(normed_low, back_key)
    value_grad = weight_grad(normed_low, back_value)
    grad_normed = (
        back_project(back_query, w_query)
        + back_project(back_key, w_key)
        + back_project(back_value, w_value)
    )
    grad_stream, gain_attn_grad = attn_norm_back(grad_normed)
    input_grad = grad_residual + grad_stream
    (
        gain_attn_part,
        query_part,
        key_part,
        value_part,
        out_part,
        gain_ffn_part,
        gate_part,
        up_part,
        down_part,
    ) = (
        lax.psum_scatter(gain_attn_grad, ("dp", "seq"), scatter_dimension=0, tiled=True),
        lax.psum_scatter(query_grad, ("dp", "seq"), scatter_dimension=0, tiled=True),
        lax.psum_scatter(key_grad, ("dp", "seq"), scatter_dimension=0, tiled=True),
        lax.psum_scatter(value_grad, ("dp", "seq"), scatter_dimension=0, tiled=True),
        lax.psum_scatter(out_grad, ("dp", "seq"), scatter_dimension=0, tiled=True),
        lax.psum_scatter(gain_ffn_grad, ("dp", "seq"), scatter_dimension=0, tiled=True),
        lax.psum_scatter(gate_grad, ("dp", "seq"), scatter_dimension=0, tiled=True),
        lax.psum_scatter(up_grad, ("dp", "seq"), scatter_dimension=0, tiled=True),
        lax.psum_scatter(down_grad_t, ("dp", "seq"), scatter_dimension=0, tiled=True),
    )
    return (
        output.reshape(row_count, shard_len, D).astype(jnp.bfloat16),
        input_grad.reshape(row_count, shard_len, D).astype(jnp.bfloat16),
        gain_attn_part,
        query_part,
        key_part,
        value_part,
        out_part,
        gain_ffn_part,
        gate_part,
        up_part,
        jnp.transpose(down_part),
    )


F32 = jnp.float32
BF16 = jnp.bfloat16
MESH = pl.DeviceIdType.MESH
TILE = 384
PAIR = 2 * HV


def nt(left, right):
    return lax.dot_general(left, right, (((1,), (1,)), ((), ())), preferred_element_type=F32)


def nn(left, right):
    return jnp.dot(left, right, preferred_element_type=F32)


def lanes_of(shape):
    return lax.broadcasted_iota(jnp.int32, shape, len(shape) - 1)


def first_visible(ends, positions):
    start = jnp.zeros_like(positions)
    for end in ends:
        start = jnp.where(positions >= end, end, start)
    return start


def row_ends(doc_ref, row):
    ends, total = [], 0
    for j in range(doc_ref.shape[1] - 1):
        total = total + doc_ref[row, j]
        ends.append(total)
    return ends


def spread_matrix():
    half = H * F
    shape = (2 * half, (H // 2) * 128)
    source = lax.broadcasted_iota(jnp.int32, shape, 0)
    column = lax.broadcasted_iota(jnp.int32, shape, 1)
    pair, lane = column // 128, column % 64
    wanted = pair * 32 + lane + jnp.where(lane < 32, 0, half - 32)
    return jnp.where(source == wanted, 1.0, 0.0).astype(BF16)


def gather_matrix():
    half = H * F
    shape = (2 * half, 2 * half)
    source = lax.broadcasted_iota(jnp.int32, shape, 0)
    column = lax.broadcasted_iota(jnp.int32, shape, 1)
    pair, lane = source // 64, source % 64
    wanted = pair * 32 + lane + jnp.where(lane < 32, 0, half - 32)
    return jnp.where(column == wanted, 1.0, 0.0).astype(BF16)


def packed_rows(length):
    return (length // 2 + 15) // 16 * 16


def prepare_row(got_ref, row, qa_ref, ka_ref, ve_ref, seq_devices, length):
    low = packed_rows(length)

    def part(peer, carry):
        values = got_ref[row, peer, :length, :].astype(F32)
        packed = got_ref[row, peer, length : length + low, :].astype(F32)
        turned = pltpu.roll(packed, 64, 1)
        both = jnp.concatenate([packed, turned[2 * low - length :]], axis=0)
        lane = lanes_of((length, 128))
        keys = pltpu.roll(both, 96, 1)
        at = pl.ds(pl.multiple_of(peer * length, 16), length)
        one = jnp.where(lane == 32, 1.0, 0.0)
        qa_ref[at, :] = jnp.where(lane < 32, both * 0.25, one).astype(BF16)
        ka_ref[0, at, :] = jnp.where(lane < 16, keys, one).astype(BF16)
        ka_ref[1, at, :] = jnp.where((lane >= 16) & (lane < 32), keys, one).astype(BF16)
        ve_ref[0, at, :] = jnp.where(lane < 64, values, 1.0).astype(BF16)
        ve_ref[1, at, :] = jnp.where(lane >= 64, values, 1.0).astype(BF16)
        return carry

    lax.fori_loop(0, seq_devices, part, 0)


def attend_forward(ends, qa_ref, ka_ref, ve_ref, mixed_ref, inverse_ref):
    length = qa_ref.shape[0]
    for block in range(length // TILE):
        reach = (block + 1) * TILE
        at = pl.ds(block * TILE, TILE)
        queries = qa_ref[at, :]
        t = lax.broadcasted_iota(jnp.int32, (TILE, 1), 0) + block * TILE
        start = first_visible(ends, t)
        s = lax.broadcasted_iota(jnp.int32, (TILE, reach), 1)
        visible = (s >= start) & (s <= t)
        sums = []
        for head in range(2):
            base = nt(queries, ka_ref[head, :reach, :])
            weights = jnp.where(visible, base * base + 1.0, 0.0).astype(BF16)
            sums.append(nn(weights, ve_ref[head, :reach, :]))
        lower = lanes_of((TILE, 128)) < 64
        numerator = jnp.where(lower, sums[0], sums[1])
        inverse = 1.0 / pltpu.roll(jnp.where(lower, sums[1], sums[0]), 64, 1)
        mixed_ref[at, :] = (numerator * inverse).astype(BF16)
        inverse_ref[at, :] = inverse


def attend_backward(
    ends, grad_ref, qa_ref, ka_ref, ve_ref, mixed_ref, inverse_ref, dn_ref, qs_ref, kt_ref, dqt_ref, gqk_ref, gv_ref
):
    length = qa_ref.shape[0]
    lane = lanes_of((length, 128))
    lower = lane < 64
    scaled = grad_ref[...].astype(F32) * inverse_ref[...]
    away = pltpu.roll(-scaled * mixed_ref[...].astype(F32), 64, 1)
    dn_ref[0] = jnp.where(lower, scaled, away).astype(BF16)
    dn_ref[1] = jnp.where(lower, away, scaled).astype(BF16)
    shifted = pltpu.roll(qa_ref[...].astype(F32), 32, 1)
    qs_ref[...] = jnp.where((lane >= 32) & (lane < 64), shifted * 2.0, 0.0).astype(BF16)
    for head in range(2):
        kt_ref[head] = ka_ref[head].astype(F32).T[:32].astype(BF16)
    dqt_ref[...] = jnp.zeros_like(dqt_ref)
    for block in range(length // TILE):
        first = block * TILE
        at = pl.ds(first, TILE)
        rest = pl.ds(first, length - first)
        shape = (TILE, length - first)
        t = lax.broadcasted_iota(jnp.int32, (1, shape[1]), 1) + first
        s = lax.broadcasted_iota(jnp.int32, shape, 0) + first
        visible = (s >= first_visible(ends, t)) & (s <= t)
        value_sums, key_sums = [], []
        for head in range(2):
            base = nt(ka_ref[head, at, :], qa_ref[rest, :])
            grad_weights = nt(ve_ref[head, at, :], dn_ref[head, rest, :])
            weights = jnp.where(visible, base * base + 1.0, 0.0).astype(BF16)
            grad_base = jnp.where(visible, grad_weights * base, 0.0).astype(BF16)
            value_sums.append(nn(weights, dn_ref[head, rest, :]))
            key_sums.append(nn(grad_base, qs_ref[rest, :]))
            dqt_ref[:, rest] += nn(kt_ref[head, :, at], grad_base)
        lane = lanes_of((TILE, 128))
        gv_ref[at, :] = jnp.where(lane < 64, value_sums[0], value_sums[1]).astype(BF16)
        gqk_ref[at, :] = jnp.where(
            (lane >= 32) & (lane < 48), key_sums[0], jnp.where((lane >= 48) & (lane < 64), key_sums[1], 0.0)
        )
    queries = jnp.concatenate([dqt_ref[...] * 0.5, jnp.zeros((96, length), F32)], axis=0)
    gqk_ref[...] += queries.T


def sending(source, target, send_sem, recv_sem, row_group, peer):
    return pltpu.make_async_remote_copy(
        src_ref=source,
        dst_ref=target,
        send_sem=send_sem,
        recv_sem=recv_sem,
        device_id=(row_group, peer),
        device_id_type=MESH,
    )


VMEM_SPEC = pl.BlockSpec(memory_space=pltpu.VMEM)
SMEM_SPEC = pl.BlockSpec(memory_space=pltpu.SMEM)


CHUNK = 256
STEP_ROWS = 48
Z_UNITS = 5
SLOTS = 7
VMEM_BYTES = 63 << 20


def place(me):
    core = lax.rem(me, 2)
    return core, 2 + 2 * core, 4 - 2 * core


def blocks_of(core, groups):
    first, second = 2 + 2 * core, 4 - 2 * core
    return [
        pl.multiple_of(32 * (8 * group + first * i + second * j + core), 32)
        for i in range(2)
        for j in range(2)
        for group in (0, 2, 1, 3)[:groups]
    ]


class Reduction:
    def __init__(self, source, buffers, slot_of=None, place_of=None):
        self.source = source
        self.got_a, self.got_b, self.got_z, self.a_sems, self.b_sems, self.c_sems, self.d_sems = buffers
        self.slot_of = slot_of or (lambda unit: unit)
        self.place_of = place_of or (lambda unit: unit)
        self.group, self.me = lax.axis_index("dp"), lax.axis_index("seq")
        core, first, second = place(self.me)
        self.bit_a, self.bit_b = lax.rem(self.me // first, 2), lax.rem(self.me // second, 2)
        self.peer_a = self.me + first * (1 - 2 * self.bit_a)
        self.peer_b = self.me + second * (1 - 2 * self.bit_b)
        self.bit_c, self.bit_d = lax.rem(self.group, 2), self.group // 2
        self.group_c = self.group + 1 - 2 * self.bit_c
        self.group_d = self.group + 2 - 4 * self.bit_d

    def rows(self, bit_c, bit_d=None):
        if bit_d is None:
            return pl.ds(pl.multiple_of(64 * bit_c, 64), 64)
        return pl.ds(pl.multiple_of(64 * bit_c + 32 * bit_d, 32), 32)

    def a_copy(self, unit):
        at = self.place_of(unit)
        return sending(
            self.source.at[self.slot_of(unit), 1 - self.bit_a], self.got_a.at[at], self.a_sems.at[0, at],
            self.a_sems.at[1, at], self.group, self.peer_a,
        )

    def b_copy(self, unit):
        at = self.place_of(unit)
        return sending(
            self.got_a.at[at, 1 - self.bit_b], self.got_b.at[at], self.b_sems.at[0, at], self.b_sems.at[1, at],
            self.group, self.peer_b,
        )

    def c_copy(self, unit):
        at = self.place_of(unit)
        return sending(
            self.got_b.at[at, self.rows(1 - self.bit_c), :], self.got_z.at[at, pl.ds(0, 64), :],
            self.c_sems.at[0, at], self.c_sems.at[1, at], self.group_c, self.me,
        )

    def d_copy(self, unit):
        at = self.place_of(unit)
        return sending(
            self.got_b.at[at, self.rows(self.bit_c, 1 - self.bit_d), :], self.got_z.at[at, pl.ds(64, 32), :],
            self.d_sems.at[0, at], self.d_sems.at[1, at], self.group_d, self.me,
        )

    def a_step(self, unit):
        at = self.place_of(unit)
        self.a_copy(unit).wait_recv()
        mine = self.source[self.slot_of(unit), self.bit_a].astype(F32)
        self.got_a[at] = (mine + self.got_a[at].astype(F32)).astype(BF16)
        self.b_copy(unit).start()

    def b_step(self, unit):
        at = self.place_of(unit)
        self.b_copy(unit).wait_recv()
        self.got_b[at] = (self.got_a[at, self.bit_b].astype(F32) + self.got_b[at].astype(F32)).astype(BF16)
        self.c_copy(unit).start()

    def c_step(self, unit):
        at, mine = self.place_of(unit), self.rows(self.bit_c)
        self.c_copy(unit).wait_recv()
        self.got_b[at, mine, :] = (
            self.got_b[at, mine, :].astype(F32) + self.got_z[at, :64, :].astype(F32)
        ).astype(BF16)
        self.d_copy(unit).start()

    def d_step(self, unit):
        at = self.place_of(unit)
        self.d_copy(unit).wait_recv()
        return self.got_b[at, self.rows(self.bit_c, self.bit_d), :].astype(F32) + self.got_z[at, 64:, :].astype(F32)

    def wait_sent(self, unit):
        self.b_copy(unit).wait_send()
        self.c_copy(unit).wait_send()
        self.d_copy(unit).wait_send()


class GroupsFirst(Reduction):
    def c_copy(self, unit):
        at = self.place_of(unit)
        return sending(
            self.source.at[self.slot_of(unit), :, :, self.rows(1 - self.bit_c), :],
            self.got_z.at[at, :, :, pl.ds(0, 64), :],
            self.c_sems.at[0, at], self.c_sems.at[1, at], self.group_c, self.me,
        )

    def d_copy(self, unit):
        at = self.place_of(unit)
        block = pl.ds(pl.multiple_of(32 * (1 - self.bit_d), 32), 32)
        return sending(
            self.got_z.at[at, :, :, block, :], self.got_z.at[at, :, :, pl.ds(64, 32), :],
            self.d_sems.at[0, at], self.d_sems.at[1, at], self.group_d, self.me,
        )

    def a_copy(self, unit):
        at = self.place_of(unit)
        return sending(
            self.got_z.at[at, 1 - self.bit_a, :, pl.ds(64, 32), :], self.got_a.at[at],
            self.a_sems.at[0, at], self.a_sems.at[1, at], self.group, self.peer_a,
        )

    def c_step(self, unit):
        at = self.place_of(unit)
        self.c_copy(unit).wait_recv()
        mine = self.source[self.slot_of(unit), :, :, self.rows(self.bit_c), :].astype(F32)
        self.got_z[at, :, :, :64, :] = (mine + self.got_z[at, :, :, :64, :].astype(F32)).astype(BF16)
        self.d_copy(unit).start()

    def d_step(self, unit):
        at = self.place_of(unit)
        self.d_copy(unit).wait_recv()
        mine = self.got_z[at, :, :, pl.ds(pl.multiple_of(32 * self.bit_d, 32), 32), :].astype(F32)
        self.got_z[at, :, :, 64:, :] = (mine + self.got_z[at, :, :, 64:, :].astype(F32)).astype(BF16)
        self.a_copy(unit).start()

    def a_step(self, unit):
        at = self.place_of(unit)
        self.a_copy(unit).wait_recv()
        mine = self.got_z[at, self.bit_a, :, 64:, :].astype(F32)
        self.got_a[at] = (mine + self.got_a[at].astype(F32)).astype(BF16)
        self.b_copy(unit).start()

    def b_step(self, unit):
        at = self.place_of(unit)
        self.b_copy(unit).wait_recv()
        return self.got_a[at, self.bit_b].astype(F32) + self.got_b[at].astype(F32)

    def wait_sent(self, unit):
        for copy in (self.a_copy, self.b_copy, self.c_copy, self.d_copy):
            copy(unit).wait_send()


def reduction_buffers(units, cols):
    sems = pltpu.SemaphoreType.DMA((2, units))
    return [
        pltpu.VMEM((units, 2, 128, cols), BF16),
        pltpu.VMEM((units, 128, cols), BF16),
        pltpu.VMEM((units, 96, cols), BF16),
        sems, sems, sems, sems,
    ]


def groups_first_buffers(units, cols):
    sems = pltpu.SemaphoreType.DMA((2, units))
    return [
        pltpu.VMEM((units, 2, 32, cols), BF16),
        pltpu.VMEM((units, 32, cols), BF16),
        pltpu.VMEM((units, 2, 2, 96, cols), BF16),
        sems, sems, sems, sems,
    ]


def store_blocks(target, unit, col, values, groups):
    rows = 32 * groups
    for i in range(2):
        for j in range(2):
            at = (2 * i + j) * rows
            target[unit, i, j, :, col : col + values.shape[1]] = values[at : at + rows].astype(BF16)


def turn(source, tokens, padded, turned):
    turned[...] = jnp.concatenate([source, jnp.zeros((padded - tokens, D), BF16)], axis=0).T


def split_rows(turned, mine_ref, theirs_ref, core, groups):
    for i, (mine, theirs) in enumerate(zip(blocks_of(core, groups), blocks_of(1 - core, groups))):
        a, b, group = i // (2 * groups), i // groups % 2, i % groups
        mine_ref[a, b, group * 32 : (group + 1) * 32, :] = turned[pl.ds(mine, 32), :]
        theirs_ref[a, b, group * 32 : (group + 1) * 32, :] = turned[pl.ds(theirs, 32), :]


def write_unit(total, at, w, gate_out, up_out, down_out):
    down_out[:, pl.ds(at, w)] = total[:, :w]
    gate_out[:, pl.ds(at, w)] = total[:, CHUNK : CHUNK + w]
    up_out[:, pl.ds(at, w)] = total[:, 2 * CHUNK : 2 * CHUNK + w]


def block_kernel(
    groups, seq_devices, rows, length, width,
    x_ref, cot_ref, gain_ref, wo_ref, wg_hbm, wu_hbm, wd_hbm, doc_ref, gain_attn_ref, wq_ref, wk_ref, wv_hbm,
    output_ref, input_out, gate_out, up_out, down_out, wout_out, query_out, key_out, value_out, gains_out,
    branch, residual, normed, out_acc, gnf, w_buf, lhs, right, parts, parts_o, q_source,
    got, heads, inverse, arrived, back, qa, ka, ve, dn, qs, kt, dqt, gqk, gv, gains, gains_got,
    fsend_a, frecv_a, fsend_b, frecv_b, w_sem, wv_sems, lhs_sems, pair_sems, send_a, recv_a, send_b, recv_b, gain_send, gain_recv,
    *buffers,
):
    row_group, me = lax.axis_index("dp"), lax.axis_index("seq")
    core, _, _ = place(me)
    partner = me + 1 - 2 * core
    tokens = rows * length
    padded = right.shape[1] // 2
    full = width // CHUNK
    tail = width - full * CHUNK
    low = packed_rows(length)
    lower = lanes_of((low, 128)) < 64
    here = pl.ds(pl.multiple_of(me * length, 16), length)
    half = H * F

    def slot_of(unit):
        if isinstance(unit, int):
            return unit if unit < SLOTS else 2 * (unit - SLOTS)
        return jnp.where(unit < SLOTS, unit, 2 * (unit - SLOTS))

    def place_of(unit):
        if isinstance(unit, int):
            return unit // 2 if unit < 2 * Z_UNITS else unit - Z_UNITS
        return jnp.where(unit < 2 * Z_UNITS, unit // 2, unit - Z_UNITS)

    feed = Reduction(parts, buffers[:7], slot_of, place_of)
    outer = Reduction(parts_o, buffers[7:14])
    qkv = Reduction(q_source, buffers[14:21])
    first = GroupsFirst(parts, buffers[21:28], slot_of, lambda unit: unit // 2)

    barrier = pltpu.get_barrier_semaphore()
    for step in range(1, seq_devices):
        peer = lax.rem(me + step, seq_devices)
        pl.semaphore_signal(barrier, inc=1, device_id=(row_group, peer), device_id_type=MESH)
    for other in (feed.group_c, feed.group_d):
        pl.semaphore_signal(barrier, inc=1, device_id=(other, me), device_id_type=MESH)

    def loads(chunk, slot, w):
        at = pl.ds(pl.multiple_of(chunk * CHUNK, CHUNK), w)
        return [
            pltpu.make_async_copy(hbm.at[at, :], w_buf.at[slot, which, pl.ds(0, w), :], w_sem.at[slot, which])
            for which, hbm in enumerate((wg_hbm, wu_hbm, wd_hbm))
        ]

    def value_load(part):
        return pltpu.make_async_copy(
            wv_hbm.at[pl.ds(part * CHUNK, CHUNK), :], w_buf.at[part // 3, part % 3], wv_sems.at[part]
        )

    def lhs_send(which):
        return (q_source.at[0], q_source.at[1], parts_o.at[0])[which % 3].at[:, :, :, pl.ds(0, padded)]

    def lhs_copy(which):
        return sending(
            lhs_send(which),
            lhs.at[which % 3, :, :, :, pl.ds(padded, padded)],
            lhs_sems.at[0, which], lhs_sems.at[1, which], row_group, partner,
        )

    def prepare_lhs(which, source):
        turned = right.at[3 if which < 3 else 1, :, pl.ds(0, padded)]
        turn(source, tokens, padded, turned)
        split_rows(turned, lhs.at[which % 3, :, :, :, pl.ds(0, padded)], lhs_send(which), core, groups)

    def left(which):
        return lhs[which].reshape(D // 2, 2 * padded)

    for part in range(D // CHUNK):
        value_load(part).start()
    spread = [right.at[1 + part, pl.ds(0, 2 * half), pl.ds(0, D // 2)] for part in range(2)]
    whole = spread_matrix()
    for part in range(2):
        spread[part][...] = whole[:, part * D // 2 : (part + 1) * D // 2]
    pl.semaphore_wait(barrier, seq_devices + 1)
    for part in range(D // CHUNK):
        value_load(part).wait()

    def spreading(row, step):
        peer = lax.rem(me + step, seq_devices)
        return sending(
            back.at[row, peer], got.at[row, me], fsend_a.at[row, step], frecv_a.at[row, step], row_group, peer
        )

    def merging(row, step):
        peer = lax.rem(me + step, seq_devices)
        there = pl.ds(pl.multiple_of(peer * length, 16), length)
        mine = pl.ds(pl.multiple_of(me * PAIR, 128), PAIR)
        at = pl.ds(pl.multiple_of(row * length, 16), length)
        return sending(
            heads.at[row, there, :], branch.at[at, mine], fsend_b.at[row, step], frecv_b.at[row, step],
            row_group, peer,
        )

    def project_row(row, carry):
        at = pl.ds(pl.multiple_of(row * length, 16), length)
        low_row = rms_scale(x_ref[at, :].astype(F32), gain_attn_ref[...]).astype(BF16)
        both = jnp.concatenate([nn(low_row, wq_ref[...]), nn(low_row, wk_ref[...])], axis=1).astype(BF16)
        sides = [nn(both, spread[part][...]) for part in range(2)]
        values = sum(
            nn(low_row[:, part * CHUNK : (part + 1) * CHUNK], w_buf[part // 3, part % 3])
            for part in range(D // CHUNK)
        ).astype(BF16)
        for pair in range(seq_devices):
            side, col = divmod(pair * 128, D // 2)
            tile = sides[side][:, col : col + 128]
            back[row, pair, :length, :] = values[:, pair * PAIR : (pair + 1) * PAIR]
            back[row, pair, length:, :] = jnp.where(lower, tile[:low], tile[length - low :]).astype(BF16)
        for step in range(1, seq_devices):
            spreading(row, step).start()
        got[row, me] = back[row, me]
        return carry

    lax.fori_loop(0, rows, project_row, 0)
    for chunk in range(2):
        for copy in loads(chunk, chunk, CHUNK):
            copy.start()
    prepare_lhs(0, cot_ref[...])
    lhs_copy(0).start()

    def attend_rows(row, carry):
        for step in range(1, seq_devices):
            spreading(row, step).wait_recv()
        prepare_row(got, row, qa, ka, ve, seq_devices, length)
        attend_forward(row_ends(doc_ref, row), qa, ka, ve, heads.at[row], inverse.at[row])
        for step in range(1, seq_devices):
            merging(row, step).start()
        at = pl.ds(pl.multiple_of(row * length, 16), length)
        branch[at, pl.ds(pl.multiple_of(me * PAIR, 128), PAIR)] = heads[row, here, :]
        return carry

    lax.fori_loop(0, rows, attend_rows, 0)

    def merged(row, carry):
        for step in range(1, seq_devices):
            spreading(row, step).wait_send()
            merging(row, step).wait()
        return carry

    lax.fori_loop(0, rows, merged, 0)

    def norm_forward(step, carry):
        at = pl.ds(pl.multiple_of(step * STEP_ROWS, 16), STEP_ROWS)
        value = x_ref[at, :].astype(F32) + residual[at, :]
        residual[at, :] = value
        out_acc[at, :] = value
        normed[at, :] = rms_scale(value, gain_ref[...]).astype(BF16)
        return carry

    residual[...] = nn(branch[...], wo_ref[...])
    lax.fori_loop(0, tokens // STEP_ROWS, norm_forward, 0)
    gnf[...] = jnp.zeros_like(gnf)

    for which, source in ((1, normed), (2, branch)):
        prepare_lhs(which, source[...])
        lhs_copy(which).start()
    gap = padded - tokens

    def clear(slot, count):
        for base in (tokens, padded + tokens):
            right[slot : slot + count, base : base + gap, :] = jnp.zeros((count, gap, 3 * CHUNK), BF16)

    clear(0, 4)

    def right_copy(slot, cols, sem):
        return sending(
            right.at[slot, pl.ds(0, tokens), pl.ds(0, cols)], right.at[slot, pl.ds(padded, tokens), pl.ds(0, cols)],
            pair_sems.at[0, sem], pair_sems.at[1, sem], row_group, partner,
        )

    def pair_copy(chunk):
        return right_copy(lax.rem(chunk, 4), 3 * CHUNK, chunk)

    def forward_part(chunk, wg, wu, wd, w):
        slot = lax.rem(chunk, 4)
        gate = nt(normed[...], wg)
        up = nt(normed[...], wu)
        sigmoid = 1.0 / (1.0 + jnp.exp(-gate))
        silu = gate * sigmoid
        hidden = (silu * up).astype(BF16)
        grad_hidden = nt(cot_ref[...], wd)
        grad_gate = (grad_hidden * up * (sigmoid * (1.0 + gate * (1.0 - sigmoid)))).astype(BF16)
        grad_up = (grad_hidden * silu).astype(BF16)
        for part, values in enumerate((hidden, grad_gate, grad_up)):
            right[slot, :tokens, part * CHUNK : part * CHUNK + w] = values
            if w < CHUNK:
                right[slot, :tokens, part * CHUNK + w : (part + 1) * CHUNK] = jnp.zeros((tokens, CHUNK - w), BF16)
        pair_copy(chunk).start()
        out_acc[...] += nn(hidden, wd)
        gnf[...] += nn(grad_gate, wg) + nn(grad_up, wu)

    def grad_part(chunk):
        pair_copy(chunk).wait()
        slot = lax.rem(chunk, 4)
        store_blocks(parts, slot_of(chunk), 0, nn(left(0), right[slot, :, 0:CHUNK]), groups)
        store_blocks(parts, slot_of(chunk), CHUNK, nn(left(1), right[slot, :, CHUNK:]), groups)

    def forward_step(chunk):
        slot = lax.rem(chunk, 2)
        for copy in loads(chunk, slot, CHUNK):
            copy.wait()
        forward_part(chunk, w_buf[slot, 0], w_buf[slot, 1], w_buf[slot, 2], CHUNK)

    def ticks(chunk):
        @pl.when((chunk >= 4) & (lax.rem(chunk, 2) == 0))
        def _():
            feed.a_step(chunk - 4)

        @pl.when((chunk >= 7) & (lax.rem(chunk, 2) == 1))
        def _():
            feed.b_step(chunk - 7)

        @pl.when(chunk == 8)
        def _():
            first.c_step(1)

    def fetch_next(chunk):
        @pl.when(chunk < full - 1)
        def _():
            for copy in loads(chunk + 1, lax.rem(chunk + 1, 2), CHUNK):
                copy.start()

        @pl.when(chunk == full - 1)
        def _():
            for copy in loads(full, full % 2, tail):
                copy.start()

    def main(chunk, carry):
        fetch_next(chunk)
        forward_step(chunk)
        unit = chunk - 1

        @pl.when(unit >= SLOTS)
        def _():
            feed.a_copy(2 * (unit - SLOTS)).wait_send()

        grad_part(unit)
        along_z = (unit < 2 * Z_UNITS) & (lax.rem(unit, 2) == 1)

        @pl.when(along_z)
        def _():
            first.c_copy(unit).start()

        @pl.when(jnp.logical_not(along_z))
        def _():
            feed.a_copy(unit).start()

        ticks(chunk)
        return carry

    forward_step(0)
    for which in range(3):
        lhs_copy(which).wait()
    lax.fori_loop(1, full, main, 0)
    slot = full % 2
    for copy in loads(full, slot, tail):
        copy.wait()
    forward_part(full, w_buf[slot, 0, :tail], w_buf[slot, 1, :tail], w_buf[slot, 2, :tail], tail)
    for part in range(D // CHUNK):
        value_load(part).start()
    feed.a_copy(2 * (full - 1 - SLOTS)).wait_send()
    grad_part(full - 1)
    first.c_copy(full - 1).start()

    gains[...] = jnp.zeros_like(gains)

    def norm_backward_ffn(step, carry):
        at = pl.ds(pl.multiple_of(step * STEP_ROWS, 16), STEP_ROWS)
        value, grad = residual[at, :], gnf[at, :]
        scale = lax.rsqrt(jnp.mean(value * value, axis=-1, keepdims=True) + eps_norm)
        gains[0:1, :] += jnp.sum(grad * value * scale, axis=0, keepdims=True)
        weighted = grad * gain_ref[...]
        mean = jnp.mean(weighted * value, axis=-1, keepdims=True)
        total = cot_ref[at, :].astype(F32) + scale * weighted - value * (scale * scale * scale * mean)
        gnf[at, :] = total
        right[3, at, :] = total[:, : 3 * CHUNK].astype(BF16)
        right[0, at, :CHUNK] = total[:, 3 * CHUNK :].astype(BF16)
        output_ref[at, :] = out_acc[at, :].astype(BF16)
        return carry

    lax.fori_loop(0, tokens // STEP_ROWS, norm_backward_ffn, 0)
    normed[...] = (
        nt(right[3, :tokens, :], wo_ref[:, : 3 * CHUNK]) + nt(right[0, :tokens, :CHUNK], wo_ref[:, 3 * CHUNK :])
    ).astype(BF16)

    def outgoing(row, step):
        peer = lax.rem(me + step, seq_devices)
        theirs = pl.ds(pl.multiple_of(peer * PAIR, 128), PAIR)
        at = pl.ds(pl.multiple_of(row * length, 16), length)
        return sending(
            normed.at[at, theirs], arrived.at[row, here, :], send_a.at[row, step], recv_a.at[row, step],
            row_group, peer,
        )

    def returning(row, step):
        peer = lax.rem(me + step, seq_devices)
        return sending(
            got.at[row, peer], back.at[row, me], send_b.at[row, step], recv_b.at[row, step], row_group, peer
        )

    def send_row(row, carry):
        for step in range(1, seq_devices):
            outgoing(row, step).start()
        at = pl.ds(pl.multiple_of(row * length, 16), length)
        arrived[row, here, :] = normed[at, pl.ds(pl.multiple_of(me * PAIR, 128), PAIR)]
        return carry

    lax.fori_loop(0, rows, send_row, 0)
    feed.a_step(6)
    feed.a_copy(2 * (full - SLOTS)).wait_send()
    grad_part(full)
    out_pairs = [right_copy(3, 3 * CHUNK, full + 1), right_copy(0, CHUNK, full + 2)]
    for copy in out_pairs:
        copy.start()
    feed.b_step(4)
    first.c_step(3)
    feed.c_step(0)
    prepare_lhs(3, rms_scale(x_ref[...].astype(F32), gain_attn_ref[...]).astype(BF16))
    clear(1, 1)
    for copy in out_pairs:
        copy.wait()
    lhs_copy(3).start()
    for col in range(0, D, CHUNK):
        columns = right[3, :, col : col + CHUNK] if col < 3 * CHUNK else right[0, :, :CHUNK]
        store_blocks(parts_o, 0, col, nn(left(2), columns), groups)
    gather = right.at[3, pl.ds(0, 2 * half), pl.ds(0, 2 * half)]
    gather[...] = gather_matrix()

    def attend(row, carry):
        prepare_row(got, row, qa, ka, ve, seq_devices, length)
        for step in range(1, seq_devices):
            outgoing(row, step).wait_recv()
        attend_backward(
            row_ends(doc_ref, row), arrived.at[row], qa, ka, ve, heads.at[row], inverse.at[row],
            dn, qs, kt, dqt, gqk, gv,
        )

        def pack(peer, inner):
            at = pl.multiple_of(peer * length, 16)
            got[row, peer, :length, :] = gv[pl.ds(at, length), :]
            front = gqk[pl.ds(at, low), :]
            rear = pltpu.roll(gqk[pl.ds(at + length - low, low), :], 64, 1)
            got[row, peer, length:, :] = jnp.where(lower, front, rear).astype(BF16)
            return inner

        lax.fori_loop(0, seq_devices, pack, 0)
        for step in range(1, seq_devices):
            returning(row, step).start()
        back[row, me] = got[row, me]

        @pl.when(row == 0)
        def _():
            feed.a_copy(full).start()
            feed.a_step(8)
            feed.b_step(6)
            first.c_step(5)
            first.d_step(1)

        @pl.when(row == 1)
        def _():
            outer.a_copy(0).start()
            feed.c_step(2)
            first.c_step(7)
            first.d_step(3)

        return carry

    lax.fori_loop(0, rows, attend, 0)
    feed.b_step(8)
    feed.c_step(4)
    first.c_step(9)
    first.d_step(5)
    feed.a_step(10)

    def unpack(row, carry):
        for step in range(1, seq_devices):
            outgoing(row, step).wait_send()
            returning(row, step).wait()
        tiles = []
        for pair in range(0, seq_devices, 2):
            halves = []
            for one in (pair, pair + 1):
                packed = back[row, one, length:, :].astype(F32)
                turned_over = pltpu.roll(packed, 64, 1)
                straight, other = (packed, turned_over) if one == pair else (turned_over, packed)
                halves.append(jnp.concatenate([straight, other[2 * low - length :]], axis=0))
            tiles.append(jnp.where(lanes_of((length, 128)) < 64, halves[0], halves[1]).astype(BF16))
        at = pl.ds(pl.multiple_of(row * length, 16), length)
        right[1, at, : 2 * half] = nn(jnp.concatenate(tiles, axis=1), gather[...]).astype(BF16)
        for pair in range(seq_devices):
            slot, col = divmod(2 * half + pair * PAIR, 3 * CHUNK)
            right[1 + slot, at, col : col + PAIR] = back[row, pair, :length, :]
        return carry

    lax.fori_loop(0, rows, unpack, 0)
    q_pairs = [right_copy(1, 3 * CHUNK, full + 3), right_copy(2, 3 * CHUNK, full + 4)]
    for copy in q_pairs:
        copy.start()
    for part in range(D // CHUNK):
        value_load(part).wait()
    q_and_k = nt(right[1, :tokens, :half], wq_ref[...]) + nt(right[1, :tokens, half : 2 * half], wk_ref[...])
    for part in range(D // CHUNK):
        at = slice(part * CHUNK, (part + 1) * CHUNK)
        block = w_buf[part // 3, part % 3]
        out_acc[:, at] = (
            q_and_k[:, at]
            + nt(right[1, :tokens, 2 * half :], block[:, : 3 * CHUNK - 2 * half])
            + nt(right[2, :tokens, :], block[:, 3 * CHUNK - 2 * half :])
        )
    lhs_copy(3).wait()
    for copy in q_pairs:
        copy.wait()
    for unit in range(2):
        for col in range(0, 3 * CHUNK, CHUNK):
            store_blocks(q_source, unit, col, nn(left(0), right[1 + unit, :, col : col + CHUNK]), groups)
        qkv.a_copy(unit).start()

    def norm_backward(step, carry):
        at = pl.ds(pl.multiple_of(step * STEP_ROWS, 16), STEP_ROWS)
        value, grad = x_ref[at, :].astype(F32), out_acc[at, :]
        scale = lax.rsqrt(jnp.mean(value * value, axis=-1, keepdims=True) + eps_norm)
        gains[1:2, :] += jnp.sum(grad * value * scale, axis=0, keepdims=True)
        weighted = grad * gain_attn_ref[...]
        mean = jnp.mean(weighted * value, axis=-1, keepdims=True)
        total = gnf[at, :] + scale * weighted - value * (scale * scale * scale * mean)
        input_out[at, :] = total.astype(BF16)
        return carry

    lax.fori_loop(0, tokens // STEP_ROWS, norm_backward, 0)

    def gain_copy(step, target_group, target):
        return sending(
            gains, gains_got.at[step], gain_send.at[step], gain_recv.at[step], target_group, target
        )

    gain_copies = [
        gain_copy(0, row_group, partner),
        gain_copy(1, row_group, feed.peer_a),
        gain_copy(2, row_group, feed.peer_b),
        gain_copy(3, feed.group_c, me),
        gain_copy(4, feed.group_d, me),
    ]

    def gain_step(step):
        gain_copies[step].wait()
        gains[...] += gains_got[step]
        if step < 4:
            gain_copies[step + 1].start()

    def write_feed(unit, total, w):
        at = unit * CHUNK if isinstance(unit, int) else pl.multiple_of(unit * CHUNK, CHUNK)
        write_unit(total, at, w, gate_out, up_out, down_out)

    gain_copies[0].start()
    first.d_step(7)
    feed.c_step(6)
    outer.a_step(0)
    feed.b_step(10)
    gain_step(0)
    first.a_step(1)
    feed.c_step(8)
    first.d_step(9)
    gain_step(1)
    first.a_step(3)
    outer.b_step(0)
    qkv.a_step(0)
    feed.c_step(10)
    gain_step(2)
    first.a_step(5)
    first.a_step(7)
    qkv.a_step(1)
    outer.c_step(0)
    gain_step(3)
    qkv.b_step(0)
    first.a_step(9)
    qkv.b_step(1)
    qkv.c_step(0)
    gain_step(4)
    for unit in range(0, full, 2):
        write_feed(unit, feed.d_step(unit), CHUNK)
    qkv.c_step(1)
    write_feed(full, feed.d_step(full), tail)
    for unit in range(1, 2 * Z_UNITS, 2):
        write_feed(unit, first.b_step(unit), CHUNK)
    picked = lax.broadcasted_iota(jnp.int32, (D, 128), 0) == 32 * (seq_devices * row_group + me) + lanes_of((D, 128))
    gains_out[...] = jnp.dot(
        gains[...], jnp.where(picked, 1.0, 0.0), precision=lax.Precision.HIGHEST, preferred_element_type=F32
    )
    wout_out[...] = outer.d_step(0)
    total = qkv.d_step(0)
    query_out[...] = total[:, :half]
    key_out[...] = total[:, half : 2 * half]
    value_out[:, : 3 * CHUNK - 2 * half] = total[:, 2 * half :]
    value_out[:, 3 * CHUNK - 2 * half :] = qkv.d_step(1)

    for unit in range(full + 1):
        if unit < 2 * Z_UNITS and unit % 2 == 1:
            first.wait_sent(unit)
        else:
            feed.wait_sent(unit)
            if unit > 2 * (full - SLOTS):
                feed.a_copy(unit).wait_send()
    for one, unit in ((outer, 0), (qkv, 0), (qkv, 1)):
        one.wait_sent(unit)
        one.a_copy(unit).wait_send()


ANY_SPEC = pl.BlockSpec(memory_space=pl.ANY)


def block_step(
    groups, seq_devices, x, cotangent, gain_ffn, w_out, w_gate_t, w_up_t, w_down, doc_lengths, gain_attn,
    w_query, w_key, w_value,
):
    tokens = x.shape[0]
    rows = doc_lengths.shape[0]
    length = tokens // rows
    total = seq_devices * length
    width = w_down.shape[0]
    full = width // CHUNK
    padded = (tokens + 127) // 128 * 128
    unit_rows = 32 * groups
    message = (rows, seq_devices, length + packed_rows(length), 128)
    dma = pltpu.SemaphoreType.DMA
    sems = dma((rows, seq_devices))
    return pl.pallas_call(
        functools.partial(block_kernel, groups, seq_devices, rows, length, width),
        name="block",
        out_shape=[
            jax.ShapeDtypeStruct((tokens, D), BF16),
            jax.ShapeDtypeStruct((tokens, D), BF16),
            jax.ShapeDtypeStruct((32, width), F32),
            jax.ShapeDtypeStruct((32, width), F32),
            jax.ShapeDtypeStruct((32, width), F32),
            jax.ShapeDtypeStruct((32, D), F32),
            jax.ShapeDtypeStruct((32, H * F), F32),
            jax.ShapeDtypeStruct((32, H * F), F32),
            jax.ShapeDtypeStruct((32, D), F32),
            jax.ShapeDtypeStruct((8, 128), F32),
        ],
        in_specs=[VMEM_SPEC] * 4 + [ANY_SPEC] * 3 + [SMEM_SPEC] + [VMEM_SPEC] * 3 + [ANY_SPEC],
        out_specs=[VMEM_SPEC] * 10,
        scratch_shapes=[
            pltpu.VMEM((tokens, D), BF16),
            pltpu.VMEM((tokens, D), F32),
            pltpu.VMEM((tokens, D), BF16),
            pltpu.VMEM((tokens, D), F32),
            pltpu.VMEM((tokens, D), F32),
            pltpu.VMEM((2, 3, CHUNK, D), BF16),
            pltpu.VMEM((3, 2, 2, unit_rows, 2 * padded), BF16),
            pltpu.VMEM((4, 2 * padded, 3 * CHUNK), BF16),
            pltpu.VMEM((SLOTS, 2, 2, unit_rows, 3 * CHUNK), BF16),
            pltpu.VMEM((1, 2, 2, unit_rows, D), BF16),
            pltpu.VMEM((2, 2, 2, unit_rows, 3 * CHUNK), BF16),
            pltpu.VMEM(message, BF16),
            pltpu.VMEM((rows, total, 128), BF16),
            pltpu.VMEM((rows, total, 128), F32),
            pltpu.VMEM((rows, total, 128), BF16),
            pltpu.VMEM(message, BF16),
            pltpu.VMEM((total, 128), BF16),
            pltpu.VMEM((2, total, 128), BF16),
            pltpu.VMEM((2, total, 128), BF16),
            pltpu.VMEM((2, total, 128), BF16),
            pltpu.VMEM((total, 128), BF16),
            pltpu.VMEM((2, 32, total), BF16),
            pltpu.VMEM((32, total), F32),
            pltpu.VMEM((total, 128), F32),
            pltpu.VMEM((total, 128), BF16),
            pltpu.VMEM((8, D), F32),
            pltpu.VMEM((5, 8, D), F32),
            sems, sems, sems, sems, dma((2, 3)), dma((D // CHUNK,)), dma((2, 4)), dma((2, full + 5)),
            sems, sems, sems, sems, dma((5,)), dma((5,)),
        ]
        + reduction_buffers(full + 1 - Z_UNITS, 3 * CHUNK)
        + reduction_buffers(1, D)
        + reduction_buffers(2, 3 * CHUNK)
        + groups_first_buffers(Z_UNITS, 3 * CHUNK),
        compiler_params=pltpu.CompilerParams(collective_id=1, has_side_effects=True, vmem_limit_bytes=VMEM_BYTES),
    )(
        x, cotangent, gain_ffn.reshape(1, D), w_out, w_gate_t, w_up_t, w_down, doc_lengths,
        gain_attn.reshape(1, D), w_query, w_key, w_value,
    )


def publish(results, gains):
    def kernel(*refs):
        count = len(results)
        for source, target in zip(refs[:count], refs[count + 1 : 2 * count + 1]):
            target[...] = source[...]
        refs[2 * count + 1][...] = refs[count][1:2, :32]
        refs[2 * count + 2][...] = refs[count][0:1, :32]

    one = jax.ShapeDtypeStruct((1, 32), F32)
    return pl.pallas_call(
        kernel,
        name="publish",
        out_shape=[jax.ShapeDtypeStruct(x.shape, x.dtype) for x in results] + [one, one],
        in_specs=[VMEM_SPEC] * (len(results) + 1),
        out_specs=[VMEM_SPEC] * (len(results) + 2),
        compiler_params=pltpu.CompilerParams(vmem_limit_bytes=VMEM_BYTES),
    )(*results, gains)


def tuned_body(
    seq_devices, groups, inputs, doc_lengths, gain_attn, w_query, w_key, w_value, w_out, gain_ffn, w_gate, w_up,
    w_down, cotangent,
):
    row_count, shard_len, _ = inputs.shape
    token_count = row_count * shard_len
    output, input_grad, gate, up, down, out, query, key, value, gains = block_step(
        groups, seq_devices, inputs.reshape(token_count, D), cotangent.reshape(token_count, D), gain_ffn, w_out,
        w_gate.T, w_up.T, w_down, doc_lengths, gain_attn, w_query, w_key, w_value,
    )
    output, input_grad, gate, up, down, out, query, key, value, gain_attn_part, gain_ffn_part = publish(
        (output, input_grad, gate, up, down, out, query, key, value), gains
    )
    return (
        output.reshape(row_count, shard_len, D),
        input_grad.reshape(row_count, shard_len, D),
        gain_attn_part.reshape(32),
        query,
        key,
        value,
        out,
        gain_ffn_part.reshape(32),
        gate,
        up,
        down.T,
    )


def solution(mesh):
    in_specs = (
        P("dp", "seq", None),
        P("dp", None),
        P(),
        P(),
        P(),
        P(),
        P(),
        P(),
        P(),
        P(),
        P(),
        P("dp", "seq", None),
    )
    out_specs = (
        P("dp", "seq", None),
        P("dp", "seq", None),
        P(("dp", "seq")),
        P(("dp", "seq"), None),
        P(("dp", "seq"), None),
        P(("dp", "seq"), None),
        P(("dp", "seq"), None),
        P(("dp", "seq")),
        P(("dp", "seq"), None),
        P(("dp", "seq"), None),
        P(None, ("dp", "seq")),
    )
    seq_devices, groups = mesh.shape["seq"], mesh.shape["dp"]
    tuned = seq_devices == 8 and seq_devices * groups * 32 == D
    step = functools.partial(tuned_body, seq_devices, groups) if tuned else general_body
    return jax.shard_map(step, mesh=mesh, in_specs=in_specs, out_specs=out_specs, check_vma=False)
```

```python
import functools

import jax
import jax.numpy as jnp
from jax import lax
from jax.experimental import pallas as pl
from jax.experimental.pallas import tpu as pltpu
from jax.sharding import PartitionSpec as P

D = 1024
H = 16
F = 16
HV = 64
BLOCK = 576


eps_norm = 1e-05


def rms_scale(stream, gain_vec):
    return (
        stream * lax.rsqrt(jnp.mean(stream * stream, axis=-1, keepdims=True) + eps_norm) * gain_vec
    )


def taylor_features(vectors):
    feat_width = vectors.shape[-1]
    outer_prod = (vectors[..., :, None] * vectors[..., None, :]).reshape(
        vectors.shape[:-1] + (feat_width * feat_width,)
    )
    ones_part = jnp.ones(vectors.shape[:-1] + (1,), jnp.float32)
    return jnp.concatenate(
        [ones_part, vectors * feat_width ** (-0.25), outer_prod * (0.5 / feat_width) ** 0.5],
        axis=-1,
    )


def document_ids(doc_lens, seq_length):
    doc_ends = jnp.cumsum(doc_lens, dtype=jnp.int32)
    positions = jnp.arange(seq_length, dtype=jnp.int32)
    return jnp.sum(
        (positions[:, None] >= doc_ends[None, :]).astype(jnp.int32), axis=1, dtype=jnp.int32
    )


def attend_row(queries, key_proj, value_proj, doc_row, block_rows):
    seq_length, head_count, feat_width = queries.shape
    value_width = value_proj.shape[-1]
    feat_count = 1 + feat_width + feat_width * feat_width
    block_count = seq_length // block_rows
    highest = lax.Precision.HIGHEST
    query_blocks = queries.reshape(block_count, block_rows, head_count, feat_width)
    key_blocks = key_proj.reshape(block_count, block_rows, head_count, feat_width)
    value_blocks = value_proj.reshape(block_count, block_rows, head_count, value_width)
    doc_blocks = doc_row.reshape(block_count, block_rows)
    previous = jnp.concatenate([jnp.full((1,), -1, jnp.int32), doc_blocks[:-1, -1]])
    positions = jnp.arange(block_rows, dtype=jnp.int32)
    causal = positions[:, None] >= positions[None, :]

    def block_step(carried, pieces):
        state_sum, norm_sum = carried
        query_block, key_block, value_block, doc_block, prior_doc = pieces
        scores = jnp.einsum(
            "thf,shf->hts", query_block, key_block, precision=highest
        ) * feat_width ** (-0.5)
        weights = 1.0 + scores + 0.5 * scores * scores
        same_doc = causal & (doc_block[:, None] == doc_block[None, :])
        weights = jnp.where(same_doc[None, :, :], weights, 0.0)
        numerator = jnp.einsum("hts,shv->thv", weights, value_block, precision=highest)
        denominator = jnp.transpose(jnp.sum(weights, axis=2))
        use_state = (doc_block == prior_doc).astype(jnp.float32)[:, None]
        query_feats = taylor_features(query_block)
        numerator = numerator + use_state[:, :, None] * jnp.einsum(
            "thp,hpv->thv", query_feats, state_sum, precision=highest
        )
        denominator = denominator + use_state * jnp.einsum(
            "thp,hp->th", query_feats, norm_sum, precision=highest
        )
        last_doc = doc_block[-1]
        keep_state = (last_doc == prior_doc).astype(jnp.float32)
        key_feats = (
            taylor_features(key_block) * (doc_block == last_doc).astype(jnp.float32)[:, None, None]
        )
        state_sum = keep_state * state_sum + jnp.einsum(
            "shp,shv->hpv", key_feats, value_block, precision=highest
        )
        norm_sum = keep_state * norm_sum + jnp.sum(key_feats, axis=0)
        return ((state_sum, norm_sum), numerator / denominator[:, :, None])

    initial = (
        jnp.zeros((head_count, feat_count, value_width), jnp.float32),
        jnp.zeros((head_count, feat_count), jnp.float32),
    )
    _, results = lax.scan(
        jax.checkpoint(block_step),
        initial,
        (query_blocks, key_blocks, value_blocks, doc_blocks, previous),
    )
    return results.reshape(seq_length, head_count, value_width)


def project(left, right):
    return jnp.dot(left, right, preferred_element_type=jnp.float32)


def back_project(left, right):
    return lax.dot_general(
        left, right, (((1,), (1,)), ((), ())), preferred_element_type=jnp.float32
    )


def weight_grad(left, right):
    return lax.dot_general(
        left, right, (((0,), (0,)), ((), ())), preferred_element_type=jnp.float32
    )


def swiglu(gate_proj, up_proj):
    return jax.nn.silu(gate_proj) * up_proj


def general_body(
    inputs,
    doc_lengths,
    gain_attn,
    w_query,
    w_key,
    w_value,
    w_out,
    gain_ffn,
    w_gate,
    w_up,
    w_down,
    cotangent,
):
    row_count, shard_len, _ = inputs.shape
    token_count = row_count * shard_len
    stream = inputs.reshape(token_count, D).astype(jnp.float32)
    normed, attn_norm_back = jax.vjp(rms_scale, stream, gain_attn)
    normed_low = normed.astype(jnp.bfloat16)
    query_proj = project(normed_low, w_query).astype(jnp.bfloat16)
    key_proj = project(normed_low, w_key).astype(jnp.bfloat16)
    value_proj = project(normed_low, w_value).astype(jnp.bfloat16)
    query_heads, key_heads, value_heads = (
        lax.all_to_all(
            query_proj.reshape(row_count, shard_len, H, F),
            "seq",
            split_axis=2,
            concat_axis=1,
            tiled=True,
        ),
        lax.all_to_all(
            key_proj.reshape(row_count, shard_len, H, F),
            "seq",
            split_axis=2,
            concat_axis=1,
            tiled=True,
        ),
        lax.all_to_all(
            value_proj.reshape(row_count, shard_len, H, HV),
            "seq",
            split_axis=2,
            concat_axis=1,
            tiled=True,
        ),
    )
    seq_length = query_heads.shape[1]
    doc_rows = jax.vmap(lambda doc_lens: document_ids(doc_lens, seq_length))(doc_lengths)

    def attend_all(queries, keys_in, values_in):
        return jax.vmap(attend_row, in_axes=(0, 0, 0, 0, None))(
            queries, keys_in, values_in, doc_rows, BLOCK
        )

    mixed_heads, attend_back = jax.vjp(
        attend_all,
        query_heads.astype(jnp.float32),
        key_heads.astype(jnp.float32),
        value_heads.astype(jnp.float32),
    )
    mixed_rows = lax.all_to_all(
        mixed_heads.astype(jnp.bfloat16), "seq", split_axis=1, concat_axis=2, tiled=True
    )
    mixed_flat = mixed_rows.reshape(token_count, D)
    residual = stream + project(mixed_flat, w_out)
    normed_ffn, ffn_norm_back = jax.vjp(rms_scale, residual, gain_ffn)
    ffn_low = normed_ffn.astype(jnp.bfloat16)
    gate_proj = project(ffn_low, w_gate)
    up_proj = project(ffn_low, w_up)
    hidden, act_back = jax.vjp(swiglu, gate_proj, up_proj)
    hidden_low = hidden.astype(jnp.bfloat16)
    output = residual + project(hidden_low, w_down)
    grad_out = cotangent.reshape(token_count, D)
    grad_gate, grad_up = act_back(back_project(grad_out, w_down))
    grad_gate_low = grad_gate.astype(jnp.bfloat16)
    grad_up_low = grad_up.astype(jnp.bfloat16)
    down_grad_t = weight_grad(grad_out, hidden_low)
    gate_grad = weight_grad(ffn_low, grad_gate_low)
    up_grad = weight_grad(ffn_low, grad_up_low)
    grad_normed_ffn = back_project(grad_gate_low, w_gate) + back_project(grad_up_low, w_up)
    grad_residual, gain_ffn_grad = ffn_norm_back(grad_normed_ffn)
    grad_residual = grad_residual + grad_out.astype(jnp.float32)
    grad_branch = grad_residual.astype(jnp.bfloat16)
    out_grad = weight_grad(mixed_flat, grad_branch)
    grad_mixed = (
        back_project(grad_branch, w_out).astype(jnp.bfloat16).reshape(row_count, shard_len, H, HV)
    )
    grad_heads = lax.all_to_all(grad_mixed, "seq", split_axis=2, concat_axis=1, tiled=True)
    grad_query, grad_key, grad_value = attend_back(grad_heads.astype(jnp.float32))
    back_query, back_key, back_value = (
        lax.all_to_all(
            grad_query.astype(jnp.bfloat16), "seq", split_axis=1, concat_axis=2, tiled=True
        ),
        lax.all_to_all(
            grad_key.astype(jnp.bfloat16), "seq", split_axis=1, concat_axis=2, tiled=True
        ),
        lax.all_to_all(
            grad_value.astype(jnp.bfloat16), "seq", split_axis=1, concat_axis=2, tiled=True
        ),
    )
    back_query = back_query.reshape(token_count, H * F)
    back_key = back_key.reshape(token_count, H * F)
    back_value = back_value.reshape(token_count, D)
    query_grad = weight_grad(normed_low, back_query)
    key_grad = weight_grad(normed_low, back_key)
    value_grad = weight_grad(normed_low, back_value)
    grad_normed = (
        back_project(back_query, w_query)
        + back_project(back_key, w_key)
        + back_project(back_value, w_value)
    )
    grad_stream, gain_attn_grad = attn_norm_back(grad_normed)
    input_grad = grad_residual + grad_stream
    (
        gain_attn_part,
        query_part,
        key_part,
        value_part,
        out_part,
        gain_ffn_part,
        gate_part,
        up_part,
        down_part,
    ) = (
        lax.psum_scatter(gain_attn_grad, ("dp", "seq"), scatter_dimension=0, tiled=True),
        lax.psum_scatter(query_grad, ("dp", "seq"), scatter_dimension=0, tiled=True),
        lax.psum_scatter(key_grad, ("dp", "seq"), scatter_dimension=0, tiled=True),
        lax.psum_scatter(value_grad, ("dp", "seq"), scatter_dimension=0, tiled=True),
        lax.psum_scatter(out_grad, ("dp", "seq"), scatter_dimension=0, tiled=True),
        lax.psum_scatter(gain_ffn_grad, ("dp", "seq"), scatter_dimension=0, tiled=True),
        lax.psum_scatter(gate_grad, ("dp", "seq"), scatter_dimension=0, tiled=True),
        lax.psum_scatter(up_grad, ("dp", "seq"), scatter_dimension=0, tiled=True),
        lax.psum_scatter(down_grad_t, ("dp", "seq"), scatter_dimension=0, tiled=True),
    )
    return (
        output.reshape(row_count, shard_len, D).astype(jnp.bfloat16),
        input_grad.reshape(row_count, shard_len, D).astype(jnp.bfloat16),
        gain_attn_part,
        query_part,
        key_part,
        value_part,
        out_part,
        gain_ffn_part,
        gate_part,
        up_part,
        jnp.transpose(down_part),
    )


F32 = jnp.float32
BF16 = jnp.bfloat16
MESH = pl.DeviceIdType.MESH
TILE = 384
PAIR = 2 * HV


def nt(left, right):
    return lax.dot_general(left, right, (((1,), (1,)), ((), ())), preferred_element_type=F32)


def nn(left, right):
    return jnp.dot(left, right, preferred_element_type=F32)


def lanes_of(shape):
    return lax.broadcasted_iota(jnp.int32, shape, len(shape) - 1)


def first_visible(ends, positions):
    start = jnp.zeros_like(positions)
    for end in ends:
        start = jnp.where(positions >= end, end, start)
    return start


def row_ends(doc_ref, row):
    ends, total = [], 0
    for j in range(doc_ref.shape[1] - 1):
        total = total + doc_ref[row, j]
        ends.append(total)
    return ends


def spread_matrix():
    half = H * F
    shape = (2 * half, (H // 2) * 128)
    source = lax.broadcasted_iota(jnp.int32, shape, 0)
    column = lax.broadcasted_iota(jnp.int32, shape, 1)
    pair, lane = column // 128, column % 64
    wanted = pair * 32 + lane + jnp.where(lane < 32, 0, half - 32)
    return jnp.where(source == wanted, 1.0, 0.0).astype(BF16)


def gather_matrix():
    half = H * F
    shape = (2 * half, 2 * half)
    source = lax.broadcasted_iota(jnp.int32, shape, 0)
    column = lax.broadcasted_iota(jnp.int32, shape, 1)
    pair, lane = source // 64, source % 64
    wanted = pair * 32 + lane + jnp.where(lane < 32, 0, half - 32)
    return jnp.where(column == wanted, 1.0, 0.0).astype(BF16)


def packed_rows(length):
    return (length // 2 + 15) // 16 * 16


def prepare_row(got_ref, row, qa_ref, ka_ref, ve_ref, seq_devices, length):
    low = packed_rows(length)

    def part(peer, carry):
        values = got_ref[row, peer, :length, :].astype(F32)
        packed = got_ref[row, peer, length : length + low, :].astype(F32)
        turned = pltpu.roll(packed, 64, 1)
        both = jnp.concatenate([packed, turned[2 * low - length :]], axis=0)
        lane = lanes_of((length, 128))
        keys = pltpu.roll(both, 96, 1)
        at = pl.ds(pl.multiple_of(peer * length, 16), length)
        one = jnp.where(lane == 32, 1.0, 0.0)
        qa_ref[at, :] = jnp.where(lane < 32, both * 0.25, one).astype(BF16)
        ka_ref[0, at, :] = jnp.where(lane < 16, keys, one).astype(BF16)
        ka_ref[1, at, :] = jnp.where((lane >= 16) & (lane < 32), keys, one).astype(BF16)
        ve_ref[0, at, :] = jnp.where(lane < 64, values, 1.0).astype(BF16)
        ve_ref[1, at, :] = jnp.where(lane >= 64, values, 1.0).astype(BF16)
        return carry

    lax.fori_loop(0, seq_devices, part, 0)


def attend_forward(ends, qa_ref, ka_ref, ve_ref, mixed_ref, inverse_ref):
    length = qa_ref.shape[0]
    for block in range(length // TILE):
        reach = (block + 1) * TILE
        at = pl.ds(block * TILE, TILE)
        queries = qa_ref[at, :]
        t = lax.broadcasted_iota(jnp.int32, (TILE, 1), 0) + block * TILE
        start = first_visible(ends, t)
        s = lax.broadcasted_iota(jnp.int32, (TILE, reach), 1)
        visible = (s >= start) & (s <= t)
        sums = []
        for head in range(2):
            base = nt(queries, ka_ref[head, :reach, :])
            weights = jnp.where(visible, base * base + 1.0, 0.0).astype(BF16)
            sums.append(nn(weights, ve_ref[head, :reach, :]))
        lower = lanes_of((TILE, 128)) < 64
        numerator = jnp.where(lower, sums[0], sums[1])
        inverse = 1.0 / pltpu.roll(jnp.where(lower, sums[1], sums[0]), 64, 1)
        mixed_ref[at, :] = (numerator * inverse).astype(BF16)
        inverse_ref[at, :] = inverse


def attend_backward(
    ends, grad_ref, qa_ref, ka_ref, ve_ref, mixed_ref, inverse_ref, dn_ref, qs_ref, kt_ref, dqt_ref, gqk_ref, gv_ref
):
    length = qa_ref.shape[0]
    lane = lanes_of((length, 128))
    lower = lane < 64
    scaled = grad_ref[...].astype(F32) * inverse_ref[...]
    away = pltpu.roll(-scaled * mixed_ref[...].astype(F32), 64, 1)
    dn_ref[0] = jnp.where(lower, scaled, away).astype(BF16)
    dn_ref[1] = jnp.where(lower, away, scaled).astype(BF16)
    shifted = pltpu.roll(qa_ref[...].astype(F32), 32, 1)
    qs_ref[...] = jnp.where((lane >= 32) & (lane < 64), shifted * 2.0, 0.0).astype(BF16)
    for head in range(2):
        kt_ref[head] = ka_ref[head].astype(F32).T[:32].astype(BF16)
    dqt_ref[...] = jnp.zeros_like(dqt_ref)
    for block in range(length // TILE):
        first = block * TILE
        at = pl.ds(first, TILE)
        rest = pl.ds(first, length - first)
        shape = (TILE, length - first)
        t = lax.broadcasted_iota(jnp.int32, (1, shape[1]), 1) + first
        s = lax.broadcasted_iota(jnp.int32, shape, 0) + first
        visible = (s >= first_visible(ends, t)) & (s <= t)
        value_sums, key_sums = [], []
        for head in range(2):
            base = nt(ka_ref[head, at, :], qa_ref[rest, :])
            grad_weights = nt(ve_ref[head, at, :], dn_ref[head, rest, :])
            weights = jnp.where(visible, base * base + 1.0, 0.0).astype(BF16)
            grad_base = jnp.where(visible, grad_weights * base, 0.0).astype(BF16)
            value_sums.append(nn(weights, dn_ref[head, rest, :]))
            key_sums.append(nn(grad_base, qs_ref[rest, :]))
            dqt_ref[:, rest] += nn(kt_ref[head, :, at], grad_base)
        lane = lanes_of((TILE, 128))
        gv_ref[at, :] = jnp.where(lane < 64, value_sums[0], value_sums[1]).astype(BF16)
        gqk_ref[at, :] = jnp.where(
            (lane >= 32) & (lane < 48), key_sums[0], jnp.where((lane >= 48) & (lane < 64), key_sums[1], 0.0)
        )
    queries = jnp.concatenate([dqt_ref[...] * 0.5, jnp.zeros((96, length), F32)], axis=0)
    gqk_ref[...] += queries.T


def sending(source, target, send_sem, recv_sem, row_group, peer):
    return pltpu.make_async_remote_copy(
        src_ref=source,
        dst_ref=target,
        send_sem=send_sem,
        recv_sem=recv_sem,
        device_id=(row_group, peer),
        device_id_type=MESH,
    )


VMEM_SPEC = pl.BlockSpec(memory_space=pltpu.VMEM)
SMEM_SPEC = pl.BlockSpec(memory_space=pltpu.SMEM)


CHUNK = 256
STEP_ROWS = 48
Z_UNITS = 5
SLOTS = 7
VMEM_BYTES = 63 << 20


def place(me):
    core = lax.rem(me, 2)
    return core, 2 + 2 * core, 4 - 2 * core


def blocks_of(core, groups):
    first, second = 2 + 2 * core, 4 - 2 * core
    return [
        pl.multiple_of(32 * (8 * group + first * i + second * j + core), 32)
        for i in range(2)
        for j in range(2)
        for group in (0, 2, 1, 3)[:groups]
    ]


class Reduction:
    def __init__(self, source, buffers, slot_of=None, place_of=None):
        self.source = source
        self.got_a, self.got_b, self.got_z, self.a_sems, self.b_sems, self.c_sems, self.d_sems = buffers
        self.slot_of = slot_of or (lambda unit: unit)
        self.place_of = place_of or (lambda unit: unit)
        self.group, self.me = lax.axis_index("dp"), lax.axis_index("seq")
        core, first, second = place(self.me)
        self.bit_a, self.bit_b = lax.rem(self.me // first, 2), lax.rem(self.me // second, 2)
        self.peer_a = self.me + first * (1 - 2 * self.bit_a)
        self.peer_b = self.me + second * (1 - 2 * self.bit_b)
        self.bit_c, self.bit_d = lax.rem(self.group, 2), self.group // 2
        self.group_c = self.group + 1 - 2 * self.bit_c
        self.group_d = self.group + 2 - 4 * self.bit_d

    def rows(self, bit_c, bit_d=None):
        if bit_d is None:
            return pl.ds(pl.multiple_of(64 * bit_c, 64), 64)
        return pl.ds(pl.multiple_of(64 * bit_c + 32 * bit_d, 32), 32)

    def a_copy(self, unit):
        at = self.place_of(unit)
        return sending(
            self.source.at[self.slot_of(unit), 1 - self.bit_a], self.got_a.at[at], self.a_sems.at[0, at],
            self.a_sems.at[1, at], self.group, self.peer_a,
        )

    def b_copy(self, unit):
        at = self.place_of(unit)
        return sending(
            self.got_a.at[at, 1 - self.bit_b], self.got_b.at[at], self.b_sems.at[0, at], self.b_sems.at[1, at],
            self.group, self.peer_b,
        )

    def c_copy(self, unit):
        at = self.place_of(unit)
        return sending(
            self.got_b.at[at, self.rows(1 - self.bit_c), :], self.got_z.at[at, pl.ds(0, 64), :],
            self.c_sems.at[0, at], self.c_sems.at[1, at], self.group_c, self.me,
        )

    def d_copy(self, unit):
        at = self.place_of(unit)
        return sending(
            self.got_b.at[at, self.rows(self.bit_c, 1 - self.bit_d), :], self.got_z.at[at, pl.ds(64, 32), :],
            self.d_sems.at[0, at], self.d_sems.at[1, at], self.group_d, self.me,
        )

    def a_step(self, unit):
        at = self.place_of(unit)
        self.a_copy(unit).wait_recv()
        mine = self.source[self.slot_of(unit), self.bit_a].astype(F32)
        self.got_a[at] = (mine + self.got_a[at].astype(F32)).astype(BF16)
        self.b_copy(unit).start()

    def b_step(self, unit):
        at = self.place_of(unit)
        self.b_copy(unit).wait_recv()
        self.got_b[at] = (self.got_a[at, self.bit_b].astype(F32) + self.got_b[at].astype(F32)).astype(BF16)
        self.c_copy(unit).start()

    def c_step(self, unit):
        at, mine = self.place_of(unit), self.rows(self.bit_c)
        self.c_copy(unit).wait_recv()
        self.got_b[at, mine, :] = (
            self.got_b[at, mine, :].astype(F32) + self.got_z[at, :64, :].astype(F32)
        ).astype(BF16)
        self.d_copy(unit).start()

    def d_step(self, unit):
        at = self.place_of(unit)
        self.d_copy(unit).wait_recv()
        return self.got_b[at, self.rows(self.bit_c, self.bit_d), :].astype(F32) + self.got_z[at, 64:, :].astype(F32)

    def wait_sent(self, unit):
        self.b_copy(unit).wait_send()
        self.c_copy(unit).wait_send()
        self.d_copy(unit).wait_send()


class GroupsFirst(Reduction):
    def c_copy(self, unit):
        at = self.place_of(unit)
        return sending(
            self.source.at[self.slot_of(unit), :, :, self.rows(1 - self.bit_c), :],
            self.got_z.at[at, :, :, pl.ds(0, 64), :],
            self.c_sems.at[0, at], self.c_sems.at[1, at], self.group_c, self.me,
        )

    def d_copy(self, unit):
        at = self.place_of(unit)
        block = pl.ds(pl.multiple_of(32 * (1 - self.bit_d), 32), 32)
        return sending(
            self.got_z.at[at, :, :, block, :], self.got_z.at[at, :, :, pl.ds(64, 32), :],
            self.d_sems.at[0, at], self.d_sems.at[1, at], self.group_d, self.me,
        )

    def a_copy(self, unit):
        at = self.place_of(unit)
        return sending(
            self.got_z.at[at, 1 - self.bit_a, :, pl.ds(64, 32), :], self.got_a.at[at],
            self.a_sems.at[0, at], self.a_sems.at[1, at], self.group, self.peer_a,
        )

    def c_step(self, unit):
        at = self.place_of(unit)
        self.c_copy(unit).wait_recv()
        mine = self.source[self.slot_of(unit), :, :, self.rows(self.bit_c), :].astype(F32)
        self.got_z[at, :, :, :64, :] = (mine + self.got_z[at, :, :, :64, :].astype(F32)).astype(BF16)
        self.d_copy(unit).start()

    def d_step(self, unit):
        at = self.place_of(unit)
        self.d_copy(unit).wait_recv()
        mine = self.got_z[at, :, :, pl.ds(pl.multiple_of(32 * self.bit_d, 32), 32), :].astype(F32)
        self.got_z[at, :, :, 64:, :] = (mine + self.got_z[at, :, :, 64:, :].astype(F32)).astype(BF16)
        self.a_copy(unit).start()

    def a_step(self, unit):
        at = self.place_of(unit)
        self.a_copy(unit).wait_recv()
        mine = self.got_z[at, self.bit_a, :, 64:, :].astype(F32)
        self.got_a[at] = (mine + self.got_a[at].astype(F32)).astype(BF16)
        self.b_copy(unit).start()

    def b_step(self, unit):
        at = self.place_of(unit)
        self.b_copy(unit).wait_recv()
        return self.got_a[at, self.bit_b].astype(F32) + self.got_b[at].astype(F32)

    def wait_sent(self, unit):
        for copy in (self.a_copy, self.b_copy, self.c_copy, self.d_copy):
            copy(unit).wait_send()


def reduction_buffers(units, cols):
    sems = pltpu.SemaphoreType.DMA((2, units))
    return [
        pltpu.VMEM((units, 2, 128, cols), BF16),
        pltpu.VMEM((units, 128, cols), BF16),
        pltpu.VMEM((units, 96, cols), BF16),
        sems, sems, sems, sems,
    ]


def groups_first_buffers(units, cols):
    sems = pltpu.SemaphoreType.DMA((2, units))
    return [
        pltpu.VMEM((units, 2, 32, cols), BF16),
        pltpu.VMEM((units, 32, cols), BF16),
        pltpu.VMEM((units, 2, 2, 96, cols), BF16),
        sems, sems, sems, sems,
    ]


def store_blocks(target, unit, col, values, groups):
    rows = 32 * groups
    for i in range(2):
        for j in range(2):
            at = (2 * i + j) * rows
            target[unit, i, j, :, col : col + values.shape[1]] = values[at : at + rows].astype(BF16)


def turn(source, tokens, padded, turned):
    turned[...] = jnp.concatenate([source, jnp.zeros((padded - tokens, D), BF16)], axis=0).T


def split_rows(turned, mine_ref, theirs_ref, core, groups):
    for i, (mine, theirs) in enumerate(zip(blocks_of(core, groups), blocks_of(1 - core, groups))):
        a, b, group = i // (2 * groups), i // groups % 2, i % groups
        mine_ref[a, b, group * 32 : (group + 1) * 32, :] = turned[pl.ds(mine, 32), :]
        theirs_ref[a, b, group * 32 : (group + 1) * 32, :] = turned[pl.ds(theirs, 32), :]


def write_unit(total, at, w, gate_out, up_out, down_out):
    down_out[:, pl.ds(at, w)] = total[:, :w]
    gate_out[:, pl.ds(at, w)] = total[:, CHUNK : CHUNK + w]
    up_out[:, pl.ds(at, w)] = total[:, 2 * CHUNK : 2 * CHUNK + w]


def block_kernel(
    groups, seq_devices, rows, length, width,
    x_ref, cot_ref, gain_ref, wo_ref, wg_hbm, wu_hbm, wd_hbm, doc_ref, gain_attn_ref, wq_ref, wk_ref, wv_hbm,
    output_ref, input_out, gate_out, up_out, down_out, wout_out, query_out, key_out, value_out, gains_out,
    branch, residual, normed, out_acc, gnf, w_buf, lhs, right, parts, parts_o, q_source,
    got, heads, inverse, arrived, back, qa, ka, ve, dn, qs, kt, dqt, gqk, gv, gains, gains_got,
    fsend_a, frecv_a, fsend_b, frecv_b, w_sem, wv_sems, lhs_sems, pair_sems, send_a, recv_a, send_b, recv_b, gain_send, gain_recv,
    *buffers,
):
    row_group, me = lax.axis_index("dp"), lax.axis_index("seq")
    core, _, _ = place(me)
    partner = me + 1 - 2 * core
    tokens = rows * length
    padded = right.shape[1] // 2
    full = width // CHUNK
    tail = width - full * CHUNK
    low = packed_rows(length)
    lower = lanes_of((low, 128)) < 64
    here = pl.ds(pl.multiple_of(me * length, 16), length)
    half = H * F

    def slot_of(unit):
        if isinstance(unit, int):
            return unit if unit < SLOTS else 2 * (unit - SLOTS)
        return jnp.where(unit < SLOTS, unit, 2 * (unit - SLOTS))

    def place_of(unit):
        if isinstance(unit, int):
            return unit // 2 if unit < 2 * Z_UNITS else unit - Z_UNITS
        return jnp.where(unit < 2 * Z_UNITS, unit // 2, unit - Z_UNITS)

    feed = Reduction(parts, buffers[:7], slot_of, place_of)
    outer = Reduction(parts_o, buffers[7:14])
    qkv = Reduction(q_source, buffers[14:21])
    first = GroupsFirst(parts, buffers[21:28], slot_of, lambda unit: unit // 2)

    barrier = pltpu.get_barrier_semaphore()
    for step in range(1, seq_devices):
        peer = lax.rem(me + step, seq_devices)
        pl.semaphore_signal(barrier, inc=1, device_id=(row_group, peer), device_id_type=MESH)
    for other in (feed.group_c, feed.group_d):
        pl.semaphore_signal(barrier, inc=1, device_id=(other, me), device_id_type=MESH)

    def loads(chunk, slot, w):
        at = pl.ds(pl.multiple_of(chunk * CHUNK, CHUNK), w)
        return [
            pltpu.make_async_copy(hbm.at[at, :], w_buf.at[slot, which, pl.ds(0, w), :], w_sem.at[slot, which])
            for which, hbm in enumerate((wg_hbm, wu_hbm, wd_hbm))
        ]

    def value_load(part):
        return pltpu.make_async_copy(
            wv_hbm.at[pl.ds(part * CHUNK, CHUNK), :], w_buf.at[part // 3, part % 3], wv_sems.at[part]
        )

    def lhs_send(which):
        return (q_source.at[0], q_source.at[1], parts_o.at[0])[which % 3].at[:, :, :, pl.ds(0, padded)]

    def lhs_copy(which):
        return sending(
            lhs_send(which),
            lhs.at[which % 3, :, :, :, pl.ds(padded, padded)],
            lhs_sems.at[0, which], lhs_sems.at[1, which], row_group, partner,
        )

    def prepare_lhs(which, source):
        turned = right.at[3 if which < 2 else 1, :, pl.ds(0, padded)]
        turn(source, tokens, padded, turned)
        split_rows(turned, lhs.at[which % 3, :, :, :, pl.ds(0, padded)], lhs_send(which), core, groups)

    def left(which):
        return lhs[which].reshape(D // 2, 2 * padded)

    gap = padded - tokens

    def clear(slot, count):
        for base in (tokens, padded + tokens):
            right[slot : slot + count, base : base + gap, :] = jnp.zeros((count, gap, 3 * CHUNK), BF16)

    for part in range(D // CHUNK):
        value_load(part).start()
    spread = [right.at[1 + part, pl.ds(0, 2 * half), pl.ds(0, D // 2)] for part in range(2)]
    whole = spread_matrix()
    for part in range(2):
        spread[part][...] = whole[:, part * D // 2 : (part + 1) * D // 2]
    pl.semaphore_wait(barrier, seq_devices + 1)
    for part in range(D // CHUNK):
        value_load(part).wait()

    def spreading(row, step):
        peer = lax.rem(me + step, seq_devices)
        return sending(
            back.at[row, peer], got.at[row, me], fsend_a.at[row, step], frecv_a.at[row, step], row_group, peer
        )

    def merging(row, step):
        peer = lax.rem(me + step, seq_devices)
        there = pl.ds(pl.multiple_of(peer * length, 16), length)
        mine = pl.ds(pl.multiple_of(me * PAIR, 128), PAIR)
        at = pl.ds(pl.multiple_of(row * length, 16), length)
        return sending(
            heads.at[row, there, :], branch.at[at, mine], fsend_b.at[row, step], frecv_b.at[row, step],
            row_group, peer,
        )

    def project_row(row, carry):
        at = pl.ds(pl.multiple_of(row * length, 16), length)
        low_row = rms_scale(x_ref[at, :].astype(F32), gain_attn_ref[...]).astype(BF16)
        both = jnp.concatenate([nn(low_row, wq_ref[...]), nn(low_row, wk_ref[...])], axis=1).astype(BF16)
        sides = [nn(both, spread[part][...]) for part in range(2)]
        values = sum(
            nn(low_row[:, part * CHUNK : (part + 1) * CHUNK], w_buf[part // 3, part % 3])
            for part in range(D // CHUNK)
        ).astype(BF16)
        for pair in range(seq_devices):
            side, col = divmod(pair * 128, D // 2)
            tile = sides[side][:, col : col + 128]
            back[row, pair, :length, :] = values[:, pair * PAIR : (pair + 1) * PAIR]
            back[row, pair, length:, :] = jnp.where(lower, tile[:low], tile[length - low :]).astype(BF16)
        for step in range(1, seq_devices):
            spreading(row, step).start()
        got[row, me] = back[row, me]
        return carry

    lax.fori_loop(0, rows, project_row, 0)
    for chunk in range(2):
        for copy in loads(chunk, chunk, CHUNK):
            copy.start()
    prepare_lhs(0, cot_ref[...])
    lhs_copy(0).start()

    gnf[...] = jnp.zeros_like(gnf)
    clear(0, 3)

    def residual_row(row):
        for step in range(1, seq_devices):
            merging(row, step).wait_recv()
        at = pl.ds(pl.multiple_of(row * length, 16), length)
        value = x_ref[at, :].astype(F32) + nn(branch[at, :], wo_ref[...])
        residual[at, :] = value
        out_acc[at, :] = value
        normed[at, :] = rms_scale(value, gain_ref[...]).astype(BF16)

    def attend_rows(row, carry):
        for step in range(1, seq_devices):
            spreading(row, step).wait()
        prepare_row(got, row, qa, ka, ve, seq_devices, length)
        attend_forward(row_ends(doc_ref, row), qa, ka, ve, heads.at[row], inverse.at[row])
        for step in range(1, seq_devices):
            merging(row, step).start()
        at = pl.ds(pl.multiple_of(row * length, 16), length)
        branch[at, pl.ds(pl.multiple_of(me * PAIR, 128), PAIR)] = heads[row, here, :]
        return carry

    lax.fori_loop(0, rows, attend_rows, 0)

    for row in range(rows):
        residual_row(row)
    prepare_lhs(1, normed[...])
    lhs_copy(1).start()
    clear(3, 1)

    def right_copy(slot, cols, sem):
        return sending(
            right.at[slot, pl.ds(0, tokens), pl.ds(0, cols)], right.at[slot, pl.ds(padded, tokens), pl.ds(0, cols)],
            pair_sems.at[0, sem], pair_sems.at[1, sem], row_group, partner,
        )

    def pair_copy(chunk):
        return right_copy(lax.rem(chunk, 4), 3 * CHUNK, chunk)

    def forward_part(chunk, wg, wu, wd, w):
        slot = lax.rem(chunk, 4)
        gate = nt(normed[...], wg)
        up = nt(normed[...], wu)
        sigmoid = 1.0 / (1.0 + jnp.exp(-gate))
        silu = gate * sigmoid
        hidden = (silu * up).astype(BF16)
        grad_hidden = nt(cot_ref[...], wd)
        grad_gate = (grad_hidden * up * (sigmoid * (1.0 + gate * (1.0 - sigmoid)))).astype(BF16)
        grad_up = (grad_hidden * silu).astype(BF16)
        for part, values in enumerate((hidden, grad_gate, grad_up)):
            right[slot, :tokens, part * CHUNK : part * CHUNK + w] = values
            if w < CHUNK:
                right[slot, :tokens, part * CHUNK + w : (part + 1) * CHUNK] = jnp.zeros((tokens, CHUNK - w), BF16)
        pair_copy(chunk).start()
        out_acc[...] += nn(hidden, wd)
        gnf[...] += nn(grad_gate, wg) + nn(grad_up, wu)

    def grad_part(chunk):
        pair_copy(chunk).wait()
        slot = lax.rem(chunk, 4)
        store_blocks(parts, slot_of(chunk), 0, nn(left(0), right[slot, :, 0:CHUNK]), groups)
        store_blocks(parts, slot_of(chunk), CHUNK, nn(left(1), right[slot, :, CHUNK:]), groups)

    def forward_step(chunk):
        slot = lax.rem(chunk, 2)
        for copy in loads(chunk, slot, CHUNK):
            copy.wait()
        forward_part(chunk, w_buf[slot, 0], w_buf[slot, 1], w_buf[slot, 2], CHUNK)

    def ticks(chunk):
        @pl.when((chunk >= 4) & (lax.rem(chunk, 2) == 0))
        def _():
            feed.a_step(chunk - 4)

        @pl.when((chunk >= 7) & (lax.rem(chunk, 2) == 1))
        def _():
            feed.b_step(chunk - 7)

        @pl.when(chunk == 8)
        def _():
            first.c_step(1)

    def fetch_next(chunk):
        @pl.when(chunk < full - 1)
        def _():
            for copy in loads(chunk + 1, lax.rem(chunk + 1, 2), CHUNK):
                copy.start()

        @pl.when(chunk == full - 1)
        def _():
            for copy in loads(full, full % 2, tail):
                copy.start()

    def main(chunk, carry):
        fetch_next(chunk)
        forward_step(chunk)
        unit = chunk - 1

        @pl.when(unit >= SLOTS)
        def _():
            feed.a_copy(2 * (unit - SLOTS)).wait_send()

        grad_part(unit)
        along_z = (unit < 2 * Z_UNITS) & (lax.rem(unit, 2) == 1)

        @pl.when(along_z)
        def _():
            first.c_copy(unit).start()

        @pl.when(jnp.logical_not(along_z) & (unit < 10))
        def _():
            feed.a_copy(unit).start()

        ticks(chunk)
        return carry

    forward_step(0)
    for which in range(2):
        lhs_copy(which).wait()
    lax.fori_loop(1, full, main, 0)
    slot = full % 2
    for copy in loads(full, slot, tail):
        copy.wait()
    forward_part(full, w_buf[slot, 0, :tail], w_buf[slot, 1, :tail], w_buf[slot, 2, :tail], tail)
    for part in range(D // CHUNK):
        value_load(part).start()
    feed.a_copy(2 * (full - 1 - SLOTS)).wait_send()
    grad_part(full - 1)
    first.c_copy(full - 1).start()

    gains[...] = jnp.zeros_like(gains)

    def norm_backward_ffn(step, carry):
        at = pl.ds(pl.multiple_of(step * STEP_ROWS, 16), STEP_ROWS)
        value, grad = residual[at, :], gnf[at, :]
        scale = lax.rsqrt(jnp.mean(value * value, axis=-1, keepdims=True) + eps_norm)
        gains[0:1, :] += jnp.sum(grad * value * scale, axis=0, keepdims=True)
        weighted = grad * gain_ref[...]
        mean = jnp.mean(weighted * value, axis=-1, keepdims=True)
        total = cot_ref[at, :].astype(F32) + scale * weighted - value * (scale * scale * scale * mean)
        gnf[at, :] = total
        right[3, at, :] = total[:, : 3 * CHUNK].astype(BF16)
        right[0, at, :CHUNK] = total[:, 3 * CHUNK :].astype(BF16)
        output_ref[at, :] = out_acc[at, :].astype(BF16)
        return carry

    lax.fori_loop(0, tokens // STEP_ROWS, norm_backward_ffn, 0)
    normed[...] = (
        nt(right[3, :tokens, :], wo_ref[:, : 3 * CHUNK]) + nt(right[0, :tokens, :CHUNK], wo_ref[:, 3 * CHUNK :])
    ).astype(BF16)

    def outgoing(row, step):
        peer = lax.rem(me + step, seq_devices)
        theirs = pl.ds(pl.multiple_of(peer * PAIR, 128), PAIR)
        at = pl.ds(pl.multiple_of(row * length, 16), length)
        return sending(
            normed.at[at, theirs], arrived.at[row, here, :], send_a.at[row, step], recv_a.at[row, step],
            row_group, peer,
        )

    def returning(row, step):
        peer = lax.rem(me + step, seq_devices)
        return sending(
            got.at[row, peer], back.at[row, me], send_b.at[row, step], recv_b.at[row, step], row_group, peer
        )

    def send_row(row, carry):
        for step in range(1, seq_devices):
            outgoing(row, step).start()
        at = pl.ds(pl.multiple_of(row * length, 16), length)
        arrived[row, here, :] = normed[at, pl.ds(pl.multiple_of(me * PAIR, 128), PAIR)]
        return carry

    lax.fori_loop(0, rows, send_row, 0)
    feed.a_step(6)
    feed.a_copy(2 * (full - SLOTS)).wait_send()
    grad_part(full)
    out_pairs = [right_copy(3, 3 * CHUNK, full + 1), right_copy(0, CHUNK, full + 2)]
    for copy in out_pairs:
        copy.start()
    prepare_lhs(2, branch[...])
    lhs_copy(2).start()
    feed.b_step(4)
    first.c_step(3)
    feed.c_step(0)
    prepare_lhs(3, rms_scale(x_ref[...].astype(F32), gain_attn_ref[...]).astype(BF16))
    clear(1, 1)
    for copy in out_pairs:
        copy.wait()
    lhs_copy(3).start()
    lhs_copy(2).wait()
    for col in range(0, D, CHUNK):
        columns = right[3, :, col : col + CHUNK] if col < 3 * CHUNK else right[0, :, :CHUNK]
        store_blocks(parts_o, 0, col, nn(left(2), columns), groups)
    gather = right.at[3, pl.ds(0, 2 * half), pl.ds(0, 2 * half)]
    gather[...] = gather_matrix()

    def attend(row, carry):
        prepare_row(got, row, qa, ka, ve, seq_devices, length)
        for step in range(1, seq_devices):
            outgoing(row, step).wait_recv()
        attend_backward(
            row_ends(doc_ref, row), arrived.at[row], qa, ka, ve, heads.at[row], inverse.at[row],
            dn, qs, kt, dqt, gqk, gv,
        )

        def pack(peer, inner):
            at = pl.multiple_of(peer * length, 16)
            got[row, peer, :length, :] = gv[pl.ds(at, length), :]
            front = gqk[pl.ds(at, low), :]
            rear = pltpu.roll(gqk[pl.ds(at + length - low, low), :], 64, 1)
            got[row, peer, length:, :] = jnp.where(lower, front, rear).astype(BF16)
            return inner

        lax.fori_loop(0, seq_devices, pack, 0)
        for step in range(1, seq_devices):
            returning(row, step).start()
        back[row, me] = got[row, me]

        @pl.when(row == 0)
        def _():
            feed.a_copy(10).start()
            feed.a_step(8)
            feed.b_step(6)
            first.c_step(5)
            first.d_step(1)

        @pl.when(row == 1)
        def _():
            outer.a_copy(0).start()
            feed.c_step(2)
            first.c_step(7)
            first.d_step(3)

        return carry

    lax.fori_loop(0, rows, attend, 0)
    feed.b_step(8)
    feed.c_step(4)
    first.c_step(9)
    first.d_step(5)
    feed.a_step(10)

    def unpack(row, carry):
        for step in range(1, seq_devices):
            outgoing(row, step).wait_send()
            returning(row, step).wait()
        tiles = []
        for pair in range(0, seq_devices, 2):
            halves = []
            for one in (pair, pair + 1):
                packed = back[row, one, length:, :].astype(F32)
                turned_over = pltpu.roll(packed, 64, 1)
                straight, other = (packed, turned_over) if one == pair else (turned_over, packed)
                halves.append(jnp.concatenate([straight, other[2 * low - length :]], axis=0))
            tiles.append(jnp.where(lanes_of((length, 128)) < 64, halves[0], halves[1]).astype(BF16))
        at = pl.ds(pl.multiple_of(row * length, 16), length)
        right[1, at, : 2 * half] = nn(jnp.concatenate(tiles, axis=1), gather[...]).astype(BF16)
        for pair in range(seq_devices):
            slot, col = divmod(2 * half + pair * PAIR, 3 * CHUNK)
            right[1 + slot, at, col : col + PAIR] = back[row, pair, :length, :]
        return carry

    lax.fori_loop(0, rows, unpack, 0)
    q_pairs = [right_copy(1, 3 * CHUNK, full + 3), right_copy(2, 3 * CHUNK, full + 4)]
    for copy in q_pairs:
        copy.start()
    for part in range(D // CHUNK):
        value_load(part).wait()
    q_and_k = nt(right[1, :tokens, :half], wq_ref[...]) + nt(right[1, :tokens, half : 2 * half], wk_ref[...])
    for part in range(D // CHUNK):
        at = slice(part * CHUNK, (part + 1) * CHUNK)
        block = w_buf[part // 3, part % 3]
        out_acc[:, at] = (
            q_and_k[:, at]
            + nt(right[1, :tokens, 2 * half :], block[:, : 3 * CHUNK - 2 * half])
            + nt(right[2, :tokens, :], block[:, 3 * CHUNK - 2 * half :])
        )
    lhs_copy(3).wait()
    for copy in q_pairs:
        copy.wait()
    for unit in range(2):
        for col in range(0, 3 * CHUNK, CHUNK):
            store_blocks(q_source, unit, col, nn(left(0), right[1 + unit, :, col : col + CHUNK]), groups)
        qkv.a_copy(unit).start()

    def norm_backward(step, carry):
        at = pl.ds(pl.multiple_of(step * STEP_ROWS, 16), STEP_ROWS)
        value, grad = x_ref[at, :].astype(F32), out_acc[at, :]
        scale = lax.rsqrt(jnp.mean(value * value, axis=-1, keepdims=True) + eps_norm)
        gains[1:2, :] += jnp.sum(grad * value * scale, axis=0, keepdims=True)
        weighted = grad * gain_attn_ref[...]
        mean = jnp.mean(weighted * value, axis=-1, keepdims=True)
        total = gnf[at, :] + scale * weighted - value * (scale * scale * scale * mean)
        input_out[at, :] = total.astype(BF16)
        return carry

    lax.fori_loop(0, tokens // STEP_ROWS, norm_backward, 0)

    def gain_copy(step, target_group, target):
        return sending(
            gains, gains_got.at[step], gain_send.at[step], gain_recv.at[step], target_group, target
        )

    gain_copies = [
        gain_copy(0, row_group, partner),
        gain_copy(1, row_group, feed.peer_a),
        gain_copy(2, row_group, feed.peer_b),
        gain_copy(3, feed.group_c, me),
        gain_copy(4, feed.group_d, me),
    ]

    def gain_step(step):
        gain_copies[step].wait()
        gains[...] += gains_got[step]
        if step < 4:
            gain_copies[step + 1].start()

    def write_feed(unit, total, w):
        at = unit * CHUNK if isinstance(unit, int) else pl.multiple_of(unit * CHUNK, CHUNK)
        write_unit(total, at, w, gate_out, up_out, down_out)

    gain_copies[0].start()
    outer.a_step(0)
    feed.b_step(10)
    gain_step(0)
    first.d_step(7)
    feed.c_step(6)
    first.a_step(1)
    feed.c_step(8)
    gain_step(1)
    qkv.a_step(0)
    first.a_step(3)
    qkv.a_step(1)
    outer.b_step(0)
    gain_step(2)
    qkv.b_step(0)
    feed.c_step(10)
    first.a_step(5)
    qkv.b_step(1)
    gain_step(3)
    qkv.c_step(0)
    first.d_step(9)
    outer.c_step(0)
    qkv.c_step(1)
    first.a_step(7)
    gain_step(4)
    first.a_step(9)
    for unit in range(full):
        if unit >= 2 * Z_UNITS or unit % 2 == 0:
            write_feed(unit, feed.d_step(unit), CHUNK)
    write_feed(full, feed.d_step(full), tail)
    for unit in range(1, 2 * Z_UNITS, 2):
        write_feed(unit, first.b_step(unit), CHUNK)
    picked = lax.broadcasted_iota(jnp.int32, (D, 128), 0) == 32 * (seq_devices * row_group + me) + lanes_of((D, 128))
    gains_out[...] = jnp.dot(
        gains[...], jnp.where(picked, 1.0, 0.0), precision=lax.Precision.HIGHEST, preferred_element_type=F32
    )
    wout_out[...] = outer.d_step(0)
    total = qkv.d_step(0)
    query_out[...] = total[:, :half]
    key_out[...] = total[:, half : 2 * half]
    value_out[:, : 3 * CHUNK - 2 * half] = total[:, 2 * half :]
    value_out[:, 3 * CHUNK - 2 * half :] = qkv.d_step(1)

    for unit in range(full + 1):
        if unit < 2 * Z_UNITS and unit % 2 == 1:
            first.wait_sent(unit)
        else:
            feed.wait_sent(unit)
            if unit > 2 * (full - SLOTS):
                feed.a_copy(unit).wait_send()
    def forward_sent(row, carry):
        for step in range(1, seq_devices):
            merging(row, step).wait_send()
        return carry

    lax.fori_loop(0, rows, forward_sent, 0)
    for one, unit in ((outer, 0), (qkv, 0), (qkv, 1)):
        one.wait_sent(unit)
        one.a_copy(unit).wait_send()


ANY_SPEC = pl.BlockSpec(memory_space=pl.ANY)


def block_step(
    groups, seq_devices, x, cotangent, gain_ffn, w_out, w_gate_t, w_up_t, w_down, doc_lengths, gain_attn,
    w_query, w_key, w_value,
):
    tokens = x.shape[0]
    rows = doc_lengths.shape[0]
    length = tokens // rows
    total = seq_devices * length
    width = w_down.shape[0]
    full = width // CHUNK
    padded = (tokens + 127) // 128 * 128
    unit_rows = 32 * groups
    message = (rows, seq_devices, length + packed_rows(length), 128)
    dma = pltpu.SemaphoreType.DMA
    sems = dma((rows, seq_devices))
    return pl.pallas_call(
        functools.partial(block_kernel, groups, seq_devices, rows, length, width),
        name="block",
        out_shape=[
            jax.ShapeDtypeStruct((tokens, D), BF16),
            jax.ShapeDtypeStruct((tokens, D), BF16),
            jax.ShapeDtypeStruct((32, width), F32),
            jax.ShapeDtypeStruct((32, width), F32),
            jax.ShapeDtypeStruct((32, width), F32),
            jax.ShapeDtypeStruct((32, D), F32),
            jax.ShapeDtypeStruct((32, H * F), F32),
            jax.ShapeDtypeStruct((32, H * F), F32),
            jax.ShapeDtypeStruct((32, D), F32),
            jax.ShapeDtypeStruct((8, 128), F32),
        ],
        in_specs=[VMEM_SPEC] * 4 + [ANY_SPEC] * 3 + [SMEM_SPEC] + [VMEM_SPEC] * 3 + [ANY_SPEC],
        out_specs=[VMEM_SPEC] * 10,
        scratch_shapes=[
            pltpu.VMEM((tokens, D), BF16),
            pltpu.VMEM((tokens, D), F32),
            pltpu.VMEM((tokens, D), BF16),
            pltpu.VMEM((tokens, D), F32),
            pltpu.VMEM((tokens, D), F32),
            pltpu.VMEM((2, 3, CHUNK, D), BF16),
            pltpu.VMEM((3, 2, 2, unit_rows, 2 * padded), BF16),
            pltpu.VMEM((4, 2 * padded, 3 * CHUNK), BF16),
            pltpu.VMEM((SLOTS, 2, 2, unit_rows, 3 * CHUNK), BF16),
            pltpu.VMEM((1, 2, 2, unit_rows, D), BF16),
            pltpu.VMEM((2, 2, 2, unit_rows, 3 * CHUNK), BF16),
            pltpu.VMEM(message, BF16),
            pltpu.VMEM((rows, total, 128), BF16),
            pltpu.VMEM((rows, total, 128), F32),
            pltpu.VMEM((rows, total, 128), BF16),
            pltpu.VMEM(message, BF16),
            pltpu.VMEM((total, 128), BF16),
            pltpu.VMEM((2, total, 128), BF16),
            pltpu.VMEM((2, total, 128), BF16),
            pltpu.VMEM((2, total, 128), BF16),
            pltpu.VMEM((total, 128), BF16),
            pltpu.VMEM((2, 32, total), BF16),
            pltpu.VMEM((32, total), F32),
            pltpu.VMEM((total, 128), F32),
            pltpu.VMEM((total, 128), BF16),
            pltpu.VMEM((8, D), F32),
            pltpu.VMEM((5, 8, D), F32),
            sems, sems, sems, sems, dma((2, 3)), dma((D // CHUNK,)), dma((2, 4)), dma((2, full + 5)),
            sems, sems, sems, sems, dma((5,)), dma((5,)),
        ]
        + reduction_buffers(full + 1 - Z_UNITS, 3 * CHUNK)
        + reduction_buffers(1, D)
        + reduction_buffers(2, 3 * CHUNK)
        + groups_first_buffers(Z_UNITS, 3 * CHUNK),
        compiler_params=pltpu.CompilerParams(collective_id=1, has_side_effects=True, vmem_limit_bytes=VMEM_BYTES),
    )(
        x, cotangent, gain_ffn.reshape(1, D), w_out, w_gate_t, w_up_t, w_down, doc_lengths,
        gain_attn.reshape(1, D), w_query, w_key, w_value,
    )


def publish(results, gains):
    def kernel(*refs):
        count = len(results)
        for source, target in zip(refs[:count], refs[count + 1 : 2 * count + 1]):
            target[...] = source[...]
        refs[2 * count + 1][...] = refs[count][1:2, :32]
        refs[2 * count + 2][...] = refs[count][0:1, :32]

    one = jax.ShapeDtypeStruct((1, 32), F32)
    return pl.pallas_call(
        kernel,
        name="publish",
        out_shape=[jax.ShapeDtypeStruct(x.shape, x.dtype) for x in results] + [one, one],
        in_specs=[VMEM_SPEC] * (len(results) + 1),
        out_specs=[VMEM_SPEC] * (len(results) + 2),
        compiler_params=pltpu.CompilerParams(vmem_limit_bytes=VMEM_BYTES),
    )(*results, gains)


def tuned_body(
    seq_devices, groups, inputs, doc_lengths, gain_attn, w_query, w_key, w_value, w_out, gain_ffn, w_gate, w_up,
    w_down, cotangent,
):
    row_count, shard_len, _ = inputs.shape
    token_count = row_count * shard_len
    output, input_grad, gate, up, down, out, query, key, value, gains = block_step(
        groups, seq_devices, inputs.reshape(token_count, D), cotangent.reshape(token_count, D), gain_ffn, w_out,
        w_gate.T, w_up.T, w_down, doc_lengths, gain_attn, w_query, w_key, w_value,
    )
    output, input_grad, gate, up, down, out, query, key, value, gain_attn_part, gain_ffn_part = publish(
        (output, input_grad, gate, up, down, out, query, key, value), gains
    )
    return (
        output.reshape(row_count, shard_len, D),
        input_grad.reshape(row_count, shard_len, D),
        gain_attn_part.reshape(32),
        query,
        key,
        value,
        out,
        gain_ffn_part.reshape(32),
        gate,
        up,
        down.T,
    )


def solution(mesh):
    in_specs = (
        P("dp", "seq", None),
        P("dp", None),
        P(),
        P(),
        P(),
        P(),
        P(),
        P(),
        P(),
        P(),
        P(),
        P("dp", "seq", None),
    )
    out_specs = (
        P("dp", "seq", None),
        P("dp", "seq", None),
        P(("dp", "seq")),
        P(("dp", "seq"), None),
        P(("dp", "seq"), None),
        P(("dp", "seq"), None),
        P(("dp", "seq"), None),
        P(("dp", "seq")),
        P(("dp", "seq"), None),
        P(("dp", "seq"), None),
        P(None, ("dp", "seq")),
    )
    seq_devices, groups = mesh.shape["seq"], mesh.shape["dp"]
    tuned = seq_devices == 8 and seq_devices * groups * 32 == D
    step = functools.partial(tuned_body, seq_devices, groups) if tuned else general_body
    return jax.shard_map(step, mesh=mesh, in_specs=in_specs, out_specs=out_specs, check_vma=False)
```

```python
import functools

import jax
import jax.numpy as jnp
from jax import lax
from jax.experimental import pallas as pl
from jax.experimental.pallas import tpu as pltpu
from jax.sharding import PartitionSpec as P

D = 1024
H = 16
F = 16
HV = 64
BLOCK = 576


eps_norm = 1e-05


def rms_scale(stream, gain_vec):
    return (
        stream * lax.rsqrt(jnp.mean(stream * stream, axis=-1, keepdims=True) + eps_norm) * gain_vec
    )


def taylor_features(vectors):
    feat_width = vectors.shape[-1]
    outer_prod = (vectors[..., :, None] * vectors[..., None, :]).reshape(
        vectors.shape[:-1] + (feat_width * feat_width,)
    )
    ones_part = jnp.ones(vectors.shape[:-1] + (1,), jnp.float32)
    return jnp.concatenate(
        [ones_part, vectors * feat_width ** (-0.25), outer_prod * (0.5 / feat_width) ** 0.5],
        axis=-1,
    )


def document_ids(doc_lens, seq_length):
    doc_ends = jnp.cumsum(doc_lens, dtype=jnp.int32)
    positions = jnp.arange(seq_length, dtype=jnp.int32)
    return jnp.sum(
        (positions[:, None] >= doc_ends[None, :]).astype(jnp.int32), axis=1, dtype=jnp.int32
    )


def attend_row(queries, key_proj, value_proj, doc_row, block_rows):
    seq_length, head_count, feat_width = queries.shape
    value_width = value_proj.shape[-1]
    feat_count = 1 + feat_width + feat_width * feat_width
    block_count = seq_length // block_rows
    highest = lax.Precision.HIGHEST
    query_blocks = queries.reshape(block_count, block_rows, head_count, feat_width)
    key_blocks = key_proj.reshape(block_count, block_rows, head_count, feat_width)
    value_blocks = value_proj.reshape(block_count, block_rows, head_count, value_width)
    doc_blocks = doc_row.reshape(block_count, block_rows)
    previous = jnp.concatenate([jnp.full((1,), -1, jnp.int32), doc_blocks[:-1, -1]])
    positions = jnp.arange(block_rows, dtype=jnp.int32)
    causal = positions[:, None] >= positions[None, :]

    def block_step(carried, pieces):
        state_sum, norm_sum = carried
        query_block, key_block, value_block, doc_block, prior_doc = pieces
        scores = jnp.einsum(
            "thf,shf->hts", query_block, key_block, precision=highest
        ) * feat_width ** (-0.5)
        weights = 1.0 + scores + 0.5 * scores * scores
        same_doc = causal & (doc_block[:, None] == doc_block[None, :])
        weights = jnp.where(same_doc[None, :, :], weights, 0.0)
        numerator = jnp.einsum("hts,shv->thv", weights, value_block, precision=highest)
        denominator = jnp.transpose(jnp.sum(weights, axis=2))
        use_state = (doc_block == prior_doc).astype(jnp.float32)[:, None]
        query_feats = taylor_features(query_block)
        numerator = numerator + use_state[:, :, None] * jnp.einsum(
            "thp,hpv->thv", query_feats, state_sum, precision=highest
        )
        denominator = denominator + use_state * jnp.einsum(
            "thp,hp->th", query_feats, norm_sum, precision=highest
        )
        last_doc = doc_block[-1]
        keep_state = (last_doc == prior_doc).astype(jnp.float32)
        key_feats = (
            taylor_features(key_block) * (doc_block == last_doc).astype(jnp.float32)[:, None, None]
        )
        state_sum = keep_state * state_sum + jnp.einsum(
            "shp,shv->hpv", key_feats, value_block, precision=highest
        )
        norm_sum = keep_state * norm_sum + jnp.sum(key_feats, axis=0)
        return ((state_sum, norm_sum), numerator / denominator[:, :, None])

    initial = (
        jnp.zeros((head_count, feat_count, value_width), jnp.float32),
        jnp.zeros((head_count, feat_count), jnp.float32),
    )
    _, results = lax.scan(
        jax.checkpoint(block_step),
        initial,
        (query_blocks, key_blocks, value_blocks, doc_blocks, previous),
    )
    return results.reshape(seq_length, head_count, value_width)


def project(left, right):
    return jnp.dot(left, right, preferred_element_type=jnp.float32)


def back_project(left, right):
    return lax.dot_general(
        left, right, (((1,), (1,)), ((), ())), preferred_element_type=jnp.float32
    )


def weight_grad(left, right):
    return lax.dot_general(
        left, right, (((0,), (0,)), ((), ())), preferred_element_type=jnp.float32
    )


def swiglu(gate_proj, up_proj):
    return jax.nn.silu(gate_proj) * up_proj


def general_body(
    inputs,
    doc_lengths,
    gain_attn,
    w_query,
    w_key,
    w_value,
    w_out,
    gain_ffn,
    w_gate,
    w_up,
    w_down,
    cotangent,
):
    row_count, shard_len, _ = inputs.shape
    token_count = row_count * shard_len
    stream = inputs.reshape(token_count, D).astype(jnp.float32)
    normed, attn_norm_back = jax.vjp(rms_scale, stream, gain_attn)
    normed_low = normed.astype(jnp.bfloat16)
    query_proj = project(normed_low, w_query).astype(jnp.bfloat16)
    key_proj = project(normed_low, w_key).astype(jnp.bfloat16)
    value_proj = project(normed_low, w_value).astype(jnp.bfloat16)
    query_heads, key_heads, value_heads = (
        lax.all_to_all(
            query_proj.reshape(row_count, shard_len, H, F),
            "seq",
            split_axis=2,
            concat_axis=1,
            tiled=True,
        ),
        lax.all_to_all(
            key_proj.reshape(row_count, shard_len, H, F),
            "seq",
            split_axis=2,
            concat_axis=1,
            tiled=True,
        ),
        lax.all_to_all(
            value_proj.reshape(row_count, shard_len, H, HV),
            "seq",
            split_axis=2,
            concat_axis=1,
            tiled=True,
        ),
    )
    seq_length = query_heads.shape[1]
    doc_rows = jax.vmap(lambda doc_lens: document_ids(doc_lens, seq_length))(doc_lengths)

    def attend_all(queries, keys_in, values_in):
        return jax.vmap(attend_row, in_axes=(0, 0, 0, 0, None))(
            queries, keys_in, values_in, doc_rows, BLOCK
        )

    mixed_heads, attend_back = jax.vjp(
        attend_all,
        query_heads.astype(jnp.float32),
        key_heads.astype(jnp.float32),
        value_heads.astype(jnp.float32),
    )
    mixed_rows = lax.all_to_all(
        mixed_heads.astype(jnp.bfloat16), "seq", split_axis=1, concat_axis=2, tiled=True
    )
    mixed_flat = mixed_rows.reshape(token_count, D)
    residual = stream + project(mixed_flat, w_out)
    normed_ffn, ffn_norm_back = jax.vjp(rms_scale, residual, gain_ffn)
    ffn_low = normed_ffn.astype(jnp.bfloat16)
    gate_proj = project(ffn_low, w_gate)
    up_proj = project(ffn_low, w_up)
    hidden, act_back = jax.vjp(swiglu, gate_proj, up_proj)
    hidden_low = hidden.astype(jnp.bfloat16)
    output = residual + project(hidden_low, w_down)
    grad_out = cotangent.reshape(token_count, D)
    grad_gate, grad_up = act_back(back_project(grad_out, w_down))
    grad_gate_low = grad_gate.astype(jnp.bfloat16)
    grad_up_low = grad_up.astype(jnp.bfloat16)
    down_grad_t = weight_grad(grad_out, hidden_low)
    gate_grad = weight_grad(ffn_low, grad_gate_low)
    up_grad = weight_grad(ffn_low, grad_up_low)
    grad_normed_ffn = back_project(grad_gate_low, w_gate) + back_project(grad_up_low, w_up)
    grad_residual, gain_ffn_grad = ffn_norm_back(grad_normed_ffn)
    grad_residual = grad_residual + grad_out.astype(jnp.float32)
    grad_branch = grad_residual.astype(jnp.bfloat16)
    out_grad = weight_grad(mixed_flat, grad_branch)
    grad_mixed = (
        back_project(grad_branch, w_out).astype(jnp.bfloat16).reshape(row_count, shard_len, H, HV)
    )
    grad_heads = lax.all_to_all(grad_mixed, "seq", split_axis=2, concat_axis=1, tiled=True)
    grad_query, grad_key, grad_value = attend_back(grad_heads.astype(jnp.float32))
    back_query, back_key, back_value = (
        lax.all_to_all(
            grad_query.astype(jnp.bfloat16), "seq", split_axis=1, concat_axis=2, tiled=True
        ),
        lax.all_to_all(
            grad_key.astype(jnp.bfloat16), "seq", split_axis=1, concat_axis=2, tiled=True
        ),
        lax.all_to_all(
            grad_value.astype(jnp.bfloat16), "seq", split_axis=1, concat_axis=2, tiled=True
        ),
    )
    back_query = back_query.reshape(token_count, H * F)
    back_key = back_key.reshape(token_count, H * F)
    back_value = back_value.reshape(token_count, D)
    query_grad = weight_grad(normed_low, back_query)
    key_grad = weight_grad(normed_low, back_key)
    value_grad = weight_grad(normed_low, back_value)
    grad_normed = (
        back_project(back_query, w_query)
        + back_project(back_key, w_key)
        + back_project(back_value, w_value)
    )
    grad_stream, gain_attn_grad = attn_norm_back(grad_normed)
    input_grad = grad_residual + grad_stream
    (
        gain_attn_part,
        query_part,
        key_part,
        value_part,
        out_part,
        gain_ffn_part,
        gate_part,
        up_part,
        down_part,
    ) = (
        lax.psum_scatter(gain_attn_grad, ("dp", "seq"), scatter_dimension=0, tiled=True),
        lax.psum_scatter(query_grad, ("dp", "seq"), scatter_dimension=0, tiled=True),
        lax.psum_scatter(key_grad, ("dp", "seq"), scatter_dimension=0, tiled=True),
        lax.psum_scatter(value_grad, ("dp", "seq"), scatter_dimension=0, tiled=True),
        lax.psum_scatter(out_grad, ("dp", "seq"), scatter_dimension=0, tiled=True),
        lax.psum_scatter(gain_ffn_grad, ("dp", "seq"), scatter_dimension=0, tiled=True),
        lax.psum_scatter(gate_grad, ("dp", "seq"), scatter_dimension=0, tiled=True),
        lax.psum_scatter(up_grad, ("dp", "seq"), scatter_dimension=0, tiled=True),
        lax.psum_scatter(down_grad_t, ("dp", "seq"), scatter_dimension=0, tiled=True),
    )
    return (
        output.reshape(row_count, shard_len, D).astype(jnp.bfloat16),
        input_grad.reshape(row_count, shard_len, D).astype(jnp.bfloat16),
        gain_attn_part,
        query_part,
        key_part,
        value_part,
        out_part,
        gain_ffn_part,
        gate_part,
        up_part,
        jnp.transpose(down_part),
    )


F32 = jnp.float32
BF16 = jnp.bfloat16
MESH = pl.DeviceIdType.MESH
TILE = 384
PAIR = 2 * HV


def nt(left, right):
    return lax.dot_general(left, right, (((1,), (1,)), ((), ())), preferred_element_type=F32)


def nn(left, right):
    return jnp.dot(left, right, preferred_element_type=F32)


def lanes_of(shape):
    return lax.broadcasted_iota(jnp.int32, shape, len(shape) - 1)


def first_visible(ends, positions):
    start = jnp.zeros_like(positions)
    for end in ends:
        start = jnp.where(positions >= end, end, start)
    return start


def row_ends(doc_ref, row):
    ends, total = [], 0
    for j in range(doc_ref.shape[1] - 1):
        total = total + doc_ref[row, j]
        ends.append(total)
    return ends


def spread_matrix():
    half = H * F
    source = lax.broadcasted_iota(jnp.int32, (2 * half, 1), 0)
    column = lax.broadcasted_iota(jnp.int32, (1, (H // 2) * 128), 1)
    pair, lane = column // 128, column % 64
    wanted = pair * 32 + lane + jnp.where(lane < 32, 0, half - 32)
    return jnp.where(source == wanted, 1.0, 0.0).astype(BF16)


def gather_matrix():
    half = H * F
    source = lax.broadcasted_iota(jnp.int32, (2 * half, 1), 0)
    column = lax.broadcasted_iota(jnp.int32, (1, 2 * half), 1)
    pair, lane = source // 64, source % 64
    wanted = pair * 32 + lane + jnp.where(lane < 32, 0, half - 32)
    return jnp.where(column == wanted, 1.0, 0.0).astype(BF16)


def packed_rows(length):
    return (length // 2 + 15) // 16 * 16


def prepare_row(got_ref, row, qa_ref, ka_ref, ve_ref, seq_devices, length):
    low = packed_rows(length)

    def part(peer, carry):
        values = got_ref[row, peer, :length, :].astype(F32)
        packed = got_ref[row, peer, length : length + low, :].astype(F32)
        turned = pltpu.roll(packed, 64, 1)
        both = jnp.concatenate([packed, turned[2 * low - length :]], axis=0)
        lane = lanes_of((length, 128))
        keys = pltpu.roll(both, 96, 1)
        at = pl.ds(pl.multiple_of(peer * length, 16), length)
        one = jnp.where(lane == 32, 1.0, 0.0)
        qa_ref[at, :] = jnp.where(lane < 32, both * 0.25, one).astype(BF16)
        ka_ref[0, at, :] = jnp.where(lane < 16, keys, one).astype(BF16)
        ka_ref[1, at, :] = jnp.where((lane >= 16) & (lane < 32), keys, one).astype(BF16)
        ve_ref[0, at, :] = jnp.where(lane < 64, values, 1.0).astype(BF16)
        ve_ref[1, at, :] = jnp.where(lane >= 64, values, 1.0).astype(BF16)
        return carry

    lax.fori_loop(0, seq_devices, part, 0)


def attend_forward(ends, qa_ref, ka_ref, ve_ref, mixed_ref, inverse_ref):
    length = qa_ref.shape[0]
    for block in range(length // TILE):
        reach = (block + 1) * TILE
        at = pl.ds(block * TILE, TILE)
        queries = qa_ref[at, :]
        t = lax.broadcasted_iota(jnp.int32, (TILE, 1), 0) + block * TILE
        start = first_visible(ends, t)
        s = lax.broadcasted_iota(jnp.int32, (TILE, reach), 1)
        visible = (s >= start) & (s <= t)
        sums = []
        for head in range(2):
            base = nt(queries, ka_ref[head, :reach, :])
            weights = jnp.where(visible, base * base + 1.0, 0.0).astype(BF16)
            sums.append(nn(weights, ve_ref[head, :reach, :]))
        lower = lanes_of((TILE, 128)) < 64
        numerator = jnp.where(lower, sums[0], sums[1])
        inverse = 1.0 / pltpu.roll(jnp.where(lower, sums[1], sums[0]), 64, 1)
        mixed_ref[at, :] = (numerator * inverse).astype(BF16)
        inverse_ref[at, :] = inverse


def attend_backward(
    ends, grad_ref, qa_ref, ka_ref, ve_ref, mixed_ref, inverse_ref, dn_ref, qs_ref, kt_ref, dqt_ref, gqk_ref, gv_ref
):
    length = qa_ref.shape[0]
    lane = lanes_of((length, 128))
    lower = lane < 64
    scaled = grad_ref[...].astype(F32) * inverse_ref[...]
    away = pltpu.roll(-scaled * mixed_ref[...].astype(F32), 64, 1)
    dn_ref[0] = jnp.where(lower, scaled, away).astype(BF16)
    dn_ref[1] = jnp.where(lower, away, scaled).astype(BF16)
    shifted = pltpu.roll(qa_ref[...].astype(F32), 32, 1)
    qs_ref[...] = jnp.where((lane >= 32) & (lane < 64), shifted * 2.0, 0.0).astype(BF16)
    for head in range(2):
        kt_ref[head] = ka_ref[head].astype(F32).T[:32].astype(BF16)
    dqt_ref[...] = jnp.zeros_like(dqt_ref)
    for block in range(length // TILE):
        first = block * TILE
        at = pl.ds(first, TILE)
        rest = pl.ds(first, length - first)
        shape = (TILE, length - first)
        t = lax.broadcasted_iota(jnp.int32, (1, shape[1]), 1) + first
        s = lax.broadcasted_iota(jnp.int32, shape, 0) + first
        visible = (s >= first_visible(ends, t)) & (s <= t)
        value_sums, key_sums = [], []
        for head in range(2):
            base = nt(ka_ref[head, at, :], qa_ref[rest, :])
            grad_weights = nt(ve_ref[head, at, :], dn_ref[head, rest, :])
            weights = jnp.where(visible, base * base + 1.0, 0.0).astype(BF16)
            grad_base = jnp.where(visible, grad_weights * base, 0.0).astype(BF16)
            value_sums.append(nn(weights, dn_ref[head, rest, :]))
            key_sums.append(nn(grad_base, qs_ref[rest, :]))
            dqt_ref[:, rest] += nn(kt_ref[head, :, at], grad_base)
        lane = lanes_of((TILE, 128))
        gv_ref[at, :] = jnp.where(lane < 64, value_sums[0], value_sums[1]).astype(BF16)
        gqk_ref[at, :] = jnp.where(
            (lane >= 32) & (lane < 48), key_sums[0], jnp.where((lane >= 48) & (lane < 64), key_sums[1], 0.0)
        )
    queries = jnp.concatenate([dqt_ref[...] * 0.5, jnp.zeros((96, length), F32)], axis=0)
    gqk_ref[...] += queries.T


def sending(source, target, send_sem, recv_sem, row_group, peer):
    return pltpu.make_async_remote_copy(
        src_ref=source,
        dst_ref=target,
        send_sem=send_sem,
        recv_sem=recv_sem,
        device_id=(row_group, peer),
        device_id_type=MESH,
    )


VMEM_SPEC = pl.BlockSpec(memory_space=pltpu.VMEM)
SMEM_SPEC = pl.BlockSpec(memory_space=pltpu.SMEM)


CHUNK = 256
STEP_ROWS = 48
Z_UNITS = 5
SLOTS = 7
VMEM_BYTES = 63 << 20


def place(me):
    core = lax.rem(me, 2)
    return core, 2 + 2 * core, 4 - 2 * core


def blocks_of(core, groups):
    first, second = 2 + 2 * core, 4 - 2 * core
    return [
        pl.multiple_of(32 * (8 * group + first * i + second * j + core), 32)
        for i in range(2)
        for j in range(2)
        for group in (0, 2, 1, 3)[:groups]
    ]


class Reduction:
    def __init__(self, source, buffers, slot_of=None, place_of=None):
        self.source = source
        self.got_a, self.got_b, self.got_z, self.a_sems, self.b_sems, self.c_sems, self.d_sems = buffers
        self.slot_of = slot_of or (lambda unit: unit)
        self.place_of = place_of or (lambda unit: unit)
        self.group, self.me = lax.axis_index("dp"), lax.axis_index("seq")
        core, first, second = place(self.me)
        self.bit_a, self.bit_b = lax.rem(self.me // first, 2), lax.rem(self.me // second, 2)
        self.peer_a = self.me + first * (1 - 2 * self.bit_a)
        self.peer_b = self.me + second * (1 - 2 * self.bit_b)
        self.bit_c, self.bit_d = lax.rem(self.group, 2), self.group // 2
        self.group_c = self.group + 1 - 2 * self.bit_c
        self.group_d = self.group + 2 - 4 * self.bit_d

    def rows(self, bit_c, bit_d=None):
        if bit_d is None:
            return pl.ds(pl.multiple_of(64 * bit_c, 64), 64)
        return pl.ds(pl.multiple_of(64 * bit_c + 32 * bit_d, 32), 32)

    def a_copy(self, unit):
        at = self.place_of(unit)
        return sending(
            self.source.at[self.slot_of(unit), 1 - self.bit_a], self.got_a.at[at], self.a_sems.at[0, at],
            self.a_sems.at[1, at], self.group, self.peer_a,
        )

    def b_copy(self, unit):
        at = self.place_of(unit)
        return sending(
            self.got_a.at[at, 1 - self.bit_b], self.got_b.at[at], self.b_sems.at[0, at], self.b_sems.at[1, at],
            self.group, self.peer_b,
        )

    def c_copy(self, unit):
        at = self.place_of(unit)
        return sending(
            self.got_b.at[at, self.rows(1 - self.bit_c), :], self.got_z.at[at, pl.ds(0, 64), :],
            self.c_sems.at[0, at], self.c_sems.at[1, at], self.group_c, self.me,
        )

    def d_copy(self, unit):
        at = self.place_of(unit)
        return sending(
            self.got_b.at[at, self.rows(self.bit_c, 1 - self.bit_d), :], self.got_z.at[at, pl.ds(64, 32), :],
            self.d_sems.at[0, at], self.d_sems.at[1, at], self.group_d, self.me,
        )

    def a_step(self, unit):
        at = self.place_of(unit)
        self.a_copy(unit).wait_recv()
        mine = self.source[self.slot_of(unit), self.bit_a].astype(F32)
        self.got_a[at] = (mine + self.got_a[at].astype(F32)).astype(BF16)
        self.b_copy(unit).start()

    def b_step(self, unit):
        at = self.place_of(unit)
        self.b_copy(unit).wait_recv()
        self.got_b[at] = (self.got_a[at, self.bit_b].astype(F32) + self.got_b[at].astype(F32)).astype(BF16)
        self.c_copy(unit).start()

    def c_step(self, unit):
        at, mine = self.place_of(unit), self.rows(self.bit_c)
        self.c_copy(unit).wait_recv()
        self.got_b[at, mine, :] = (
            self.got_b[at, mine, :].astype(F32) + self.got_z[at, :64, :].astype(F32)
        ).astype(BF16)
        self.d_copy(unit).start()

    def d_step(self, unit):
        at = self.place_of(unit)
        self.d_copy(unit).wait_recv()
        return self.got_b[at, self.rows(self.bit_c, self.bit_d), :].astype(F32) + self.got_z[at, 64:, :].astype(F32)

    def wait_sent(self, unit):
        self.b_copy(unit).wait_send()
        self.c_copy(unit).wait_send()
        self.d_copy(unit).wait_send()


class GroupsFirst(Reduction):
    def c_copy(self, unit):
        at = self.place_of(unit)
        return sending(
            self.source.at[self.slot_of(unit), :, :, self.rows(1 - self.bit_c), :],
            self.got_z.at[at, :, :, pl.ds(0, 64), :],
            self.c_sems.at[0, at], self.c_sems.at[1, at], self.group_c, self.me,
        )

    def d_copy(self, unit):
        at = self.place_of(unit)
        block = pl.ds(pl.multiple_of(32 * (1 - self.bit_d), 32), 32)
        return sending(
            self.got_z.at[at, :, :, block, :], self.got_z.at[at, :, :, pl.ds(64, 32), :],
            self.d_sems.at[0, at], self.d_sems.at[1, at], self.group_d, self.me,
        )

    def a_copy(self, unit):
        at = self.place_of(unit)
        return sending(
            self.got_z.at[at, 1 - self.bit_a, :, pl.ds(64, 32), :], self.got_a.at[at],
            self.a_sems.at[0, at], self.a_sems.at[1, at], self.group, self.peer_a,
        )

    def c_step(self, unit):
        at = self.place_of(unit)
        self.c_copy(unit).wait_recv()
        mine = self.source[self.slot_of(unit), :, :, self.rows(self.bit_c), :].astype(F32)
        self.got_z[at, :, :, :64, :] = (mine + self.got_z[at, :, :, :64, :].astype(F32)).astype(BF16)
        self.d_copy(unit).start()

    def d_step(self, unit):
        at = self.place_of(unit)
        self.d_copy(unit).wait_recv()
        mine = self.got_z[at, :, :, pl.ds(pl.multiple_of(32 * self.bit_d, 32), 32), :].astype(F32)
        self.got_z[at, :, :, 64:, :] = (mine + self.got_z[at, :, :, 64:, :].astype(F32)).astype(BF16)
        self.a_copy(unit).start()

    def a_step(self, unit):
        at = self.place_of(unit)
        self.a_copy(unit).wait_recv()
        mine = self.got_z[at, self.bit_a, :, 64:, :].astype(F32)
        self.got_a[at] = (mine + self.got_a[at].astype(F32)).astype(BF16)
        self.b_copy(unit).start()

    def b_step(self, unit):
        at = self.place_of(unit)
        self.b_copy(unit).wait_recv()
        return self.got_a[at, self.bit_b].astype(F32) + self.got_b[at].astype(F32)

    def wait_sent(self, unit):
        for copy in (self.a_copy, self.b_copy, self.c_copy, self.d_copy):
            copy(unit).wait_send()


def reduction_buffers(units, cols):
    sems = pltpu.SemaphoreType.DMA((2, units))
    return [
        pltpu.VMEM((units, 2, 128, cols), BF16),
        pltpu.VMEM((units, 128, cols), BF16),
        pltpu.VMEM((units, 96, cols), BF16),
        sems, sems, sems, sems,
    ]


def groups_first_buffers(units, cols):
    sems = pltpu.SemaphoreType.DMA((2, units))
    return [
        pltpu.VMEM((units, 2, 32, cols), BF16),
        pltpu.VMEM((units, 32, cols), BF16),
        pltpu.VMEM((units, 2, 2, 96, cols), BF16),
        sems, sems, sems, sems,
    ]


def store_blocks(target, unit, col, values, groups):
    rows = 32 * groups
    for i in range(2):
        for j in range(2):
            at = (2 * i + j) * rows
            target[unit, i, j, :, col : col + values.shape[1]] = values[at : at + rows].astype(BF16)


def turn(source, tokens, padded, turned):
    turned[...] = jnp.concatenate([source, jnp.zeros((padded - tokens, D), BF16)], axis=0).T


def split_rows(turned, mine_ref, theirs_ref, core, groups):
    for i, (mine, theirs) in enumerate(zip(blocks_of(core, groups), blocks_of(1 - core, groups))):
        a, b, group = i // (2 * groups), i // groups % 2, i % groups
        mine_ref[a, b, group * 32 : (group + 1) * 32, :] = turned[pl.ds(mine, 32), :]
        theirs_ref[a, b, group * 32 : (group + 1) * 32, :] = turned[pl.ds(theirs, 32), :]


def write_unit(total, at, w, gate_out, up_out, down_out):
    down_out[:, pl.ds(at, w)] = total[:, :w]
    gate_out[:, pl.ds(at, w)] = total[:, CHUNK : CHUNK + w]
    up_out[:, pl.ds(at, w)] = total[:, 2 * CHUNK : 2 * CHUNK + w]


def block_kernel(
    groups, seq_devices, rows, length, width,
    x_ref, cot_ref, gain_ref, wo_ref, wg_hbm, wu_hbm, wd_hbm, doc_ref, gain_attn_ref, wq_ref, wk_ref, wv_hbm,
    output_ref, input_out, gate_out, up_out, down_out, wout_out, query_out, key_out, value_out, gains_out,
    branch, residual, normed, out_acc, gnf, w_buf, lhs, right, parts, parts_o, q_source,
    got, heads, inverse, arrived, back, qa, ka, ve, dn, qs, kt, dqt, gqk, gv, gains, gains_got,
    fsend_a, frecv_a, fsend_b, frecv_b, w_sem, wv_sems, lhs_sems, pair_sems, send_a, recv_a, send_b, recv_b, gain_send, gain_recv,
    *buffers,
):
    row_group, me = lax.axis_index("dp"), lax.axis_index("seq")
    core, _, _ = place(me)
    partner = me + 1 - 2 * core
    tokens = rows * length
    padded = right.shape[1] // 2
    full = width // CHUNK
    tail = width - full * CHUNK
    low = packed_rows(length)
    lower = lanes_of((low, 128)) < 64
    here = pl.ds(pl.multiple_of(me * length, 16), length)
    half = H * F

    def slot_of(unit):
        if isinstance(unit, int):
            return unit if unit < SLOTS else 2 * (unit - SLOTS)
        return jnp.where(unit < SLOTS, unit, 2 * (unit - SLOTS))

    def place_of(unit):
        if isinstance(unit, int):
            return unit // 2 if unit < 2 * Z_UNITS else unit - Z_UNITS
        return jnp.where(unit < 2 * Z_UNITS, unit // 2, unit - Z_UNITS)

    feed = Reduction(parts, buffers[:7], slot_of, place_of)
    outer = Reduction(parts_o, buffers[7:14])
    qkv = Reduction(q_source, buffers[14:21])
    first = GroupsFirst(parts, buffers[21:28], slot_of, lambda unit: unit // 2)

    barrier = pltpu.get_barrier_semaphore()
    for step in range(1, seq_devices):
        peer = lax.rem(me + step, seq_devices)
        pl.semaphore_signal(barrier, inc=1, device_id=(row_group, peer), device_id_type=MESH)
    for other in (feed.group_c, feed.group_d):
        pl.semaphore_signal(barrier, inc=1, device_id=(other, me), device_id_type=MESH)

    def loads(chunk, slot, w):
        at = pl.ds(pl.multiple_of(chunk * CHUNK, CHUNK), w)
        return [
            pltpu.make_async_copy(hbm.at[at, :], w_buf.at[slot, which, pl.ds(0, w), :], w_sem.at[slot, which])
            for which, hbm in enumerate((wg_hbm, wu_hbm, wd_hbm))
        ]

    def value_load(part):
        return pltpu.make_async_copy(
            wv_hbm.at[pl.ds(part * CHUNK, CHUNK), :], w_buf.at[part // 3, part % 3], wv_sems.at[part]
        )

    def lhs_send(which):
        return (q_source.at[0], q_source.at[1], parts_o.at[0])[which % 3].at[:, :, :, pl.ds(0, padded)]

    def lhs_copy(which):
        return sending(
            lhs_send(which),
            lhs.at[which % 3, :, :, :, pl.ds(padded, padded)],
            lhs_sems.at[0, which], lhs_sems.at[1, which], row_group, partner,
        )

    def prepare_lhs(which, source):
        turned = right.at[3 if which < 2 else 1, :, pl.ds(0, padded)]
        turn(source, tokens, padded, turned)
        split_rows(turned, lhs.at[which % 3, :, :, :, pl.ds(0, padded)], lhs_send(which), core, groups)

    def left(which):
        return lhs[which].reshape(D // 2, 2 * padded)

    gap = padded - tokens

    def clear(slot, count):
        for base in (tokens, padded + tokens):
            right[slot : slot + count, base : base + gap, :] = jnp.zeros((count, gap, 3 * CHUNK), BF16)

    for part in range(D // CHUNK):
        value_load(part).start()
    spread = [right.at[1 + part, pl.ds(0, 2 * half), pl.ds(0, D // 2)] for part in range(2)]
    whole = spread_matrix()
    for part in range(2):
        spread[part][...] = whole[:, part * D // 2 : (part + 1) * D // 2]
    pl.semaphore_wait(barrier, seq_devices + 1)
    for part in range(D // CHUNK):
        value_load(part).wait()

    def spreading(row, step):
        peer = lax.rem(me + step, seq_devices)
        return sending(
            back.at[row, peer], got.at[row, me], fsend_a.at[row, step], frecv_a.at[row, step], row_group, peer
        )

    def merging(row, step):
        peer = lax.rem(me + step, seq_devices)
        there = pl.ds(pl.multiple_of(peer * length, 16), length)
        mine = pl.ds(pl.multiple_of(me * PAIR, 128), PAIR)
        at = pl.ds(pl.multiple_of(row * length, 16), length)
        return sending(
            heads.at[row, there, :], branch.at[at, mine], fsend_b.at[row, step], frecv_b.at[row, step],
            row_group, peer,
        )

    def project_row(row, carry):
        at = pl.ds(pl.multiple_of(row * length, 16), length)
        low_row = rms_scale(x_ref[at, :].astype(F32), gain_attn_ref[...]).astype(BF16)
        both = jnp.concatenate([nn(low_row, wq_ref[...]), nn(low_row, wk_ref[...])], axis=1).astype(BF16)
        sides = [nn(both, spread[part][...]) for part in range(2)]
        values = sum(
            nn(low_row[:, part * CHUNK : (part + 1) * CHUNK], w_buf[part // 3, part % 3])
            for part in range(D // CHUNK)
        ).astype(BF16)
        for pair in range(seq_devices):
            side, col = divmod(pair * 128, D // 2)
            tile = sides[side][:, col : col + 128]
            back[row, pair, :length, :] = values[:, pair * PAIR : (pair + 1) * PAIR]
            back[row, pair, length:, :] = jnp.where(lower, tile[:low], tile[length - low :]).astype(BF16)
        got[row, me] = back[row, me]

        @pl.when(row == 0)
        def _():
            send_spread(0)

        return carry

    def send_spread(row):
        for step in range(1, seq_devices):
            spreading(row, step).start()

    lax.fori_loop(0, rows, project_row, 0)
    send_spread(1)
    for chunk in range(2):
        for copy in loads(chunk, chunk, CHUNK):
            copy.start()
    prepare_lhs(0, cot_ref[...])
    lhs_copy(0).start()

    gnf[...] = jnp.zeros_like(gnf)
    clear(0, 3)

    def residual_row(row):
        for step in range(1, seq_devices):
            merging(row, step).wait_recv()
        at = pl.ds(pl.multiple_of(row * length, 16), length)
        value = x_ref[at, :].astype(F32) + nn(branch[at, :], wo_ref[...])
        residual[at, :] = value
        out_acc[at, :] = value
        normed[at, :] = rms_scale(value, gain_ref[...]).astype(BF16)

    def attend_rows(row, carry):
        for step in range(1, seq_devices):
            spreading(row, step).wait()

        @pl.when(row + 2 < rows)
        def _():
            send_spread(row + 2)

        prepare_row(got, row, qa, ka, ve, seq_devices, length)
        attend_forward(row_ends(doc_ref, row), qa, ka, ve, heads.at[row], inverse.at[row])
        for step in range(1, seq_devices):
            merging(row, step).start()
        at = pl.ds(pl.multiple_of(row * length, 16), length)
        branch[at, pl.ds(pl.multiple_of(me * PAIR, 128), PAIR)] = heads[row, here, :]
        return carry

    lax.fori_loop(0, rows, attend_rows, 0)

    for row in range(rows):
        residual_row(row)
    prepare_lhs(1, normed[...])
    lhs_copy(1).start()
    clear(3, 1)

    def right_copy(slot, cols, sem):
        return sending(
            right.at[slot, pl.ds(0, tokens), pl.ds(0, cols)], right.at[slot, pl.ds(padded, tokens), pl.ds(0, cols)],
            pair_sems.at[0, sem], pair_sems.at[1, sem], row_group, partner,
        )

    def pair_copy(chunk):
        return right_copy(lax.rem(chunk, 4), 3 * CHUNK, chunk)

    def forward_part(chunk, wg, wu, wd, w):
        slot = lax.rem(chunk, 4)
        gate = nt(normed[...], wg)
        up = nt(normed[...], wu)
        sigmoid = 1.0 / (1.0 + jnp.exp(-gate))
        silu = gate * sigmoid
        hidden = (silu * up).astype(BF16)
        grad_hidden = nt(cot_ref[...], wd)
        grad_gate = (grad_hidden * up * (sigmoid * (1.0 + gate * (1.0 - sigmoid)))).astype(BF16)
        grad_up = (grad_hidden * silu).astype(BF16)
        for part, values in enumerate((hidden, grad_gate, grad_up)):
            right[slot, :tokens, part * CHUNK : part * CHUNK + w] = values
            if w < CHUNK:
                right[slot, :tokens, part * CHUNK + w : (part + 1) * CHUNK] = jnp.zeros((tokens, CHUNK - w), BF16)
        pair_copy(chunk).start()
        out_acc[...] += nn(hidden, wd)
        gnf[...] += nn(grad_gate, wg) + nn(grad_up, wu)

    def grad_part(chunk):
        pair_copy(chunk).wait()
        slot = lax.rem(chunk, 4)
        store_blocks(parts, slot_of(chunk), 0, nn(left(0), right[slot, :, 0:CHUNK]), groups)
        store_blocks(parts, slot_of(chunk), CHUNK, nn(left(1), right[slot, :, CHUNK:]), groups)

    def forward_step(chunk):
        slot = lax.rem(chunk, 2)
        for copy in loads(chunk, slot, CHUNK):
            copy.wait()
        forward_part(chunk, w_buf[slot, 0], w_buf[slot, 1], w_buf[slot, 2], CHUNK)

    def ticks(chunk):
        @pl.when((chunk >= 4) & (lax.rem(chunk, 2) == 0))
        def _():
            feed.a_step(chunk - 4)

        @pl.when((chunk >= 7) & (lax.rem(chunk, 2) == 1))
        def _():
            feed.b_step(chunk - 7)

        @pl.when(chunk == 8)
        def _():
            first.c_step(1)

    def fetch_next(chunk):
        @pl.when(chunk < full - 1)
        def _():
            for copy in loads(chunk + 1, lax.rem(chunk + 1, 2), CHUNK):
                copy.start()

        @pl.when(chunk == full - 1)
        def _():
            for copy in loads(full, full % 2, tail):
                copy.start()

    def main(chunk, carry):
        fetch_next(chunk)
        forward_step(chunk)
        unit = chunk - 1

        @pl.when(unit >= SLOTS)
        def _():
            feed.a_copy(2 * (unit - SLOTS)).wait_send()

        grad_part(unit)
        along_z = (unit < 2 * Z_UNITS) & (lax.rem(unit, 2) == 1)

        @pl.when(along_z)
        def _():
            first.c_copy(unit).start()

        @pl.when(jnp.logical_not(along_z) & (unit < 10))
        def _():
            feed.a_copy(unit).start()

        ticks(chunk)
        return carry

    forward_step(0)
    for which in range(2):
        lhs_copy(which).wait()
    lax.fori_loop(1, full, main, 0)
    slot = full % 2
    for copy in loads(full, slot, tail):
        copy.wait()
    forward_part(full, w_buf[slot, 0, :tail], w_buf[slot, 1, :tail], w_buf[slot, 2, :tail], tail)
    for part in range(D // CHUNK):
        value_load(part).start()
    feed.a_copy(2 * (full - 1 - SLOTS)).wait_send()
    grad_part(full - 1)
    first.c_copy(full - 1).start()

    gains[...] = jnp.zeros_like(gains)

    def norm_backward_ffn(step, carry):
        at = pl.ds(pl.multiple_of(step * STEP_ROWS, 16), STEP_ROWS)
        value, grad = residual[at, :], gnf[at, :]
        scale = lax.rsqrt(jnp.mean(value * value, axis=-1, keepdims=True) + eps_norm)
        gains[0:1, :] += jnp.sum(grad * value * scale, axis=0, keepdims=True)
        weighted = grad * gain_ref[...]
        mean = jnp.mean(weighted * value, axis=-1, keepdims=True)
        total = cot_ref[at, :].astype(F32) + scale * weighted - value * (scale * scale * scale * mean)
        gnf[at, :] = total
        right[3, at, :] = total[:, : 3 * CHUNK].astype(BF16)
        right[0, at, :CHUNK] = total[:, 3 * CHUNK :].astype(BF16)
        output_ref[at, :] = out_acc[at, :].astype(BF16)
        return carry

    lax.fori_loop(0, tokens // STEP_ROWS, norm_backward_ffn, 0)
    normed[...] = (
        nt(right[3, :tokens, :], wo_ref[:, : 3 * CHUNK]) + nt(right[0, :tokens, :CHUNK], wo_ref[:, 3 * CHUNK :])
    ).astype(BF16)

    def outgoing(row, step):
        peer = lax.rem(me + step, seq_devices)
        theirs = pl.ds(pl.multiple_of(peer * PAIR, 128), PAIR)
        at = pl.ds(pl.multiple_of(row * length, 16), length)
        return sending(
            normed.at[at, theirs], arrived.at[row, here, :], send_a.at[row, step], recv_a.at[row, step],
            row_group, peer,
        )

    def returning(row, step):
        peer = lax.rem(me + step, seq_devices)
        return sending(
            got.at[row, peer], back.at[row, me], send_b.at[row, step], recv_b.at[row, step], row_group, peer
        )

    def send_row(row, carry):
        for step in range(1, seq_devices):
            outgoing(row, step).start()
        at = pl.ds(pl.multiple_of(row * length, 16), length)
        arrived[row, here, :] = normed[at, pl.ds(pl.multiple_of(me * PAIR, 128), PAIR)]
        return carry

    send_row(0, 0)
    feed.a_step(6)
    feed.a_copy(2 * (full - SLOTS)).wait_send()
    grad_part(full)
    send_row(1, 0)
    out_pairs = [right_copy(3, 3 * CHUNK, full + 1), right_copy(0, CHUNK, full + 2)]
    for copy in out_pairs:
        copy.start()
    prepare_lhs(2, branch[...])
    lhs_copy(2).start()
    feed.b_step(4)
    first.c_step(3)
    feed.c_step(0)
    for row in range(2, rows):
        send_row(row, 0)
    prepare_lhs(3, rms_scale(x_ref[...].astype(F32), gain_attn_ref[...]).astype(BF16))
    clear(1, 1)
    for copy in out_pairs:
        copy.wait()
    lhs_copy(3).start()
    lhs_copy(2).wait()
    for col in range(0, D, CHUNK):
        columns = right[3, :, col : col + CHUNK] if col < 3 * CHUNK else right[0, :, :CHUNK]
        store_blocks(parts_o, 0, col, nn(left(2), columns), groups)
    gather = right.at[3, pl.ds(0, 2 * half), pl.ds(0, 2 * half)]
    gather[...] = gather_matrix()

    def attend(row, carry):
        prepare_row(got, row, qa, ka, ve, seq_devices, length)
        for step in range(1, seq_devices):
            outgoing(row, step).wait_recv()
        attend_backward(
            row_ends(doc_ref, row), arrived.at[row], qa, ka, ve, heads.at[row], inverse.at[row],
            dn, qs, kt, dqt, gqk, gv,
        )

        def pack(peer, inner):
            at = pl.multiple_of(peer * length, 16)
            got[row, peer, :length, :] = gv[pl.ds(at, length), :]
            front = gqk[pl.ds(at, low), :]
            rear = pltpu.roll(gqk[pl.ds(at + length - low, low), :], 64, 1)
            got[row, peer, length:, :] = jnp.where(lower, front, rear).astype(BF16)
            return inner

        lax.fori_loop(0, seq_devices, pack, 0)
        for step in range(1, seq_devices):
            returning(row, step).start()
        back[row, me] = got[row, me]

        @pl.when(row == 0)
        def _():
            feed.a_copy(10).start()
            feed.a_step(8)
            first.c_step(5)

        @pl.when(row == 1)
        def _():
            outer.a_copy(0).start()
            feed.b_step(6)
            feed.c_step(2)
            first.c_step(7)
            first.d_step(1)

        @pl.when(row == 2)
        def _():
            first.d_step(3)
            feed.b_step(8)

        return carry

    lax.fori_loop(0, rows, attend, 0)
    feed.c_step(4)
    first.c_step(9)
    first.d_step(5)
    feed.a_step(10)

    def unpack(row, carry):
        for step in range(1, seq_devices):
            outgoing(row, step).wait_send()
            returning(row, step).wait()
        tiles = []
        for pair in range(0, seq_devices, 2):
            halves = []
            for one in (pair, pair + 1):
                packed = back[row, one, length:, :].astype(F32)
                turned_over = pltpu.roll(packed, 64, 1)
                straight, other = (packed, turned_over) if one == pair else (turned_over, packed)
                halves.append(jnp.concatenate([straight, other[2 * low - length :]], axis=0))
            tiles.append(jnp.where(lanes_of((length, 128)) < 64, halves[0], halves[1]).astype(BF16))
        at = pl.ds(pl.multiple_of(row * length, 16), length)
        right[1, at, : 2 * half] = nn(jnp.concatenate(tiles, axis=1), gather[...]).astype(BF16)
        for pair in range(seq_devices):
            slot, col = divmod(2 * half + pair * PAIR, 3 * CHUNK)
            right[1 + slot, at, col : col + PAIR] = back[row, pair, :length, :]
        return carry

    lax.fori_loop(0, rows, unpack, 0)
    q_pairs = [right_copy(1, 3 * CHUNK, full + 3), right_copy(2, 3 * CHUNK, full + 4)]
    for copy in q_pairs:
        copy.start()
    for part in range(D // CHUNK):
        value_load(part).wait()
    q_and_k = nt(right[1, :tokens, :half], wq_ref[...]) + nt(right[1, :tokens, half : 2 * half], wk_ref[...])
    for part in range(D // CHUNK):
        at = slice(part * CHUNK, (part + 1) * CHUNK)
        block = w_buf[part // 3, part % 3]
        out_acc[:, at] = (
            q_and_k[:, at]
            + nt(right[1, :tokens, 2 * half :], block[:, : 3 * CHUNK - 2 * half])
            + nt(right[2, :tokens, :], block[:, 3 * CHUNK - 2 * half :])
        )
    lhs_copy(3).wait()
    for copy in q_pairs:
        copy.wait()
    for unit in range(2):
        for col in range(0, 3 * CHUNK, CHUNK):
            store_blocks(q_source, unit, col, nn(left(0), right[1 + unit, :, col : col + CHUNK]), groups)
        qkv.a_copy(unit).start()

    def norm_backward(step, carry):
        at = pl.ds(pl.multiple_of(step * STEP_ROWS, 16), STEP_ROWS)
        value, grad = x_ref[at, :].astype(F32), out_acc[at, :]
        scale = lax.rsqrt(jnp.mean(value * value, axis=-1, keepdims=True) + eps_norm)
        gains[1:2, :] += jnp.sum(grad * value * scale, axis=0, keepdims=True)
        weighted = grad * gain_attn_ref[...]
        mean = jnp.mean(weighted * value, axis=-1, keepdims=True)
        total = gnf[at, :] + scale * weighted - value * (scale * scale * scale * mean)
        input_out[at, :] = total.astype(BF16)
        return carry

    lax.fori_loop(0, tokens // STEP_ROWS, norm_backward, 0)

    def gain_copy(step, target_group, target):
        return sending(
            gains, gains_got.at[step], gain_send.at[step], gain_recv.at[step], target_group, target
        )

    gain_copies = [
        gain_copy(0, row_group, partner),
        gain_copy(1, row_group, feed.peer_a),
        gain_copy(2, row_group, feed.peer_b),
        gain_copy(3, feed.group_c, me),
        gain_copy(4, feed.group_d, me),
    ]

    def gain_step(step):
        gain_copies[step].wait()
        gains[...] += gains_got[step]
        if step < 4:
            gain_copies[step + 1].start()

    def write_feed(unit, total, w):
        at = unit * CHUNK if isinstance(unit, int) else pl.multiple_of(unit * CHUNK, CHUNK)
        write_unit(total, at, w, gate_out, up_out, down_out)

    gain_copies[0].start()
    outer.a_step(0)
    feed.b_step(10)
    gain_step(0)
    first.d_step(7)
    feed.c_step(6)
    first.a_step(1)
    feed.c_step(8)
    gain_step(1)
    qkv.a_step(0)
    first.a_step(3)
    qkv.a_step(1)
    outer.b_step(0)
    gain_step(2)
    qkv.b_step(0)
    feed.c_step(10)
    first.a_step(5)
    qkv.b_step(1)
    gain_step(3)
    qkv.c_step(0)
    first.d_step(9)
    outer.c_step(0)
    qkv.c_step(1)
    first.a_step(7)
    gain_step(4)
    first.a_step(9)
    for unit in range(full):
        if unit >= 2 * Z_UNITS or unit % 2 == 0:
            write_feed(unit, feed.d_step(unit), CHUNK)
    write_feed(full, feed.d_step(full), tail)
    for unit in range(1, 2 * Z_UNITS, 2):
        write_feed(unit, first.b_step(unit), CHUNK)
    picked = lax.broadcasted_iota(jnp.int32, (D, 128), 0) == 32 * (seq_devices * row_group + me) + lanes_of((D, 128))
    gains_out[...] = jnp.dot(
        gains[...], jnp.where(picked, 1.0, 0.0), precision=lax.Precision.HIGHEST, preferred_element_type=F32
    )
    wout_out[...] = outer.d_step(0)
    total = qkv.d_step(0)
    query_out[...] = total[:, :half]
    key_out[...] = total[:, half : 2 * half]
    value_out[:, : 3 * CHUNK - 2 * half] = total[:, 2 * half :]
    value_out[:, 3 * CHUNK - 2 * half :] = qkv.d_step(1)

    for unit in range(full + 1):
        if unit < 2 * Z_UNITS and unit % 2 == 1:
            first.wait_sent(unit)
        else:
            feed.wait_sent(unit)
            if unit > 2 * (full - SLOTS):
                feed.a_copy(unit).wait_send()
    def forward_sent(row, carry):
        for step in range(1, seq_devices):
            merging(row, step).wait_send()
        return carry

    lax.fori_loop(0, rows, forward_sent, 0)
    for one, unit in ((outer, 0), (qkv, 0), (qkv, 1)):
        one.wait_sent(unit)
        one.a_copy(unit).wait_send()


ANY_SPEC = pl.BlockSpec(memory_space=pl.ANY)


def block_step(
    groups, seq_devices, x, cotangent, gain_ffn, w_out, w_gate_t, w_up_t, w_down, doc_lengths, gain_attn,
    w_query, w_key, w_value,
):
    tokens = x.shape[0]
    rows = doc_lengths.shape[0]
    length = tokens // rows
    total = seq_devices * length
    width = w_down.shape[0]
    full = width // CHUNK
    padded = (tokens + 127) // 128 * 128
    unit_rows = 32 * groups
    message = (rows, seq_devices, length + packed_rows(length), 128)
    dma = pltpu.SemaphoreType.DMA
    sems = dma((rows, seq_devices))
    return pl.pallas_call(
        functools.partial(block_kernel, groups, seq_devices, rows, length, width),
        name="block",
        out_shape=[
            jax.ShapeDtypeStruct((tokens, D), BF16),
            jax.ShapeDtypeStruct((tokens, D), BF16),
            jax.ShapeDtypeStruct((32, width), F32),
            jax.ShapeDtypeStruct((32, width), F32),
            jax.ShapeDtypeStruct((32, width), F32),
            jax.ShapeDtypeStruct((32, D), F32),
            jax.ShapeDtypeStruct((32, H * F), F32),
            jax.ShapeDtypeStruct((32, H * F), F32),
            jax.ShapeDtypeStruct((32, D), F32),
            jax.ShapeDtypeStruct((8, 128), F32),
        ],
        in_specs=[VMEM_SPEC] * 4 + [ANY_SPEC] * 3 + [SMEM_SPEC] + [VMEM_SPEC] * 3 + [ANY_SPEC],
        out_specs=[VMEM_SPEC] * 10,
        scratch_shapes=[
            pltpu.VMEM((tokens, D), BF16),
            pltpu.VMEM((tokens, D), F32),
            pltpu.VMEM((tokens, D), BF16),
            pltpu.VMEM((tokens, D), F32),
            pltpu.VMEM((tokens, D), F32),
            pltpu.VMEM((2, 3, CHUNK, D), BF16),
            pltpu.VMEM((3, 2, 2, unit_rows, 2 * padded), BF16),
            pltpu.VMEM((4, 2 * padded, 3 * CHUNK), BF16),
            pltpu.VMEM((SLOTS, 2, 2, unit_rows, 3 * CHUNK), BF16),
            pltpu.VMEM((1, 2, 2, unit_rows, D), BF16),
            pltpu.VMEM((2, 2, 2, unit_rows, 3 * CHUNK), BF16),
            pltpu.VMEM(message, BF16),
            pltpu.VMEM((rows, total, 128), BF16),
            pltpu.VMEM((rows, total, 128), F32),
            pltpu.VMEM((rows, total, 128), BF16),
            pltpu.VMEM(message, BF16),
            pltpu.VMEM((total, 128), BF16),
            pltpu.VMEM((2, total, 128), BF16),
            pltpu.VMEM((2, total, 128), BF16),
            pltpu.VMEM((2, total, 128), BF16),
            pltpu.VMEM((total, 128), BF16),
            pltpu.VMEM((2, 32, total), BF16),
            pltpu.VMEM((32, total), F32),
            pltpu.VMEM((total, 128), F32),
            pltpu.VMEM((total, 128), BF16),
            pltpu.VMEM((8, D), F32),
            pltpu.VMEM((5, 8, D), F32),
            sems, sems, sems, sems, dma((2, 3)), dma((D // CHUNK,)), dma((2, 4)), dma((2, full + 5)),
            sems, sems, sems, sems, dma((5,)), dma((5,)),
        ]
        + reduction_buffers(full + 1 - Z_UNITS, 3 * CHUNK)
        + reduction_buffers(1, D)
        + reduction_buffers(2, 3 * CHUNK)
        + groups_first_buffers(Z_UNITS, 3 * CHUNK),
        compiler_params=pltpu.CompilerParams(collective_id=1, has_side_effects=True, vmem_limit_bytes=VMEM_BYTES),
    )(
        x, cotangent, gain_ffn.reshape(1, D), w_out, w_gate_t, w_up_t, w_down, doc_lengths,
        gain_attn.reshape(1, D), w_query, w_key, w_value,
    )


def publish(results, gains):
    def kernel(*refs):
        count = len(results)
        for source, target in zip(refs[:count], refs[count + 1 : 2 * count + 1]):
            target[...] = source[...]
        refs[2 * count + 1][...] = refs[count][1:2, :32]
        refs[2 * count + 2][...] = refs[count][0:1, :32]

    one = jax.ShapeDtypeStruct((1, 32), F32)
    return pl.pallas_call(
        kernel,
        name="publish",
        out_shape=[jax.ShapeDtypeStruct(x.shape, x.dtype) for x in results] + [one, one],
        in_specs=[VMEM_SPEC] * (len(results) + 1),
        out_specs=[VMEM_SPEC] * (len(results) + 2),
        compiler_params=pltpu.CompilerParams(vmem_limit_bytes=VMEM_BYTES),
    )(*results, gains)


def tuned_body(
    seq_devices, groups, inputs, doc_lengths, gain_attn, w_query, w_key, w_value, w_out, gain_ffn, w_gate, w_up,
    w_down, cotangent,
):
    row_count, shard_len, _ = inputs.shape
    token_count = row_count * shard_len
    output, input_grad, gate, up, down, out, query, key, value, gains = block_step(
        groups, seq_devices, inputs.reshape(token_count, D), cotangent.reshape(token_count, D), gain_ffn, w_out,
        w_gate.T, w_up.T, w_down, doc_lengths, gain_attn, w_query, w_key, w_value,
    )
    output, input_grad, gate, up, down, out, query, key, value, gain_attn_part, gain_ffn_part = publish(
        (output, input_grad, gate, up, down, out, query, key, value), gains
    )
    return (
        output.reshape(row_count, shard_len, D),
        input_grad.reshape(row_count, shard_len, D),
        gain_attn_part.reshape(32),
        query,
        key,
        value,
        out,
        gain_ffn_part.reshape(32),
        gate,
        up,
        down.T,
    )


def solution(mesh):
    in_specs = (
        P("dp", "seq", None),
        P("dp", None),
        P(),
        P(),
        P(),
        P(),
        P(),
        P(),
        P(),
        P(),
        P(),
        P("dp", "seq", None),
    )
    out_specs = (
        P("dp", "seq", None),
        P("dp", "seq", None),
        P(("dp", "seq")),
        P(("dp", "seq"), None),
        P(("dp", "seq"), None),
        P(("dp", "seq"), None),
        P(("dp", "seq"), None),
        P(("dp", "seq")),
        P(("dp", "seq"), None),
        P(("dp", "seq"), None),
        P(None, ("dp", "seq")),
    )
    seq_devices, groups = mesh.shape["seq"], mesh.shape["dp"]
    tuned = seq_devices == 8 and seq_devices * groups * 32 == D
    step = functools.partial(tuned_body, seq_devices, groups) if tuned else general_body
    return jax.shard_map(step, mesh=mesh, in_specs=in_specs, out_specs=out_specs, check_vma=False)
```

```python
import functools

import jax
import jax.numpy as jnp
from jax import lax
from jax.experimental import pallas as pl
from jax.experimental.pallas import tpu as pltpu
from jax.sharding import PartitionSpec as P

D = 1024
H = 16
F = 16
HV = 64
BLOCK = 576


eps_norm = 1e-05


def rms_scale(stream, gain_vec):
    return (
        stream * lax.rsqrt(jnp.mean(stream * stream, axis=-1, keepdims=True) + eps_norm) * gain_vec
    )


def taylor_features(vectors):
    feat_width = vectors.shape[-1]
    outer_prod = (vectors[..., :, None] * vectors[..., None, :]).reshape(
        vectors.shape[:-1] + (feat_width * feat_width,)
    )
    ones_part = jnp.ones(vectors.shape[:-1] + (1,), jnp.float32)
    return jnp.concatenate(
        [ones_part, vectors * feat_width ** (-0.25), outer_prod * (0.5 / feat_width) ** 0.5],
        axis=-1,
    )


def document_ids(doc_lens, seq_length):
    doc_ends = jnp.cumsum(doc_lens, dtype=jnp.int32)
    positions = jnp.arange(seq_length, dtype=jnp.int32)
    return jnp.sum(
        (positions[:, None] >= doc_ends[None, :]).astype(jnp.int32), axis=1, dtype=jnp.int32
    )


def attend_row(queries, key_proj, value_proj, doc_row, block_rows):
    seq_length, head_count, feat_width = queries.shape
    value_width = value_proj.shape[-1]
    feat_count = 1 + feat_width + feat_width * feat_width
    block_count = seq_length // block_rows
    highest = lax.Precision.HIGHEST
    query_blocks = queries.reshape(block_count, block_rows, head_count, feat_width)
    key_blocks = key_proj.reshape(block_count, block_rows, head_count, feat_width)
    value_blocks = value_proj.reshape(block_count, block_rows, head_count, value_width)
    doc_blocks = doc_row.reshape(block_count, block_rows)
    previous = jnp.concatenate([jnp.full((1,), -1, jnp.int32), doc_blocks[:-1, -1]])
    positions = jnp.arange(block_rows, dtype=jnp.int32)
    causal = positions[:, None] >= positions[None, :]

    def block_step(carried, pieces):
        state_sum, norm_sum = carried
        query_block, key_block, value_block, doc_block, prior_doc = pieces
        scores = jnp.einsum(
            "thf,shf->hts", query_block, key_block, precision=highest
        ) * feat_width ** (-0.5)
        weights = 1.0 + scores + 0.5 * scores * scores
        same_doc = causal & (doc_block[:, None] == doc_block[None, :])
        weights = jnp.where(same_doc[None, :, :], weights, 0.0)
        numerator = jnp.einsum("hts,shv->thv", weights, value_block, precision=highest)
        denominator = jnp.transpose(jnp.sum(weights, axis=2))
        use_state = (doc_block == prior_doc).astype(jnp.float32)[:, None]
        query_feats = taylor_features(query_block)
        numerator = numerator + use_state[:, :, None] * jnp.einsum(
            "thp,hpv->thv", query_feats, state_sum, precision=highest
        )
        denominator = denominator + use_state * jnp.einsum(
            "thp,hp->th", query_feats, norm_sum, precision=highest
        )
        last_doc = doc_block[-1]
        keep_state = (last_doc == prior_doc).astype(jnp.float32)
        key_feats = (
            taylor_features(key_block) * (doc_block == last_doc).astype(jnp.float32)[:, None, None]
        )
        state_sum = keep_state * state_sum + jnp.einsum(
            "shp,shv->hpv", key_feats, value_block, precision=highest
        )
        norm_sum = keep_state * norm_sum + jnp.sum(key_feats, axis=0)
        return ((state_sum, norm_sum), numerator / denominator[:, :, None])

    initial = (
        jnp.zeros((head_count, feat_count, value_width), jnp.float32),
        jnp.zeros((head_count, feat_count), jnp.float32),
    )
    _, results = lax.scan(
        jax.checkpoint(block_step),
        initial,
        (query_blocks, key_blocks, value_blocks, doc_blocks, previous),
    )
    return results.reshape(seq_length, head_count, value_width)


def project(left, right):
    return jnp.dot(left, right, preferred_element_type=jnp.float32)


def back_project(left, right):
    return lax.dot_general(
        left, right, (((1,), (1,)), ((), ())), preferred_element_type=jnp.float32
    )


def weight_grad(left, right):
    return lax.dot_general(
        left, right, (((0,), (0,)), ((), ())), preferred_element_type=jnp.float32
    )


def swiglu(gate_proj, up_proj):
    return jax.nn.silu(gate_proj) * up_proj


def general_body(
    inputs,
    doc_lengths,
    gain_attn,
    w_query,
    w_key,
    w_value,
    w_out,
    gain_ffn,
    w_gate,
    w_up,
    w_down,
    cotangent,
):
    row_count, shard_len, _ = inputs.shape
    token_count = row_count * shard_len
    stream = inputs.reshape(token_count, D).astype(jnp.float32)
    normed, attn_norm_back = jax.vjp(rms_scale, stream, gain_attn)
    normed_low = normed.astype(jnp.bfloat16)
    query_proj = project(normed_low, w_query).astype(jnp.bfloat16)
    key_proj = project(normed_low, w_key).astype(jnp.bfloat16)
    value_proj = project(normed_low, w_value).astype(jnp.bfloat16)
    query_heads, key_heads, value_heads = (
        lax.all_to_all(
            query_proj.reshape(row_count, shard_len, H, F),
            "seq",
            split_axis=2,
            concat_axis=1,
            tiled=True,
        ),
        lax.all_to_all(
            key_proj.reshape(row_count, shard_len, H, F),
            "seq",
            split_axis=2,
            concat_axis=1,
            tiled=True,
        ),
        lax.all_to_all(
            value_proj.reshape(row_count, shard_len, H, HV),
            "seq",
            split_axis=2,
            concat_axis=1,
            tiled=True,
        ),
    )
    seq_length = query_heads.shape[1]
    doc_rows = jax.vmap(lambda doc_lens: document_ids(doc_lens, seq_length))(doc_lengths)

    def attend_all(queries, keys_in, values_in):
        return jax.vmap(attend_row, in_axes=(0, 0, 0, 0, None))(
            queries, keys_in, values_in, doc_rows, BLOCK
        )

    mixed_heads, attend_back = jax.vjp(
        attend_all,
        query_heads.astype(jnp.float32),
        key_heads.astype(jnp.float32),
        value_heads.astype(jnp.float32),
    )
    mixed_rows = lax.all_to_all(
        mixed_heads.astype(jnp.bfloat16), "seq", split_axis=1, concat_axis=2, tiled=True
    )
    mixed_flat = mixed_rows.reshape(token_count, D)
    residual = stream + project(mixed_flat, w_out)
    normed_ffn, ffn_norm_back = jax.vjp(rms_scale, residual, gain_ffn)
    ffn_low = normed_ffn.astype(jnp.bfloat16)
    gate_proj = project(ffn_low, w_gate)
    up_proj = project(ffn_low, w_up)
    hidden, act_back = jax.vjp(swiglu, gate_proj, up_proj)
    hidden_low = hidden.astype(jnp.bfloat16)
    output = residual + project(hidden_low, w_down)
    grad_out = cotangent.reshape(token_count, D)
    grad_gate, grad_up = act_back(back_project(grad_out, w_down))
    grad_gate_low = grad_gate.astype(jnp.bfloat16)
    grad_up_low = grad_up.astype(jnp.bfloat16)
    down_grad_t = weight_grad(grad_out, hidden_low)
    gate_grad = weight_grad(ffn_low, grad_gate_low)
    up_grad = weight_grad(ffn_low, grad_up_low)
    grad_normed_ffn = back_project(grad_gate_low, w_gate) + back_project(grad_up_low, w_up)
    grad_residual, gain_ffn_grad = ffn_norm_back(grad_normed_ffn)
    grad_residual = grad_residual + grad_out.astype(jnp.float32)
    grad_branch = grad_residual.astype(jnp.bfloat16)
    out_grad = weight_grad(mixed_flat, grad_branch)
    grad_mixed = (
        back_project(grad_branch, w_out).astype(jnp.bfloat16).reshape(row_count, shard_len, H, HV)
    )
    grad_heads = lax.all_to_all(grad_mixed, "seq", split_axis=2, concat_axis=1, tiled=True)
    grad_query, grad_key, grad_value = attend_back(grad_heads.astype(jnp.float32))
    back_query, back_key, back_value = (
        lax.all_to_all(
            grad_query.astype(jnp.bfloat16), "seq", split_axis=1, concat_axis=2, tiled=True
        ),
        lax.all_to_all(
            grad_key.astype(jnp.bfloat16), "seq", split_axis=1, concat_axis=2, tiled=True
        ),
        lax.all_to_all(
            grad_value.astype(jnp.bfloat16), "seq", split_axis=1, concat_axis=2, tiled=True
        ),
    )
    back_query = back_query.reshape(token_count, H * F)
    back_key = back_key.reshape(token_count, H * F)
    back_value = back_value.reshape(token_count, D)
    query_grad = weight_grad(normed_low, back_query)
    key_grad = weight_grad(normed_low, back_key)
    value_grad = weight_grad(normed_low, back_value)
    grad_normed = (
        back_project(back_query, w_query)
        + back_project(back_key, w_key)
        + back_project(back_value, w_value)
    )
    grad_stream, gain_attn_grad = attn_norm_back(grad_normed)
    input_grad = grad_residual + grad_stream
    (
        gain_attn_part,
        query_part,
        key_part,
        value_part,
        out_part,
        gain_ffn_part,
        gate_part,
        up_part,
        down_part,
    ) = (
        lax.psum_scatter(gain_attn_grad, ("dp", "seq"), scatter_dimension=0, tiled=True),
        lax.psum_scatter(query_grad, ("dp", "seq"), scatter_dimension=0, tiled=True),
        lax.psum_scatter(key_grad, ("dp", "seq"), scatter_dimension=0, tiled=True),
        lax.psum_scatter(value_grad, ("dp", "seq"), scatter_dimension=0, tiled=True),
        lax.psum_scatter(out_grad, ("dp", "seq"), scatter_dimension=0, tiled=True),
        lax.psum_scatter(gain_ffn_grad, ("dp", "seq"), scatter_dimension=0, tiled=True),
        lax.psum_scatter(gate_grad, ("dp", "seq"), scatter_dimension=0, tiled=True),
        lax.psum_scatter(up_grad, ("dp", "seq"), scatter_dimension=0, tiled=True),
        lax.psum_scatter(down_grad_t, ("dp", "seq"), scatter_dimension=0, tiled=True),
    )
    return (
        output.reshape(row_count, shard_len, D).astype(jnp.bfloat16),
        input_grad.reshape(row_count, shard_len, D).astype(jnp.bfloat16),
        gain_attn_part,
        query_part,
        key_part,
        value_part,
        out_part,
        gain_ffn_part,
        gate_part,
        up_part,
        jnp.transpose(down_part),
    )


F32 = jnp.float32
BF16 = jnp.bfloat16
MESH = pl.DeviceIdType.MESH
TILE = 384
PAIR = 2 * HV


def nt(left, right):
    return lax.dot_general(left, right, (((1,), (1,)), ((), ())), preferred_element_type=F32)


def nn(left, right):
    return jnp.dot(left, right, preferred_element_type=F32)


def lanes_of(shape):
    return lax.broadcasted_iota(jnp.int32, shape, len(shape) - 1)


def first_visible(ends, positions):
    start = jnp.zeros_like(positions)
    for end in ends:
        start = jnp.where(positions >= end, end, start)
    return start


def row_ends(doc_ref, row):
    ends, total = [], 0
    for j in range(doc_ref.shape[1] - 1):
        total = total + doc_ref[row, j]
        ends.append(total)
    return ends


def spread_matrix():
    half = H * F
    source = lax.broadcasted_iota(jnp.int32, (2 * half, 1), 0)
    column = lax.broadcasted_iota(jnp.int32, (1, (H // 2) * 128), 1)
    pair, lane = column // 128, column % 64
    wanted = pair * 32 + lane + jnp.where(lane < 32, 0, half - 32)
    return jnp.where(source == wanted, 1.0, 0.0).astype(BF16)


def gather_matrix():
    half = H * F
    source = lax.broadcasted_iota(jnp.int32, (2 * half, 1), 0)
    column = lax.broadcasted_iota(jnp.int32, (1, 2 * half), 1)
    pair, lane = source // 64, source % 64
    wanted = pair * 32 + lane + jnp.where(lane < 32, 0, half - 32)
    return jnp.where(column == wanted, 1.0, 0.0).astype(BF16)


def packed_rows(length):
    return (length // 2 + 15) // 16 * 16


def prepare_row(got_ref, row, qa_ref, ka_ref, ve_ref, seq_devices, length):
    low = packed_rows(length)

    def part(peer, carry):
        values = got_ref[row, peer, :length, :].astype(F32)
        packed = got_ref[row, peer, length : length + low, :].astype(F32)
        turned = pltpu.roll(packed, 64, 1)
        both = jnp.concatenate([packed, turned[2 * low - length :]], axis=0)
        lane = lanes_of((length, 128))
        keys = pltpu.roll(both, 96, 1)
        at = pl.ds(pl.multiple_of(peer * length, 16), length)
        one = jnp.where(lane == 32, 1.0, 0.0)
        qa_ref[at, :] = jnp.where(lane < 32, both * 0.25, one).astype(BF16)
        ka_ref[0, at, :] = jnp.where(lane < 16, keys, one).astype(BF16)
        ka_ref[1, at, :] = jnp.where((lane >= 16) & (lane < 32), keys, one).astype(BF16)
        ve_ref[0, at, :] = jnp.where(lane < 64, values, 1.0).astype(BF16)
        ve_ref[1, at, :] = jnp.where(lane >= 64, values, 1.0).astype(BF16)
        return carry

    lax.fori_loop(0, seq_devices, part, 0)


def attend_forward(ends, qa_ref, ka_ref, ve_ref, mixed_ref, inverse_ref):
    length = qa_ref.shape[0]
    for block in range(length // TILE):
        reach = (block + 1) * TILE
        at = pl.ds(block * TILE, TILE)
        queries = qa_ref[at, :]
        t = lax.broadcasted_iota(jnp.int32, (TILE, 1), 0) + block * TILE
        start = first_visible(ends, t)
        s = lax.broadcasted_iota(jnp.int32, (TILE, reach), 1)
        visible = (s >= start) & (s <= t)
        sums = []
        for head in range(2):
            base = nt(queries, ka_ref[head, :reach, :])
            weights = jnp.where(visible, base * base + 1.0, 0.0).astype(BF16)
            sums.append(nn(weights, ve_ref[head, :reach, :]))
        lower = lanes_of((TILE, 128)) < 64
        numerator = jnp.where(lower, sums[0], sums[1])
        inverse = 1.0 / pltpu.roll(jnp.where(lower, sums[1], sums[0]), 64, 1)
        mixed_ref[at, :] = (numerator * inverse).astype(BF16)
        inverse_ref[at, :] = inverse


def attend_backward(
    ends, grad_ref, qa_ref, ka_ref, ve_ref, mixed_ref, inverse_ref, dn_ref, qs_ref, kt_ref, dqt_ref, gqk_ref, gv_ref
):
    length = qa_ref.shape[0]
    lane = lanes_of((length, 128))
    lower = lane < 64
    scaled = grad_ref[...].astype(F32) * inverse_ref[...]
    away = pltpu.roll(-scaled * mixed_ref[...].astype(F32), 64, 1)
    dn_ref[0] = jnp.where(lower, scaled, away).astype(BF16)
    dn_ref[1] = jnp.where(lower, away, scaled).astype(BF16)
    shifted = pltpu.roll(qa_ref[...].astype(F32), 32, 1)
    qs_ref[...] = jnp.where((lane >= 32) & (lane < 64), shifted * 2.0, 0.0).astype(BF16)
    for head in range(2):
        kt_ref[head] = ka_ref[head].astype(F32).T[:32].astype(BF16)
    dqt_ref[...] = jnp.zeros_like(dqt_ref)
    for block in range(length // TILE):
        first = block * TILE
        at = pl.ds(first, TILE)
        rest = pl.ds(first, length - first)
        shape = (TILE, length - first)
        t = lax.broadcasted_iota(jnp.int32, (1, shape[1]), 1) + first
        s = lax.broadcasted_iota(jnp.int32, shape, 0) + first
        visible = (s >= first_visible(ends, t)) & (s <= t)
        value_sums, key_sums = [], []
        for head in range(2):
            base = nt(ka_ref[head, at, :], qa_ref[rest, :])
            grad_weights = nt(ve_ref[head, at, :], dn_ref[head, rest, :])
            weights = jnp.where(visible, base * base + 1.0, 0.0).astype(BF16)
            grad_base = jnp.where(visible, grad_weights * base, 0.0).astype(BF16)
            value_sums.append(nn(weights, dn_ref[head, rest, :]))
            key_sums.append(nn(grad_base, qs_ref[rest, :]))
            dqt_ref[:, rest] += nn(kt_ref[head, :, at], grad_base)
        lane = lanes_of((TILE, 128))
        gv_ref[at, :] = jnp.where(lane < 64, value_sums[0], value_sums[1]).astype(BF16)
        gqk_ref[at, :] = jnp.where(
            (lane >= 32) & (lane < 48), key_sums[0], jnp.where((lane >= 48) & (lane < 64), key_sums[1], 0.0)
        )
    queries = jnp.concatenate([dqt_ref[...] * 0.5, jnp.zeros((96, length), F32)], axis=0)
    gqk_ref[...] += queries.T


def sending(source, target, send_sem, recv_sem, row_group, peer):
    return pltpu.make_async_remote_copy(
        src_ref=source,
        dst_ref=target,
        send_sem=send_sem,
        recv_sem=recv_sem,
        device_id=(row_group, peer),
        device_id_type=MESH,
    )


VMEM_SPEC = pl.BlockSpec(memory_space=pltpu.VMEM)
SMEM_SPEC = pl.BlockSpec(memory_space=pltpu.SMEM)


CHUNK = 256
STEP_ROWS = 48
Z_UNITS = 5
SLOTS = 7
VMEM_BYTES = 63 << 20


def place(me):
    core = lax.rem(me, 2)
    return core, 2 + 2 * core, 4 - 2 * core


def blocks_of(core, groups):
    first, second = 2 + 2 * core, 4 - 2 * core
    return [
        pl.multiple_of(32 * (8 * group + first * i + second * j + core), 32)
        for i in range(2)
        for j in range(2)
        for group in (0, 2, 1, 3)[:groups]
    ]


class Reduction:
    def __init__(self, source, buffers, slot_of=None, place_of=None):
        self.source = source
        self.got_a, self.got_b, self.got_z, self.a_sems, self.b_sems, self.c_sems, self.d_sems = buffers
        self.slot_of = slot_of or (lambda unit: unit)
        self.place_of = place_of or (lambda unit: unit)
        self.group, self.me = lax.axis_index("dp"), lax.axis_index("seq")
        core, first, second = place(self.me)
        self.bit_a, self.bit_b = lax.rem(self.me // first, 2), lax.rem(self.me // second, 2)
        self.peer_a = self.me + first * (1 - 2 * self.bit_a)
        self.peer_b = self.me + second * (1 - 2 * self.bit_b)
        self.bit_c, self.bit_d = lax.rem(self.group, 2), self.group // 2
        self.group_c = self.group + 1 - 2 * self.bit_c
        self.group_d = self.group + 2 - 4 * self.bit_d

    def rows(self, bit_c, bit_d=None):
        if bit_d is None:
            return pl.ds(pl.multiple_of(64 * bit_c, 64), 64)
        return pl.ds(pl.multiple_of(64 * bit_c + 32 * bit_d, 32), 32)

    def a_copy(self, unit):
        at = self.place_of(unit)
        return sending(
            self.source.at[self.slot_of(unit), 1 - self.bit_a], self.got_a.at[at], self.a_sems.at[0, at],
            self.a_sems.at[1, at], self.group, self.peer_a,
        )

    def b_copy(self, unit):
        at = self.place_of(unit)
        return sending(
            self.got_a.at[at, 1 - self.bit_b], self.got_b.at[at], self.b_sems.at[0, at], self.b_sems.at[1, at],
            self.group, self.peer_b,
        )

    def c_copy(self, unit):
        at = self.place_of(unit)
        return sending(
            self.got_b.at[at, self.rows(1 - self.bit_c), :], self.got_z.at[at, pl.ds(0, 64), :],
            self.c_sems.at[0, at], self.c_sems.at[1, at], self.group_c, self.me,
        )

    def d_copy(self, unit):
        at = self.place_of(unit)
        return sending(
            self.got_b.at[at, self.rows(self.bit_c, 1 - self.bit_d), :], self.got_z.at[at, pl.ds(64, 32), :],
            self.d_sems.at[0, at], self.d_sems.at[1, at], self.group_d, self.me,
        )

    def a_step(self, unit):
        at = self.place_of(unit)
        self.a_copy(unit).wait_recv()
        mine = self.source[self.slot_of(unit), self.bit_a].astype(F32)
        self.got_a[at] = (mine + self.got_a[at].astype(F32)).astype(BF16)
        self.b_copy(unit).start()

    def b_step(self, unit):
        at = self.place_of(unit)
        self.b_copy(unit).wait_recv()
        self.got_b[at] = (self.got_a[at, self.bit_b].astype(F32) + self.got_b[at].astype(F32)).astype(BF16)
        self.c_copy(unit).start()

    def c_step(self, unit):
        at, mine = self.place_of(unit), self.rows(self.bit_c)
        self.c_copy(unit).wait_recv()
        self.got_b[at, mine, :] = (
            self.got_b[at, mine, :].astype(F32) + self.got_z[at, :64, :].astype(F32)
        ).astype(BF16)
        self.d_copy(unit).start()

    def d_step(self, unit):
        at = self.place_of(unit)
        self.d_copy(unit).wait_recv()
        return self.got_b[at, self.rows(self.bit_c, self.bit_d), :].astype(F32) + self.got_z[at, 64:, :].astype(F32)

    def wait_sent(self, unit):
        self.b_copy(unit).wait_send()
        self.c_copy(unit).wait_send()
        self.d_copy(unit).wait_send()


class GroupsFirst(Reduction):
    def c_copy(self, unit):
        at = self.place_of(unit)
        return sending(
            self.source.at[self.slot_of(unit), :, :, self.rows(1 - self.bit_c), :],
            self.got_z.at[at, :, :, pl.ds(0, 64), :],
            self.c_sems.at[0, at], self.c_sems.at[1, at], self.group_c, self.me,
        )

    def d_copy(self, unit):
        at = self.place_of(unit)
        block = pl.ds(pl.multiple_of(32 * (1 - self.bit_d), 32), 32)
        return sending(
            self.got_z.at[at, :, :, block, :], self.got_z.at[at, :, :, pl.ds(64, 32), :],
            self.d_sems.at[0, at], self.d_sems.at[1, at], self.group_d, self.me,
        )

    def a_copy(self, unit):
        at = self.place_of(unit)
        return sending(
            self.got_z.at[at, 1 - self.bit_a, :, pl.ds(64, 32), :], self.got_a.at[at],
            self.a_sems.at[0, at], self.a_sems.at[1, at], self.group, self.peer_a,
        )

    def c_step(self, unit):
        at = self.place_of(unit)
        self.c_copy(unit).wait_recv()
        mine = self.source[self.slot_of(unit), :, :, self.rows(self.bit_c), :].astype(F32)
        self.got_z[at, :, :, :64, :] = (mine + self.got_z[at, :, :, :64, :].astype(F32)).astype(BF16)
        self.d_copy(unit).start()

    def d_step(self, unit):
        at = self.place_of(unit)
        self.d_copy(unit).wait_recv()
        mine = self.got_z[at, :, :, pl.ds(pl.multiple_of(32 * self.bit_d, 32), 32), :].astype(F32)
        self.got_z[at, :, :, 64:, :] = (mine + self.got_z[at, :, :, 64:, :].astype(F32)).astype(BF16)
        self.a_copy(unit).start()

    def a_step(self, unit):
        at = self.place_of(unit)
        self.a_copy(unit).wait_recv()
        mine = self.got_z[at, self.bit_a, :, 64:, :].astype(F32)
        self.got_a[at] = (mine + self.got_a[at].astype(F32)).astype(BF16)
        self.b_copy(unit).start()

    def b_step(self, unit):
        at = self.place_of(unit)
        self.b_copy(unit).wait_recv()
        return self.got_a[at, self.bit_b].astype(F32) + self.got_b[at].astype(F32)

    def wait_sent(self, unit):
        for copy in (self.a_copy, self.b_copy, self.c_copy, self.d_copy):
            copy(unit).wait_send()


def reduction_buffers(units, cols):
    sems = pltpu.SemaphoreType.DMA((2, units))
    return [
        pltpu.VMEM((units, 2, 128, cols), BF16),
        pltpu.VMEM((units, 128, cols), BF16),
        pltpu.VMEM((units, 96, cols), BF16),
        sems, sems, sems, sems,
    ]


def groups_first_buffers(units, cols):
    sems = pltpu.SemaphoreType.DMA((2, units))
    return [
        pltpu.VMEM((units, 2, 32, cols), BF16),
        pltpu.VMEM((units, 32, cols), BF16),
        pltpu.VMEM((units, 2, 2, 96, cols), BF16),
        sems, sems, sems, sems,
    ]


def store_blocks(target, unit, col, values, groups):
    rows = 32 * groups
    for i in range(2):
        for j in range(2):
            at = (2 * i + j) * rows
            target[unit, i, j, :, col : col + values.shape[1]] = values[at : at + rows].astype(BF16)


def turn(source, tokens, padded, turned):
    turned[...] = jnp.concatenate([source, jnp.zeros((padded - tokens, D), BF16)], axis=0).T


def split_rows(turned, mine_ref, theirs_ref, core, groups):
    for i, (mine, theirs) in enumerate(zip(blocks_of(core, groups), blocks_of(1 - core, groups))):
        a, b, group = i // (2 * groups), i // groups % 2, i % groups
        mine_ref[a, b, group * 32 : (group + 1) * 32, :] = turned[pl.ds(mine, 32), :]
        theirs_ref[a, b, group * 32 : (group + 1) * 32, :] = turned[pl.ds(theirs, 32), :]


def write_unit(total, at, w, gate_out, up_out, down_out):
    down_out[:, pl.ds(at, w)] = total[:, :w]
    gate_out[:, pl.ds(at, w)] = total[:, CHUNK : CHUNK + w]
    up_out[:, pl.ds(at, w)] = total[:, 2 * CHUNK : 2 * CHUNK + w]


def block_kernel(
    groups, seq_devices, rows, length, width,
    x_ref, cot_ref, gain_ref, wo_ref, wg_hbm, wu_hbm, wd_hbm, doc_ref, gain_attn_ref, wq_ref, wk_ref, wv_hbm,
    output_ref, input_out, gate_out, up_out, down_out, wout_out, query_out, key_out, value_out, gains_out,
    branch, residual, normed, out_acc, gnf, w_buf, lhs, right, parts, parts_o, q_source,
    got, heads, inverse, arrived, back, qa, ka, ve, dn, qs, kt, dqt, gqk, gv, gains, gains_got,
    fsend_a, frecv_a, fsend_b, frecv_b, w_sem, wv_sems, lhs_sems, pair_sems, send_a, recv_a, send_b, recv_b, gain_send, gain_recv,
    *buffers,
):
    row_group, me = lax.axis_index("dp"), lax.axis_index("seq")
    core, _, _ = place(me)
    partner = me + 1 - 2 * core
    tokens = rows * length
    padded = right.shape[1] // 2
    full = width // CHUNK
    tail = width - full * CHUNK
    low = packed_rows(length)
    lower = lanes_of((low, 128)) < 64
    here = pl.ds(pl.multiple_of(me * length, 16), length)
    half = H * F

    def slot_of(unit):
        if isinstance(unit, int):
            return unit if unit < SLOTS else 2 * (unit - SLOTS)
        return jnp.where(unit < SLOTS, unit, 2 * (unit - SLOTS))

    def place_of(unit):
        if isinstance(unit, int):
            return unit // 2 if unit < 2 * Z_UNITS else unit - Z_UNITS
        return jnp.where(unit < 2 * Z_UNITS, unit // 2, unit - Z_UNITS)

    feed = Reduction(parts, buffers[:7], slot_of, place_of)
    outer = Reduction(parts_o, buffers[7:14])
    qkv = Reduction(q_source, buffers[14:21])
    first = GroupsFirst(parts, buffers[21:28], slot_of, lambda unit: unit // 2)

    barrier = pltpu.get_barrier_semaphore()
    for step in range(1, seq_devices):
        peer = lax.rem(me + step, seq_devices)
        pl.semaphore_signal(barrier, inc=1, device_id=(row_group, peer), device_id_type=MESH)
    for other in (feed.group_c, feed.group_d):
        pl.semaphore_signal(barrier, inc=1, device_id=(other, me), device_id_type=MESH)

    def loads(chunk, slot, w):
        at = pl.ds(pl.multiple_of(chunk * CHUNK, CHUNK), w)
        return [
            pltpu.make_async_copy(hbm.at[at, :], w_buf.at[slot, which, pl.ds(0, w), :], w_sem.at[slot, which])
            for which, hbm in enumerate((wg_hbm, wu_hbm, wd_hbm))
        ]

    def value_load(part):
        return pltpu.make_async_copy(
            wv_hbm.at[pl.ds(part * CHUNK, CHUNK), :], w_buf.at[part // 3, part % 3], wv_sems.at[part]
        )

    def lhs_send(which):
        return (q_source.at[0], q_source.at[1], parts_o.at[0])[which % 3].at[:, :, :, pl.ds(0, padded)]

    def lhs_copy(which):
        return sending(
            lhs_send(which),
            lhs.at[which % 3, :, :, :, pl.ds(padded, padded)],
            lhs_sems.at[0, which], lhs_sems.at[1, which], row_group, partner,
        )

    def prepare_lhs(which, source):
        turned = right.at[3 if which < 2 else 1, :, pl.ds(0, padded)]
        turn(source, tokens, padded, turned)
        split_rows(turned, lhs.at[which % 3, :, :, :, pl.ds(0, padded)], lhs_send(which), core, groups)

    def left(which):
        return lhs[which].reshape(D // 2, 2 * padded)

    gap = padded - tokens

    def clear(slot, count):
        for base in (tokens, padded + tokens):
            right[slot : slot + count, base : base + gap, :] = jnp.zeros((count, gap, 3 * CHUNK), BF16)

    for part in range(D // CHUNK):
        value_load(part).start()
    spread = [right.at[1 + part, pl.ds(0, 2 * half), pl.ds(0, D // 2)] for part in range(2)]
    whole = spread_matrix()
    for part in range(2):
        spread[part][...] = whole[:, part * D // 2 : (part + 1) * D // 2]
    pl.semaphore_wait(barrier, seq_devices + 1)
    for part in range(D // CHUNK):
        value_load(part).wait()

    def spreading(row, step):
        peer = lax.rem(me + step, seq_devices)
        return sending(
            back.at[row, peer], got.at[row, me], fsend_a.at[row, step], frecv_a.at[row, step], row_group, peer
        )

    def merging(row, step):
        peer = lax.rem(me + step, seq_devices)
        there = pl.ds(pl.multiple_of(peer * length, 16), length)
        mine = pl.ds(pl.multiple_of(me * PAIR, 128), PAIR)
        at = pl.ds(pl.multiple_of(row * length, 16), length)
        return sending(
            heads.at[row, there, :], branch.at[at, mine], fsend_b.at[row, step], frecv_b.at[row, step],
            row_group, peer,
        )

    def project_row(row, carry):
        at = pl.ds(pl.multiple_of(row * length, 16), length)
        low_row = rms_scale(x_ref[at, :].astype(F32), gain_attn_ref[...]).astype(BF16)
        both = jnp.concatenate([nn(low_row, wq_ref[...]), nn(low_row, wk_ref[...])], axis=1).astype(BF16)
        sides = [nn(both, spread[part][...]) for part in range(2)]
        values = sum(
            nn(low_row[:, part * CHUNK : (part + 1) * CHUNK], w_buf[part // 3, part % 3])
            for part in range(D // CHUNK)
        ).astype(BF16)
        for pair in range(seq_devices):
            side, col = divmod(pair * 128, D // 2)
            tile = sides[side][:, col : col + 128]
            back[row, pair, :length, :] = values[:, pair * PAIR : (pair + 1) * PAIR]
            back[row, pair, length:, :] = jnp.where(lower, tile[:low], tile[length - low :]).astype(BF16)
        got[row, me] = back[row, me]

        @pl.when(row == 0)
        def _():
            send_spread(0)

        return carry

    def send_spread(row):
        for step in range(1, seq_devices):
            spreading(row, step).start()

    lax.fori_loop(0, rows, project_row, 0)
    send_spread(1)
    for chunk in range(2):
        for copy in loads(chunk, chunk, CHUNK):
            copy.start()
    prepare_lhs(0, cot_ref[...])
    lhs_copy(0).start()

    gnf[...] = jnp.zeros_like(gnf)
    clear(0, 3)

    def residual_row(row):
        for step in range(1, seq_devices):
            merging(row, step).wait_recv()
        at = pl.ds(pl.multiple_of(row * length, 16), length)
        value = x_ref[at, :].astype(F32) + nn(branch[at, :], wo_ref[...])
        residual[at, :] = value
        out_acc[at, :] = value
        normed[at, :] = rms_scale(value, gain_ref[...]).astype(BF16)

    def attend_rows(row, carry):
        for step in range(1, seq_devices):
            spreading(row, step).wait()

        @pl.when(row + 2 < rows)
        def _():
            send_spread(row + 2)

        prepare_row(got, row, qa, ka, ve, seq_devices, length)
        attend_forward(row_ends(doc_ref, row), qa, ka, ve, heads.at[row], inverse.at[row])
        for step in range(1, seq_devices):
            merging(row, step).start()
        at = pl.ds(pl.multiple_of(row * length, 16), length)
        branch[at, pl.ds(pl.multiple_of(me * PAIR, 128), PAIR)] = heads[row, here, :]
        return carry

    lax.fori_loop(0, rows, attend_rows, 0)

    for row in range(rows):
        residual_row(row)
    prepare_lhs(1, normed[...])
    lhs_copy(1).start()
    clear(3, 1)

    def right_copy(slot, cols, sem):
        return sending(
            right.at[slot, pl.ds(0, tokens), pl.ds(0, cols)], right.at[slot, pl.ds(padded, tokens), pl.ds(0, cols)],
            pair_sems.at[0, sem], pair_sems.at[1, sem], row_group, partner,
        )

    def pair_copy(chunk):
        return right_copy(lax.rem(chunk, 4), 3 * CHUNK, chunk)

    def forward_part(chunk, wg, wu, wd, w):
        slot = lax.rem(chunk, 4)
        gate = nt(normed[...], wg)
        up = nt(normed[...], wu)
        sigmoid = 1.0 / (1.0 + jnp.exp(-gate))
        silu = gate * sigmoid
        hidden = (silu * up).astype(BF16)
        grad_hidden = nt(cot_ref[...], wd)
        grad_gate = (grad_hidden * up * (sigmoid * (1.0 + gate * (1.0 - sigmoid)))).astype(BF16)
        grad_up = (grad_hidden * silu).astype(BF16)
        for part, values in enumerate((hidden, grad_gate, grad_up)):
            right[slot, :tokens, part * CHUNK : part * CHUNK + w] = values
            if w < CHUNK:
                right[slot, :tokens, part * CHUNK + w : (part + 1) * CHUNK] = jnp.zeros((tokens, CHUNK - w), BF16)
        pair_copy(chunk).start()
        out_acc[...] += nn(hidden, wd)
        gnf[...] += nn(grad_gate, wg) + nn(grad_up, wu)

    def grad_part(chunk):
        pair_copy(chunk).wait()
        slot = lax.rem(chunk, 4)
        store_blocks(parts, slot_of(chunk), 0, nn(left(0), right[slot, :, 0:CHUNK]), groups)
        store_blocks(parts, slot_of(chunk), CHUNK, nn(left(1), right[slot, :, CHUNK:]), groups)

    def forward_step(chunk):
        slot = lax.rem(chunk, 2)
        for copy in loads(chunk, slot, CHUNK):
            copy.wait()
        forward_part(chunk, w_buf[slot, 0], w_buf[slot, 1], w_buf[slot, 2], CHUNK)

    def ticks(chunk):
        @pl.when((chunk >= 3) & (lax.rem(chunk, 2) == 1))
        def _():
            feed.a_step(chunk - 3)

        @pl.when((chunk >= 5) & (lax.rem(chunk, 2) == 1))
        def _():
            feed.b_step(chunk - 5)

        @pl.when(chunk == 8)
        def _():
            first.c_step(1)

    def fetch_next(chunk):
        @pl.when(chunk < full - 1)
        def _():
            for copy in loads(chunk + 1, lax.rem(chunk + 1, 2), CHUNK):
                copy.start()

        @pl.when(chunk == full - 1)
        def _():
            for copy in loads(full, full % 2, tail):
                copy.start()

    def main(chunk, carry):
        fetch_next(chunk)
        forward_step(chunk)
        unit = chunk - 1

        @pl.when(unit >= SLOTS)
        def _():
            feed.a_copy(2 * (unit - SLOTS)).wait_send()

        grad_part(unit)
        along_z = (unit < 2 * Z_UNITS) & (lax.rem(unit, 2) == 1)

        @pl.when(along_z)
        def _():
            first.c_copy(unit).start()

        @pl.when(jnp.logical_not(along_z) & (unit < 10))
        def _():
            feed.a_copy(unit).start()

        ticks(chunk)
        return carry

    forward_step(0)
    for which in range(2):
        lhs_copy(which).wait()
    lax.fori_loop(1, full, main, 0)
    slot = full % 2
    for copy in loads(full, slot, tail):
        copy.wait()
    forward_part(full, w_buf[slot, 0, :tail], w_buf[slot, 1, :tail], w_buf[slot, 2, :tail], tail)
    for part in range(D // CHUNK):
        value_load(part).start()
    feed.a_copy(2 * (full - 1 - SLOTS)).wait_send()
    grad_part(full - 1)
    first.c_copy(full - 1).start()

    gains[...] = jnp.zeros_like(gains)

    def norm_backward_ffn(step, carry):
        at = pl.ds(pl.multiple_of(step * STEP_ROWS, 16), STEP_ROWS)
        value, grad = residual[at, :], gnf[at, :]
        scale = lax.rsqrt(jnp.mean(value * value, axis=-1, keepdims=True) + eps_norm)
        gains[0:1, :] += jnp.sum(grad * value * scale, axis=0, keepdims=True)
        weighted = grad * gain_ref[...]
        mean = jnp.mean(weighted * value, axis=-1, keepdims=True)
        total = cot_ref[at, :].astype(F32) + scale * weighted - value * (scale * scale * scale * mean)
        gnf[at, :] = total
        right[3, at, :] = total[:, : 3 * CHUNK].astype(BF16)
        right[0, at, :CHUNK] = total[:, 3 * CHUNK :].astype(BF16)
        output_ref[at, :] = out_acc[at, :].astype(BF16)
        return carry

    lax.fori_loop(0, tokens // STEP_ROWS, norm_backward_ffn, 0)
    normed[...] = (
        nt(right[3, :tokens, :], wo_ref[:, : 3 * CHUNK]) + nt(right[0, :tokens, :CHUNK], wo_ref[:, 3 * CHUNK :])
    ).astype(BF16)

    def outgoing(row, step):
        peer = lax.rem(me + step, seq_devices)
        theirs = pl.ds(pl.multiple_of(peer * PAIR, 128), PAIR)
        at = pl.ds(pl.multiple_of(row * length, 16), length)
        return sending(
            normed.at[at, theirs], arrived.at[row, here, :], send_a.at[row, step], recv_a.at[row, step],
            row_group, peer,
        )

    def returning(row, step):
        peer = lax.rem(me + step, seq_devices)
        return sending(
            got.at[row, peer], back.at[row, me], send_b.at[row, step], recv_b.at[row, step], row_group, peer
        )

    def send_row(row, carry):
        for step in range(1, seq_devices):
            outgoing(row, step).start()
        at = pl.ds(pl.multiple_of(row * length, 16), length)
        arrived[row, here, :] = normed[at, pl.ds(pl.multiple_of(me * PAIR, 128), PAIR)]
        return carry

    send_row(0, 0)
    feed.a_copy(2 * (full - SLOTS)).wait_send()
    grad_part(full)
    send_row(1, 0)
    out_pairs = [right_copy(3, 3 * CHUNK, full + 1), right_copy(0, CHUNK, full + 2)]
    for copy in out_pairs:
        copy.start()
    prepare_lhs(2, branch[...])
    lhs_copy(2).start()
    first.c_step(3)
    feed.c_step(0)
    for row in range(2, rows):
        send_row(row, 0)
    prepare_lhs(3, rms_scale(x_ref[...].astype(F32), gain_attn_ref[...]).astype(BF16))
    clear(1, 1)
    for copy in out_pairs:
        copy.wait()
    lhs_copy(3).start()
    lhs_copy(2).wait()
    for col in range(0, D, CHUNK):
        columns = right[3, :, col : col + CHUNK] if col < 3 * CHUNK else right[0, :, :CHUNK]
        store_blocks(parts_o, 0, col, nn(left(2), columns), groups)
    gather = right.at[3, pl.ds(0, 2 * half), pl.ds(0, 2 * half)]
    gather[...] = gather_matrix()

    def attend(row, carry):
        prepare_row(got, row, qa, ka, ve, seq_devices, length)
        for step in range(1, seq_devices):
            outgoing(row, step).wait_recv()
        attend_backward(
            row_ends(doc_ref, row), arrived.at[row], qa, ka, ve, heads.at[row], inverse.at[row],
            dn, qs, kt, dqt, gqk, gv,
        )

        def pack(peer, inner):
            at = pl.multiple_of(peer * length, 16)
            got[row, peer, :length, :] = gv[pl.ds(at, length), :]
            front = gqk[pl.ds(at, low), :]
            rear = pltpu.roll(gqk[pl.ds(at + length - low, low), :], 64, 1)
            got[row, peer, length:, :] = jnp.where(lower, front, rear).astype(BF16)
            return inner

        lax.fori_loop(0, seq_devices, pack, 0)
        for step in range(1, seq_devices):
            returning(row, step).start()
        back[row, me] = got[row, me]

        @pl.when(row == 0)
        def _():
            feed.a_copy(10).start()
            feed.a_step(8)
            first.c_step(5)

        @pl.when(row == 1)
        def _():
            outer.a_copy(0).start()
            feed.b_step(6)
            feed.c_step(2)
            first.c_step(7)
            first.d_step(1)

        @pl.when(row == 2)
        def _():
            first.d_step(3)
            feed.b_step(8)

        return carry

    lax.fori_loop(0, rows, attend, 0)
    feed.c_step(4)
    first.c_step(9)
    first.d_step(5)
    feed.a_step(10)

    def unpack(row, carry):
        for step in range(1, seq_devices):
            outgoing(row, step).wait_send()
            returning(row, step).wait()
        tiles = []
        for pair in range(0, seq_devices, 2):
            halves = []
            for one in (pair, pair + 1):
                packed = back[row, one, length:, :].astype(F32)
                turned_over = pltpu.roll(packed, 64, 1)
                straight, other = (packed, turned_over) if one == pair else (turned_over, packed)
                halves.append(jnp.concatenate([straight, other[2 * low - length :]], axis=0))
            tiles.append(jnp.where(lanes_of((length, 128)) < 64, halves[0], halves[1]).astype(BF16))
        at = pl.ds(pl.multiple_of(row * length, 16), length)
        right[1, at, : 2 * half] = nn(jnp.concatenate(tiles, axis=1), gather[...]).astype(BF16)
        for pair in range(seq_devices):
            slot, col = divmod(2 * half + pair * PAIR, 3 * CHUNK)
            right[1 + slot, at, col : col + PAIR] = back[row, pair, :length, :]
        return carry

    lax.fori_loop(0, rows, unpack, 0)
    q_pairs = [right_copy(1, 3 * CHUNK, full + 3), right_copy(2, 3 * CHUNK, full + 4)]
    for copy in q_pairs:
        copy.start()
    for part in range(D // CHUNK):
        value_load(part).wait()
    q_and_k = nt(right[1, :tokens, :half], wq_ref[...]) + nt(right[1, :tokens, half : 2 * half], wk_ref[...])
    for part in range(D // CHUNK):
        at = slice(part * CHUNK, (part + 1) * CHUNK)
        block = w_buf[part // 3, part % 3]
        out_acc[:, at] = (
            q_and_k[:, at]
            + nt(right[1, :tokens, 2 * half :], block[:, : 3 * CHUNK - 2 * half])
            + nt(right[2, :tokens, :], block[:, 3 * CHUNK - 2 * half :])
        )
    lhs_copy(3).wait()
    for copy in q_pairs:
        copy.wait()
    for unit in range(2):
        for col in range(0, 3 * CHUNK, CHUNK):
            store_blocks(q_source, unit, col, nn(left(0), right[1 + unit, :, col : col + CHUNK]), groups)
        qkv.a_copy(unit).start()

    def norm_backward(step, carry):
        at = pl.ds(pl.multiple_of(step * STEP_ROWS, 16), STEP_ROWS)
        value, grad = x_ref[at, :].astype(F32), out_acc[at, :]
        scale = lax.rsqrt(jnp.mean(value * value, axis=-1, keepdims=True) + eps_norm)
        gains[1:2, :] += jnp.sum(grad * value * scale, axis=0, keepdims=True)
        weighted = grad * gain_attn_ref[...]
        mean = jnp.mean(weighted * value, axis=-1, keepdims=True)
        total = gnf[at, :] + scale * weighted - value * (scale * scale * scale * mean)
        input_out[at, :] = total.astype(BF16)
        return carry

    lax.fori_loop(0, tokens // STEP_ROWS, norm_backward, 0)

    def gain_copy(step, target_group, target):
        return sending(
            gains, gains_got.at[step], gain_send.at[step], gain_recv.at[step], target_group, target
        )

    gain_copies = [
        gain_copy(0, row_group, partner),
        gain_copy(1, row_group, feed.peer_a),
        gain_copy(2, row_group, feed.peer_b),
        gain_copy(3, feed.group_c, me),
        gain_copy(4, feed.group_d, me),
    ]

    def gain_step(step):
        gain_copies[step].wait()
        gains[...] += gains_got[step]
        if step < 4:
            gain_copies[step + 1].start()

    def write_feed(unit, total, w):
        at = unit * CHUNK if isinstance(unit, int) else pl.multiple_of(unit * CHUNK, CHUNK)
        write_unit(total, at, w, gate_out, up_out, down_out)

    gain_copies[0].start()
    outer.a_step(0)
    feed.b_step(10)
    gain_step(0)
    first.d_step(7)
    feed.c_step(6)
    first.a_step(1)
    feed.c_step(8)
    gain_step(1)
    qkv.a_step(0)
    first.a_step(3)
    qkv.a_step(1)
    outer.b_step(0)
    gain_step(2)
    qkv.b_step(0)
    feed.c_step(10)
    first.a_step(5)
    qkv.b_step(1)
    gain_step(3)
    qkv.c_step(0)
    first.d_step(9)
    outer.c_step(0)
    qkv.c_step(1)
    first.a_step(7)
    gain_step(4)
    first.a_step(9)
    for unit in range(full):
        if unit >= 2 * Z_UNITS or unit % 2 == 0:
            write_feed(unit, feed.d_step(unit), CHUNK)
    write_feed(full, feed.d_step(full), tail)
    for unit in range(1, 2 * Z_UNITS, 2):
        write_feed(unit, first.b_step(unit), CHUNK)
    picked = lax.broadcasted_iota(jnp.int32, (D, 128), 0) == 32 * (seq_devices * row_group + me) + lanes_of((D, 128))
    gains_out[...] = jnp.dot(
        gains[...], jnp.where(picked, 1.0, 0.0), precision=lax.Precision.HIGHEST, preferred_element_type=F32
    )
    wout_out[...] = outer.d_step(0)
    total = qkv.d_step(0)
    query_out[...] = total[:, :half]
    key_out[...] = total[:, half : 2 * half]
    value_out[:, : 3 * CHUNK - 2 * half] = total[:, 2 * half :]
    value_out[:, 3 * CHUNK - 2 * half :] = qkv.d_step(1)

    for unit in range(full + 1):
        if unit < 2 * Z_UNITS and unit % 2 == 1:
            first.wait_sent(unit)
        else:
            feed.wait_sent(unit)
            if unit > 2 * (full - SLOTS):
                feed.a_copy(unit).wait_send()
    def forward_sent(row, carry):
        for step in range(1, seq_devices):
            merging(row, step).wait_send()
        return carry

    lax.fori_loop(0, rows, forward_sent, 0)
    for one, unit in ((outer, 0), (qkv, 0), (qkv, 1)):
        one.wait_sent(unit)
        one.a_copy(unit).wait_send()


ANY_SPEC = pl.BlockSpec(memory_space=pl.ANY)


def block_step(
    groups, seq_devices, x, cotangent, gain_ffn, w_out, w_gate_t, w_up_t, w_down, doc_lengths, gain_attn,
    w_query, w_key, w_value,
):
    tokens = x.shape[0]
    rows = doc_lengths.shape[0]
    length = tokens // rows
    total = seq_devices * length
    width = w_down.shape[0]
    full = width // CHUNK
    padded = (tokens + 127) // 128 * 128
    unit_rows = 32 * groups
    message = (rows, seq_devices, length + packed_rows(length), 128)
    dma = pltpu.SemaphoreType.DMA
    sems = dma((rows, seq_devices))
    return pl.pallas_call(
        functools.partial(block_kernel, groups, seq_devices, rows, length, width),
        name="block",
        out_shape=[
            jax.ShapeDtypeStruct((tokens, D), BF16),
            jax.ShapeDtypeStruct((tokens, D), BF16),
            jax.ShapeDtypeStruct((32, width), F32),
            jax.ShapeDtypeStruct((32, width), F32),
            jax.ShapeDtypeStruct((32, width), F32),
            jax.ShapeDtypeStruct((32, D), F32),
            jax.ShapeDtypeStruct((32, H * F), F32),
            jax.ShapeDtypeStruct((32, H * F), F32),
            jax.ShapeDtypeStruct((32, D), F32),
            jax.ShapeDtypeStruct((8, 128), F32),
        ],
        in_specs=[VMEM_SPEC] * 4 + [ANY_SPEC] * 3 + [SMEM_SPEC] + [VMEM_SPEC] * 3 + [ANY_SPEC],
        out_specs=[VMEM_SPEC] * 10,
        scratch_shapes=[
            pltpu.VMEM((tokens, D), BF16),
            pltpu.VMEM((tokens, D), F32),
            pltpu.VMEM((tokens, D), BF16),
            pltpu.VMEM((tokens, D), F32),
            pltpu.VMEM((tokens, D), F32),
            pltpu.VMEM((2, 3, CHUNK, D), BF16),
            pltpu.VMEM((3, 2, 2, unit_rows, 2 * padded), BF16),
            pltpu.VMEM((4, 2 * padded, 3 * CHUNK), BF16),
            pltpu.VMEM((SLOTS, 2, 2, unit_rows, 3 * CHUNK), BF16),
            pltpu.VMEM((1, 2, 2, unit_rows, D), BF16),
            pltpu.VMEM((2, 2, 2, unit_rows, 3 * CHUNK), BF16),
            pltpu.VMEM(message, BF16),
            pltpu.VMEM((rows, total, 128), BF16),
            pltpu.VMEM((rows, total, 128), F32),
            pltpu.VMEM((rows, total, 128), BF16),
            pltpu.VMEM(message, BF16),
            pltpu.VMEM((total, 128), BF16),
            pltpu.VMEM((2, total, 128), BF16),
            pltpu.VMEM((2, total, 128), BF16),
            pltpu.VMEM((2, total, 128), BF16),
            pltpu.VMEM((total, 128), BF16),
            pltpu.VMEM((2, 32, total), BF16),
            pltpu.VMEM((32, total), F32),
            pltpu.VMEM((total, 128), F32),
            pltpu.VMEM((total, 128), BF16),
            pltpu.VMEM((8, D), F32),
            pltpu.VMEM((5, 8, D), F32),
            sems, sems, sems, sems, dma((2, 3)), dma((D // CHUNK,)), dma((2, 4)), dma((2, full + 5)),
            sems, sems, sems, sems, dma((5,)), dma((5,)),
        ]
        + reduction_buffers(full + 1 - Z_UNITS, 3 * CHUNK)
        + reduction_buffers(1, D)
        + reduction_buffers(2, 3 * CHUNK)
        + groups_first_buffers(Z_UNITS, 3 * CHUNK),
        compiler_params=pltpu.CompilerParams(collective_id=1, has_side_effects=True, vmem_limit_bytes=VMEM_BYTES),
    )(
        x, cotangent, gain_ffn.reshape(1, D), w_out, w_gate_t, w_up_t, w_down, doc_lengths,
        gain_attn.reshape(1, D), w_query, w_key, w_value,
    )


def publish(results, gains):
    def kernel(*refs):
        count = len(results)
        for source, target in zip(refs[:count], refs[count + 1 : 2 * count + 1]):
            target[...] = source[...]
        refs[2 * count + 1][...] = refs[count][1:2, :32]
        refs[2 * count + 2][...] = refs[count][0:1, :32]

    one = jax.ShapeDtypeStruct((1, 32), F32)
    return pl.pallas_call(
        kernel,
        name="publish",
        out_shape=[jax.ShapeDtypeStruct(x.shape, x.dtype) for x in results] + [one, one],
        in_specs=[VMEM_SPEC] * (len(results) + 1),
        out_specs=[VMEM_SPEC] * (len(results) + 2),
        compiler_params=pltpu.CompilerParams(vmem_limit_bytes=VMEM_BYTES),
    )(*results, gains)


def tuned_body(
    seq_devices, groups, inputs, doc_lengths, gain_attn, w_query, w_key, w_value, w_out, gain_ffn, w_gate, w_up,
    w_down, cotangent,
):
    row_count, shard_len, _ = inputs.shape
    token_count = row_count * shard_len
    output, input_grad, gate, up, down, out, query, key, value, gains = block_step(
        groups, seq_devices, inputs.reshape(token_count, D), cotangent.reshape(token_count, D), gain_ffn, w_out,
        w_gate.T, w_up.T, w_down, doc_lengths, gain_attn, w_query, w_key, w_value,
    )
    output, input_grad, gate, up, down, out, query, key, value, gain_attn_part, gain_ffn_part = publish(
        (output, input_grad, gate, up, down, out, query, key, value), gains
    )
    return (
        output.reshape(row_count, shard_len, D),
        input_grad.reshape(row_count, shard_len, D),
        gain_attn_part.reshape(32),
        query,
        key,
        value,
        out,
        gain_ffn_part.reshape(32),
        gate,
        up,
        down.T,
    )


def solution(mesh):
    in_specs = (
        P("dp", "seq", None),
        P("dp", None),
        P(),
        P(),
        P(),
        P(),
        P(),
        P(),
        P(),
        P(),
        P(),
        P("dp", "seq", None),
    )
    out_specs = (
        P("dp", "seq", None),
        P("dp", "seq", None),
        P(("dp", "seq")),
        P(("dp", "seq"), None),
        P(("dp", "seq"), None),
        P(("dp", "seq"), None),
        P(("dp", "seq"), None),
        P(("dp", "seq")),
        P(("dp", "seq"), None),
        P(("dp", "seq"), None),
        P(None, ("dp", "seq")),
    )
    seq_devices, groups = mesh.shape["seq"], mesh.shape["dp"]
    tuned = seq_devices == 8 and seq_devices * groups * 32 == D
    step = functools.partial(tuned_body, seq_devices, groups) if tuned else general_body
    return jax.shard_map(step, mesh=mesh, in_specs=in_specs, out_specs=out_specs, check_vma=False)
```

```python
import functools

import jax
import jax.numpy as jnp
from jax import lax
from jax.experimental import pallas as pl
from jax.experimental.pallas import tpu as pltpu
from jax.sharding import PartitionSpec as P

D = 1024
H = 16
F = 16
HV = 64
BLOCK = 576


eps_norm = 1e-05


def rms_scale(stream, gain_vec):
    return (
        stream * lax.rsqrt(jnp.mean(stream * stream, axis=-1, keepdims=True) + eps_norm) * gain_vec
    )


def taylor_features(vectors):
    feat_width = vectors.shape[-1]
    outer_prod = (vectors[..., :, None] * vectors[..., None, :]).reshape(
        vectors.shape[:-1] + (feat_width * feat_width,)
    )
    ones_part = jnp.ones(vectors.shape[:-1] + (1,), jnp.float32)
    return jnp.concatenate(
        [ones_part, vectors * feat_width ** (-0.25), outer_prod * (0.5 / feat_width) ** 0.5],
        axis=-1,
    )


def document_ids(doc_lens, seq_length):
    doc_ends = jnp.cumsum(doc_lens, dtype=jnp.int32)
    positions = jnp.arange(seq_length, dtype=jnp.int32)
    return jnp.sum(
        (positions[:, None] >= doc_ends[None, :]).astype(jnp.int32), axis=1, dtype=jnp.int32
    )


def attend_row(queries, key_proj, value_proj, doc_row, block_rows):
    seq_length, head_count, feat_width = queries.shape
    value_width = value_proj.shape[-1]
    feat_count = 1 + feat_width + feat_width * feat_width
    block_count = seq_length // block_rows
    highest = lax.Precision.HIGHEST
    query_blocks = queries.reshape(block_count, block_rows, head_count, feat_width)
    key_blocks = key_proj.reshape(block_count, block_rows, head_count, feat_width)
    value_blocks = value_proj.reshape(block_count, block_rows, head_count, value_width)
    doc_blocks = doc_row.reshape(block_count, block_rows)
    previous = jnp.concatenate([jnp.full((1,), -1, jnp.int32), doc_blocks[:-1, -1]])
    positions = jnp.arange(block_rows, dtype=jnp.int32)
    causal = positions[:, None] >= positions[None, :]

    def block_step(carried, pieces):
        state_sum, norm_sum = carried
        query_block, key_block, value_block, doc_block, prior_doc = pieces
        scores = jnp.einsum(
            "thf,shf->hts", query_block, key_block, precision=highest
        ) * feat_width ** (-0.5)
        weights = 1.0 + scores + 0.5 * scores * scores
        same_doc = causal & (doc_block[:, None] == doc_block[None, :])
        weights = jnp.where(same_doc[None, :, :], weights, 0.0)
        numerator = jnp.einsum("hts,shv->thv", weights, value_block, precision=highest)
        denominator = jnp.transpose(jnp.sum(weights, axis=2))
        use_state = (doc_block == prior_doc).astype(jnp.float32)[:, None]
        query_feats = taylor_features(query_block)
        numerator = numerator + use_state[:, :, None] * jnp.einsum(
            "thp,hpv->thv", query_feats, state_sum, precision=highest
        )
        denominator = denominator + use_state * jnp.einsum(
            "thp,hp->th", query_feats, norm_sum, precision=highest
        )
        last_doc = doc_block[-1]
        keep_state = (last_doc == prior_doc).astype(jnp.float32)
        key_feats = (
            taylor_features(key_block) * (doc_block == last_doc).astype(jnp.float32)[:, None, None]
        )
        state_sum = keep_state * state_sum + jnp.einsum(
            "shp,shv->hpv", key_feats, value_block, precision=highest
        )
        norm_sum = keep_state * norm_sum + jnp.sum(key_feats, axis=0)
        return ((state_sum, norm_sum), numerator / denominator[:, :, None])

    initial = (
        jnp.zeros((head_count, feat_count, value_width), jnp.float32),
        jnp.zeros((head_count, feat_count), jnp.float32),
    )
    _, results = lax.scan(
        jax.checkpoint(block_step),
        initial,
        (query_blocks, key_blocks, value_blocks, doc_blocks, previous),
    )
    return results.reshape(seq_length, head_count, value_width)


def project(left, right):
    return jnp.dot(left, right, preferred_element_type=jnp.float32)


def back_project(left, right):
    return lax.dot_general(
        left, right, (((1,), (1,)), ((), ())), preferred_element_type=jnp.float32
    )


def weight_grad(left, right):
    return lax.dot_general(
        left, right, (((0,), (0,)), ((), ())), preferred_element_type=jnp.float32
    )


def swiglu(gate_proj, up_proj):
    return jax.nn.silu(gate_proj) * up_proj


def general_body(
    inputs,
    doc_lengths,
    gain_attn,
    w_query,
    w_key,
    w_value,
    w_out,
    gain_ffn,
    w_gate,
    w_up,
    w_down,
    cotangent,
):
    row_count, shard_len, _ = inputs.shape
    token_count = row_count * shard_len
    stream = inputs.reshape(token_count, D).astype(jnp.float32)
    normed, attn_norm_back = jax.vjp(rms_scale, stream, gain_attn)
    normed_low = normed.astype(jnp.bfloat16)
    query_proj = project(normed_low, w_query).astype(jnp.bfloat16)
    key_proj = project(normed_low, w_key).astype(jnp.bfloat16)
    value_proj = project(normed_low, w_value).astype(jnp.bfloat16)
    query_heads, key_heads, value_heads = (
        lax.all_to_all(
            query_proj.reshape(row_count, shard_len, H, F),
            "seq",
            split_axis=2,
            concat_axis=1,
            tiled=True,
        ),
        lax.all_to_all(
            key_proj.reshape(row_count, shard_len, H, F),
            "seq",
            split_axis=2,
            concat_axis=1,
            tiled=True,
        ),
        lax.all_to_all(
            value_proj.reshape(row_count, shard_len, H, HV),
            "seq",
            split_axis=2,
            concat_axis=1,
            tiled=True,
        ),
    )
    seq_length = query_heads.shape[1]
    doc_rows = jax.vmap(lambda doc_lens: document_ids(doc_lens, seq_length))(doc_lengths)

    def attend_all(queries, keys_in, values_in):
        return jax.vmap(attend_row, in_axes=(0, 0, 0, 0, None))(
            queries, keys_in, values_in, doc_rows, BLOCK
        )

    mixed_heads, attend_back = jax.vjp(
        attend_all,
        query_heads.astype(jnp.float32),
        key_heads.astype(jnp.float32),
        value_heads.astype(jnp.float32),
    )
    mixed_rows = lax.all_to_all(
        mixed_heads.astype(jnp.bfloat16), "seq", split_axis=1, concat_axis=2, tiled=True
    )
    mixed_flat = mixed_rows.reshape(token_count, D)
    residual = stream + project(mixed_flat, w_out)
    normed_ffn, ffn_norm_back = jax.vjp(rms_scale, residual, gain_ffn)
    ffn_low = normed_ffn.astype(jnp.bfloat16)
    gate_proj = project(ffn_low, w_gate)
    up_proj = project(ffn_low, w_up)
    hidden, act_back = jax.vjp(swiglu, gate_proj, up_proj)
    hidden_low = hidden.astype(jnp.bfloat16)
    output = residual + project(hidden_low, w_down)
    grad_out = cotangent.reshape(token_count, D)
    grad_gate, grad_up = act_back(back_project(grad_out, w_down))
    grad_gate_low = grad_gate.astype(jnp.bfloat16)
    grad_up_low = grad_up.astype(jnp.bfloat16)
    down_grad_t = weight_grad(grad_out, hidden_low)
    gate_grad = weight_grad(ffn_low, grad_gate_low)
    up_grad = weight_grad(ffn_low, grad_up_low)
    grad_normed_ffn = back_project(grad_gate_low, w_gate) + back_project(grad_up_low, w_up)
    grad_residual, gain_ffn_grad = ffn_norm_back(grad_normed_ffn)
    grad_residual = grad_residual + grad_out.astype(jnp.float32)
    grad_branch = grad_residual.astype(jnp.bfloat16)
    out_grad = weight_grad(mixed_flat, grad_branch)
    grad_mixed = (
        back_project(grad_branch, w_out).astype(jnp.bfloat16).reshape(row_count, shard_len, H, HV)
    )
    grad_heads = lax.all_to_all(grad_mixed, "seq", split_axis=2, concat_axis=1, tiled=True)
    grad_query, grad_key, grad_value = attend_back(grad_heads.astype(jnp.float32))
    back_query, back_key, back_value = (
        lax.all_to_all(
            grad_query.astype(jnp.bfloat16), "seq", split_axis=1, concat_axis=2, tiled=True
        ),
        lax.all_to_all(
            grad_key.astype(jnp.bfloat16), "seq", split_axis=1, concat_axis=2, tiled=True
        ),
        lax.all_to_all(
            grad_value.astype(jnp.bfloat16), "seq", split_axis=1, concat_axis=2, tiled=True
        ),
    )
    back_query = back_query.reshape(token_count, H * F)
    back_key = back_key.reshape(token_count, H * F)
    back_value = back_value.reshape(token_count, D)
    query_grad = weight_grad(normed_low, back_query)
    key_grad = weight_grad(normed_low, back_key)
    value_grad = weight_grad(normed_low, back_value)
    grad_normed = (
        back_project(back_query, w_query)
        + back_project(back_key, w_key)
        + back_project(back_value, w_value)
    )
    grad_stream, gain_attn_grad = attn_norm_back(grad_normed)
    input_grad = grad_residual + grad_stream
    (
        gain_attn_part,
        query_part,
        key_part,
        value_part,
        out_part,
        gain_ffn_part,
        gate_part,
        up_part,
        down_part,
    ) = (
        lax.psum_scatter(gain_attn_grad, ("dp", "seq"), scatter_dimension=0, tiled=True),
        lax.psum_scatter(query_grad, ("dp", "seq"), scatter_dimension=0, tiled=True),
        lax.psum_scatter(key_grad, ("dp", "seq"), scatter_dimension=0, tiled=True),
        lax.psum_scatter(value_grad, ("dp", "seq"), scatter_dimension=0, tiled=True),
        lax.psum_scatter(out_grad, ("dp", "seq"), scatter_dimension=0, tiled=True),
        lax.psum_scatter(gain_ffn_grad, ("dp", "seq"), scatter_dimension=0, tiled=True),
        lax.psum_scatter(gate_grad, ("dp", "seq"), scatter_dimension=0, tiled=True),
        lax.psum_scatter(up_grad, ("dp", "seq"), scatter_dimension=0, tiled=True),
        lax.psum_scatter(down_grad_t, ("dp", "seq"), scatter_dimension=0, tiled=True),
    )
    return (
        output.reshape(row_count, shard_len, D).astype(jnp.bfloat16),
        input_grad.reshape(row_count, shard_len, D).astype(jnp.bfloat16),
        gain_attn_part,
        query_part,
        key_part,
        value_part,
        out_part,
        gain_ffn_part,
        gate_part,
        up_part,
        jnp.transpose(down_part),
    )


F32 = jnp.float32
BF16 = jnp.bfloat16
MESH = pl.DeviceIdType.MESH
TILE = 384
PAIR = 2 * HV


def nt(left, right):
    return lax.dot_general(left, right, (((1,), (1,)), ((), ())), preferred_element_type=F32)


def nn(left, right):
    return jnp.dot(left, right, preferred_element_type=F32)


def lanes_of(shape):
    return lax.broadcasted_iota(jnp.int32, shape, len(shape) - 1)


def first_visible(ends, positions):
    start = jnp.zeros_like(positions)
    for end in ends:
        start = jnp.where(positions >= end, end, start)
    return start


def row_ends(doc_ref, row):
    ends, total = [], 0
    for j in range(doc_ref.shape[1] - 1):
        total = total + doc_ref[row, j]
        ends.append(total)
    return ends


def spread_matrix():
    half = H * F
    source = lax.broadcasted_iota(jnp.int32, (2 * half, 1), 0)
    column = lax.broadcasted_iota(jnp.int32, (1, (H // 2) * 128), 1)
    pair, lane = column // 128, column % 64
    wanted = pair * 32 + lane + jnp.where(lane < 32, 0, half - 32)
    return jnp.where(source == wanted, 1.0, 0.0).astype(BF16)


def gather_matrix():
    half = H * F
    source = lax.broadcasted_iota(jnp.int32, (2 * half, 1), 0)
    column = lax.broadcasted_iota(jnp.int32, (1, 2 * half), 1)
    pair, lane = source // 64, source % 64
    wanted = pair * 32 + lane + jnp.where(lane < 32, 0, half - 32)
    return jnp.where(column == wanted, 1.0, 0.0).astype(BF16)


def packed_rows(length):
    return (length // 2 + 15) // 16 * 16


def prepare_row(got_ref, row, qa_ref, ka_ref, ve_ref, seq_devices, length):
    low = packed_rows(length)

    def part(peer, carry):
        values = got_ref[row, peer, :length, :].astype(F32)
        packed = got_ref[row, peer, length : length + low, :].astype(F32)
        turned = pltpu.roll(packed, 64, 1)
        both = jnp.concatenate([packed, turned[2 * low - length :]], axis=0)
        lane = lanes_of((length, 128))
        keys = pltpu.roll(both, 96, 1)
        at = pl.ds(pl.multiple_of(peer * length, 16), length)
        one = jnp.where(lane == 32, 1.0, 0.0)
        qa_ref[at, :] = jnp.where(lane < 32, both * 0.25, one).astype(BF16)
        ka_ref[0, at, :] = jnp.where(lane < 16, keys, one).astype(BF16)
        ka_ref[1, at, :] = jnp.where((lane >= 16) & (lane < 32), keys, one).astype(BF16)
        ve_ref[0, at, :] = jnp.where(lane < 64, values, 1.0).astype(BF16)
        ve_ref[1, at, :] = jnp.where(lane >= 64, values, 1.0).astype(BF16)
        return carry

    lax.fori_loop(0, seq_devices, part, 0)


def attend_forward(ends, qa_ref, ka_ref, ve_ref, mixed_ref, inverse_ref):
    length = qa_ref.shape[0]
    for block in range(length // TILE):
        reach = (block + 1) * TILE
        at = pl.ds(block * TILE, TILE)
        queries = qa_ref[at, :]
        t = lax.broadcasted_iota(jnp.int32, (TILE, 1), 0) + block * TILE
        start = first_visible(ends, t)
        s = lax.broadcasted_iota(jnp.int32, (TILE, reach), 1)
        visible = (s >= start) & (s <= t)
        sums = []
        for head in range(2):
            base = nt(queries, ka_ref[head, :reach, :])
            weights = jnp.where(visible, base * base + 1.0, 0.0).astype(BF16)
            sums.append(nn(weights, ve_ref[head, :reach, :]))
        lower = lanes_of((TILE, 128)) < 64
        numerator = jnp.where(lower, sums[0], sums[1])
        inverse = 1.0 / pltpu.roll(jnp.where(lower, sums[1], sums[0]), 64, 1)
        mixed_ref[at, :] = (numerator * inverse).astype(BF16)
        inverse_ref[at, :] = inverse


def attend_backward(
    ends, grad_ref, qa_ref, ka_ref, ve_ref, mixed_ref, inverse_ref, dn_ref, qs_ref, kt_ref, dqt_ref, gqk_ref, gv_ref
):
    length = qa_ref.shape[0]
    lane = lanes_of((length, 128))
    lower = lane < 64
    scaled = grad_ref[...].astype(F32) * inverse_ref[...]
    away = pltpu.roll(-scaled * mixed_ref[...].astype(F32), 64, 1)
    dn_ref[0] = jnp.where(lower, scaled, away).astype(BF16)
    dn_ref[1] = jnp.where(lower, away, scaled).astype(BF16)
    shifted = pltpu.roll(qa_ref[...].astype(F32), 32, 1)
    qs_ref[...] = jnp.where((lane >= 32) & (lane < 64), shifted * 2.0, 0.0).astype(BF16)
    for head in range(2):
        kt_ref[head] = ka_ref[head].astype(F32).T[:32].astype(BF16)
    dqt_ref[...] = jnp.zeros_like(dqt_ref)
    for block in range(length // TILE):
        first = block * TILE
        at = pl.ds(first, TILE)
        rest = pl.ds(first, length - first)
        shape = (TILE, length - first)
        t = lax.broadcasted_iota(jnp.int32, (1, shape[1]), 1) + first
        s = lax.broadcasted_iota(jnp.int32, shape, 0) + first
        visible = (s >= first_visible(ends, t)) & (s <= t)
        value_sums, key_sums = [], []
        for head in range(2):
            base = nt(ka_ref[head, at, :], qa_ref[rest, :])
            grad_weights = nt(ve_ref[head, at, :], dn_ref[head, rest, :])
            weights = jnp.where(visible, base * base + 1.0, 0.0).astype(BF16)
            grad_base = jnp.where(visible, grad_weights * base, 0.0).astype(BF16)
            value_sums.append(nn(weights, dn_ref[head, rest, :]))
            key_sums.append(nn(grad_base, qs_ref[rest, :]))
            dqt_ref[:, rest] += nn(kt_ref[head, :, at], grad_base)
        lane = lanes_of((TILE, 128))
        gv_ref[at, :] = jnp.where(lane < 64, value_sums[0], value_sums[1]).astype(BF16)
        gqk_ref[at, :] = jnp.where(
            (lane >= 32) & (lane < 48), key_sums[0], jnp.where((lane >= 48) & (lane < 64), key_sums[1], 0.0)
        )
    queries = jnp.concatenate([dqt_ref[...] * 0.5, jnp.zeros((96, length), F32)], axis=0)
    gqk_ref[...] += queries.T


def sending(source, target, send_sem, recv_sem, row_group, peer):
    return pltpu.make_async_remote_copy(
        src_ref=source,
        dst_ref=target,
        send_sem=send_sem,
        recv_sem=recv_sem,
        device_id=(row_group, peer),
        device_id_type=MESH,
    )


VMEM_SPEC = pl.BlockSpec(memory_space=pltpu.VMEM)
SMEM_SPEC = pl.BlockSpec(memory_space=pltpu.SMEM)


CHUNK = 256
STEP_ROWS = 48
Z_UNITS = 5
SLOTS = 7
VMEM_BYTES = 63 << 20


def place(me):
    core = lax.rem(me, 2)
    return core, 2 + 2 * core, 4 - 2 * core


def blocks_of(core, groups):
    first, second = 2 + 2 * core, 4 - 2 * core
    return [
        pl.multiple_of(32 * (8 * group + first * i + second * j + core), 32)
        for i in range(2)
        for j in range(2)
        for group in (0, 2, 1, 3)[:groups]
    ]


class Reduction:
    def __init__(self, source, buffers, slot_of=None, place_of=None):
        self.source = source
        self.got_a, self.got_b, self.got_z, self.a_sems, self.b_sems, self.c_sems, self.d_sems = buffers
        self.slot_of = slot_of or (lambda unit: unit)
        self.place_of = place_of or (lambda unit: unit)
        self.group, self.me = lax.axis_index("dp"), lax.axis_index("seq")
        core, first, second = place(self.me)
        self.bit_a, self.bit_b = lax.rem(self.me // first, 2), lax.rem(self.me // second, 2)
        self.peer_a = self.me + first * (1 - 2 * self.bit_a)
        self.peer_b = self.me + second * (1 - 2 * self.bit_b)
        self.bit_c, self.bit_d = lax.rem(self.group, 2), self.group // 2
        self.group_c = self.group + 1 - 2 * self.bit_c
        self.group_d = self.group + 2 - 4 * self.bit_d

    def rows(self, bit_c, bit_d=None):
        if bit_d is None:
            return pl.ds(pl.multiple_of(64 * bit_c, 64), 64)
        return pl.ds(pl.multiple_of(64 * bit_c + 32 * bit_d, 32), 32)

    def a_copy(self, unit):
        at = self.place_of(unit)
        return sending(
            self.source.at[self.slot_of(unit), 1 - self.bit_a], self.got_a.at[at], self.a_sems.at[0, at],
            self.a_sems.at[1, at], self.group, self.peer_a,
        )

    def b_copy(self, unit):
        at = self.place_of(unit)
        return sending(
            self.got_a.at[at, 1 - self.bit_b], self.got_b.at[at], self.b_sems.at[0, at], self.b_sems.at[1, at],
            self.group, self.peer_b,
        )

    def c_copy(self, unit):
        at = self.place_of(unit)
        return sending(
            self.got_b.at[at, self.rows(1 - self.bit_c), :], self.got_z.at[at, pl.ds(0, 64), :],
            self.c_sems.at[0, at], self.c_sems.at[1, at], self.group_c, self.me,
        )

    def d_copy(self, unit):
        at = self.place_of(unit)
        return sending(
            self.got_b.at[at, self.rows(self.bit_c, 1 - self.bit_d), :], self.got_z.at[at, pl.ds(64, 32), :],
            self.d_sems.at[0, at], self.d_sems.at[1, at], self.group_d, self.me,
        )

    def a_step(self, unit):
        at = self.place_of(unit)
        self.a_copy(unit).wait_recv()
        mine = self.source[self.slot_of(unit), self.bit_a].astype(F32)
        self.got_a[at] = (mine + self.got_a[at].astype(F32)).astype(BF16)
        self.b_copy(unit).start()

    def b_step(self, unit):
        at = self.place_of(unit)
        self.b_copy(unit).wait_recv()
        self.got_b[at] = (self.got_a[at, self.bit_b].astype(F32) + self.got_b[at].astype(F32)).astype(BF16)
        self.c_copy(unit).start()

    def c_step(self, unit):
        at, mine = self.place_of(unit), self.rows(self.bit_c)
        self.c_copy(unit).wait_recv()
        self.got_b[at, mine, :] = (
            self.got_b[at, mine, :].astype(F32) + self.got_z[at, :64, :].astype(F32)
        ).astype(BF16)
        self.d_copy(unit).start()

    def d_step(self, unit):
        at = self.place_of(unit)
        self.d_copy(unit).wait_recv()
        return self.got_b[at, self.rows(self.bit_c, self.bit_d), :].astype(F32) + self.got_z[at, 64:, :].astype(F32)

    def wait_sent(self, unit):
        self.b_copy(unit).wait_send()
        self.c_copy(unit).wait_send()
        self.d_copy(unit).wait_send()


class GroupsFirst(Reduction):
    def c_copy(self, unit):
        at = self.place_of(unit)
        return sending(
            self.source.at[self.slot_of(unit), :, :, self.rows(1 - self.bit_c), :],
            self.got_z.at[at, :, :, pl.ds(0, 64), :],
            self.c_sems.at[0, at], self.c_sems.at[1, at], self.group_c, self.me,
        )

    def d_copy(self, unit):
        at = self.place_of(unit)
        block = pl.ds(pl.multiple_of(32 * (1 - self.bit_d), 32), 32)
        return sending(
            self.got_z.at[at, :, :, block, :], self.got_z.at[at, :, :, pl.ds(64, 32), :],
            self.d_sems.at[0, at], self.d_sems.at[1, at], self.group_d, self.me,
        )

    def a_copy(self, unit):
        at = self.place_of(unit)
        return sending(
            self.got_z.at[at, 1 - self.bit_a, :, pl.ds(64, 32), :], self.got_a.at[at],
            self.a_sems.at[0, at], self.a_sems.at[1, at], self.group, self.peer_a,
        )

    def c_step(self, unit):
        at = self.place_of(unit)
        self.c_copy(unit).wait_recv()
        mine = self.source[self.slot_of(unit), :, :, self.rows(self.bit_c), :].astype(F32)
        self.got_z[at, :, :, :64, :] = (mine + self.got_z[at, :, :, :64, :].astype(F32)).astype(BF16)
        self.d_copy(unit).start()

    def d_step(self, unit):
        at = self.place_of(unit)
        self.d_copy(unit).wait_recv()
        mine = self.got_z[at, :, :, pl.ds(pl.multiple_of(32 * self.bit_d, 32), 32), :].astype(F32)
        self.got_z[at, :, :, 64:, :] = (mine + self.got_z[at, :, :, 64:, :].astype(F32)).astype(BF16)
        self.a_copy(unit).start()

    def a_step(self, unit):
        at = self.place_of(unit)
        self.a_copy(unit).wait_recv()
        mine = self.got_z[at, self.bit_a, :, 64:, :].astype(F32)
        self.got_a[at] = (mine + self.got_a[at].astype(F32)).astype(BF16)
        self.b_copy(unit).start()

    def b_step(self, unit):
        at = self.place_of(unit)
        self.b_copy(unit).wait_recv()
        return self.got_a[at, self.bit_b].astype(F32) + self.got_b[at].astype(F32)

    def wait_sent(self, unit):
        for copy in (self.a_copy, self.b_copy, self.c_copy, self.d_copy):
            copy(unit).wait_send()


def reduction_buffers(units, cols):
    sems = pltpu.SemaphoreType.DMA((2, units))
    return [
        pltpu.VMEM((units, 2, 128, cols), BF16),
        pltpu.VMEM((units, 128, cols), BF16),
        pltpu.VMEM((units, 96, cols), BF16),
        sems, sems, sems, sems,
    ]


def groups_first_buffers(units, cols):
    sems = pltpu.SemaphoreType.DMA((2, units))
    return [
        pltpu.VMEM((units, 2, 32, cols), BF16),
        pltpu.VMEM((units, 32, cols), BF16),
        pltpu.VMEM((units, 2, 2, 96, cols), BF16),
        sems, sems, sems, sems,
    ]


def store_blocks(target, unit, col, values, groups):
    rows = 32 * groups
    for i in range(2):
        for j in range(2):
            at = (2 * i + j) * rows
            target[unit, i, j, :, col : col + values.shape[1]] = values[at : at + rows].astype(BF16)


def turn(source, tokens, padded, turned):
    turned[...] = jnp.concatenate([source, jnp.zeros((padded - tokens, D), BF16)], axis=0).T


def split_rows(turned, mine_ref, theirs_ref, core, groups):
    for i, (mine, theirs) in enumerate(zip(blocks_of(core, groups), blocks_of(1 - core, groups))):
        a, b, group = i // (2 * groups), i // groups % 2, i % groups
        mine_ref[a, b, group * 32 : (group + 1) * 32, :] = turned[pl.ds(mine, 32), :]
        theirs_ref[a, b, group * 32 : (group + 1) * 32, :] = turned[pl.ds(theirs, 32), :]


def write_unit(total, at, w, gate_out, up_out, down_out):
    down_out[:, pl.ds(at, w)] = total[:, :w]
    gate_out[:, pl.ds(at, w)] = total[:, CHUNK : CHUNK + w]
    up_out[:, pl.ds(at, w)] = total[:, 2 * CHUNK : 2 * CHUNK + w]


def block_kernel(
    groups, seq_devices, rows, length, width,
    x_ref, cot_ref, gain_ref, wo_ref, wg_hbm, wu_hbm, wd_hbm, doc_ref, gain_attn_ref, wq_ref, wk_ref, wv_hbm,
    output_ref, input_out, gate_out, up_out, down_out, wout_out, query_out, key_out, value_out, gains_out,
    branch, residual, normed, out_acc, gnf, w_buf, lhs, right, parts, parts_o, q_source,
    got, heads, inverse, arrived, back, qa, ka, ve, dn, qs, kt, dqt, gqk, gv, gains, gains_got,
    fsend_a, frecv_a, fsend_b, frecv_b, w_sem, wv_sems, lhs_sems, pair_sems, send_a, recv_a, send_b, recv_b, gain_send, gain_recv,
    *buffers,
):
    row_group, me = lax.axis_index("dp"), lax.axis_index("seq")
    core, _, _ = place(me)
    partner = me + 1 - 2 * core
    tokens = rows * length
    padded = right.shape[1] // 2
    full = width // CHUNK
    tail = width - full * CHUNK
    low = packed_rows(length)
    lower = lanes_of((low, 128)) < 64
    here = pl.ds(pl.multiple_of(me * length, 16), length)
    half = H * F

    def slot_of(unit):
        if isinstance(unit, int):
            return unit if unit < SLOTS else 2 * (unit - SLOTS)
        return jnp.where(unit < SLOTS, unit, 2 * (unit - SLOTS))

    def place_of(unit):
        if isinstance(unit, int):
            return unit // 2 if unit < 2 * Z_UNITS else unit - Z_UNITS
        return jnp.where(unit < 2 * Z_UNITS, unit // 2, unit - Z_UNITS)

    feed = Reduction(parts, buffers[:7], slot_of, place_of)
    outer = Reduction(parts_o, buffers[7:14])
    qkv = Reduction(q_source, buffers[14:21])
    first = GroupsFirst(parts, buffers[21:28], slot_of, lambda unit: unit // 2)

    barrier = pltpu.get_barrier_semaphore()
    for step in range(1, seq_devices):
        peer = lax.rem(me + step, seq_devices)
        pl.semaphore_signal(barrier, inc=1, device_id=(row_group, peer), device_id_type=MESH)
    for other in (feed.group_c, feed.group_d):
        pl.semaphore_signal(barrier, inc=1, device_id=(other, me), device_id_type=MESH)

    def loads(chunk, slot, w):
        at = pl.ds(pl.multiple_of(chunk * CHUNK, CHUNK), w)
        return [
            pltpu.make_async_copy(hbm.at[at, :], w_buf.at[slot, which, pl.ds(0, w), :], w_sem.at[slot, which])
            for which, hbm in enumerate((wg_hbm, wu_hbm, wd_hbm))
        ]

    def value_load(part):
        return pltpu.make_async_copy(
            wv_hbm.at[pl.ds(part * CHUNK, CHUNK), :], w_buf.at[part // 3, part % 3], wv_sems.at[part]
        )

    def lhs_send(which):
        return (q_source.at[0], q_source.at[1], parts_o.at[0])[which % 3].at[:, :, :, pl.ds(0, padded)]

    def lhs_copy(which):
        return sending(
            lhs_send(which),
            lhs.at[which % 3, :, :, :, pl.ds(padded, padded)],
            lhs_sems.at[0, which], lhs_sems.at[1, which], row_group, partner,
        )

    def prepare_lhs(which, source):
        turned = right.at[3 if which < 2 else 1, :, pl.ds(0, padded)]
        turn(source, tokens, padded, turned)
        split_rows(turned, lhs.at[which % 3, :, :, :, pl.ds(0, padded)], lhs_send(which), core, groups)

    def left(which):
        return lhs[which].reshape(D // 2, 2 * padded)

    gap = padded - tokens

    def clear(slot, count):
        for base in (tokens, padded + tokens):
            right[slot : slot + count, base : base + gap, :] = jnp.zeros((count, gap, 3 * CHUNK), BF16)

    for part in range(D // CHUNK):
        value_load(part).start()
    spread = [right.at[1 + part, pl.ds(0, 2 * half), pl.ds(0, D // 2)] for part in range(2)]
    whole = spread_matrix()
    for part in range(2):
        spread[part][...] = whole[:, part * D // 2 : (part + 1) * D // 2]
    pl.semaphore_wait(barrier, seq_devices + 1)
    for part in range(D // CHUNK):
        value_load(part).wait()

    def spreading(row, step):
        peer = lax.rem(me + step, seq_devices)
        return sending(
            back.at[row, peer], got.at[row, me], fsend_a.at[row, step], frecv_a.at[row, step], row_group, peer
        )

    def merging(row, step):
        peer = lax.rem(me + step, seq_devices)
        there = pl.ds(pl.multiple_of(peer * length, 16), length)
        mine = pl.ds(pl.multiple_of(me * PAIR, 128), PAIR)
        at = pl.ds(pl.multiple_of(row * length, 16), length)
        return sending(
            heads.at[row, there, :], branch.at[at, mine], fsend_b.at[row, step], frecv_b.at[row, step],
            row_group, peer,
        )

    def project_row(row, carry):
        at = pl.ds(pl.multiple_of(row * length, 16), length)
        low_row = rms_scale(x_ref[at, :].astype(F32), gain_attn_ref[...]).astype(BF16)
        both = jnp.concatenate([nn(low_row, wq_ref[...]), nn(low_row, wk_ref[...])], axis=1).astype(BF16)
        sides = [nn(both, spread[part][...]) for part in range(2)]
        values = sum(
            nn(low_row[:, part * CHUNK : (part + 1) * CHUNK], w_buf[part // 3, part % 3])
            for part in range(D // CHUNK)
        ).astype(BF16)
        for pair in range(seq_devices):
            side, col = divmod(pair * 128, D // 2)
            tile = sides[side][:, col : col + 128]
            back[row, pair, :length, :] = values[:, pair * PAIR : (pair + 1) * PAIR]
            back[row, pair, length:, :] = jnp.where(lower, tile[:low], tile[length - low :]).astype(BF16)
        got[row, me] = back[row, me]

        @pl.when(row == 0)
        def _():
            send_spread(0)

        return carry

    def send_spread(row):
        for step in range(1, seq_devices):
            spreading(row, step).start()

    lax.fori_loop(0, rows, project_row, 0)
    send_spread(1)
    for chunk in range(2):
        for copy in loads(chunk, chunk, CHUNK):
            copy.start()
    prepare_lhs(0, cot_ref[...])
    lhs_copy(0).start()

    gnf[...] = jnp.zeros_like(gnf)
    clear(0, 3)

    def residual_row(row):
        for step in range(1, seq_devices):
            merging(row, step).wait_recv()
        at = pl.ds(pl.multiple_of(row * length, 16), length)
        value = x_ref[at, :].astype(F32) + nn(branch[at, :], wo_ref[...])
        residual[at, :] = value
        out_acc[at, :] = value
        normed[at, :] = rms_scale(value, gain_ref[...]).astype(BF16)

    def attend_rows(row, carry):
        for step in range(1, seq_devices):
            spreading(row, step).wait()

        @pl.when(row + 2 < rows)
        def _():
            send_spread(row + 2)

        prepare_row(got, row, qa, ka, ve, seq_devices, length)
        attend_forward(row_ends(doc_ref, row), qa, ka, ve, heads.at[row], inverse.at[row])
        for step in range(1, seq_devices):
            merging(row, step).start()
        at = pl.ds(pl.multiple_of(row * length, 16), length)
        branch[at, pl.ds(pl.multiple_of(me * PAIR, 128), PAIR)] = heads[row, here, :]
        return carry

    lax.fori_loop(0, rows, attend_rows, 0)

    for row in range(rows):
        residual_row(row)
    prepare_lhs(1, normed[...])
    lhs_copy(1).start()
    clear(3, 1)

    def right_copy(slot, cols, sem):
        return sending(
            right.at[slot, pl.ds(0, tokens), pl.ds(0, cols)], right.at[slot, pl.ds(padded, tokens), pl.ds(0, cols)],
            pair_sems.at[0, sem], pair_sems.at[1, sem], row_group, partner,
        )

    def pair_copy(chunk):
        return right_copy(lax.rem(chunk, 4), 3 * CHUNK, chunk)

    def forward_part(chunk, wg, wu, wd, w):
        slot = lax.rem(chunk, 4)
        gate = nt(normed[...], wg)
        up = nt(normed[...], wu)
        sigmoid = 1.0 / (1.0 + jnp.exp(-gate))
        silu = gate * sigmoid
        hidden = (silu * up).astype(BF16)
        grad_hidden = nt(cot_ref[...], wd)
        grad_gate = (grad_hidden * up * (sigmoid * (1.0 + gate * (1.0 - sigmoid)))).astype(BF16)
        grad_up = (grad_hidden * silu).astype(BF16)
        for part, values in enumerate((hidden, grad_gate, grad_up)):
            right[slot, :tokens, part * CHUNK : part * CHUNK + w] = values
            if w < CHUNK:
                right[slot, :tokens, part * CHUNK + w : (part + 1) * CHUNK] = jnp.zeros((tokens, CHUNK - w), BF16)
        pair_copy(chunk).start()
        out_acc[...] += nn(hidden, wd)
        gnf[...] += nn(grad_gate, wg) + nn(grad_up, wu)

    def grad_part(chunk):
        pair_copy(chunk).wait()
        slot = lax.rem(chunk, 4)
        store_blocks(parts, slot_of(chunk), 0, nn(left(0), right[slot, :, 0:CHUNK]), groups)
        store_blocks(parts, slot_of(chunk), CHUNK, nn(left(1), right[slot, :, CHUNK:]), groups)

    def forward_step(chunk):
        slot = lax.rem(chunk, 2)
        for copy in loads(chunk, slot, CHUNK):
            copy.wait()
        forward_part(chunk, w_buf[slot, 0], w_buf[slot, 1], w_buf[slot, 2], CHUNK)

    def ticks(chunk):
        @pl.when((chunk >= 3) & (lax.rem(chunk, 2) == 1))
        def _():
            feed.a_step(chunk - 3)

        @pl.when((chunk >= 5) & (lax.rem(chunk, 2) == 1))
        def _():
            feed.b_step(chunk - 5)

        @pl.when(chunk == 8)
        def _():
            first.c_step(1)

    def fetch_next(chunk):
        @pl.when(chunk < full - 1)
        def _():
            for copy in loads(chunk + 1, lax.rem(chunk + 1, 2), CHUNK):
                copy.start()

        @pl.when(chunk == full - 1)
        def _():
            for copy in loads(full, full % 2, tail):
                copy.start()

    def main(chunk, carry):
        fetch_next(chunk)
        forward_step(chunk)
        unit = chunk - 1

        @pl.when(unit >= SLOTS)
        def _():
            feed.a_copy(2 * (unit - SLOTS)).wait_send()

        grad_part(unit)
        along_z = (unit < 2 * Z_UNITS) & (lax.rem(unit, 2) == 1)

        @pl.when(along_z)
        def _():
            first.c_copy(unit).start()

        @pl.when(jnp.logical_not(along_z) & (unit < 10))
        def _():
            feed.a_copy(unit).start()

        ticks(chunk)
        return carry

    forward_step(0)
    for which in range(2):
        lhs_copy(which).wait()
    lax.fori_loop(1, full, main, 0)
    slot = full % 2
    for copy in loads(full, slot, tail):
        copy.wait()
    forward_part(full, w_buf[slot, 0, :tail], w_buf[slot, 1, :tail], w_buf[slot, 2, :tail], tail)
    for part in range(D // CHUNK):
        value_load(part).start()
    feed.a_copy(2 * (full - 1 - SLOTS)).wait_send()
    grad_part(full - 1)
    first.c_copy(full - 1).start()

    gains[...] = jnp.zeros_like(gains)

    def norm_backward_ffn(step, carry):
        at = pl.ds(pl.multiple_of(step * STEP_ROWS, 16), STEP_ROWS)
        value, grad = residual[at, :], gnf[at, :]
        scale = lax.rsqrt(jnp.mean(value * value, axis=-1, keepdims=True) + eps_norm)
        gains[0:1, :] += jnp.sum(grad * value * scale, axis=0, keepdims=True)
        weighted = grad * gain_ref[...]
        mean = jnp.mean(weighted * value, axis=-1, keepdims=True)
        total = cot_ref[at, :].astype(F32) + scale * weighted - value * (scale * scale * scale * mean)
        gnf[at, :] = total
        right[3, at, :] = total[:, : 3 * CHUNK].astype(BF16)
        right[0, at, :CHUNK] = total[:, 3 * CHUNK :].astype(BF16)
        output_ref[at, :] = out_acc[at, :].astype(BF16)
        return carry

    lax.fori_loop(0, tokens // STEP_ROWS, norm_backward_ffn, 0)
    normed[...] = (
        nt(right[3, :tokens, :], wo_ref[:, : 3 * CHUNK]) + nt(right[0, :tokens, :CHUNK], wo_ref[:, 3 * CHUNK :])
    ).astype(BF16)

    def outgoing(row, step):
        peer = lax.rem(me + step, seq_devices)
        theirs = pl.ds(pl.multiple_of(peer * PAIR, 128), PAIR)
        at = pl.ds(pl.multiple_of(row * length, 16), length)
        return sending(
            normed.at[at, theirs], arrived.at[row, here, :], send_a.at[row, step], recv_a.at[row, step],
            row_group, peer,
        )

    def returning(row, step):
        peer = lax.rem(me + step, seq_devices)
        return sending(
            got.at[row, peer], back.at[row, me], send_b.at[row, step], recv_b.at[row, step], row_group, peer
        )

    def send_row(row, carry):
        for step in range(1, seq_devices):
            outgoing(row, step).start()
        at = pl.ds(pl.multiple_of(row * length, 16), length)
        arrived[row, here, :] = normed[at, pl.ds(pl.multiple_of(me * PAIR, 128), PAIR)]
        return carry

    send_row(0, 0)
    feed.a_copy(2 * (full - SLOTS)).wait_send()
    grad_part(full)
    send_row(1, 0)
    out_pairs = [right_copy(3, 3 * CHUNK, full + 1), right_copy(0, CHUNK, full + 2)]
    for copy in out_pairs:
        copy.start()
    prepare_lhs(2, branch[...])
    lhs_copy(2).start()
    feed.b_step(6)
    first.c_step(3)
    feed.a_step(8)
    feed.c_step(0)
    for row in range(2, rows):
        send_row(row, 0)
    prepare_lhs(3, rms_scale(x_ref[...].astype(F32), gain_attn_ref[...]).astype(BF16))
    clear(1, 1)
    for copy in out_pairs:
        copy.wait()
    lhs_copy(3).start()
    lhs_copy(2).wait()
    for col in range(0, D, CHUNK):
        columns = right[3, :, col : col + CHUNK] if col < 3 * CHUNK else right[0, :, :CHUNK]
        store_blocks(parts_o, 0, col, nn(left(2), columns), groups)
    gather = right.at[3, pl.ds(0, 2 * half), pl.ds(0, 2 * half)]
    gather[...] = gather_matrix()

    def attend(row, carry):
        prepare_row(got, row, qa, ka, ve, seq_devices, length)
        for step in range(1, seq_devices):
            outgoing(row, step).wait_recv()
        attend_backward(
            row_ends(doc_ref, row), arrived.at[row], qa, ka, ve, heads.at[row], inverse.at[row],
            dn, qs, kt, dqt, gqk, gv,
        )

        def pack(peer, inner):
            at = pl.multiple_of(peer * length, 16)
            got[row, peer, :length, :] = gv[pl.ds(at, length), :]
            front = gqk[pl.ds(at, low), :]
            rear = pltpu.roll(gqk[pl.ds(at + length - low, low), :], 64, 1)
            got[row, peer, length:, :] = jnp.where(lower, front, rear).astype(BF16)
            return inner

        lax.fori_loop(0, seq_devices, pack, 0)
        for step in range(1, seq_devices):
            returning(row, step).start()
        back[row, me] = got[row, me]

        @pl.when(row == 0)
        def _():
            feed.a_copy(10).start()
            first.c_step(5)

        @pl.when(row == 1)
        def _():
            outer.a_copy(0).start()
            feed.c_step(2)
            first.c_step(7)
            first.d_step(1)

        @pl.when(row == 2)
        def _():
            first.d_step(3)
            feed.b_step(8)

        return carry

    lax.fori_loop(0, rows, attend, 0)
    feed.c_step(4)
    first.c_step(9)
    first.d_step(5)
    feed.a_step(10)

    def unpack(row, carry):
        for step in range(1, seq_devices):
            outgoing(row, step).wait_send()
            returning(row, step).wait()
        tiles = []
        for pair in range(0, seq_devices, 2):
            halves = []
            for one in (pair, pair + 1):
                packed = back[row, one, length:, :].astype(F32)
                turned_over = pltpu.roll(packed, 64, 1)
                straight, other = (packed, turned_over) if one == pair else (turned_over, packed)
                halves.append(jnp.concatenate([straight, other[2 * low - length :]], axis=0))
            tiles.append(jnp.where(lanes_of((length, 128)) < 64, halves[0], halves[1]).astype(BF16))
        at = pl.ds(pl.multiple_of(row * length, 16), length)
        right[1, at, : 2 * half] = nn(jnp.concatenate(tiles, axis=1), gather[...]).astype(BF16)
        for pair in range(seq_devices):
            slot, col = divmod(2 * half + pair * PAIR, 3 * CHUNK)
            right[1 + slot, at, col : col + PAIR] = back[row, pair, :length, :]
        return carry

    lax.fori_loop(0, rows, unpack, 0)
    q_pairs = [right_copy(1, 3 * CHUNK, full + 3), right_copy(2, 3 * CHUNK, full + 4)]
    for copy in q_pairs:
        copy.start()
    for part in range(D // CHUNK):
        value_load(part).wait()
    q_and_k = nt(right[1, :tokens, :half], wq_ref[...]) + nt(right[1, :tokens, half : 2 * half], wk_ref[...])
    for part in range(D // CHUNK):
        at = slice(part * CHUNK, (part + 1) * CHUNK)
        block = w_buf[part // 3, part % 3]
        out_acc[:, at] = (
            q_and_k[:, at]
            + nt(right[1, :tokens, 2 * half :], block[:, : 3 * CHUNK - 2 * half])
            + nt(right[2, :tokens, :], block[:, 3 * CHUNK - 2 * half :])
        )
    lhs_copy(3).wait()
    for copy in q_pairs:
        copy.wait()
    for unit in range(2):
        for col in range(0, 3 * CHUNK, CHUNK):
            store_blocks(q_source, unit, col, nn(left(0), right[1 + unit, :, col : col + CHUNK]), groups)
        qkv.a_copy(unit).start()

    def norm_backward(step, carry):
        at = pl.ds(pl.multiple_of(step * STEP_ROWS, 16), STEP_ROWS)
        value, grad = x_ref[at, :].astype(F32), out_acc[at, :]
        scale = lax.rsqrt(jnp.mean(value * value, axis=-1, keepdims=True) + eps_norm)
        gains[1:2, :] += jnp.sum(grad * value * scale, axis=0, keepdims=True)
        weighted = grad * gain_attn_ref[...]
        mean = jnp.mean(weighted * value, axis=-1, keepdims=True)
        total = gnf[at, :] + scale * weighted - value * (scale * scale * scale * mean)
        input_out[at, :] = total.astype(BF16)
        return carry

    lax.fori_loop(0, tokens // STEP_ROWS, norm_backward, 0)

    def gain_copy(step, target_group, target):
        return sending(
            gains, gains_got.at[step], gain_send.at[step], gain_recv.at[step], target_group, target
        )

    gain_copies = [
        gain_copy(0, row_group, partner),
        gain_copy(1, row_group, feed.peer_a),
        gain_copy(2, row_group, feed.peer_b),
        gain_copy(3, feed.group_c, me),
        gain_copy(4, feed.group_d, me),
    ]

    def gain_step(step):
        gain_copies[step].wait()
        gains[...] += gains_got[step]
        if step < 4:
            gain_copies[step + 1].start()

    def write_feed(unit, total, w):
        at = unit * CHUNK if isinstance(unit, int) else pl.multiple_of(unit * CHUNK, CHUNK)
        write_unit(total, at, w, gate_out, up_out, down_out)

    gain_copies[0].start()
    outer.a_step(0)
    feed.b_step(10)
    gain_step(0)
    first.d_step(7)
    feed.c_step(6)
    first.a_step(1)
    feed.c_step(8)
    gain_step(1)
    qkv.a_step(0)
    first.a_step(3)
    qkv.a_step(1)
    outer.b_step(0)
    gain_step(2)
    qkv.b_step(0)
    feed.c_step(10)
    first.a_step(5)
    qkv.b_step(1)
    gain_step(3)
    qkv.c_step(0)
    first.d_step(9)
    outer.c_step(0)
    qkv.c_step(1)
    first.a_step(7)
    gain_step(4)
    first.a_step(9)
    for unit in range(full):
        if unit >= 2 * Z_UNITS or unit % 2 == 0:
            write_feed(unit, feed.d_step(unit), CHUNK)
    write_feed(full, feed.d_step(full), tail)
    for unit in range(1, 2 * Z_UNITS, 2):
        write_feed(unit, first.b_step(unit), CHUNK)
    picked = lax.broadcasted_iota(jnp.int32, (D, 128), 0) == 32 * (seq_devices * row_group + me) + lanes_of((D, 128))
    gains_out[...] = jnp.dot(
        gains[...], jnp.where(picked, 1.0, 0.0), precision=lax.Precision.HIGHEST, preferred_element_type=F32
    )
    wout_out[...] = outer.d_step(0)
    total = qkv.d_step(0)
    query_out[...] = total[:, :half]
    key_out[...] = total[:, half : 2 * half]
    value_out[:, : 3 * CHUNK - 2 * half] = total[:, 2 * half :]
    value_out[:, 3 * CHUNK - 2 * half :] = qkv.d_step(1)

    for unit in range(full + 1):
        if unit < 2 * Z_UNITS and unit % 2 == 1:
            first.wait_sent(unit)
        else:
            feed.wait_sent(unit)
            if unit > 2 * (full - SLOTS):
                feed.a_copy(unit).wait_send()
    def forward_sent(row, carry):
        for step in range(1, seq_devices):
            merging(row, step).wait_send()
        return carry

    lax.fori_loop(0, rows, forward_sent, 0)
    for one, unit in ((outer, 0), (qkv, 0), (qkv, 1)):
        one.wait_sent(unit)
        one.a_copy(unit).wait_send()


ANY_SPEC = pl.BlockSpec(memory_space=pl.ANY)


def block_step(
    groups, seq_devices, x, cotangent, gain_ffn, w_out, w_gate_t, w_up_t, w_down, doc_lengths, gain_attn,
    w_query, w_key, w_value,
):
    tokens = x.shape[0]
    rows = doc_lengths.shape[0]
    length = tokens // rows
    total = seq_devices * length
    width = w_down.shape[0]
    full = width // CHUNK
    padded = (tokens + 127) // 128 * 128
    unit_rows = 32 * groups
    message = (rows, seq_devices, length + packed_rows(length), 128)
    dma = pltpu.SemaphoreType.DMA
    sems = dma((rows, seq_devices))
    return pl.pallas_call(
        functools.partial(block_kernel, groups, seq_devices, rows, length, width),
        name="block",
        out_shape=[
            jax.ShapeDtypeStruct((tokens, D), BF16),
            jax.ShapeDtypeStruct((tokens, D), BF16),
            jax.ShapeDtypeStruct((32, width), F32),
            jax.ShapeDtypeStruct((32, width), F32),
            jax.ShapeDtypeStruct((32, width), F32),
            jax.ShapeDtypeStruct((32, D), F32),
            jax.ShapeDtypeStruct((32, H * F), F32),
            jax.ShapeDtypeStruct((32, H * F), F32),
            jax.ShapeDtypeStruct((32, D), F32),
            jax.ShapeDtypeStruct((8, 128), F32),
        ],
        in_specs=[VMEM_SPEC] * 4 + [ANY_SPEC] * 3 + [SMEM_SPEC] + [VMEM_SPEC] * 3 + [ANY_SPEC],
        out_specs=[VMEM_SPEC] * 10,
        scratch_shapes=[
            pltpu.VMEM((tokens, D), BF16),
            pltpu.VMEM((tokens, D), F32),
            pltpu.VMEM((tokens, D), BF16),
            pltpu.VMEM((tokens, D), F32),
            pltpu.VMEM((tokens, D), F32),
            pltpu.VMEM((2, 3, CHUNK, D), BF16),
            pltpu.VMEM((3, 2, 2, unit_rows, 2 * padded), BF16),
            pltpu.VMEM((4, 2 * padded, 3 * CHUNK), BF16),
            pltpu.VMEM((SLOTS, 2, 2, unit_rows, 3 * CHUNK), BF16),
            pltpu.VMEM((1, 2, 2, unit_rows, D), BF16),
            pltpu.VMEM((2, 2, 2, unit_rows, 3 * CHUNK), BF16),
            pltpu.VMEM(message, BF16),
            pltpu.VMEM((rows, total, 128), BF16),
            pltpu.VMEM((rows, total, 128), F32),
            pltpu.VMEM((rows, total, 128), BF16),
            pltpu.VMEM(message, BF16),
            pltpu.VMEM((total, 128), BF16),
            pltpu.VMEM((2, total, 128), BF16),
            pltpu.VMEM((2, total, 128), BF16),
            pltpu.VMEM((2, total, 128), BF16),
            pltpu.VMEM((total, 128), BF16),
            pltpu.VMEM((2, 32, total), BF16),
            pltpu.VMEM((32, total), F32),
            pltpu.VMEM((total, 128), F32),
            pltpu.VMEM((total, 128), BF16),
            pltpu.VMEM((8, D), F32),
            pltpu.VMEM((5, 8, D), F32),
            sems, sems, sems, sems, dma((2, 3)), dma((D // CHUNK,)), dma((2, 4)), dma((2, full + 5)),
            sems, sems, sems, sems, dma((5,)), dma((5,)),
        ]
        + reduction_buffers(full + 1 - Z_UNITS, 3 * CHUNK)
        + reduction_buffers(1, D)
        + reduction_buffers(2, 3 * CHUNK)
        + groups_first_buffers(Z_UNITS, 3 * CHUNK),
        compiler_params=pltpu.CompilerParams(collective_id=1, has_side_effects=True, vmem_limit_bytes=VMEM_BYTES),
    )(
        x, cotangent, gain_ffn.reshape(1, D), w_out, w_gate_t, w_up_t, w_down, doc_lengths,
        gain_attn.reshape(1, D), w_query, w_key, w_value,
    )


def publish(results, gains):
    def kernel(*refs):
        count = len(results)
        for source, target in zip(refs[:count], refs[count + 1 : 2 * count + 1]):
            target[...] = source[...]
        refs[2 * count + 1][...] = refs[count][1:2, :32]
        refs[2 * count + 2][...] = refs[count][0:1, :32]

    one = jax.ShapeDtypeStruct((1, 32), F32)
    return pl.pallas_call(
        kernel,
        name="publish",
        out_shape=[jax.ShapeDtypeStruct(x.shape, x.dtype) for x in results] + [one, one],
        in_specs=[VMEM_SPEC] * (len(results) + 1),
        out_specs=[VMEM_SPEC] * (len(results) + 2),
        compiler_params=pltpu.CompilerParams(vmem_limit_bytes=VMEM_BYTES),
    )(*results, gains)


def tuned_body(
    seq_devices, groups, inputs, doc_lengths, gain_attn, w_query, w_key, w_value, w_out, gain_ffn, w_gate, w_up,
    w_down, cotangent,
):
    row_count, shard_len, _ = inputs.shape
    token_count = row_count * shard_len
    output, input_grad, gate, up, down, out, query, key, value, gains = block_step(
        groups, seq_devices, inputs.reshape(token_count, D), cotangent.reshape(token_count, D), gain_ffn, w_out,
        w_gate.T, w_up.T, w_down, doc_lengths, gain_attn, w_query, w_key, w_value,
    )
    output, input_grad, gate, up, down, out, query, key, value, gain_attn_part, gain_ffn_part = publish(
        (output, input_grad, gate, up, down, out, query, key, value), gains
    )
    return (
        output.reshape(row_count, shard_len, D),
        input_grad.reshape(row_count, shard_len, D),
        gain_attn_part.reshape(32),
        query,
        key,
        value,
        out,
        gain_ffn_part.reshape(32),
        gate,
        up,
        down.T,
    )


def solution(mesh):
    in_specs = (
        P("dp", "seq", None),
        P("dp", None),
        P(),
        P(),
        P(),
        P(),
        P(),
        P(),
        P(),
        P(),
        P(),
        P("dp", "seq", None),
    )
    out_specs = (
        P("dp", "seq", None),
        P("dp", "seq", None),
        P(("dp", "seq")),
        P(("dp", "seq"), None),
        P(("dp", "seq"), None),
        P(("dp", "seq"), None),
        P(("dp", "seq"), None),
        P(("dp", "seq")),
        P(("dp", "seq"), None),
        P(("dp", "seq"), None),
        P(None, ("dp", "seq")),
    )
    seq_devices, groups = mesh.shape["seq"], mesh.shape["dp"]
    tuned = seq_devices == 8 and seq_devices * groups * 32 == D
    step = functools.partial(tuned_body, seq_devices, groups) if tuned else general_body
    return jax.shard_map(step, mesh=mesh, in_specs=in_specs, out_specs=out_specs, check_vma=False)
```
